32 devices in a mesh: dp: 8 (over y, x, core), fsdp: 4 (over z).
Axes of the slice: x: 2, y: 2, z: 4, core: 2. Of those that a mesh axis runs over, the one named last changes fastest.
Arguments:
- hidden_in: bfloat16 [8192, 2048], P(('dp', 'fsdp')), may hold values from -6 to 6
- piece_starts: int32 [8, 2], P('dp'), may hold values from 0 to 768, as said below
- out_cotangent: bfloat16 [8192, 2048], P(('dp', 'fsdp')), may hold values from -6 to 6
- owners: int32 [1856], replicated, may hold values from 0 to 31, as said below
- master: float32 [2432, 16, 2048], P(('dp', 'fsdp'))
- moment_one: float32 [2432, 16, 2048], P(('dp', 'fsdp'))
- moment_two: float32 [2432, 16, 2048], P(('dp', 'fsdp')), as said below
- gain_master: float32 [2, 2048], P(None, ('dp', 'fsdp')), may hold values from 0.5 to 1.5
- gain_one: float32 [2, 2048], P(None, ('dp', 'fsdp'))
- gain_two: float32 [2, 2048], P(None, ('dp', 'fsdp')), as said below
Outputs:
- block_out: bfloat16 [8192, 2048], P(('dp', 'fsdp'))
- input_grad: float32 [8192, 2048], P(('dp', 'fsdp'))
- weight_grad: float32 [2432, 16, 2048], P(('dp', 'fsdp'))
- new_master: float32 [2432, 16, 2048], P(('dp', 'fsdp'))
- new_moment_one: float32 [2432, 16, 2048], P(('dp', 'fsdp'))
- new_moment_two: float32 [2432, 16, 2048], P(('dp', 'fsdp'))
- gain_grad: float32 [2, 2048], P(None, ('dp', 'fsdp'))
- new_gains: float32 [2, 2048], P(None, ('dp', 'fsdp'))
- new_gain_one: float32 [2, 2048], P(None, ('dp', 'fsdp'))
- new_gain_two: float32 [2, 2048], P(None, ('dp', 'fsdp'))
The draws below stay inside these ranges and needn't reach their ends.
Inputs may be any that keep to these rules, and one draw needn't show every extreme that they name: `owners`: within each of the four groups of tiles a device owns at most 8, 6, 41 or 21 tiles of that group, and some device owns exactly that many. `piece_starts`: piece c of a sequence lies within positions c * 512 to (c + 1) * 512 - 1; pieces don't intersect. `moment_two`: positive in every entry. `gain_two`: positive in every entry.
All inputs are finite; a program needn't handle non-finite values.
Results may differ from the reference program's by a relative error of at most 0.015.
The reference program's roundings to bfloat16 on the way count: a program that leaves them out, or rounds other values in their place, can miss the bound.
Values may be sent and summed in bfloat16 or wider, within the bound.
A program may use at most 704 MiB of HBM per device.

```python
import math
import jax
import jax.numpy as jnp
from jax import lax

D = 2048
HEADS = 32
KV_HEADS = 8
HEAD = 64
FF = 8192
SEQ_LEN = 1024
PIECE = 256
TR = 16
STEP = 5
SEQS = 8
TOKENS = 8192
PIECES = 2
TILES_A = 192
TILES_B = 128
TILES_C = 1024
TILES_D = 512
TILES = 1856
CAP_A = 8
CAP_B = 6
CAP_C = 41
CAP_D = 21
CAPS = 76
N_DP = 8
N_FSDP = 4


def section_owners(key, number, capacity):
    slot_total = N_DP * N_FSDP * capacity
    shuffled = jax.random.permutation(key, slot_total)
    lead_device = shuffled[0] // capacity
    slot_ids = jnp.arange(slot_total, dtype=jnp.int32)
    placing = jnp.argsort(shuffled).astype(jnp.int32)
    priority = jnp.where(slot_ids // capacity == lead_device, slot_ids % capacity - capacity, placing)
    ordered = jnp.argsort(priority)
    chosen = ordered[:number]
    mixed = chosen[jax.random.permutation(jax.random.fold_in(key, 7), number)]
    return (mixed // capacity).astype(jnp.int32)


def draw_owners(key, part):
    return jnp.concatenate([section_owners(jax.random.fold_in(key, 1), TILES_A, CAP_A), section_owners(jax.random.fold_in(key, 2), TILES_B, CAP_B), section_owners(jax.random.fold_in(key, 3), TILES_C, CAP_C), section_owners(jax.random.fold_in(key, 4), TILES_D, CAP_D)]).astype(jnp.int32)


def slot_factor(first_a, second_b, third_c, fourth_d):
    slot_total = N_DP * N_FSDP * CAPS
    within = jnp.arange(slot_total, dtype=jnp.int32) % CAPS
    return jnp.where(within < CAP_A, first_a, jnp.where(within < CAP_A + CAP_B, second_b, jnp.where(within < CAP_A + CAP_B + CAP_C, third_c, fourth_d))).astype(jnp.float32)


def draw_master(key, part):
    slot_total = N_DP * N_FSDP * CAPS
    factor = slot_factor(1.2 / math.sqrt(D), 5.0 / math.sqrt(D), 1.0 / math.sqrt(D), 2.0 / math.sqrt(FF))
    values = jax.random.normal(key, (slot_total, TR, D), jnp.float32)
    return (values * factor[:, None, None]).astype(jnp.float32)


def draw_moment_one(key, part):
    key = jax.random.fold_in(key, 11)
    slot_total = N_DP * N_FSDP * CAPS
    factor = slot_factor(1.0, 0.3, 1.2, 0.6) * math.sqrt(TOKENS)
    values = jax.random.truncated_normal(key, -4.0, 4.0, (slot_total, TR, D), jnp.float32)
    return (values * factor[:, None, None]).astype(jnp.float32)


def draw_moment_two(key, part):
    key = jax.random.fold_in(key, 12)
    slot_total = N_DP * N_FSDP * CAPS
    factor = slot_factor(1.0, 0.09, 1.44, 0.36) * (2.0 * TOKENS)
    spread = jnp.exp(jax.random.uniform(key, (slot_total, TR, D), jnp.float32, math.log(0.5), math.log(2.0)))
    return (spread * factor[:, None, None]).astype(jnp.float32)


def draw_gain_one(key, part):
    key = jax.random.fold_in(key, 13)
    values = jax.random.truncated_normal(key, -4.0, 4.0, (2, D), jnp.float32)
    return (values * (3.0 * math.sqrt(TOKENS))).astype(jnp.float32)


def draw_gain_two(key, part):
    key = jax.random.fold_in(key, 14)
    spread = jnp.exp(jax.random.uniform(key, (2, D), jnp.float32, math.log(0.5), math.log(2.0)))
    return (spread * (18.0 * TOKENS)).astype(jnp.float32)


def draw_piece_starts(key, part):
    span = SEQ_LEN // PIECES
    offsets = jax.random.randint(jax.random.fold_in(key, 1), (SEQS, PIECES), 0, span - PIECE + 1)
    high_seq = jax.random.randint(jax.random.fold_in(key, 2), (), 0, SEQS)
    low_seq = jax.random.randint(jax.random.fold_in(key, 3), (), 0, SEQS)
    seq_ids = jnp.arange(SEQS, dtype=jnp.int32)[:, None]
    piece_ids = jnp.arange(PIECES, dtype=jnp.int32)[None, :]
    offsets = jnp.where((seq_ids == high_seq) & (piece_ids == PIECES - 1), span - PIECE, offsets)
    offsets = jnp.where((seq_ids == low_seq) & (piece_ids == 0), 0, offsets)
    return (piece_ids * span + offsets).astype(jnp.int32)


def shard_levels(own_key, shape, shards, least, largest):
    factor_of, own = 1.0, jax.random.fold_in(own_key, 6)
    for position, shards_of in shards:
        steps = jnp.exp(jax.random.uniform(jax.random.fold_in(own, position), (shards_of,), jnp.float32, least / len(shards), largest / len(shards)))
        factor_of = factor_of * jnp.repeat(steps, shape[position] // shards_of).reshape([-1 if axis == position else 1 for axis in range(len(shape))])
    return factor_of


def normal_values(rng, dims, scale, reach, split=(), kind=jnp.bfloat16):
    drawn = scale * jax.random.normal(rng, dims, jnp.float32)
    if split:
        drawn = drawn * shard_levels(rng, dims, split, -0.22, 0.18)
    return jnp.clip(drawn, -reach, reach).astype(kind)


def setup_inputs(seed: int = 0) -> dict:
    key_of = jax.random.split(jax.random.key(seed), 11)
    hidden_in = normal_values(key_of[0], (TOKENS, D), 1.0, 6.0, ((0, 32),))
    piece_starts = draw_piece_starts(jax.random.fold_in(key_of[10], 71), 0)
    out_cotangent = normal_values(key_of[2], (TOKENS, D), 1.0, 6.0, ((0, 32),))
    owners = draw_owners(jax.random.fold_in(key_of[10], 71), 0)
    master = draw_master(jax.random.fold_in(key_of[10], 71), 0)
    moment_one = draw_moment_one(jax.random.fold_in(key_of[10], 71), 0)
    moment_two = draw_moment_two(jax.random.fold_in(key_of[10], 71), 0)
    gain_master = jnp.clip(1.0 + 0.1 * jax.random.normal(key_of[7], (2, D), jnp.float32), 0.5, 1.5)
    gain_one = draw_gain_one(jax.random.fold_in(key_of[10], 71), 0)
    gain_two = draw_gain_two(jax.random.fold_in(key_of[10], 71), 0)
    return dict(hidden_in=hidden_in, piece_starts=piece_starts, out_cotangent=out_cotangent, owners=owners, master=master, moment_one=moment_one, moment_two=moment_two, gain_master=gain_master, gain_one=gain_one, gain_two=gain_two)


highest = lax.Precision.HIGHEST
norm_eps = 1e-05
adam_eps = 1e-08
beta_one = 0.5
beta_two = 0.5
learn_rate = 0.02
gain_rate = 0.3
decay_rate = 0.1
rope_base = 500000.0
masked_score = -1e+30

@jax.custom_vjp
def low(v):
    return lax.optimization_barrier(v.astype(jnp.bfloat16)).astype(jnp.float32)

@jax.custom_vjp
def low_back(v):
    return v

def low_keep(v):
    return (low(v), None)

def low_pass(kept, grad):
    return (grad,)

def back_keep(v):
    return (v, None)

def back_low(kept, grad):
    return (low(grad),)
low.defvjp(low_keep, low_pass)
low_back.defvjp(back_keep, back_low)

def section_layout():
    return [(0, TILES_A, CAP_A, 0), (TILES_A, TILES_B, CAP_B, CAP_A), (TILES_A + TILES_B, TILES_C, CAP_C, CAP_A + CAP_B), (TILES_A + TILES_B + TILES_C, TILES_D, CAP_D, CAP_A + CAP_B + CAP_C)]

def slot_numbers(owners):
    placed = []
    for first_tile, number, capacity, first_slot in section_layout():
        mine = owners[first_tile:first_tile + number].astype(jnp.int32)
        order = jnp.arange(number, dtype=jnp.int32)
        earlier = (mine[:, None] == mine[None, :]) & (order[None, :] < order[:, None])
        ranked = lax.optimization_barrier(jnp.sum(earlier.astype(jnp.int32), axis=1)).astype(jnp.int32)
        placed.append(mine * CAPS + first_slot + ranked)
    return jnp.concatenate(placed).astype(jnp.int32)

def piece_labels(positions, starts):
    inside = (positions[:, None] >= starts[None, :]) & (positions[:, None] < starts[None, :] + PIECE)
    labels = jnp.arange(1, starts.shape[0] + 1, dtype=jnp.int32)
    return (lax.optimization_barrier(jnp.sum(jnp.where(inside, labels[None, :], 0), axis=1)) - 1).astype(jnp.int32)

def attention_mask(query_pos, key_pos, starts):
    query_label = piece_labels(query_pos, starts)
    key_label = piece_labels(key_pos, starts)
    causal = key_pos[None, :] <= query_pos[:, None]
    shared = (query_label[:, None] == key_label[None, :]) & (query_label[:, None] >= 0)
    return causal | shared

def rope_tables(positions):
    half_dim = HEAD // 2
    inverse = rope_base ** (-(jnp.arange(half_dim, dtype=jnp.float32) * 2.0 / HEAD))
    angles = positions[:, None] * inverse[None, :]
    return (jnp.cos(angles)[:, None, :], jnp.sin(angles)[:, None, :])

def rope_apply(values, cosine, sine):
    half_dim = HEAD // 2
    first_half = values[..., :half_dim]
    second_half = values[..., half_dim:]
    return jnp.concatenate([first_half * cosine - second_half * sine, second_half * cosine + first_half * sine], axis=-1)

def sequence_out(tokens, starts, wqkv, wout, wffn, wdown, gain_attn, gain_ffn):
    group_size = HEADS // KV_HEADS
    kv_width = KV_HEADS * HEAD
    positions = jnp.arange(SEQ_LEN, dtype=jnp.int32)
    allowed = attention_mask(positions, positions, starts)
    cosine, sine = rope_tables(positions.astype(jnp.float32))
    inv_one = lax.rsqrt(lax.optimization_barrier(jnp.mean(tokens * tokens, axis=1, keepdims=True)) + norm_eps)
    normed = low(tokens * inv_one * gain_attn)
    projected = low_back(jnp.dot(normed, wqkv.T, precision=highest))
    queries = low(rope_apply(projected[:, :D].reshape(SEQ_LEN, HEADS, HEAD), cosine, sine))
    queries = queries.reshape(SEQ_LEN, KV_HEADS, group_size, HEAD)
    keys = low(rope_apply(projected[:, D:D + kv_width].reshape(SEQ_LEN, KV_HEADS, HEAD), cosine, sine))
    values = low(projected[:, D + kv_width:]).reshape(SEQ_LEN, KV_HEADS, HEAD)
    scores = low_back(jnp.einsum('tkgh,skh->kgts', queries, keys, precision=highest) * (1.0 / math.sqrt(HEAD)))
    scores = jnp.where(allowed[None, None], scores, masked_score)
    probs = low(jax.nn.softmax(scores, axis=-1))
    attended = low(low_back(jnp.einsum('kgts,skh->tkgh', probs, values, precision=highest))).reshape(SEQ_LEN, D)
    middle = tokens + low_back(jnp.dot(attended, wout, precision=highest))
    inv_two = lax.rsqrt(lax.optimization_barrier(jnp.mean(middle * middle, axis=1, keepdims=True)) + norm_eps)
    normed_two = low(middle * inv_two * gain_ffn)
    gate_up = low_back(jnp.dot(normed_two, wffn.T, precision=highest))
    activated = low(jax.nn.silu(gate_up[:, :FF]) * gate_up[:, FF:])
    return middle + low_back(jnp.dot(activated, wdown, precision=highest))

def forward(tokens, wqkv, wout, wffn, wdown, gains, starts):
    qkv_low = low(wqkv)
    out_low = low(wout)
    ffn_low = low(wffn)
    down_low = low(wdown)
    gains_low = low(gains)

    def one_sequence(sequence_item):
        return sequence_out(sequence_item[0], sequence_item[1], qkv_low, out_low, ffn_low, down_low, gains_low[0], gains_low[1])
    return lax.map(jax.checkpoint(one_sequence), (tokens, starts))

def adam_step(weights, first_moment, second_moment, grads, step, decay, rate):
    new_one = beta_one * first_moment + (1.0 - beta_one) * grads
    new_two = beta_two * second_moment + (1.0 - beta_two) * grads * grads
    correct_one = 1.0 - beta_one ** step
    correct_two = 1.0 - beta_two ** step
    update = -rate * (new_one / correct_one / (jnp.sqrt(new_two / correct_two) + adam_eps) + decay * weights)
    return (new_one, new_two, weights + update)

def reference(hidden_in, piece_starts, out_cotangent, owners, master, moment_one, moment_two, gain_master, gain_one, gain_two):
    slots = slot_numbers(owners)
    tiles = master[slots]
    flat_rows = tiles.reshape(TILES * TR, D)
    edge_a = TILES_A * TR
    edge_b = edge_a + TILES_B * TR
    edge_c = edge_b + TILES_C * TR
    inputs = hidden_in.astype(jnp.float32).reshape(SEQS, SEQ_LEN, D)

    def whole_block(tokens, wqkv, wout, wffn, wdown, gains):
        return forward(tokens, wqkv, wout, wffn, wdown, gains, piece_starts)
    outputs, pullback = jax.vjp(whole_block, inputs, flat_rows[:edge_a], flat_rows[edge_a:edge_b], flat_rows[edge_b:edge_c], flat_rows[edge_c:], gain_master)
    cotangent = out_cotangent.astype(jnp.float32).reshape(SEQS, SEQ_LEN, D)
    grad_in, grad_qkv, grad_attn, grad_ffn, grad_down, gain_grad = pullback(cotangent)
    tile_grads = jnp.concatenate([grad_qkv, grad_attn, grad_ffn, grad_down], axis=0).reshape(TILES, TR, D)
    step = float(STEP)
    new_one, new_two, new_tiles = adam_step(tiles, moment_one[slots], moment_two[slots], tile_grads, step, decay_rate, learn_rate)
    blank = jnp.zeros_like(master)
    weight_grad = blank.at[slots].set(tile_grads)
    new_master = blank.at[slots].set(new_tiles)
    new_moment_one = blank.at[slots].set(new_one)
    new_moment_two = blank.at[slots].set(new_two)
    new_gain_one, new_gain_two, new_gains = adam_step(gain_master, gain_one, gain_two, gain_grad, step, 0.0, gain_rate)
    block_out = outputs.reshape(TOKENS, D).astype(jnp.bfloat16)
    input_grad = grad_in.reshape(TOKENS, D)
    return (block_out, input_grad, weight_grad, new_master, new_moment_one, new_moment_two, gain_grad, new_gains, new_gain_one, new_gain_two)
```

```python
import functools
import math

import jax
import jax.experimental.pallas as pl
import jax.experimental.pallas.tpu as pltpu
import jax.numpy as jnp
from jax import lax
from jax.sharding import PartitionSpec as P

D = 2048
HEADS = 32
KV_HEADS = 8
HEAD = 64
FF = 8192
PIECE = 256
STEP = 5


norm_eps = 1e-05
adam_eps = 1e-08
beta_one = 0.5
beta_two = 0.5
learn_rate = 0.02
gain_rate = 0.3
decay_rate = 0.1
rope_base = 500000.0
masked_score = -1e30


def section_layout(devices, tile_rows):
    counts = [
        (D + 2 * KV_HEADS * HEAD) // tile_rows,
        HEADS * HEAD // tile_rows,
        2 * FF // tile_rows,
        FF // tile_rows,
    ]
    layout = []
    first_tile = 0
    first_slot = 0
    for number in counts:
        capacity = 5 * number // (4 * devices) + 1
        layout.append((first_tile, number, capacity, first_slot))
        first_tile += number
        first_slot += capacity
    return layout


def slot_numbers(owners, layout, caps):
    placed = []
    for first_tile, number, capacity, first_slot in layout:
        mine = owners[first_tile : first_tile + number]
        order = jnp.arange(number, dtype=jnp.int32)
        earlier = (mine[:, None] == mine[None, :]) & (order[None, :] < order[:, None])
        ranked = jnp.sum(earlier.astype(jnp.int32), axis=1)
        placed.append(mine * caps + first_slot + ranked)
    return placed


def filled_mask(owners, layout, device):
    masks = []
    for first_tile, number, capacity, first_slot in layout:
        count = jnp.sum((owners[first_tile : first_tile + number] == device).astype(jnp.int32))
        masks.append(jnp.arange(capacity, dtype=jnp.int32) < count)
    return jnp.concatenate(masks)


def pick_kernel(table, wall_ref, out_ref, sem):
    number = out_ref.shape[0]

    @pl.loop(0, number)
    def _(t):
        pltpu.make_async_copy(wall_ref.at[table[t]], out_ref.at[t], sem).start()

    pltpu.make_async_copy(out_ref, out_ref, sem).wait()


def pick_tiles(table, wall):
    return pl.pallas_call(
        pick_kernel,
        grid_spec=pltpu.PrefetchScalarGridSpec(
            num_scalar_prefetch=1,
            grid=(1,),
            in_specs=[pl.BlockSpec(memory_space=pl.ANY)],
            out_specs=pl.BlockSpec(memory_space=pl.ANY),
            scratch_shapes=[pltpu.SemaphoreType.DMA],
        ),
        out_shape=jax.ShapeDtypeStruct((table.shape[0],) + wall.shape[1:], wall.dtype),
        name="pick",
    )(table, wall)


def place_kernel(table, tiles_ref, old_ref, out_ref, sem):
    number = tiles_ref.shape[0]

    @pl.loop(0, number)
    def _(t):
        pltpu.make_async_copy(tiles_ref.at[t], out_ref.at[table[t]], sem).start()

    pltpu.make_async_copy(tiles_ref, tiles_ref, sem).wait()


def place_tiles(table, tiles, wall):
    return pl.pallas_call(
        place_kernel,
        grid_spec=pltpu.PrefetchScalarGridSpec(
            num_scalar_prefetch=1,
            grid=(1,),
            in_specs=[pl.BlockSpec(memory_space=pl.ANY)] * 2,
            out_specs=pl.BlockSpec(memory_space=pl.ANY),
            scratch_shapes=[pltpu.SemaphoreType.DMA],
        ),
        out_shape=jax.ShapeDtypeStruct(wall.shape, wall.dtype),
        input_output_aliases={2: 0},
        name="place",
    )(table, tiles, wall)


def ffn_kernel(group, gate_s, up_s, down_s, normed_ref, cot_ref, wall_ref, out_ref, back_ref, grads_ref, held, made, load_sem, store_sem):
    step = pl.program_id(0)
    steps = pl.num_programs(0)
    tables = (gate_s, up_s, down_s)
    tile_rows = wall_ref.shape[1]
    width = wall_ref.shape[2]
    rows = group * tile_rows

    def fetch(at, buf):
        for kind in range(3):
            @pl.loop(0, group)
            def _(t, kind=kind):
                pltpu.make_async_copy(wall_ref.at[tables[kind][at * group + t]], held.at[buf, kind, t], load_sem.at[buf]).start()

    def drain(buf):
        pltpu.make_async_copy(made.at[buf], made.at[buf], store_sem.at[buf]).wait()

    buf = lax.rem(step, 2)

    @pl.when(step == 0)
    def _():
        fetch(0, 0)
        out_ref[...] = jnp.zeros_like(out_ref)
        back_ref[...] = jnp.zeros_like(back_ref)

    @pl.when(step + 1 < steps)
    def _():
        fetch(step + 1, 1 - buf)

    pltpu.make_async_copy(held.at[buf], held.at[buf], load_sem.at[buf]).wait()

    @pl.when(step >= 2)
    def _():
        drain(buf)

    normed = normed_ref[...]
    cot = cot_ref[...]
    w_gate = held[buf, 0].reshape(rows, width)
    w_up = held[buf, 1].reshape(rows, width)
    w_down = held[buf, 2].reshape(rows, width)
    nt = (((1,), (1,)), ((), ()))
    nn = (((1,), (0,)), ((), ()))
    tn = (((0,), (0,)), ((), ()))

    def dot(a, b, dims):
        return lax.dot_general(a, b, dims, preferred_element_type=jnp.float32)

    gate = dot(normed, w_gate, nt)
    up = dot(normed, w_up, nt)
    hidden = dot(cot, w_down, nt)
    sig = jax.nn.sigmoid(gate)
    silu = gate * sig
    act = (silu * up).astype(jnp.bfloat16)
    g_gate = (hidden * up * sig * (1.0 + gate * (1.0 - sig))).astype(jnp.bfloat16)
    g_up = (hidden * silu).astype(jnp.bfloat16)
    out_ref[...] += dot(act, w_down, nn)
    back_ref[...] += dot(g_gate, w_gate, nn) + dot(g_up, w_up, nn)
    made[buf, 0] = dot(g_gate, normed, tn).astype(jnp.bfloat16).reshape(group, tile_rows, width)
    made[buf, 1] = dot(g_up, normed, tn).astype(jnp.bfloat16).reshape(group, tile_rows, width)
    made[buf, 2] = dot(act, cot, tn).astype(jnp.bfloat16).reshape(group, tile_rows, width)
    for kind in range(3):
        @pl.loop(0, group)
        def _(t, kind=kind):
            pltpu.make_async_copy(made.at[buf, kind, t], grads_ref.at[tables[kind][step * group + t]], store_sem.at[buf]).start()

    @pl.when(step == steps - 1)
    def _():
        drain(1 - buf)
        drain(buf)

def ffn_call(gate_s, up_s, down_s, normed, cot, wall, group=16):
    tokens, width = normed.shape
    steps = gate_s.shape[0] // group
    tr = wall.shape[1]
    full = pl.BlockSpec((tokens, width), lambda i, *_: (0, 0))
    return pl.pallas_call(
        functools.partial(ffn_kernel, group),
        grid_spec=pltpu.PrefetchScalarGridSpec(
            num_scalar_prefetch=3, grid=(steps,),
            in_specs=[full, full, pl.BlockSpec(memory_space=pl.ANY)],
            out_specs=[full, full, pl.BlockSpec(memory_space=pl.ANY)],
            scratch_shapes=[pltpu.VMEM((2, 3, group, tr, width), jnp.bfloat16), pltpu.VMEM((2, 3, group, tr, width), jnp.bfloat16),
                pltpu.SemaphoreType.DMA((2,)), pltpu.SemaphoreType.DMA((2,))]),
        out_shape=[jax.ShapeDtypeStruct((tokens, width), jnp.float32), jax.ShapeDtypeStruct((tokens, width), jnp.float32), jax.ShapeDtypeStruct(wall.shape, jnp.bfloat16)],
        compiler_params=pltpu.CompilerParams(vmem_limit_bytes=56 << 20, dimension_semantics=("arbitrary",)),
        name="ffn",
    )(gate_s, up_s, down_s, normed, cot, wall)


def gather_slots(low_tiles):
    return lax.all_gather(low_tiles, ("dp", "fsdp"), axis=0, tiled=True)


def scatter_slots(grads_wall, caps):
    return lax.psum_scatter(
        grads_wall, ("dp", "fsdp"), scatter_dimension=0, tiled=True
    ).astype(jnp.float32)


def piece_labels(positions, starts):
    inside = (positions[:, None] >= starts[None, :]) & (
        positions[:, None] < starts[None, :] + PIECE
    )
    labels = jnp.arange(1, starts.shape[0] + 1, dtype=jnp.int32)
    return jnp.sum(jnp.where(inside, labels[None, :], 0), axis=1) - 1


def attention_mask(query_pos, key_pos, starts):
    query_label = piece_labels(query_pos, starts)
    key_label = piece_labels(key_pos, starts)
    causal = key_pos[None, :] <= query_pos[:, None]
    shared = (query_label[:, None] == key_label[None, :]) & (query_label[:, None] >= 0)
    return causal | shared


def rope_tables(positions):
    half_dim = HEAD // 2
    inverse = rope_base ** (-(jnp.arange(half_dim, dtype=jnp.float32) * 2.0 / HEAD))
    angles = positions[:, None] * inverse[None, :]
    return (jnp.cos(angles)[:, None, :], jnp.sin(angles)[:, None, :])


def rope_apply(values, cosine, sine):
    half_dim = HEAD // 2
    first_half = values[..., :half_dim]
    second_half = values[..., half_dim:]
    return jnp.concatenate(
        [first_half * cosine - second_half * sine, second_half * cosine + first_half * sine],
        axis=-1,
    )


def rope_back(grads, cosine, sine):
    half_dim = HEAD // 2
    first_half = grads[..., :half_dim]
    second_half = grads[..., half_dim:]
    return jnp.concatenate(
        [first_half * cosine + second_half * sine, second_half * cosine - first_half * sine],
        axis=-1,
    )


def adam_step(weights, first_moment, second_moment, grads, step, decay, rate):
    new_one = beta_one * first_moment + (1.0 - beta_one) * grads
    new_two = beta_two * second_moment + (1.0 - beta_two) * grads * grads
    correct_one = 1.0 - beta_one**step
    correct_two = 1.0 - beta_two**step
    update = -rate * (
        new_one / correct_one / (jnp.sqrt(new_two / correct_two) + adam_eps) + decay * weights
    )
    return (new_one, new_two, weights + update)


def shards(
    hidden_in,
    piece_starts,
    out_cotangent,
    owners,
    master,
    moment_one,
    moment_two,
    gain_master,
    gain_one,
    gain_two,
):
    devices = lax.axis_size("dp") * lax.axis_size("fsdp")
    caps, tile_rows, model_width = master.shape
    layout = section_layout(devices, tile_rows)
    slot_qkv, slot_out, slot_ffn, slot_down = slot_numbers(owners, layout, caps)
    wall = gather_slots(master.astype(jnp.bfloat16))
    slot_attn = jnp.concatenate([slot_qkv, slot_out])
    attn_rows = pick_tiles(slot_attn, wall).reshape(-1, model_width)
    w_qkv = attn_rows[: slot_qkv.shape[0] * tile_rows]
    w_out = attn_rows[slot_qkv.shape[0] * tile_rows :]

    def times(left, right):
        return jnp.dot(left, right, preferred_element_type=jnp.float32)

    def times_nt(left, right):
        return lax.dot_general(
            left, right, (((1,), (1,)), ((), ())), preferred_element_type=jnp.float32
        )

    def times_tn(left, right):
        return lax.dot_general(
            left, right, (((0,), (0,)), ((), ())), preferred_element_type=jnp.float32
        )

    gains_low = lax.all_gather(
        gain_master.astype(jnp.bfloat16), ("dp", "fsdp"), axis=1, tiled=True
    ).astype(jnp.float32)
    gain_attn = gains_low[0]
    gain_ffn = gains_low[1]
    tokens = hidden_in.astype(jnp.float32)
    local_len = tokens.shape[0]
    seq_len = local_len * lax.axis_size("fsdp")
    group_size = HEADS // KV_HEADS
    kv_width = KV_HEADS * HEAD
    qkv_width = model_width + 2 * kv_width
    score_scale = 1.0 / math.sqrt(HEAD)
    query_pos = lax.axis_index("fsdp") * local_len + jnp.arange(local_len, dtype=jnp.int32)
    key_pos = jnp.arange(seq_len, dtype=jnp.int32)
    allowed = attention_mask(query_pos, key_pos, piece_starts[0])
    cosine, sine = rope_tables(query_pos.astype(jnp.float32))
    inv_one = lax.rsqrt(jnp.mean(tokens * tokens, axis=1, keepdims=True) + norm_eps)
    normed = (tokens * inv_one * gain_attn).astype(jnp.bfloat16)
    projected = times_nt(normed, w_qkv)
    queries = rope_apply(
        projected[:, :model_width].reshape(local_len, HEADS, HEAD), cosine, sine
    ).astype(jnp.bfloat16)
    queries = queries.reshape(local_len, KV_HEADS, group_size, HEAD)
    keys_local = rope_apply(
        projected[:, model_width : model_width + kv_width].reshape(local_len, KV_HEADS, HEAD),
        cosine,
        sine,
    )
    keys_local = keys_local.astype(jnp.bfloat16).reshape(local_len, kv_width)
    values_local = projected[:, model_width + kv_width :].astype(jnp.bfloat16)
    keys_all, values_all = (
        lax.all_gather(keys_local, "fsdp", axis=0, tiled=True),
        lax.all_gather(values_local, "fsdp", axis=0, tiled=True),
    )
    keys_all = keys_all.reshape(seq_len, KV_HEADS, HEAD)
    values_all = values_all.reshape(seq_len, KV_HEADS, HEAD)

    def masked_scores():
        raw = (
            jnp.einsum("tkgh,skh->kgts", queries, keys_all, preferred_element_type=jnp.float32)
            * score_scale
        )
        return jnp.where(allowed[None, None], raw, masked_score)

    scores = masked_scores()
    row_top = jnp.max(scores, axis=-1, keepdims=True)
    shifted = jnp.exp(scores - row_top)
    row_total = jnp.sum(shifted, axis=-1, keepdims=True)
    log_total = row_top + jnp.log(row_total)
    probs_low = (shifted / row_total).astype(jnp.bfloat16)
    attended = jnp.einsum(
        "kgts,skh->tkgh", probs_low, values_all, preferred_element_type=jnp.float32
    )
    attended = attended.reshape(local_len, model_width).astype(jnp.bfloat16)
    branch = times(attended, w_out)
    middle = tokens + branch
    inv_two = lax.rsqrt(jnp.mean(middle * middle, axis=1, keepdims=True) + norm_eps)
    normed_two = (middle * inv_two * gain_ffn).astype(jnp.bfloat16)
    half = slot_ffn.shape[0] // 2
    ffn_out, grad_normed_two, grads_wall = ffn_call(
        slot_ffn[:half], slot_ffn[half:], slot_down, normed_two, out_cotangent, wall
    )
    block_out = (middle + ffn_out).astype(jnp.bfloat16)
    grad_out = out_cotangent.astype(jnp.float32)
    scaled_two = grad_normed_two * gain_ffn
    grad_middle = (
        grad_out
        + inv_two * scaled_two
        - middle * inv_two**3 * jnp.mean(scaled_two * middle, axis=1, keepdims=True)
    )
    gain_two_term = jnp.sum(grad_normed_two * middle * inv_two, axis=0)
    grad_branch = grad_middle.astype(jnp.bfloat16)
    grad_attended = times_nt(grad_branch, w_out)
    grad_attn_low = grad_attended.astype(jnp.bfloat16).reshape(
        local_len, KV_HEADS, group_size, HEAD
    )
    probs_again = jnp.exp(masked_scores() - log_total)
    grad_probs = jnp.einsum(
        "tkgh,skh->kgts", grad_attn_low, values_all, preferred_element_type=jnp.float32
    )
    row_dot = jnp.sum(probs_again * grad_probs, axis=-1, keepdims=True)
    grad_scores = (probs_again * (grad_probs - row_dot)).astype(jnp.bfloat16)
    grad_queries = (
        jnp.einsum("kgts,skh->tkgh", grad_scores, keys_all, preferred_element_type=jnp.float32)
        * score_scale
    )
    key_terms = (
        jnp.einsum("kgts,tkgh->skh", grad_scores, queries, preferred_element_type=jnp.float32)
        * score_scale
    )
    value_terms = jnp.einsum(
        "kgts,tkgh->skh",
        probs_again.astype(jnp.bfloat16),
        grad_attn_low,
        preferred_element_type=jnp.float32,
    )
    grad_keys, grad_values = (
        lax.psum_scatter(
            key_terms.reshape(seq_len, kv_width), "fsdp", scatter_dimension=0, tiled=True
        ),
        lax.psum_scatter(
            value_terms.reshape(seq_len, kv_width), "fsdp", scatter_dimension=0, tiled=True
        ),
    )
    grad_query_pre = rope_back(grad_queries.reshape(local_len, HEADS, HEAD), cosine, sine).reshape(
        local_len, model_width
    )
    grad_key_pre = rope_back(grad_keys.reshape(local_len, KV_HEADS, HEAD), cosine, sine).reshape(
        local_len, kv_width
    )
    grad_projected = jnp.concatenate([grad_query_pre, grad_key_pre, grad_values], axis=1).astype(
        jnp.bfloat16
    )
    grad_normed = times(grad_projected, w_qkv)
    attn_grads = jnp.concatenate(
        [
            times_tn(grad_projected, normed).astype(jnp.bfloat16),
            times_tn(attended, grad_branch).astype(jnp.bfloat16),
        ]
    ).reshape(-1, tile_rows, model_width)
    grads_wall = place_tiles(slot_attn, attn_grads, grads_wall)
    keep_slot = filled_mask(owners, layout, lax.axis_index(("dp", "fsdp")))[:, None, None]
    weight_grad = jnp.where(keep_slot, scatter_slots(grads_wall, caps), 0.0)
    scaled_one = grad_normed * gain_attn
    input_grad = (
        grad_middle
        + inv_one * scaled_one
        - tokens * inv_one**3 * jnp.mean(scaled_one * tokens, axis=1, keepdims=True)
    )
    gain_one_term = jnp.sum(grad_normed * tokens * inv_one, axis=0)
    gain_grad = lax.psum_scatter(
        jnp.stack([gain_one_term, gain_two_term]), ("dp", "fsdp"), scatter_dimension=1, tiled=True
    )
    step = float(STEP)
    new_one, new_two, new_weights = adam_step(
        master, moment_one, moment_two, weight_grad, step, decay_rate, learn_rate
    )
    new_one = jnp.where(keep_slot, new_one, 0.0)
    new_two = jnp.where(keep_slot, new_two, 0.0)
    new_weights = jnp.where(keep_slot, new_weights, 0.0)
    new_gain_one, new_gain_two, new_gains = adam_step(
        gain_master, gain_one, gain_two, gain_grad, step, 0.0, gain_rate
    )
    return (
        block_out,
        input_grad,
        weight_grad,
        new_weights,
        new_one,
        new_two,
        gain_grad,
        new_gains,
        new_gain_one,
        new_gain_two,
    )


def solution(mesh):
    return jax.shard_map(
        shards,
        mesh=mesh,
        in_specs=(
            P(("dp", "fsdp"), None),
            P("dp", None),
            P(("dp", "fsdp"), None),
            P(),
            P(("dp", "fsdp"), None, None),
            P(("dp", "fsdp"), None, None),
            P(("dp", "fsdp"), None, None),
            P(None, ("dp", "fsdp")),
            P(None, ("dp", "fsdp")),
            P(None, ("dp", "fsdp")),
        ),
        out_specs=(
            P(("dp", "fsdp"), None),
            P(("dp", "fsdp"), None),
            P(("dp", "fsdp"), None, None),
            P(("dp", "fsdp"), None, None),
            P(("dp", "fsdp"), None, None),
            P(("dp", "fsdp"), None, None),
            P(None, ("dp", "fsdp")),
            P(None, ("dp", "fsdp")),
            P(None, ("dp", "fsdp")),
            P(None, ("dp", "fsdp")),
        ),
        check_vma=False,
    )
```

```python
import functools
import math

import jax
import jax.experimental.pallas as pl
import jax.experimental.pallas.tpu as pltpu
import jax.numpy as jnp
from jax import lax
from jax.sharding import PartitionSpec as P

D = 2048
HEADS = 32
KV_HEADS = 8
HEAD = 64
FF = 8192
PIECE = 256
STEP = 5


norm_eps = 1e-05
adam_eps = 1e-08
beta_one = 0.5
beta_two = 0.5
learn_rate = 0.02
gain_rate = 0.3
decay_rate = 0.1
rope_base = 500000.0
masked_score = -1e30


def section_layout(devices, tile_rows):
    counts = [
        (D + 2 * KV_HEADS * HEAD) // tile_rows,
        HEADS * HEAD // tile_rows,
        2 * FF // tile_rows,
        FF // tile_rows,
    ]
    layout = []
    first_tile = 0
    first_slot = 0
    for number in counts:
        capacity = 5 * number // (4 * devices) + 1
        layout.append((first_tile, number, capacity, first_slot))
        first_tile += number
        first_slot += capacity
    return layout


def slot_numbers(owners, layout, caps):
    placed = []
    for first_tile, number, capacity, first_slot in layout:
        mine = owners[first_tile : first_tile + number]
        order = jnp.arange(number, dtype=jnp.int32)
        earlier = (mine[:, None] == mine[None, :]) & (order[None, :] < order[:, None])
        ranked = jnp.sum(earlier.astype(jnp.int32), axis=1)
        placed.append(mine * caps + first_slot + ranked)
    return placed


def filled_mask(owners, layout, device):
    masks = []
    for first_tile, number, capacity, first_slot in layout:
        count = jnp.sum((owners[first_tile : first_tile + number] == device).astype(jnp.int32))
        masks.append(jnp.arange(capacity, dtype=jnp.int32) < count)
    return jnp.concatenate(masks)


def pick_kernel(table, wall_ref, out_ref, sem):
    number = out_ref.shape[0]

    @pl.loop(0, number)
    def _(t):
        pltpu.make_async_copy(wall_ref.at[table[t]], out_ref.at[t], sem).start()

    pltpu.make_async_copy(out_ref, out_ref, sem).wait()


def pick_tiles(table, wall):
    return pl.pallas_call(
        pick_kernel,
        grid_spec=pltpu.PrefetchScalarGridSpec(
            num_scalar_prefetch=1,
            grid=(1,),
            in_specs=[pl.BlockSpec(memory_space=pl.ANY)],
            out_specs=pl.BlockSpec((table.shape[0],) + wall.shape[1:], lambda i, *_: (0, 0, 0)),
            scratch_shapes=[pltpu.SemaphoreType.DMA],
        ),
        out_shape=jax.ShapeDtypeStruct((table.shape[0],) + wall.shape[1:], wall.dtype),
        compiler_params=pltpu.CompilerParams(vmem_limit_bytes=50 << 20),
        name="pick",
    )(table, wall)


def place_kernel(table, tiles_ref, old_ref, out_ref, sem):
    number = tiles_ref.shape[0]

    @pl.loop(0, number)
    def _(t):
        pltpu.make_async_copy(tiles_ref.at[t], out_ref.at[table[t]], sem).start()

    pltpu.make_async_copy(tiles_ref, tiles_ref, sem).wait()


def place_tiles(table, tiles, wall):
    return pl.pallas_call(
        place_kernel,
        grid_spec=pltpu.PrefetchScalarGridSpec(
            num_scalar_prefetch=1,
            grid=(1,),
            in_specs=[
                pl.BlockSpec(tiles.shape, lambda i, *_: (0, 0, 0)),
                pl.BlockSpec(memory_space=pl.ANY),
            ],
            out_specs=pl.BlockSpec(memory_space=pl.ANY),
            scratch_shapes=[pltpu.SemaphoreType.DMA],
        ),
        out_shape=jax.ShapeDtypeStruct(wall.shape, wall.dtype),
        input_output_aliases={2: 0},
        compiler_params=pltpu.CompilerParams(vmem_limit_bytes=50 << 20),
        name="place",
    )(table, tiles, wall)


def ffn_kernel(group, gate_s, up_s, down_s, normed_ref, cot_ref, wall_ref, out_ref, back_ref, grads_ref, held, made, load_sem, store_sem):
    step = pl.program_id(0)
    steps = pl.num_programs(0)
    tables = (gate_s, up_s, down_s)
    tile_rows = wall_ref.shape[1]
    width = wall_ref.shape[2]
    rows = group * tile_rows

    def fetch(at, buf):
        for kind in range(3):
            @pl.loop(0, group)
            def _(t, kind=kind):
                pltpu.make_async_copy(wall_ref.at[tables[kind][at * group + t]], held.at[buf, kind, t], load_sem.at[buf]).start()

    def drain(buf):
        pltpu.make_async_copy(made.at[buf], made.at[buf], store_sem.at[buf]).wait()

    buf = lax.rem(step, 2)

    @pl.when(step == 0)
    def _():
        fetch(0, 0)
        out_ref[...] = jnp.zeros_like(out_ref)
        back_ref[...] = jnp.zeros_like(back_ref)

    @pl.when(step + 1 < steps)
    def _():
        fetch(step + 1, 1 - buf)

    pltpu.make_async_copy(held.at[buf], held.at[buf], load_sem.at[buf]).wait()

    @pl.when(step >= 2)
    def _():
        drain(buf)

    normed = normed_ref[...]
    cot = cot_ref[...]
    w_gate = held[buf, 0].reshape(rows, width)
    w_up = held[buf, 1].reshape(rows, width)
    w_down = held[buf, 2].reshape(rows, width)
    nt = (((1,), (1,)), ((), ()))
    nn = (((1,), (0,)), ((), ()))
    tn = (((0,), (0,)), ((), ()))

    def dot(a, b, dims):
        return lax.dot_general(a, b, dims, preferred_element_type=jnp.float32)

    gate = dot(normed, w_gate, nt)
    up = dot(normed, w_up, nt)
    hidden = dot(cot, w_down, nt)
    sig = jax.nn.sigmoid(gate)
    silu = gate * sig
    act = (silu * up).astype(jnp.bfloat16)
    g_gate = (hidden * up * sig * (1.0 + gate * (1.0 - sig))).astype(jnp.bfloat16)
    g_up = (hidden * silu).astype(jnp.bfloat16)
    out_ref[...] += dot(act, w_down, nn)
    back_ref[...] += dot(g_gate, w_gate, nn) + dot(g_up, w_up, nn)
    made[buf, 0] = dot(g_gate, normed, tn).astype(jnp.bfloat16).reshape(group, tile_rows, width)
    made[buf, 1] = dot(g_up, normed, tn).astype(jnp.bfloat16).reshape(group, tile_rows, width)
    made[buf, 2] = dot(act, cot, tn).astype(jnp.bfloat16).reshape(group, tile_rows, width)
    for kind in range(3):
        @pl.loop(0, group)
        def _(t, kind=kind):
            pltpu.make_async_copy(made.at[buf, kind, t], grads_ref.at[tables[kind][step * group + t]], store_sem.at[buf]).start()

    @pl.when(step == steps - 1)
    def _():
        drain(1 - buf)
        drain(buf)

def ffn_call(gate_s, up_s, down_s, normed, cot, wall, group=16):
    tokens, width = normed.shape
    steps = gate_s.shape[0] // group
    tr = wall.shape[1]
    full = pl.BlockSpec((tokens, width), lambda i, *_: (0, 0))
    return pl.pallas_call(
        functools.partial(ffn_kernel, group),
        grid_spec=pltpu.PrefetchScalarGridSpec(
            num_scalar_prefetch=3, grid=(steps,),
            in_specs=[full, full, pl.BlockSpec(memory_space=pl.ANY)],
            out_specs=[full, full, pl.BlockSpec(memory_space=pl.ANY)],
            scratch_shapes=[pltpu.VMEM((2, 3, group, tr, width), jnp.bfloat16), pltpu.VMEM((2, 3, group, tr, width), jnp.bfloat16),
                pltpu.SemaphoreType.DMA((2,)), pltpu.SemaphoreType.DMA((2,))]),
        out_shape=[jax.ShapeDtypeStruct((tokens, width), jnp.float32), jax.ShapeDtypeStruct((tokens, width), jnp.float32), jax.ShapeDtypeStruct(wall.shape, jnp.bfloat16)],
        compiler_params=pltpu.CompilerParams(vmem_limit_bytes=56 << 20, dimension_semantics=("arbitrary",)),
        name="ffn",
    )(gate_s, up_s, down_s, normed, cot, wall)


MESH = pl.DeviceIdType.MESH
EVERY = slice(None)
GATHER_ROUTES = (
    ("z1", "z2", "z3", "x", "y", "core"),
    ("z1", "z2", "z3", "y", "x", "core"),
    ("x", "z1", "z2", "z3", "y", "core"),
    ("y", "z1", "z2", "z3", "x", "core"),
)


def position():
    dp = lax.axis_index("dp")
    return dp // 4, lax.rem(dp // 2, 2), lax.rem(dp, 2), lax.axis_index("fsdp")


def target(hop):
    y, x, c, z = position()
    if hop == "x":
        x = 1 - x
    elif hop == "y":
        y = 1 - y
    elif hop == "core":
        c = 1 - c
    elif hop == "back":
        z = lax.rem(z + 3, 4)
    else:
        z = lax.rem(z + 1, 4)
    return (y * 4 + x * 2 + c, z)


def enter(hops):
    barrier = pltpu.get_barrier_semaphore()
    for hop in hops:
        pl.semaphore_signal(barrier, inc=1, device_id=target(hop), device_id_type=MESH)
    pl.semaphore_wait(barrier, len(hops))


def split_slots(caps):
    small = caps // 6
    third = (caps - 2 * small) // 2
    counts = (small, small, third, caps - 2 * small - third)
    starts = (0, small, 2 * small, 2 * small + third)
    rounds = max(2 * small + 1, counts[2], counts[3])
    return counts, starts, rounds


def turn(route, at, counts):
    if route < 2:
        live = (at >= route) & (lax.rem(at + 64 - route, 2) == 0) & (at - route < 2 * counts[route])
        return live, (at - route) // 2
    return (at >= 0) & (at < counts[route]), at


def gather_kernel(mine_ref, wall_ref, own_sem, send_sem, recv_sem):
    y, x, c, z = position()
    counts, starts, rounds = split_slots(mine_ref.shape[0])
    own = pltpu.make_async_copy(mine_ref, wall_ref.at[y, x, c, z], own_sem)
    own.start()
    enter(("x", "y", "core", "z", "back"))
    own.wait()

    def region(route, stage):
        hops = GATHER_ROUTES[route]
        hop = hops[stage]
        done = hops[:stage]
        at_y = EVERY if "y" in done else y
        at_x = EVERY if "x" in done else x
        at_z = EVERY if "z3" in done else z
        if hop in ("z1", "z2", "z3"):
            at_z = lax.rem(z + 5 - int(hop[1]), 4)
        return at_y, at_x, c, at_z

    def copy(route, stage, index):
        view = wall_ref.at[region(route, stage) + (starts[route] + index,)]
        return pltpu.make_async_remote_copy(
            src_ref=view,
            dst_ref=view,
            send_sem=send_sem.at[route, stage],
            recv_sem=recv_sem.at[route, stage, index],
            device_id=target(GATHER_ROUTES[route][stage]),
            device_id_type=MESH,
        )

    stages = len(GATHER_ROUTES[0])

    @pl.loop(0, rounds + stages)
    def _(t):
        for stage in range(stages + 1):
            for route in range(4):
                live, index = turn(route, t - stage, counts)

                @pl.when(live)
                def _(stage=stage, route=route, index=index):
                    if stage > 0:
                        copy(route, stage - 1, index).wait()
                    if stage < stages:
                        copy(route, stage, index).start()


def gather_slots(low_tiles):
    caps, rows, width = low_tiles.shape
    counts, starts, rounds = split_slots(caps)
    wall = pl.pallas_call(
        gather_kernel,
        out_shape=jax.ShapeDtypeStruct((2, 2, 2, 4, caps, rows, width), low_tiles.dtype),
        in_specs=[pl.BlockSpec(memory_space=pltpu.VMEM)],
        out_specs=pl.BlockSpec(memory_space=pl.ANY),
        scratch_shapes=[
            pltpu.SemaphoreType.DMA,
            pltpu.SemaphoreType.DMA((4, 6)),
            pltpu.SemaphoreType.DMA((4, 6, max(counts))),
        ],
        compiler_params=pltpu.CompilerParams(collective_id=0, has_side_effects=True, vmem_limit_bytes=24 << 20),
        name="gather_slots",
    )(low_tiles)
    return wall.reshape(32 * caps, rows, width)


SCATTER_ROUTES = (
    ("core", "y", "x", "z1", "z2", "z3", "end"),
    ("core", "x", "y", "z1", "z2", "z3", "end"),
    ("core", "y", "z1", "z2", "z3", "x", "end"),
    ("core", "x", "z1", "z2", "z3", "y", "end"),
)


def scatter_extent(route, stage):
    hops = SCATTER_ROUTES[route]
    done = hops[1 : stage + 1] if hops[stage] in ("x", "y") else hops[1:stage]
    extent = []
    if "x" not in done or "y" not in done:
        extent.append(2)
    if not any(hop[0] == "z" for hop in hops[: stage + 1]):
        extent.append(4)
    return tuple(extent)


def scatter_terms(route, stage):
    hops = SCATTER_ROUTES[route]
    done = hops[1:stage]
    return 2 + ("x" in done) + ("y" in done) + ("z1" in done)


def scatter_kernel(look, wall_ref, out_ref, core_ref, first_ref, second_ref, ring_ref, last_ref, *scratch):
    y, x, c, z = position()
    caps, rows, width = out_ref.shape
    counts, starts, rounds = split_slots(caps)
    stages = len(SCATTER_ROUTES[0])
    held = {}
    made = {}
    scratch = list(scratch)
    for route in range(4):
        for stage in range(1, stages):
            held[route, stage] = scratch.pop(0)
            if stage < stages - 1:
                made[route, stage] = scratch.pop(0)
    load_sem, send_sem, recv_sem = scratch
    enter(("x", "y", "core", "z", "back"))

    def pick(hop, mine, other):
        return other if hop else mine

    def landing(route, stage, slot):
        hops = SCATTER_ROUTES[route]
        hop = hops[stage]
        if hop == "core":
            return core_ref.at[:, :, :, slot]
        if hop[0] == "z":
            ring = ring_ref.at[int(hop[1]) - 1]
            return ring.at[0, slot] if route < 2 else ring.at[:, slot]
        if stage == 1:
            return first_ref.at[:, :, slot]
        if stage == 2:
            return second_ref.at[:, slot]
        return last_ref.at[slot]

    def terms(route, stage, slot):
        hops = SCATTER_ROUTES[route]
        hop = hops[stage]
        done = hops[1:stage]
        at_y = 1 - y if hop == "y" else (y if "y" in done else EVERY)
        at_x = 1 - x if hop == "x" else (x if "x" in done else EVERY)
        at_z = EVERY
        if hop[0] == "z":
            at_z = lax.rem(z + 4 - int(hop[1]), 4)
        elif "z3" in done:
            at_z = z
        views = [wall_ref.at[at_y, at_x, c, at_z, slot], core_ref.at[at_y, at_x, at_z, slot]]
        other = at_x if hops[1] == "y" else at_y
        if stage > 1:
            views.append(first_ref.at[other, at_z, slot])
        if route < 2 and stage > 2:
            views.append(second_ref.at[at_z, slot])
        if hop in ("z2", "z3"):
            ring = ring_ref.at[int(hop[1]) - 2]
            views.append(ring.at[0, slot] if route < 2 else ring.at[:, slot])
        elif "z3" in done:
            ring = ring_ref.at[2]
            views.append(ring.at[0, slot] if route < 2 else ring.at[other, slot])
        if route >= 2 and hop == "end":
            views.append(last_ref.at[slot])
        return views

    def send(route, stage, index):
        slot = starts[route] + index
        if stage == 0:
            source = wall_ref.at[:, :, 1 - c, :, slot]
        else:
            source = made[route, stage]
        return pltpu.make_async_remote_copy(
            src_ref=source,
            dst_ref=landing(route, stage, slot),
            send_sem=send_sem.at[route, stage],
            recv_sem=recv_sem.at[route, stage, index],
            device_id=target(SCATTER_ROUTES[route][stage]),
            device_id_type=MESH,
        )

    def prepare(route, stage, index):
        if stage > 0:
            send(route, stage - 1, index).wait()
            for k, view in enumerate(terms(route, stage, starts[route] + index)):
                pltpu.make_async_copy(view, held[route, stage].at[k], load_sem.at[route, stage]).start()

    def finish(route, stage, index):
        if stage > 0:
            buf = held[route, stage]
            pltpu.make_async_copy(buf, buf, load_sem.at[route, stage]).wait()
            number = buf.shape[0]
            extent = buf.shape[1:-2]
            blocks = 1
            for size in extent:
                blocks *= size
            part = min(width, 512)

            @pl.loop(0, blocks)
            def _(block):
                if len(extent) == 2:
                    at = (block // extent[1], lax.rem(block, extent[1]))
                elif len(extent) == 1:
                    at = (block,)
                else:
                    at = ()
                for left in range(0, width, part):
                    cols = pl.ds(left, part)
                    total = buf[(0,) + at + (EVERY, cols)].astype(jnp.float32)
                    for k in range(1, number):
                        total += buf[(k,) + at + (EVERY, cols)].astype(jnp.float32)
                    if stage == stages - 1:
                        out_ref[starts[route] + index, :, cols] = total
                    else:
                        made[route, stage][at + (EVERY, cols)] = total.astype(made[route, stage].dtype)

        if stage < stages - 1:
            send(route, stage, index).start()

    @pl.loop(0, rounds + stages - 1)
    def _(t):
        items = [(stage, route) for stage in range(stages - 1, -1, -1) for route in range(4)]

        def run(which, work):
            stage, route = items[which]
            live, index = turn(route, t - stage, counts)

            @pl.when(live)
            def _():
                work(route, stage, index)

        for which in range(len(items) + look):
            if which < len(items):
                run(which, prepare)
            if which >= look:
                run(which - look, finish)


def scatter_slots(grads_wall, caps, look=3):
    rows, width = grads_wall.shape[1:]
    kind = grads_wall.dtype
    wall = grads_wall.reshape(2, 2, 2, 4, caps, rows, width)
    counts, starts, rounds = split_slots(caps)
    stages = len(SCATTER_ROUTES[0])
    scratch = []
    for route in range(4):
        for stage in range(1, stages):
            extent = scatter_extent(route, stage)
            scratch.append(pltpu.VMEM((scatter_terms(route, stage),) + extent + (rows, width), kind))
            if stage < stages - 1:
                scratch.append(pltpu.VMEM(extent + (rows, width), kind))
    tile = (caps, rows, width)
    out = pl.pallas_call(
        functools.partial(scatter_kernel, look),
        out_shape=[
            jax.ShapeDtypeStruct(tile, jnp.float32),
            jax.ShapeDtypeStruct((2, 2, 4) + tile, kind),
            jax.ShapeDtypeStruct((2, 4) + tile, kind),
            jax.ShapeDtypeStruct((4,) + tile, kind),
            jax.ShapeDtypeStruct((3, 2) + tile, kind),
            jax.ShapeDtypeStruct(tile, kind),
        ],
        in_specs=[pl.BlockSpec(memory_space=pl.ANY)],
        out_specs=[pl.BlockSpec(memory_space=pltpu.VMEM)] + [pl.BlockSpec(memory_space=pl.ANY)] * 5,
        scratch_shapes=scratch
        + [
            pltpu.SemaphoreType.DMA((4, stages)),
            pltpu.SemaphoreType.DMA((4, stages)),
            pltpu.SemaphoreType.DMA((4, stages, max(counts))),
        ],
        compiler_params=pltpu.CompilerParams(
            collective_id=1, has_side_effects=True, vmem_limit_bytes=56 << 20
        ),
        name="scatter_slots",
    )(wall)
    return out[0]


def gather_any(low_tiles):
    if (lax.axis_size("dp"), lax.axis_size("fsdp")) == (8, 4):
        return gather_slots(low_tiles)
    return lax.all_gather(low_tiles, ("dp", "fsdp"), axis=0, tiled=True)


def scatter_any(grads_wall, caps):
    if (lax.axis_size("dp"), lax.axis_size("fsdp")) == (8, 4):
        return scatter_slots(grads_wall, caps)
    return lax.psum_scatter(
        grads_wall, ("dp", "fsdp"), scatter_dimension=0, tiled=True
    ).astype(jnp.float32)


def piece_labels(positions, starts):
    inside = (positions[:, None] >= starts[None, :]) & (
        positions[:, None] < starts[None, :] + PIECE
    )
    labels = jnp.arange(1, starts.shape[0] + 1, dtype=jnp.int32)
    return jnp.sum(jnp.where(inside, labels[None, :], 0), axis=1) - 1


def attention_mask(query_pos, key_pos, starts):
    query_label = piece_labels(query_pos, starts)
    key_label = piece_labels(key_pos, starts)
    causal = key_pos[None, :] <= query_pos[:, None]
    shared = (query_label[:, None] == key_label[None, :]) & (query_label[:, None] >= 0)
    return causal | shared


def rope_tables(positions):
    half_dim = HEAD // 2
    inverse = rope_base ** (-(jnp.arange(half_dim, dtype=jnp.float32) * 2.0 / HEAD))
    angles = positions[:, None] * inverse[None, :]
    return (jnp.cos(angles)[:, None, :], jnp.sin(angles)[:, None, :])


def rope_apply(values, cosine, sine):
    half_dim = HEAD // 2
    first_half = values[..., :half_dim]
    second_half = values[..., half_dim:]
    return jnp.concatenate(
        [first_half * cosine - second_half * sine, second_half * cosine + first_half * sine],
        axis=-1,
    )


def rope_back(grads, cosine, sine):
    half_dim = HEAD // 2
    first_half = grads[..., :half_dim]
    second_half = grads[..., half_dim:]
    return jnp.concatenate(
        [first_half * cosine + second_half * sine, second_half * cosine - first_half * sine],
        axis=-1,
    )


def adam_step(weights, first_moment, second_moment, grads, step, decay, rate):
    new_one = beta_one * first_moment + (1.0 - beta_one) * grads
    new_two = beta_two * second_moment + (1.0 - beta_two) * grads * grads
    correct_one = 1.0 - beta_one**step
    correct_two = 1.0 - beta_two**step
    update = -rate * (
        new_one / correct_one / (jnp.sqrt(new_two / correct_two) + adam_eps) + decay * weights
    )
    return (new_one, new_two, weights + update)


def shards(
    hidden_in,
    piece_starts,
    out_cotangent,
    owners,
    master,
    moment_one,
    moment_two,
    gain_master,
    gain_one,
    gain_two,
):
    devices = lax.axis_size("dp") * lax.axis_size("fsdp")
    caps, tile_rows, model_width = master.shape
    layout = section_layout(devices, tile_rows)
    slot_qkv, slot_out, slot_ffn, slot_down = slot_numbers(owners, layout, caps)
    wall = gather_any(master.astype(jnp.bfloat16))
    slot_attn = jnp.concatenate([slot_qkv, slot_out])
    attn_rows = pick_tiles(slot_attn, wall).reshape(-1, model_width)
    w_qkv = attn_rows[: slot_qkv.shape[0] * tile_rows]
    w_out = attn_rows[slot_qkv.shape[0] * tile_rows :]

    def times(left, right):
        return jnp.dot(left, right, preferred_element_type=jnp.float32)

    def times_nt(left, right):
        return lax.dot_general(
            left, right, (((1,), (1,)), ((), ())), preferred_element_type=jnp.float32
        )

    def times_tn(left, right):
        return lax.dot_general(
            left, right, (((0,), (0,)), ((), ())), preferred_element_type=jnp.float32
        )

    gains_low = lax.all_gather(
        gain_master.astype(jnp.bfloat16), ("dp", "fsdp"), axis=1, tiled=True
    ).astype(jnp.float32)
    gain_attn = gains_low[0]
    gain_ffn = gains_low[1]
    tokens = hidden_in.astype(jnp.float32)
    local_len = tokens.shape[0]
    seq_len = local_len * lax.axis_size("fsdp")
    group_size = HEADS // KV_HEADS
    kv_width = KV_HEADS * HEAD
    qkv_width = model_width + 2 * kv_width
    score_scale = 1.0 / math.sqrt(HEAD)
    query_pos = lax.axis_index("fsdp") * local_len + jnp.arange(local_len, dtype=jnp.int32)
    key_pos = jnp.arange(seq_len, dtype=jnp.int32)
    allowed = attention_mask(query_pos, key_pos, piece_starts[0])
    cosine, sine = rope_tables(query_pos.astype(jnp.float32))
    inv_one = lax.rsqrt(jnp.mean(tokens * tokens, axis=1, keepdims=True) + norm_eps)
    normed = (tokens * inv_one * gain_attn).astype(jnp.bfloat16)
    projected = times_nt(normed, w_qkv)
    queries = rope_apply(
        projected[:, :model_width].reshape(local_len, HEADS, HEAD), cosine, sine
    ).astype(jnp.bfloat16)
    queries = queries.reshape(local_len, KV_HEADS, group_size, HEAD)
    keys_local = rope_apply(
        projected[:, model_width : model_width + kv_width].reshape(local_len, KV_HEADS, HEAD),
        cosine,
        sine,
    )
    keys_local = keys_local.astype(jnp.bfloat16).reshape(local_len, kv_width)
    values_local = projected[:, model_width + kv_width :].astype(jnp.bfloat16)
    keys_all, values_all = (
        lax.all_gather(keys_local, "fsdp", axis=0, tiled=True),
        lax.all_gather(values_local, "fsdp", axis=0, tiled=True),
    )
    keys_all = keys_all.reshape(seq_len, KV_HEADS, HEAD)
    values_all = values_all.reshape(seq_len, KV_HEADS, HEAD)

    def masked_scores():
        raw = (
            jnp.einsum("tkgh,skh->kgts", queries, keys_all, preferred_element_type=jnp.float32)
            * score_scale
        )
        return jnp.where(allowed[None, None], raw, masked_score)

    scores = masked_scores()
    row_top = jnp.max(scores, axis=-1, keepdims=True)
    shifted = jnp.exp(scores - row_top)
    row_total = jnp.sum(shifted, axis=-1, keepdims=True)
    log_total = row_top + jnp.log(row_total)
    probs_low = (shifted / row_total).astype(jnp.bfloat16)
    attended = jnp.einsum(
        "kgts,skh->tkgh", probs_low, values_all, preferred_element_type=jnp.float32
    )
    attended = attended.reshape(local_len, model_width).astype(jnp.bfloat16)
    branch = times(attended, w_out)
    middle = tokens + branch
    inv_two = lax.rsqrt(jnp.mean(middle * middle, axis=1, keepdims=True) + norm_eps)
    normed_two = (middle * inv_two * gain_ffn).astype(jnp.bfloat16)
    half = slot_ffn.shape[0] // 2
    ffn_out, grad_normed_two, grads_wall = ffn_call(
        slot_ffn[:half], slot_ffn[half:], slot_down, normed_two, out_cotangent, wall
    )
    block_out = (middle + ffn_out).astype(jnp.bfloat16)
    grad_out = out_cotangent.astype(jnp.float32)
    scaled_two = grad_normed_two * gain_ffn
    grad_middle = (
        grad_out
        + inv_two * scaled_two
        - middle * inv_two**3 * jnp.mean(scaled_two * middle, axis=1, keepdims=True)
    )
    gain_two_term = jnp.sum(grad_normed_two * middle * inv_two, axis=0)
    grad_branch = grad_middle.astype(jnp.bfloat16)
    grad_attended = times_nt(grad_branch, w_out)
    grad_attn_low = grad_attended.astype(jnp.bfloat16).reshape(
        local_len, KV_HEADS, group_size, HEAD
    )
    probs_again = jnp.exp(masked_scores() - log_total)
    grad_probs = jnp.einsum(
        "tkgh,skh->kgts", grad_attn_low, values_all, preferred_element_type=jnp.float32
    )
    row_dot = jnp.sum(probs_again * grad_probs, axis=-1, keepdims=True)
    grad_scores = (probs_again * (grad_probs - row_dot)).astype(jnp.bfloat16)
    grad_queries = (
        jnp.einsum("kgts,skh->tkgh", grad_scores, keys_all, preferred_element_type=jnp.float32)
        * score_scale
    )
    key_terms = (
        jnp.einsum("kgts,tkgh->skh", grad_scores, queries, preferred_element_type=jnp.float32)
        * score_scale
    )
    value_terms = jnp.einsum(
        "kgts,tkgh->skh",
        probs_again.astype(jnp.bfloat16),
        grad_attn_low,
        preferred_element_type=jnp.float32,
    )
    grad_keys, grad_values = (
        lax.psum_scatter(
            key_terms.reshape(seq_len, kv_width), "fsdp", scatter_dimension=0, tiled=True
        ),
        lax.psum_scatter(
            value_terms.reshape(seq_len, kv_width), "fsdp", scatter_dimension=0, tiled=True
        ),
    )
    grad_query_pre = rope_back(grad_queries.reshape(local_len, HEADS, HEAD), cosine, sine).reshape(
        local_len, model_width
    )
    grad_key_pre = rope_back(grad_keys.reshape(local_len, KV_HEADS, HEAD), cosine, sine).reshape(
        local_len, kv_width
    )
    grad_projected = jnp.concatenate([grad_query_pre, grad_key_pre, grad_values], axis=1).astype(
        jnp.bfloat16
    )
    grad_normed = times(grad_projected, w_qkv)
    attn_grads = jnp.concatenate(
        [
            times_tn(grad_projected, normed).astype(jnp.bfloat16),
            times_tn(attended, grad_branch).astype(jnp.bfloat16),
        ]
    ).reshape(-1, tile_rows, model_width)
    grads_wall = place_tiles(slot_attn, attn_grads, grads_wall)
    keep_slot = filled_mask(owners, layout, lax.axis_index(("dp", "fsdp")))[:, None, None]
    weight_grad = jnp.where(keep_slot, scatter_any(grads_wall, caps), 0.0)
    scaled_one = grad_normed * gain_attn
    input_grad = (
        grad_middle
        + inv_one * scaled_one
        - tokens * inv_one**3 * jnp.mean(scaled_one * tokens, axis=1, keepdims=True)
    )
    gain_one_term = jnp.sum(grad_normed * tokens * inv_one, axis=0)
    gain_grad = lax.psum_scatter(
        jnp.stack([gain_one_term, gain_two_term]), ("dp", "fsdp"), scatter_dimension=1, tiled=True
    )
    step = float(STEP)
    new_one, new_two, new_weights = adam_step(
        master, moment_one, moment_two, weight_grad, step, decay_rate, learn_rate
    )
    new_one = jnp.where(keep_slot, new_one, 0.0)
    new_two = jnp.where(keep_slot, new_two, 0.0)
    new_weights = jnp.where(keep_slot, new_weights, 0.0)
    new_gain_one, new_gain_two, new_gains = adam_step(
        gain_master, gain_one, gain_two, gain_grad, step, 0.0, gain_rate
    )
    return (
        block_out,
        input_grad,
        weight_grad,
        new_weights,
        new_one,
        new_two,
        gain_grad,
        new_gains,
        new_gain_one,
        new_gain_two,
    )


def solution(mesh):
    return jax.shard_map(
        shards,
        mesh=mesh,
        in_specs=(
            P(("dp", "fsdp"), None),
            P("dp", None),
            P(("dp", "fsdp"), None),
            P(),
            P(("dp", "fsdp"), None, None),
            P(("dp", "fsdp"), None, None),
            P(("dp", "fsdp"), None, None),
            P(None, ("dp", "fsdp")),
            P(None, ("dp", "fsdp")),
            P(None, ("dp", "fsdp")),
        ),
        out_specs=(
            P(("dp", "fsdp"), None),
            P(("dp", "fsdp"), None),
            P(("dp", "fsdp"), None, None),
            P(("dp", "fsdp"), None, None),
            P(("dp", "fsdp"), None, None),
            P(("dp", "fsdp"), None, None),
            P(None, ("dp", "fsdp")),
            P(None, ("dp", "fsdp")),
            P(None, ("dp", "fsdp")),
            P(None, ("dp", "fsdp")),
        ),
        check_vma=False,
    )
```

```python
import functools

import jax
import jax.experimental.pallas as pl
import jax.experimental.pallas.tpu as pltpu
import jax.numpy as jnp
from jax import lax
from jax.sharding import PartitionSpec as P

D = 2048
HEADS = 32
KV_HEADS = 8
HEAD = 64
FF = 8192
PIECE = 256
STEP = 5


norm_eps = 1e-05
adam_eps = 1e-08
beta_one = 0.5
beta_two = 0.5
learn_rate = 0.02
gain_rate = 0.3
decay_rate = 0.1
rope_base = 500000.0
masked_score = -1e30


def section_layout(devices, tile_rows):
    counts = [
        (D + 2 * KV_HEADS * HEAD) // tile_rows,
        HEADS * HEAD // tile_rows,
        2 * FF // tile_rows,
        FF // tile_rows,
    ]
    layout = []
    first_tile = 0
    first_slot = 0
    for number in counts:
        capacity = 5 * number // (4 * devices) + 1
        layout.append((first_tile, number, capacity, first_slot))
        first_tile += number
        first_slot += capacity
    return layout


def adam_step(weights, first_moment, second_moment, grads, step, decay, rate):
    new_one = beta_one * first_moment + (1.0 - beta_one) * grads
    new_two = beta_two * second_moment + (1.0 - beta_two) * grads * grads
    correct_one = 1.0 - beta_one**step
    correct_two = 1.0 - beta_two**step
    update = -rate * (
        new_one / correct_one / (jnp.sqrt(new_two / correct_two) + adam_eps) + decay * weights
    )
    return (new_one, new_two, weights + update)


def slot_numbers(owners, layout, caps):
    placed = []
    for first_tile, number, capacity, first_slot in layout:
        mine = owners[first_tile : first_tile + number]
        order = jnp.arange(number, dtype=jnp.int32)
        earlier = (mine[:, None] == mine[None, :]) & (order[None, :] < order[:, None])
        ranked = jnp.sum(earlier.astype(jnp.int32), axis=1)
        placed.append(mine * caps + first_slot + ranked)
    return placed


def filled_mask(owners, layout, device):
    masks = []
    for first_tile, number, capacity, first_slot in layout:
        count = jnp.sum((owners[first_tile : first_tile + number] == device).astype(jnp.int32))
        masks.append(jnp.arange(capacity, dtype=jnp.int32) < count)
    return jnp.concatenate(masks)


def rope_tables(positions, block):
    half_dim = HEAD // 2
    inverse = rope_base ** (-(jnp.arange(half_dim, dtype=jnp.float32) * 2.0 / HEAD))
    angles = positions[:, None] * inverse[None, :]
    cosine = jnp.cos(angles)
    sine = jnp.sin(angles)
    return (
        jnp.tile(jnp.concatenate([cosine, cosine], axis=1), (1, block // HEAD)),
        jnp.tile(jnp.concatenate([-sine, sine], axis=1), (1, block // HEAD)),
    )


def turn_back(grads, cosine, sine):
    tokens, width = grads.shape
    half_dim = HEAD // 2
    heads = grads.reshape(tokens, width // HEAD, 2, half_dim)
    swapped = heads[:, :, ::-1].reshape(tokens, width)
    times = width // cosine.shape[1]
    return grads * jnp.tile(cosine, (1, times)) - swapped * jnp.tile(sine, (1, times))


def tuned_mesh():
    return (lax.axis_size("dp"), lax.axis_size("fsdp")) == (8, 4)


def gather_any(low_tiles, low_gains):
    if tuned_mesh():
        return gather_slots(low_tiles, low_gains)
    return (
        lax.all_gather(low_tiles, ("dp", "fsdp"), axis=0, tiled=True),
        lax.all_gather(low_gains, ("dp", "fsdp"), axis=1, tiled=True),
    )


def scatter_any(grads_wall, caps):
    if tuned_mesh():
        return scatter_slots(grads_wall, caps)
    return lax.psum_scatter(
        grads_wall, ("dp", "fsdp"), scatter_dimension=0, tiled=True
    ).astype(jnp.float32)


VMEM_ASK = 56 << 20
NT = (((1,), (1,)), ((), ()))
NN = (((1,), (0,)), ((), ()))
TN = (((0,), (0,)), ((), ()))


def dot(a, b, dims):
    return lax.dot_general(a, b, dims, preferred_element_type=jnp.float32)


def stream_tiles(table, wall_ref, held, sem, group):
    step = pl.program_id(0)
    steps = pl.num_programs(0)
    depth = held.shape[0]
    buf = lax.rem(step, depth)

    def fetch(at):
        into = lax.rem(at, depth)

        @pl.loop(0, group, unroll=True)
        def _(t):
            pltpu.make_async_copy(
                wall_ref.at[table[at * group + t]], held.at[into, t], sem.at[into]
            ).start()

    @pl.when(step == 0)
    def _():
        for ahead in range(depth - 1):

            @pl.when(ahead < steps)
            def _(ahead=ahead):
                fetch(jnp.int32(ahead))

    @pl.when(step + depth - 1 < steps)
    def _():
        fetch(step + depth - 1)

    pltpu.make_async_copy(held.at[buf], held.at[buf], sem.at[buf]).wait()
    rows = group * wall_ref.shape[1]
    return held[buf].reshape(rows, wall_ref.shape[2])


def store_tiles(table, grads_ref, made, sem, group, value):
    step = pl.program_id(0)
    steps = pl.num_programs(0)
    buf = lax.rem(step, 2)

    def drain(which):
        pltpu.make_async_copy(made.at[which], made.at[which], sem.at[which]).wait()

    @pl.when(step >= 2)
    def _():
        drain(buf)

    made[buf] = value.astype(made.dtype).reshape(made.shape[1:])

    @pl.loop(0, group, unroll=True)
    def _(t):
        pltpu.make_async_copy(
            made.at[buf, t], grads_ref.at[table[step * group + t]], sem.at[buf]
        ).start()

    @pl.when(step == steps - 1)
    def _():
        drain(1 - buf)
        drain(buf)


def swap_halves(u):
    width = u.shape[1]
    lane = lax.broadcasted_iota(jnp.int32, u.shape, 1)
    first = lax.rem(lane, HEAD) < HEAD // 2
    return jnp.where(
        first, pltpu.roll(u, width - HEAD // 2, 1), pltpu.roll(u, HEAD // 2, 1)
    )


def project_kernel(group, turned, table, normed_ref, cos_ref, sin_ref, wall_ref, out_ref, held, sem):
    weights = stream_tiles(table, wall_ref, held, sem, group)
    u = dot(normed_ref[...], weights, NT)
    if turned is None:
        out_ref[...] = (u * cos_ref[...] + swap_halves(u) * sin_ref[...]).astype(out_ref.dtype)
    else:

        @pl.when(pl.program_id(0) < turned)
        def _():
            out_ref[...] = (u * cos_ref[...] + swap_halves(u) * sin_ref[...]).astype(out_ref.dtype)

        @pl.when(pl.program_id(0) >= turned)
        def _():
            out_ref[...] = u.astype(out_ref.dtype)


def full_spec(shape):
    return pl.BlockSpec(shape, lambda i, *_: (0,) * len(shape))


def any_spec():
    return pl.BlockSpec(memory_space=pl.ANY)


AHEAD = 4


def held_tiles(depth, group, wall):
    return pltpu.VMEM((depth, group) + wall.shape[1:], wall.dtype)


def project(table, normed, cosine, sine, wall, turned=None, group=16):
    tokens = normed.shape[0]
    block = group * wall.shape[1]
    steps = table.shape[0] // group
    return pl.pallas_call(
        functools.partial(project_kernel, group, turned),
        grid_spec=pltpu.PrefetchScalarGridSpec(
            num_scalar_prefetch=1,
            grid=(steps,),
            in_specs=[full_spec(normed.shape), full_spec(cosine.shape), full_spec(sine.shape), any_spec()],
            out_specs=pl.BlockSpec((tokens, block), lambda i, *_: (0, i)),
            scratch_shapes=[held_tiles(AHEAD, group, wall), pltpu.SemaphoreType.DMA((AHEAD,))],
        ),
        out_shape=jax.ShapeDtypeStruct((tokens, steps * block), jnp.bfloat16),
        compiler_params=pltpu.CompilerParams(vmem_limit_bytes=VMEM_ASK),
        name="project",
    )(table, normed, cosine, sine, wall)


def mix_kernel(group, table, left_ref, hidden_ref, gain_ref, wall_ref, middle_ref, normed_ref, held, sem):
    step = pl.program_id(0)
    weights = stream_tiles(table, wall_ref, held, sem, group)

    @pl.when(step == 0)
    def _():
        middle_ref[...] = hidden_ref[...].astype(jnp.float32)

    middle_ref[...] += dot(left_ref[...], weights, NN)

    @pl.when(step == pl.num_programs(0) - 1)
    def _():
        middle = middle_ref[...]
        inv = lax.rsqrt(jnp.mean(middle * middle, axis=1, keepdims=True) + norm_eps)
        normed_ref[...] = (middle * inv * gain_ref[...]).astype(normed_ref.dtype)


def mix(table, left, hidden, gain, wall, group=16):
    tokens, width = hidden.shape
    block = group * wall.shape[1]
    return pl.pallas_call(
        functools.partial(mix_kernel, group),
        grid_spec=pltpu.PrefetchScalarGridSpec(
            num_scalar_prefetch=1,
            grid=(table.shape[0] // group,),
            in_specs=[
                pl.BlockSpec((tokens, block), lambda i, *_: (0, i)),
                full_spec(hidden.shape),
                full_spec((1, width)),
                any_spec(),
            ],
            out_specs=[full_spec(hidden.shape), full_spec(hidden.shape)],
            scratch_shapes=[held_tiles(AHEAD, group, wall), pltpu.SemaphoreType.DMA((AHEAD,))],
        ),
        out_shape=[
            jax.ShapeDtypeStruct(hidden.shape, jnp.float32),
            jax.ShapeDtypeStruct(hidden.shape, jnp.bfloat16),
        ],
        compiler_params=pltpu.CompilerParams(vmem_limit_bytes=VMEM_ASK),
        name="mix",
    )(table, left, hidden, gain.reshape(1, width), wall)


def mix_back_kernel(group, table, left_ref, right_ref, wall_ref, old_ref, out_ref, grads_ref, held, made, load_sem, store_sem):
    weights = stream_tiles(table, wall_ref, held, load_sem, group)
    right = right_ref[...]
    out_ref[...] = dot(right, weights, NT).astype(out_ref.dtype)
    store_tiles(table, grads_ref, made, store_sem, group, dot(left_ref[...], right, TN))


def mix_back(table, left, right, wall, grads, group=16):
    tokens, width = right.shape
    block = group * wall.shape[1]
    columns = pl.BlockSpec((tokens, block), lambda i, *_: (0, i))
    return pl.pallas_call(
        functools.partial(mix_back_kernel, group),
        grid_spec=pltpu.PrefetchScalarGridSpec(
            num_scalar_prefetch=1,
            grid=(table.shape[0] // group,),
            in_specs=[columns, full_spec(right.shape), any_spec(), any_spec()],
            out_specs=[columns, any_spec()],
            scratch_shapes=[
                held_tiles(AHEAD, group, wall),
                held_tiles(2, group, wall),
                pltpu.SemaphoreType.DMA((AHEAD,)),
                pltpu.SemaphoreType.DMA((2,)),
            ],
        ),
        out_shape=[
            jax.ShapeDtypeStruct(left.shape, jnp.bfloat16),
            jax.ShapeDtypeStruct(grads.shape, grads.dtype),
        ],
        input_output_aliases={4: 1},
        compiler_params=pltpu.CompilerParams(vmem_limit_bytes=VMEM_ASK),
        name="mix_back",
    )(table, left, right, wall, grads)


def project_back_kernel(group, fresh, table, left_ref, right_ref, wall_ref, old_ref, start_ref, out_ref, grads_ref, held, made, load_sem, store_sem):
    weights = stream_tiles(table, wall_ref, held, load_sem, group)

    @pl.when(pl.program_id(0) == 0)
    def _():
        out_ref[...] = jnp.zeros_like(out_ref) if fresh else start_ref[...]

    left = left_ref[...]
    out_ref[...] += dot(left, weights, NN)
    store_tiles(table, grads_ref, made, store_sem, group, dot(left, right_ref[...], TN))


def project_back(table, left, right, start, wall, grads, group=16):
    tokens, width = right.shape
    block = group * wall.shape[1]
    return pl.pallas_call(
        functools.partial(project_back_kernel, group, start is None),
        grid_spec=pltpu.PrefetchScalarGridSpec(
            num_scalar_prefetch=1,
            grid=(table.shape[0] // group,),
            in_specs=[
                pl.BlockSpec((tokens, block), lambda i, *_: (0, i)),
                full_spec(right.shape),
                any_spec(),
                any_spec(),
                any_spec() if start is None else full_spec(start.shape),
            ],
            out_specs=[full_spec(right.shape), any_spec()],
            scratch_shapes=[
                held_tiles(AHEAD, group, wall),
                held_tiles(2, group, wall),
                pltpu.SemaphoreType.DMA((AHEAD,)),
                pltpu.SemaphoreType.DMA((2,)),
            ],
        ),
        out_shape=[
            jax.ShapeDtypeStruct(right.shape, jnp.float32),
            jax.ShapeDtypeStruct(grads.shape, grads.dtype),
        ],
        input_output_aliases={4: 1},
        compiler_params=pltpu.CompilerParams(vmem_limit_bytes=VMEM_ASK),
        name="project_back",
    )(table, left, right, wall, grads, table if start is None else start)


def fill_mask(places, mask_ref):
    shape = mask_ref.shape
    query = lax.broadcasted_iota(jnp.int32, shape, 0) + places[0]
    key = lax.broadcasted_iota(jnp.int32, shape, 1)
    allowed = key <= query
    for piece in range(places.shape[0] - 1):
        low = places[1 + piece]
        inside_query = (query >= low) & (query < low + PIECE)
        inside_key = (key >= low) & (key < low + PIECE)
        allowed = allowed | (inside_query & inside_key)
    mask_ref[...] = jnp.where(allowed, 1.0, 0.0)


PAIR = 2
GROUP = HEADS // KV_HEADS


def attend_kernel(places, q_ref, k_ref, v_ref, out_ref, lse_ref, mask_ref):
    @pl.when(pl.program_id(0) == 0)
    def _():
        fill_mask(places, mask_ref)

    mask = mask_ref[...] > 0.5
    lane = lax.broadcasted_iota(jnp.int32, lse_ref.shape[1:], 1)
    logs = jnp.zeros(lse_ref.shape[1:], jnp.float32)
    scale = jnp.bfloat16(1.0 / HEAD**0.5)
    for side in range(PAIR):
        k = k_ref[:, side * HEAD : (side + 1) * HEAD]
        v = v_ref[:, side * HEAD : (side + 1) * HEAD]
        for h in range(GROUP):
            head = side * GROUP + h
            cols = slice(head * HEAD, (head + 1) * HEAD)
            scores = jnp.where(mask, dot(q_ref[:, cols] * scale, k, NT), masked_score)
            top = jnp.max(scores, axis=1, keepdims=True)
            raised = jnp.exp(scores - top)
            total = jnp.sum(raised, axis=1, keepdims=True)
            probs = (raised * (1.0 / total)).astype(jnp.bfloat16)
            out_ref[:, cols] = dot(probs, v, NN).astype(out_ref.dtype)
            logs = jnp.where(lane == head, top + jnp.log(total), logs)
    lse_ref[0] = logs


def attend(places, queries, both):
    tokens, width = queries.shape
    length = both.shape[0]
    steps = KV_HEADS // PAIR
    wide = PAIR * GROUP * HEAD
    narrow = PAIR * HEAD
    return pl.pallas_call(
        attend_kernel,
        grid_spec=pltpu.PrefetchScalarGridSpec(
            num_scalar_prefetch=1,
            grid=(steps,),
            in_specs=[
                pl.BlockSpec((tokens, wide), lambda i, *_: (0, i)),
                pl.BlockSpec((length, narrow), lambda i, *_: (0, i)),
                pl.BlockSpec((length, narrow), lambda i, *_: (0, steps + i)),
            ],
            out_specs=[
                pl.BlockSpec((tokens, wide), lambda i, *_: (0, i)),
                pl.BlockSpec((1, tokens, 128), lambda i, *_: (i, 0, 0)),
            ],
            scratch_shapes=[pltpu.VMEM((tokens, length), jnp.float32)],
        ),
        out_shape=[
            jax.ShapeDtypeStruct((tokens, width), jnp.bfloat16),
            jax.ShapeDtypeStruct((steps, tokens, 128), jnp.float32),
        ],
        compiler_params=pltpu.CompilerParams(vmem_limit_bytes=VMEM_ASK),
        name="attend",
    )(places, queries, both, both)


def attend_back_kernel(places, q_ref, k_ref, v_ref, grad_ref, lse_ref, cos_ref, sin_ref, out_ref, both_ref, mask_ref, turn_ref):
    @pl.when(pl.program_id(0) == 0)
    def _():
        fill_mask(places, mask_ref)

    mask = mask_ref[...] > 0.5
    scale = jnp.bfloat16(1.0 / HEAD**0.5)
    for side in range(PAIR):
        here = slice(side * HEAD, (side + 1) * HEAD)
        k = k_ref[:, here]
        v = v_ref[:, here]
        dk = None
        dv = None
        for h in range(GROUP):
            head = side * GROUP + h
            cols = slice(head * HEAD, (head + 1) * HEAD)
            q = q_ref[:, cols] * scale
            grad = grad_ref[:, cols]
            scores = jnp.where(mask, dot(q, k, NT), masked_score)
            probs = jnp.exp(scores - lse_ref[0, :, head : head + 1])
            grad_probs = dot(grad, v, NT)
            row_dot = jnp.sum(probs * grad_probs, axis=1, keepdims=True)
            grad_scores = (probs * (grad_probs - row_dot)).astype(jnp.bfloat16)
            turn_ref[:, cols] = dot(grad_scores, k, NN) * (1.0 / HEAD**0.5)
            dk_part = dot(q, grad_scores, TN)
            dv_part = dot(grad, probs.astype(jnp.bfloat16), TN)
            dk = dk_part if dk is None else dk + dk_part
            dv = dv_part if dv is None else dv + dv_part
        there = slice((PAIR + side) * HEAD, (PAIR + side + 1) * HEAD)
        both_ref[:, here] = dk.T.astype(both_ref.dtype)
        both_ref[:, there] = dv.T.astype(both_ref.dtype)
    wide = cos_ref.shape[1]
    for left in range(0, turn_ref.shape[1], wide):
        u = turn_ref[:, left : left + wide]
        out_ref[:, left : left + wide] = (u * cos_ref[...] - swap_halves(u) * sin_ref[...]).astype(out_ref.dtype)


def attend_back(places, queries, both, grad, lse, cosine, sine):
    tokens, width = queries.shape
    length = both.shape[0]
    steps = KV_HEADS // PAIR
    wide = PAIR * GROUP * HEAD
    narrow = PAIR * HEAD
    columns = pl.BlockSpec((tokens, wide), lambda i, *_: (0, i))
    keys = pl.BlockSpec((length, narrow), lambda i, *_: (0, i))
    return pl.pallas_call(
        attend_back_kernel,
        grid_spec=pltpu.PrefetchScalarGridSpec(
            num_scalar_prefetch=1,
            grid=(steps,),
            in_specs=[
                columns,
                keys,
                pl.BlockSpec((length, narrow), lambda i, *_: (0, steps + i)),
                columns,
                pl.BlockSpec((1, tokens, 128), lambda i, *_: (i, 0, 0)),
                full_spec(cosine.shape),
                full_spec(sine.shape),
            ],
            out_specs=[columns, pl.BlockSpec((length, 2 * narrow), lambda i, *_: (0, i))],
            scratch_shapes=[pltpu.VMEM((tokens, length), jnp.float32), pltpu.VMEM((tokens, wide), jnp.float32)],
        ),
        out_shape=[
            jax.ShapeDtypeStruct((tokens, width), jnp.bfloat16),
            jax.ShapeDtypeStruct((length, 2 * KV_HEADS * HEAD), jnp.bfloat16),
        ],
        compiler_params=pltpu.CompilerParams(vmem_limit_bytes=VMEM_ASK),
        name="attend_back",
    )(places, queries, both, both, grad, lse, cosine, sine)


def ffn_kernel(group, gate_s, up_s, down_s, normed_ref, cot_ref, wall_ref, out_ref, back_ref, grads_ref, held, made, load_sem, store_sem):
    step = pl.program_id(0)
    steps = pl.num_programs(0)
    tables = (gate_s, up_s, down_s)
    tile_rows = wall_ref.shape[1]
    width = wall_ref.shape[2]
    rows = group * tile_rows

    def fetch(at, buf):
        for kind in range(3):
            @pl.loop(0, group, unroll=True)
            def _(t, kind=kind):
                pltpu.make_async_copy(wall_ref.at[tables[kind][at * group + t]], held.at[buf, kind, t], load_sem.at[buf]).start()

    def drain(buf):
        pltpu.make_async_copy(made.at[buf], made.at[buf], store_sem.at[buf]).wait()

    buf = lax.rem(step, 2)

    @pl.when(step == 0)
    def _():
        fetch(0, 0)
        out_ref[...] = jnp.zeros_like(out_ref)
        back_ref[...] = jnp.zeros_like(back_ref)

    @pl.when(step + 1 < steps)
    def _():
        fetch(step + 1, 1 - buf)

    pltpu.make_async_copy(held.at[buf], held.at[buf], load_sem.at[buf]).wait()

    @pl.when(step >= 2)
    def _():
        drain(buf)

    normed = normed_ref[...]
    cot = cot_ref[...]
    w_gate = held[buf, 0].reshape(rows, width)
    w_up = held[buf, 1].reshape(rows, width)
    w_down = held[buf, 2].reshape(rows, width)
    nt = (((1,), (1,)), ((), ()))
    nn = (((1,), (0,)), ((), ()))
    tn = (((0,), (0,)), ((), ()))

    def dot(a, b, dims):
        return lax.dot_general(a, b, dims, preferred_element_type=jnp.float32)

    gate = dot(normed, w_gate, nt)
    up = dot(normed, w_up, nt)
    hidden = dot(cot, w_down, nt)
    sig = jax.nn.sigmoid(gate)
    silu = gate * sig
    act = (silu * up).astype(jnp.bfloat16)
    g_gate = (hidden * up * sig * (1.0 + gate * (1.0 - sig))).astype(jnp.bfloat16)
    g_up = (hidden * silu).astype(jnp.bfloat16)
    out_ref[...] += dot(act, w_down, nn)
    back_ref[...] += dot(g_gate, w_gate, nn) + dot(g_up, w_up, nn)
    made[buf, 0] = dot(g_gate, normed, tn).astype(jnp.bfloat16).reshape(group, tile_rows, width)
    made[buf, 1] = dot(g_up, normed, tn).astype(jnp.bfloat16).reshape(group, tile_rows, width)
    made[buf, 2] = dot(act, cot, tn).astype(jnp.bfloat16).reshape(group, tile_rows, width)
    for kind in range(3):
        @pl.loop(0, group, unroll=True)
        def _(t, kind=kind):
            pltpu.make_async_copy(made.at[buf, kind, t], grads_ref.at[tables[kind][step * group + t]], store_sem.at[buf]).start()

    @pl.when(step == steps - 1)
    def _():
        drain(1 - buf)
        drain(buf)

def ffn_call(gate_s, up_s, down_s, normed, cot, wall, group=16):
    tokens, width = normed.shape
    steps = gate_s.shape[0] // group
    tr = wall.shape[1]
    full = pl.BlockSpec((tokens, width), lambda i, *_: (0, 0))
    return pl.pallas_call(
        functools.partial(ffn_kernel, group),
        grid_spec=pltpu.PrefetchScalarGridSpec(
            num_scalar_prefetch=3, grid=(steps,),
            in_specs=[full, full, pl.BlockSpec(memory_space=pl.ANY)],
            out_specs=[full, full, pl.BlockSpec(memory_space=pl.ANY)],
            scratch_shapes=[pltpu.VMEM((2, 3, group, tr, width), jnp.bfloat16), pltpu.VMEM((2, 3, group, tr, width), jnp.bfloat16),
                pltpu.SemaphoreType.DMA((2,)), pltpu.SemaphoreType.DMA((2,))]),
        out_shape=[jax.ShapeDtypeStruct((tokens, width), jnp.float32), jax.ShapeDtypeStruct((tokens, width), jnp.float32), jax.ShapeDtypeStruct(wall.shape, jnp.bfloat16)],
        compiler_params=pltpu.CompilerParams(vmem_limit_bytes=56 << 20, dimension_semantics=("arbitrary",)),
        name="ffn",
    )(gate_s, up_s, down_s, normed, cot, wall)


MESH = pl.DeviceIdType.MESH
EVERY = slice(None)
GATHER_ROUTES = (
    ("z1", "z2", "z3", "x", "y", "core"),
    ("z1", "z2", "z3", "y", "x", "core"),
    ("x", "z1", "z2", "z3", "y", "core"),
    ("y", "z1", "z2", "z3", "x", "core"),
)


def position():
    dp = lax.axis_index("dp")
    return dp // 4, lax.rem(dp // 2, 2), lax.rem(dp, 2), lax.axis_index("fsdp")


def target(hop):
    y, x, c, z = position()
    if hop == "x":
        x = 1 - x
    elif hop == "y":
        y = 1 - y
    elif hop == "core":
        c = 1 - c
    elif hop == "back":
        z = lax.rem(z + 3, 4)
    else:
        z = lax.rem(z + 1, 4)
    return (y * 4 + x * 2 + c, z)


def enter(hops):
    barrier = pltpu.get_barrier_semaphore()
    for hop in hops:
        pl.semaphore_signal(barrier, inc=1, device_id=target(hop), device_id_type=MESH)
    pl.semaphore_wait(barrier, len(hops))


def split_slots(caps):
    small = caps // 6
    third = (caps - 2 * small) // 2
    counts = (small, small, third, caps - 2 * small - third)
    starts = (0, small, 2 * small, 2 * small + third)
    return counts, starts


GATHER_DELAYS = (0, 1, 0, 0)
SCATTER_DELAYS = (4, 4, 0, 0)


def round_count(counts, delays):
    return max(
        delay + (2 * count - 1 if route < 2 else count)
        for route, (count, delay) in enumerate(zip(counts, delays))
    )


def turn(route, at, counts, delays):
    at = at - delays[route]
    if route < 2:
        live = (at >= 0) & (lax.rem(at + 64, 2) == 0) & (at < 2 * counts[route])
        return live, at // 2
    return (at >= 0) & (at < counts[route]), at


def gather_kernel(mine_ref, gain_ref, wall_ref, gains_ref, own_sem, send_sem, recv_sem):
    y, x, c, z = position()
    counts, starts = split_slots(mine_ref.shape[0])
    rounds = round_count(counts, GATHER_DELAYS)
    own = pltpu.make_async_copy(mine_ref, wall_ref.at[y, x, c, z], own_sem.at[0])
    own_gain = pltpu.make_async_copy(gain_ref, gains_ref.at[y, x, c, z], own_sem.at[1])
    own.start()
    own_gain.start()
    enter(("x", "y", "core", "z", "back"))
    own.wait()
    own_gain.wait()

    def region(route, stage):
        hops = GATHER_ROUTES[route % 4]
        hop = hops[stage]
        done = hops[:stage]
        at_y = EVERY if "y" in done else y
        at_x = EVERY if "x" in done else x
        at_z = EVERY if "z3" in done else z
        if hop in ("z1", "z2", "z3"):
            at_z = lax.rem(z + 5 - int(hop[1]), 4)
        return at_y, at_x, c, at_z

    def copy(route, stage, index):
        if route == 4:
            view = gains_ref.at[region(route, stage)]
        else:
            view = wall_ref.at[region(route, stage) + (starts[route] + index,)]
        return pltpu.make_async_remote_copy(
            src_ref=view,
            dst_ref=view,
            send_sem=send_sem.at[route, stage],
            recv_sem=recv_sem.at[route, stage, index],
            device_id=target(GATHER_ROUTES[route % 4][stage]),
            device_id_type=MESH,
        )

    stages = len(GATHER_ROUTES[0])

    @pl.loop(0, rounds + stages)
    def _(t):
        for stage in range(stages + 1):
            for route in range(5):
                if route == 4:
                    live, index = t == stage, 0
                else:
                    live, index = turn(route, t - stage, counts, GATHER_DELAYS)

                @pl.when(live)
                def _(stage=stage, route=route, index=index):
                    if stage > 0:
                        copy(route, stage - 1, index).wait()
                    if stage < stages:
                        copy(route, stage, index).start()


def gather_slots(low_tiles, low_gains):
    caps, rows, width = low_tiles.shape
    counts, starts = split_slots(caps)
    kind = low_tiles.dtype
    vmem = pl.BlockSpec(memory_space=pltpu.VMEM)
    padded = jnp.pad(low_gains, ((0, 16 - low_gains.shape[0]), (0, 128 - low_gains.shape[1])))
    wall, gains = pl.pallas_call(
        gather_kernel,
        out_shape=[
            jax.ShapeDtypeStruct((2, 2, 2, 4, caps, rows, width), kind),
            jax.ShapeDtypeStruct((2, 2, 2, 4) + padded.shape, kind),
        ],
        in_specs=[vmem, vmem],
        out_specs=[pl.BlockSpec(memory_space=pl.ANY)] * 2,
        scratch_shapes=[
            pltpu.SemaphoreType.DMA((2,)),
            pltpu.SemaphoreType.DMA((5, 6)),
            pltpu.SemaphoreType.DMA((5, 6, max(counts))),
        ],
        compiler_params=pltpu.CompilerParams(
            collective_id=0, has_side_effects=True, vmem_limit_bytes=24 << 20
        ),
        name="gather_slots",
    )(low_tiles, padded)
    gains = gains.reshape((32,) + padded.shape)[:, : low_gains.shape[0], : low_gains.shape[1]]
    gains = gains.transpose(1, 0, 2).reshape(low_gains.shape[0], -1)
    return wall.reshape(32 * caps, rows, width), gains


SCATTER_ROUTES = (
    ("core", "y", "x", "z1", "z2", "z3", "end"),
    ("core", "x", "y", "z1", "z2", "z3", "end"),
    ("core", "y", "z1", "z2", "z3", "x", "end"),
    ("core", "x", "z1", "z2", "z3", "y", "end"),
)


def scatter_extent(route, stage):
    hops = SCATTER_ROUTES[route]
    done = hops[1 : stage + 1] if hops[stage] in ("x", "y") else hops[1:stage]
    extent = []
    if "x" not in done or "y" not in done:
        extent.append(2)
    if not any(hop[0] == "z" for hop in hops[: stage + 1]):
        extent.append(4)
    return tuple(extent)


def scatter_terms(route, stage):
    hops = SCATTER_ROUTES[route]
    done = hops[1:stage]
    return 2 + ("x" in done) + ("y" in done) + ("z1" in done)


def scatter_kernel(look, wall_ref, out_ref, core_ref, first_ref, second_ref, ring_ref, last_ref, *scratch):
    y, x, c, z = position()
    caps, rows, width = out_ref.shape
    counts, starts = split_slots(caps)
    rounds = round_count(counts, SCATTER_DELAYS)
    stages = len(SCATTER_ROUTES[0])
    held = {}
    made = {}
    scratch = list(scratch)
    for route in range(4):
        for stage in range(1, stages):
            held[route, stage] = scratch.pop(0)
            if stage < stages - 1:
                made[route, stage] = scratch.pop(0)
    load_sem, send_sem, recv_sem = scratch
    enter(("x", "y", "core", "z", "back"))

    def pick(hop, mine, other):
        return other if hop else mine

    def landing(route, stage, slot):
        hops = SCATTER_ROUTES[route]
        hop = hops[stage]
        if hop == "core":
            return core_ref.at[:, :, :, slot]
        if hop[0] == "z":
            ring = ring_ref.at[int(hop[1]) - 1]
            return ring.at[0, slot] if route < 2 else ring.at[:, slot]
        if stage == 1:
            return first_ref.at[:, :, slot]
        if stage == 2:
            return second_ref.at[:, slot]
        return last_ref.at[slot]

    def terms(route, stage, slot):
        hops = SCATTER_ROUTES[route]
        hop = hops[stage]
        done = hops[1:stage]
        at_y = 1 - y if hop == "y" else (y if "y" in done else EVERY)
        at_x = 1 - x if hop == "x" else (x if "x" in done else EVERY)
        at_z = EVERY
        if hop[0] == "z":
            at_z = lax.rem(z + 4 - int(hop[1]), 4)
        elif "z3" in done:
            at_z = z
        views = [wall_ref.at[at_y, at_x, c, at_z, slot], core_ref.at[at_y, at_x, at_z, slot]]
        other = at_x if hops[1] == "y" else at_y
        if stage > 1:
            views.append(first_ref.at[other, at_z, slot])
        if route < 2 and stage > 2:
            views.append(second_ref.at[at_z, slot])
        if hop in ("z2", "z3"):
            ring = ring_ref.at[int(hop[1]) - 2]
            views.append(ring.at[0, slot] if route < 2 else ring.at[:, slot])
        elif "z3" in done:
            ring = ring_ref.at[2]
            views.append(ring.at[0, slot] if route < 2 else ring.at[other, slot])
        if route >= 2 and hop == "end":
            views.append(last_ref.at[slot])
        return views

    def send(route, stage, index):
        slot = starts[route] + index
        if stage == 0:
            source = wall_ref.at[:, :, 1 - c, :, slot]
        else:
            source = made[route, stage]
        return pltpu.make_async_remote_copy(
            src_ref=source,
            dst_ref=landing(route, stage, slot),
            send_sem=send_sem.at[route, stage],
            recv_sem=recv_sem.at[route, stage, index],
            device_id=target(SCATTER_ROUTES[route][stage]),
            device_id_type=MESH,
        )

    def early(route, stage, index):
        if stage > 0:
            for k, view in enumerate(terms(route, stage, starts[route] + index)[:-1]):
                pltpu.make_async_copy(view, held[route, stage].at[k], load_sem.at[route, stage]).start()

    def late(route, stage, index):
        if stage > 0:
            send(route, stage - 1, index).wait()
            view = terms(route, stage, starts[route] + index)[-1]
            last = held[route, stage].shape[0] - 1
            pltpu.make_async_copy(view, held[route, stage].at[last], load_sem.at[route, stage]).start()

    def finish(route, stage, index):
        if stage > 0:
            buf = held[route, stage]
            pltpu.make_async_copy(buf, buf, load_sem.at[route, stage]).wait()
            number = buf.shape[0]
            extent = buf.shape[1:-2]
            blocks = 1
            for size in extent:
                blocks *= size
            part = min(width, 512)

            @pl.loop(0, blocks)
            def _(block):
                if len(extent) == 2:
                    at = (block // extent[1], lax.rem(block, extent[1]))
                elif len(extent) == 1:
                    at = (block,)
                else:
                    at = ()
                for left in range(0, width, part):
                    cols = pl.ds(left, part)
                    total = buf[(0,) + at + (EVERY, cols)].astype(jnp.float32)
                    for k in range(1, number):
                        total += buf[(k,) + at + (EVERY, cols)].astype(jnp.float32)
                    if stage == stages - 1:
                        out_ref[starts[route] + index, :, cols] = total
                    else:
                        made[route, stage][at + (EVERY, cols)] = total.astype(made[route, stage].dtype)

        if stage < stages - 1:
            send(route, stage, index).start()

    @pl.loop(0, rounds + stages - 1)
    def _(t):
        items = [(stage, route) for stage in range(stages - 1, -1, -1) for route in range(4)]

        def run(which, work):
            stage, route = items[which]
            live, index = turn(route, t - stage, counts, SCATTER_DELAYS)

            @pl.when(live)
            def _():
                work(route, stage, index)

        far, near = look
        for which in range(len(items) + far):
            if which < len(items):
                run(which, early)
            if far - near <= which < len(items) + far - near:
                run(which - far + near, late)
            if which >= far:
                run(which - far, finish)


def scatter_slots(grads_wall, caps, look=(4, 1)):
    rows, width = grads_wall.shape[1:]
    kind = grads_wall.dtype
    wall = grads_wall.reshape(2, 2, 2, 4, caps, rows, width)
    counts, starts = split_slots(caps)
    stages = len(SCATTER_ROUTES[0])
    scratch = []
    for route in range(4):
        for stage in range(1, stages):
            extent = scatter_extent(route, stage)
            scratch.append(pltpu.VMEM((scatter_terms(route, stage),) + extent + (rows, width), kind))
            if stage < stages - 1:
                scratch.append(pltpu.VMEM(extent + (rows, width), kind))
    tile = (caps, rows, width)
    out = pl.pallas_call(
        functools.partial(scatter_kernel, look),
        out_shape=[
            jax.ShapeDtypeStruct(tile, jnp.float32),
            jax.ShapeDtypeStruct((2, 2, 4) + tile, kind),
            jax.ShapeDtypeStruct((2, 4) + tile, kind),
            jax.ShapeDtypeStruct((4,) + tile, kind),
            jax.ShapeDtypeStruct((3, 2) + tile, kind),
            jax.ShapeDtypeStruct(tile, kind),
        ],
        in_specs=[pl.BlockSpec(memory_space=pl.ANY)],
        out_specs=[pl.BlockSpec(memory_space=pltpu.VMEM)] + [pl.BlockSpec(memory_space=pl.ANY)] * 5,
        scratch_shapes=scratch
        + [
            pltpu.SemaphoreType.DMA((4, stages)),
            pltpu.SemaphoreType.DMA((4, stages)),
            pltpu.SemaphoreType.DMA((4, stages, max(counts))),
        ],
        compiler_params=pltpu.CompilerParams(
            collective_id=1, has_side_effects=True, vmem_limit_bytes=56 << 20
        ),
        name="scatter_slots",
    )(wall)
    return out[0]


def shards(
    hidden_in,
    piece_starts,
    out_cotangent,
    owners,
    master,
    moment_one,
    moment_two,
    gain_master,
    gain_one,
    gain_two,
):
    devices = lax.axis_size("dp") * lax.axis_size("fsdp")
    caps, tile_rows, model_width = master.shape
    layout = section_layout(devices, tile_rows)
    slot_qkv, slot_out, slot_ffn, slot_down = slot_numbers(owners, layout, caps)
    query_tiles = model_width // tile_rows
    slot_query, slot_both = slot_qkv[:query_tiles], slot_qkv[query_tiles:]
    half = slot_ffn.shape[0] // 2
    wall, gains_low = gather_any(
        master.astype(jnp.bfloat16), gain_master.astype(jnp.bfloat16)
    )
    gains_low = gains_low.astype(jnp.float32)
    gain_attn = gains_low[0]
    gain_ffn = gains_low[1]
    tokens = hidden_in.astype(jnp.float32)
    local_len = tokens.shape[0]
    kv_width = KV_HEADS * HEAD
    first = lax.axis_index("fsdp") * local_len
    positions = first + jnp.arange(local_len, dtype=jnp.int32)
    places = jnp.concatenate([first[None].astype(jnp.int32), piece_starts[0]])
    cosine, sine = rope_tables(positions.astype(jnp.float32), 16 * tile_rows)
    inv_one = lax.rsqrt(jnp.mean(tokens * tokens, axis=1, keepdims=True) + norm_eps)
    normed = (tokens * inv_one * gain_attn).astype(jnp.bfloat16)
    both_local = project(slot_both, normed, cosine, sine, wall, turned=kv_width // (16 * tile_rows))
    both = lax.all_gather(both_local, "fsdp", axis=0, tiled=True)
    queries = project(slot_query, normed, cosine, sine, wall)
    attended, lse = attend(places, queries, both)
    middle, normed_two = mix(slot_out, attended, hidden_in, gain_ffn, wall)
    inv_two = lax.rsqrt(jnp.mean(middle * middle, axis=1, keepdims=True) + norm_eps)
    ffn_out, grad_normed_two, grads_wall = ffn_call(
        slot_ffn[:half], slot_ffn[half:], slot_down, normed_two, out_cotangent, wall
    )
    block_out = (middle + ffn_out).astype(jnp.bfloat16)
    scaled_two = grad_normed_two * gain_ffn
    grad_middle = (
        out_cotangent.astype(jnp.float32)
        + inv_two * scaled_two
        - middle * inv_two**3 * jnp.mean(scaled_two * middle, axis=1, keepdims=True)
    )
    gain_two_term = jnp.sum(grad_normed_two * middle * inv_two, axis=0)
    grad_branch = grad_middle.astype(jnp.bfloat16)
    grad_attended, grads_wall = mix_back(slot_out, attended, grad_branch, wall, grads_wall)
    grad_query, both_terms = attend_back(
        places, queries, both, grad_attended, lse, cosine, sine
    )
    both_sum = lax.psum_scatter(both_terms, "fsdp", scatter_dimension=0, tiled=True).astype(
        jnp.float32
    )
    grad_normed, grads_wall = project_back(slot_query, grad_query, normed, None, wall, grads_wall)
    both_sum = both_sum.reshape(local_len, KV_HEADS // PAIR, 2, PAIR * HEAD)
    grad_key = turn_back(both_sum[:, :, 0].reshape(local_len, kv_width), cosine, sine)
    grad_value = both_sum[:, :, 1].reshape(local_len, kv_width)
    grad_both = jnp.concatenate([grad_key, grad_value], axis=1).astype(jnp.bfloat16)
    grad_normed, grads_wall = project_back(
        slot_both, grad_both, normed, grad_normed, wall, grads_wall
    )
    keep_slot = filled_mask(owners, layout, lax.axis_index(("dp", "fsdp")))[:, None, None]
    weight_grad = jnp.where(keep_slot, scatter_any(grads_wall, caps), 0.0)
    scaled_one = grad_normed * gain_attn
    input_grad = (
        grad_middle
        + inv_one * scaled_one
        - tokens * inv_one**3 * jnp.mean(scaled_one * tokens, axis=1, keepdims=True)
    )
    gain_one_term = jnp.sum(grad_normed * tokens * inv_one, axis=0)
    gain_grad = lax.psum_scatter(
        jnp.stack([gain_one_term, gain_two_term]), ("dp", "fsdp"), scatter_dimension=1, tiled=True
    )
    step = float(STEP)
    new_one, new_two, new_weights = adam_step(
        master, moment_one, moment_two, weight_grad, step, decay_rate, learn_rate
    )
    new_one = jnp.where(keep_slot, new_one, 0.0)
    new_two = jnp.where(keep_slot, new_two, 0.0)
    new_weights = jnp.where(keep_slot, new_weights, 0.0)
    new_gain_one, new_gain_two, new_gains = adam_step(
        gain_master, gain_one, gain_two, gain_grad, step, 0.0, gain_rate
    )
    return (
        block_out,
        input_grad,
        weight_grad,
        new_weights,
        new_one,
        new_two,
        gain_grad,
        new_gains,
        new_gain_one,
        new_gain_two,
    )


def solution(mesh):
    return jax.shard_map(
        shards,
        mesh=mesh,
        in_specs=(
            P(("dp", "fsdp"), None),
            P("dp", None),
            P(("dp", "fsdp"), None),
            P(),
            P(("dp", "fsdp"), None, None),
            P(("dp", "fsdp"), None, None),
            P(("dp", "fsdp"), None, None),
            P(None, ("dp", "fsdp")),
            P(None, ("dp", "fsdp")),
            P(None, ("dp", "fsdp")),
        ),
        out_specs=(
            P(("dp", "fsdp"), None),
            P(("dp", "fsdp"), None),
            P(("dp", "fsdp"), None, None),
            P(("dp", "fsdp"), None, None),
            P(("dp", "fsdp"), None, None),
            P(("dp", "fsdp"), None, None),
            P(None, ("dp", "fsdp")),
            P(None, ("dp", "fsdp")),
            P(None, ("dp", "fsdp")),
            P(None, ("dp", "fsdp")),
        ),
        check_vma=False,
    )
```

```python
import functools

import jax
import jax.experimental.pallas as pl
import jax.experimental.pallas.tpu as pltpu
import jax.numpy as jnp
from jax import lax
from jax.sharding import PartitionSpec as P

D = 2048
HEADS = 32
KV_HEADS = 8
HEAD = 64
FF = 8192
PIECE = 256
STEP = 5


norm_eps = 1e-05
adam_eps = 1e-08
beta_one = 0.5
beta_two = 0.5
learn_rate = 0.02
gain_rate = 0.3
decay_rate = 0.1
rope_base = 500000.0
masked_score = -1e30


def section_layout(devices, tile_rows):
    counts = [
        (D + 2 * KV_HEADS * HEAD) // tile_rows,
        HEADS * HEAD // tile_rows,
        2 * FF // tile_rows,
        FF // tile_rows,
    ]
    layout = []
    first_tile = 0
    first_slot = 0
    for number in counts:
        capacity = 5 * number // (4 * devices) + 1
        layout.append((first_tile, number, capacity, first_slot))
        first_tile += number
        first_slot += capacity
    return layout


def adam_step(weights, first_moment, second_moment, grads, step, decay, rate):
    new_one = beta_one * first_moment + (1.0 - beta_one) * grads
    new_two = beta_two * second_moment + (1.0 - beta_two) * grads * grads
    correct_one = 1.0 - beta_one**step
    correct_two = 1.0 - beta_two**step
    update = -rate * (
        new_one / correct_one / (jnp.sqrt(new_two / correct_two) + adam_eps) + decay * weights
    )
    return (new_one, new_two, weights + update)


def slot_numbers(owners, layout, caps):
    placed = []
    for first_tile, number, capacity, first_slot in layout:
        mine = owners[first_tile : first_tile + number]
        order = jnp.arange(number, dtype=jnp.int32)
        earlier = (mine[:, None] == mine[None, :]) & (order[None, :] < order[:, None])
        ranked = jnp.sum(earlier.astype(jnp.int32), axis=1)
        placed.append(mine * caps + first_slot + ranked)
    return placed


def filled_mask(owners, layout, device):
    masks = []
    for first_tile, number, capacity, first_slot in layout:
        count = jnp.sum((owners[first_tile : first_tile + number] == device).astype(jnp.int32))
        masks.append(jnp.arange(capacity, dtype=jnp.int32) < count)
    return jnp.concatenate(masks)


def rope_tables(positions, block):
    half_dim = HEAD // 2
    inverse = rope_base ** (-(jnp.arange(half_dim, dtype=jnp.float32) * 2.0 / HEAD))
    angles = positions[:, None] * inverse[None, :]
    cosine = jnp.cos(angles)
    sine = jnp.sin(angles)
    return (
        jnp.tile(jnp.concatenate([cosine, cosine], axis=1), (1, block // HEAD)),
        jnp.tile(jnp.concatenate([-sine, sine], axis=1), (1, block // HEAD)),
    )


def turn_back(grads, cosine, sine):
    tokens, width = grads.shape
    half_dim = HEAD // 2
    heads = grads.reshape(tokens, width // HEAD, 2, half_dim)
    swapped = heads[:, :, ::-1].reshape(tokens, width)
    times = width // cosine.shape[1]
    return grads * jnp.tile(cosine, (1, times)) - swapped * jnp.tile(sine, (1, times))


def tuned_mesh():
    return (lax.axis_size("dp"), lax.axis_size("fsdp")) == (8, 4)


def gather_any(low_tiles, low_gains):
    if tuned_mesh():
        return gather_slots(low_tiles, low_gains)
    return (
        lax.all_gather(low_tiles, ("dp", "fsdp"), axis=0, tiled=True),
        lax.all_gather(low_gains, ("dp", "fsdp"), axis=1, tiled=True),
    )


def scatter_any(grads_wall, gain_terms, caps):
    number = gain_terms.shape[0]
    if tuned_mesh():
        padded = jnp.pad(gain_terms, ((0, 8 - number), (0, 0)))
        grads, total = scatter_slots(grads_wall, padded, caps)
        width = gain_terms.shape[1] // 32
        device = lax.axis_index(("dp", "fsdp"))
        return grads, lax.dynamic_slice_in_dim(total[:number], device * width, width, 1)
    grads = lax.psum_scatter(grads_wall, ("dp", "fsdp"), scatter_dimension=0, tiled=True)
    gain_grad = lax.psum_scatter(gain_terms, ("dp", "fsdp"), scatter_dimension=1, tiled=True)
    return grads.astype(jnp.float32), gain_grad


VMEM_ASK = 56 << 20
NT = (((1,), (1,)), ((), ()))
NN = (((1,), (0,)), ((), ()))
TN = (((0,), (0,)), ((), ()))


def dot(a, b, dims):
    return lax.dot_general(a, b, dims, preferred_element_type=jnp.float32)


def stream_tiles(table, wall_ref, held, sem, group):
    step = pl.program_id(0)
    steps = pl.num_programs(0)
    depth = held.shape[0]
    buf = lax.rem(step, depth)

    def fetch(at):
        into = lax.rem(at, depth)

        @pl.loop(0, group, unroll=True)
        def _(t):
            pltpu.make_async_copy(
                wall_ref.at[table[at * group + t]], held.at[into, t], sem.at[into]
            ).start()

    @pl.when(step == 0)
    def _():
        for ahead in range(depth - 1):

            @pl.when(ahead < steps)
            def _(ahead=ahead):
                fetch(jnp.int32(ahead))

    @pl.when(step + depth - 1 < steps)
    def _():
        fetch(step + depth - 1)

    pltpu.make_async_copy(held.at[buf], held.at[buf], sem.at[buf]).wait()
    rows = group * wall_ref.shape[1]
    return held[buf].reshape(rows, wall_ref.shape[2])


def store_tiles(table, grads_ref, made, sem, group, value):
    step = pl.program_id(0)
    steps = pl.num_programs(0)
    buf = lax.rem(step, 2)

    def drain(which):
        pltpu.make_async_copy(made.at[which], made.at[which], sem.at[which]).wait()

    @pl.when(step >= 2)
    def _():
        drain(buf)

    made[buf] = value.astype(made.dtype).reshape(made.shape[1:])

    @pl.loop(0, group, unroll=True)
    def _(t):
        pltpu.make_async_copy(
            made.at[buf, t], grads_ref.at[table[step * group + t]], sem.at[buf]
        ).start()

    @pl.when(step == steps - 1)
    def _():
        drain(1 - buf)
        drain(buf)


def swap_halves(u):
    width = u.shape[1]
    lane = lax.broadcasted_iota(jnp.int32, u.shape, 1)
    first = lax.rem(lane, HEAD) < HEAD // 2
    return jnp.where(
        first, pltpu.roll(u, width - HEAD // 2, 1), pltpu.roll(u, HEAD // 2, 1)
    )


def project_kernel(group, turned, table, normed_ref, cos_ref, sin_ref, wall_ref, out_ref, held, sem):
    weights = stream_tiles(table, wall_ref, held, sem, group)
    u = dot(normed_ref[...], weights, NT)
    if turned is None:
        out_ref[...] = (u * cos_ref[...] + swap_halves(u) * sin_ref[...]).astype(out_ref.dtype)
    else:

        @pl.when(pl.program_id(0) < turned)
        def _():
            out_ref[...] = (u * cos_ref[...] + swap_halves(u) * sin_ref[...]).astype(out_ref.dtype)

        @pl.when(pl.program_id(0) >= turned)
        def _():
            out_ref[...] = u.astype(out_ref.dtype)


def full_spec(shape):
    return pl.BlockSpec(shape, lambda i, *_: (0,) * len(shape))


def any_spec():
    return pl.BlockSpec(memory_space=pl.ANY)


AHEAD = 4


def held_tiles(depth, group, wall):
    return pltpu.VMEM((depth, group) + wall.shape[1:], wall.dtype)


def project(table, normed, cosine, sine, wall, turned=None, group=16):
    tokens = normed.shape[0]
    block = group * wall.shape[1]
    steps = table.shape[0] // group
    return pl.pallas_call(
        functools.partial(project_kernel, group, turned),
        grid_spec=pltpu.PrefetchScalarGridSpec(
            num_scalar_prefetch=1,
            grid=(steps,),
            in_specs=[full_spec(normed.shape), full_spec(cosine.shape), full_spec(sine.shape), any_spec()],
            out_specs=pl.BlockSpec((tokens, block), lambda i, *_: (0, i)),
            scratch_shapes=[held_tiles(AHEAD, group, wall), pltpu.SemaphoreType.DMA((AHEAD,))],
        ),
        out_shape=jax.ShapeDtypeStruct((tokens, steps * block), jnp.bfloat16),
        compiler_params=pltpu.CompilerParams(vmem_limit_bytes=VMEM_ASK),
        name="project",
    )(table, normed, cosine, sine, wall)


def mix_kernel(group, table, left_ref, hidden_ref, gain_ref, wall_ref, middle_ref, normed_ref, held, sem):
    step = pl.program_id(0)
    weights = stream_tiles(table, wall_ref, held, sem, group)

    @pl.when(step == 0)
    def _():
        middle_ref[...] = hidden_ref[...].astype(jnp.float32)

    middle_ref[...] += dot(left_ref[...], weights, NN)

    @pl.when(step == pl.num_programs(0) - 1)
    def _():
        middle = middle_ref[...]
        inv = lax.rsqrt(jnp.mean(middle * middle, axis=1, keepdims=True) + norm_eps)
        normed_ref[...] = (middle * inv * gain_ref[...]).astype(normed_ref.dtype)


def mix(table, left, hidden, gain, wall, group=16):
    tokens, width = hidden.shape
    block = group * wall.shape[1]
    return pl.pallas_call(
        functools.partial(mix_kernel, group),
        grid_spec=pltpu.PrefetchScalarGridSpec(
            num_scalar_prefetch=1,
            grid=(table.shape[0] // group,),
            in_specs=[
                pl.BlockSpec((tokens, block), lambda i, *_: (0, i)),
                full_spec(hidden.shape),
                full_spec((1, width)),
                any_spec(),
            ],
            out_specs=[full_spec(hidden.shape), full_spec(hidden.shape)],
            scratch_shapes=[held_tiles(AHEAD, group, wall), pltpu.SemaphoreType.DMA((AHEAD,))],
        ),
        out_shape=[
            jax.ShapeDtypeStruct(hidden.shape, jnp.float32),
            jax.ShapeDtypeStruct(hidden.shape, jnp.bfloat16),
        ],
        compiler_params=pltpu.CompilerParams(vmem_limit_bytes=VMEM_ASK),
        name="mix",
    )(table, left, hidden, gain.reshape(1, width), wall)


def mix_back_kernel(group, table, left_ref, right_ref, wall_ref, old_ref, out_ref, grads_ref, held, made, load_sem, store_sem):
    weights = stream_tiles(table, wall_ref, held, load_sem, group)
    right = right_ref[...]
    out_ref[...] = dot(right, weights, NT).astype(out_ref.dtype)
    store_tiles(table, grads_ref, made, store_sem, group, dot(left_ref[...], right, TN))


def mix_back(table, left, right, wall, grads, group=16):
    tokens, width = right.shape
    block = group * wall.shape[1]
    columns = pl.BlockSpec((tokens, block), lambda i, *_: (0, i))
    return pl.pallas_call(
        functools.partial(mix_back_kernel, group),
        grid_spec=pltpu.PrefetchScalarGridSpec(
            num_scalar_prefetch=1,
            grid=(table.shape[0] // group,),
            in_specs=[columns, full_spec(right.shape), any_spec(), any_spec()],
            out_specs=[columns, any_spec()],
            scratch_shapes=[
                held_tiles(AHEAD, group, wall),
                held_tiles(2, group, wall),
                pltpu.SemaphoreType.DMA((AHEAD,)),
                pltpu.SemaphoreType.DMA((2,)),
            ],
        ),
        out_shape=[
            jax.ShapeDtypeStruct(left.shape, jnp.bfloat16),
            jax.ShapeDtypeStruct(grads.shape, grads.dtype),
        ],
        input_output_aliases={4: 1},
        compiler_params=pltpu.CompilerParams(vmem_limit_bytes=VMEM_ASK),
        name="mix_back",
    )(table, left, right, wall, grads)


def project_back_kernel(group, fresh, table, left_ref, right_ref, wall_ref, old_ref, start_ref, out_ref, grads_ref, held, made, load_sem, store_sem):
    weights = stream_tiles(table, wall_ref, held, load_sem, group)

    @pl.when(pl.program_id(0) == 0)
    def _():
        out_ref[...] = jnp.zeros_like(out_ref) if fresh else start_ref[...]

    left = left_ref[...]
    out_ref[...] += dot(left, weights, NN)
    store_tiles(table, grads_ref, made, store_sem, group, dot(left, right_ref[...], TN))


def project_back(table, left, right, start, wall, grads, group=16):
    tokens, width = right.shape
    block = group * wall.shape[1]
    return pl.pallas_call(
        functools.partial(project_back_kernel, group, start is None),
        grid_spec=pltpu.PrefetchScalarGridSpec(
            num_scalar_prefetch=1,
            grid=(table.shape[0] // group,),
            in_specs=[
                pl.BlockSpec((tokens, block), lambda i, *_: (0, i)),
                full_spec(right.shape),
                any_spec(),
                any_spec(),
                any_spec() if start is None else full_spec(start.shape),
            ],
            out_specs=[full_spec(right.shape), any_spec()],
            scratch_shapes=[
                held_tiles(AHEAD, group, wall),
                held_tiles(2, group, wall),
                pltpu.SemaphoreType.DMA((AHEAD,)),
                pltpu.SemaphoreType.DMA((2,)),
            ],
        ),
        out_shape=[
            jax.ShapeDtypeStruct(right.shape, jnp.float32),
            jax.ShapeDtypeStruct(grads.shape, grads.dtype),
        ],
        input_output_aliases={4: 1},
        compiler_params=pltpu.CompilerParams(vmem_limit_bytes=VMEM_ASK),
        name="project_back",
    )(table, left, right, wall, grads, table if start is None else start)


def fill_mask(places, mask_ref):
    shape = mask_ref.shape
    query = lax.broadcasted_iota(jnp.int32, shape, 0) + places[0]
    key = lax.broadcasted_iota(jnp.int32, shape, 1)
    allowed = key <= query
    for piece in range(places.shape[0] - 1):
        low = places[1 + piece]
        inside_query = (query >= low) & (query < low + PIECE)
        inside_key = (key >= low) & (key < low + PIECE)
        allowed = allowed | (inside_query & inside_key)
    mask_ref[...] = jnp.where(allowed, 1.0, 0.0)


PAIR = 2
GROUP = HEADS // KV_HEADS


def attend_kernel(places, q_ref, k_ref, v_ref, out_ref, lse_ref, mask_ref):
    @pl.when(pl.program_id(0) == 0)
    def _():
        fill_mask(places, mask_ref)

    mask = mask_ref[...] > 0.5
    lane = lax.broadcasted_iota(jnp.int32, lse_ref.shape[1:], 1)
    logs = jnp.zeros(lse_ref.shape[1:], jnp.float32)
    scale = jnp.bfloat16(1.0 / HEAD**0.5)
    for side in range(PAIR):
        k = k_ref[:, side * HEAD : (side + 1) * HEAD]
        v = v_ref[:, side * HEAD : (side + 1) * HEAD]
        for h in range(GROUP):
            head = side * GROUP + h
            cols = slice(head * HEAD, (head + 1) * HEAD)
            scores = jnp.where(mask, dot(q_ref[:, cols] * scale, k, NT), masked_score)
            top = jnp.max(scores, axis=1, keepdims=True)
            raised = jnp.exp(scores - top)
            total = jnp.sum(raised, axis=1, keepdims=True)
            probs = (raised * (1.0 / total)).astype(jnp.bfloat16)
            out_ref[:, cols] = dot(probs, v, NN).astype(out_ref.dtype)
            logs = jnp.where(lane == head, top + jnp.log(total), logs)
    lse_ref[0] = logs


def attend(places, queries, both):
    tokens, width = queries.shape
    length = both.shape[0]
    steps = KV_HEADS // PAIR
    wide = PAIR * GROUP * HEAD
    narrow = PAIR * HEAD
    return pl.pallas_call(
        attend_kernel,
        grid_spec=pltpu.PrefetchScalarGridSpec(
            num_scalar_prefetch=1,
            grid=(steps,),
            in_specs=[
                pl.BlockSpec((tokens, wide), lambda i, *_: (0, i)),
                pl.BlockSpec((length, narrow), lambda i, *_: (0, i)),
                pl.BlockSpec((length, narrow), lambda i, *_: (0, steps + i)),
            ],
            out_specs=[
                pl.BlockSpec((tokens, wide), lambda i, *_: (0, i)),
                pl.BlockSpec((1, tokens, 128), lambda i, *_: (i, 0, 0)),
            ],
            scratch_shapes=[pltpu.VMEM((tokens, length), jnp.float32)],
        ),
        out_shape=[
            jax.ShapeDtypeStruct((tokens, width), jnp.bfloat16),
            jax.ShapeDtypeStruct((steps, tokens, 128), jnp.float32),
        ],
        compiler_params=pltpu.CompilerParams(vmem_limit_bytes=VMEM_ASK),
        name="attend",
    )(places, queries, both, both)


def attend_back_kernel(places, q_ref, k_ref, v_ref, grad_ref, lse_ref, cos_ref, sin_ref, out_ref, both_ref, mask_ref, turn_ref):
    @pl.when(pl.program_id(0) == 0)
    def _():
        fill_mask(places, mask_ref)

    mask = mask_ref[...] > 0.5
    scale = jnp.bfloat16(1.0 / HEAD**0.5)
    for side in range(PAIR):
        here = slice(side * HEAD, (side + 1) * HEAD)
        k = k_ref[:, here]
        v = v_ref[:, here]
        dk = None
        dv = None
        for h in range(GROUP):
            head = side * GROUP + h
            cols = slice(head * HEAD, (head + 1) * HEAD)
            q = q_ref[:, cols] * scale
            grad = grad_ref[:, cols]
            scores = jnp.where(mask, dot(q, k, NT), masked_score)
            probs = jnp.exp(scores - lse_ref[0, :, head : head + 1])
            grad_probs = dot(grad, v, NT)
            row_dot = jnp.sum(probs * grad_probs, axis=1, keepdims=True)
            grad_scores = (probs * (grad_probs - row_dot)).astype(jnp.bfloat16)
            turn_ref[:, cols] = dot(grad_scores, k, NN) * (1.0 / HEAD**0.5)
            dk_part = dot(q, grad_scores, TN)
            dv_part = dot(grad, probs.astype(jnp.bfloat16), TN)
            dk = dk_part if dk is None else dk + dk_part
            dv = dv_part if dv is None else dv + dv_part
        there = slice((PAIR + side) * HEAD, (PAIR + side + 1) * HEAD)
        both_ref[:, here] = dk.T.astype(both_ref.dtype)
        both_ref[:, there] = dv.T.astype(both_ref.dtype)
    wide = cos_ref.shape[1]
    for left in range(0, turn_ref.shape[1], wide):
        u = turn_ref[:, left : left + wide]
        out_ref[:, left : left + wide] = (u * cos_ref[...] - swap_halves(u) * sin_ref[...]).astype(out_ref.dtype)


def attend_back(places, queries, both, grad, lse, cosine, sine):
    tokens, width = queries.shape
    length = both.shape[0]
    steps = KV_HEADS // PAIR
    wide = PAIR * GROUP * HEAD
    narrow = PAIR * HEAD
    columns = pl.BlockSpec((tokens, wide), lambda i, *_: (0, i))
    keys = pl.BlockSpec((length, narrow), lambda i, *_: (0, i))
    return pl.pallas_call(
        attend_back_kernel,
        grid_spec=pltpu.PrefetchScalarGridSpec(
            num_scalar_prefetch=1,
            grid=(steps,),
            in_specs=[
                columns,
                keys,
                pl.BlockSpec((length, narrow), lambda i, *_: (0, steps + i)),
                columns,
                pl.BlockSpec((1, tokens, 128), lambda i, *_: (i, 0, 0)),
                full_spec(cosine.shape),
                full_spec(sine.shape),
            ],
            out_specs=[columns, pl.BlockSpec((length, 2 * narrow), lambda i, *_: (0, i))],
            scratch_shapes=[pltpu.VMEM((tokens, length), jnp.float32), pltpu.VMEM((tokens, wide), jnp.float32)],
        ),
        out_shape=[
            jax.ShapeDtypeStruct((tokens, width), jnp.bfloat16),
            jax.ShapeDtypeStruct((length, 2 * KV_HEADS * HEAD), jnp.bfloat16),
        ],
        compiler_params=pltpu.CompilerParams(vmem_limit_bytes=VMEM_ASK),
        name="attend_back",
    )(places, queries, both, both, grad, lse, cosine, sine)


def ffn_kernel(group, gate_s, up_s, down_s, normed_ref, cot_ref, wall_ref, out_ref, back_ref, grads_ref, held, made, load_sem, store_sem):
    step = pl.program_id(0)
    steps = pl.num_programs(0)
    tables = (gate_s, up_s, down_s)
    tile_rows = wall_ref.shape[1]
    width = wall_ref.shape[2]
    rows = group * tile_rows

    def fetch(at, buf):
        for kind in range(3):
            @pl.loop(0, group, unroll=True)
            def _(t, kind=kind):
                pltpu.make_async_copy(wall_ref.at[tables[kind][at * group + t]], held.at[buf, kind, t], load_sem.at[buf]).start()

    def drain(buf):
        pltpu.make_async_copy(made.at[buf], made.at[buf], store_sem.at[buf]).wait()

    buf = lax.rem(step, 2)

    @pl.when(step == 0)
    def _():
        fetch(0, 0)
        out_ref[...] = jnp.zeros_like(out_ref)
        back_ref[...] = jnp.zeros_like(back_ref)

    @pl.when(step + 1 < steps)
    def _():
        fetch(step + 1, 1 - buf)

    pltpu.make_async_copy(held.at[buf], held.at[buf], load_sem.at[buf]).wait()

    @pl.when(step >= 2)
    def _():
        drain(buf)

    normed = normed_ref[...]
    cot = cot_ref[...]
    w_gate = held[buf, 0].reshape(rows, width)
    w_up = held[buf, 1].reshape(rows, width)
    w_down = held[buf, 2].reshape(rows, width)
    nt = (((1,), (1,)), ((), ()))
    nn = (((1,), (0,)), ((), ()))
    tn = (((0,), (0,)), ((), ()))

    def dot(a, b, dims):
        return lax.dot_general(a, b, dims, preferred_element_type=jnp.float32)

    gate = dot(normed, w_gate, nt)
    up = dot(normed, w_up, nt)
    hidden = dot(cot, w_down, nt)
    sig = jax.nn.sigmoid(gate)
    silu = gate * sig
    act = (silu * up).astype(jnp.bfloat16)
    g_gate = (hidden * up * sig * (1.0 + gate * (1.0 - sig))).astype(jnp.bfloat16)
    g_up = (hidden * silu).astype(jnp.bfloat16)
    out_ref[...] += dot(act, w_down, nn)
    back_ref[...] += dot(g_gate, w_gate, nn) + dot(g_up, w_up, nn)
    made[buf, 0] = dot(g_gate, normed, tn).astype(jnp.bfloat16).reshape(group, tile_rows, width)
    made[buf, 1] = dot(g_up, normed, tn).astype(jnp.bfloat16).reshape(group, tile_rows, width)
    made[buf, 2] = dot(act, cot, tn).astype(jnp.bfloat16).reshape(group, tile_rows, width)
    for kind in range(3):
        @pl.loop(0, group, unroll=True)
        def _(t, kind=kind):
            pltpu.make_async_copy(made.at[buf, kind, t], grads_ref.at[tables[kind][step * group + t]], store_sem.at[buf]).start()

    @pl.when(step == steps - 1)
    def _():
        drain(1 - buf)
        drain(buf)

def ffn_call(gate_s, up_s, down_s, normed, cot, wall, group=16):
    tokens, width = normed.shape
    steps = gate_s.shape[0] // group
    tr = wall.shape[1]
    full = pl.BlockSpec((tokens, width), lambda i, *_: (0, 0))
    return pl.pallas_call(
        functools.partial(ffn_kernel, group),
        grid_spec=pltpu.PrefetchScalarGridSpec(
            num_scalar_prefetch=3, grid=(steps,),
            in_specs=[full, full, pl.BlockSpec(memory_space=pl.ANY)],
            out_specs=[full, full, pl.BlockSpec(memory_space=pl.ANY)],
            scratch_shapes=[pltpu.VMEM((2, 3, group, tr, width), jnp.bfloat16), pltpu.VMEM((2, 3, group, tr, width), jnp.bfloat16),
                pltpu.SemaphoreType.DMA((2,)), pltpu.SemaphoreType.DMA((2,))]),
        out_shape=[jax.ShapeDtypeStruct((tokens, width), jnp.float32), jax.ShapeDtypeStruct((tokens, width), jnp.float32), jax.ShapeDtypeStruct(wall.shape, jnp.bfloat16)],
        compiler_params=pltpu.CompilerParams(vmem_limit_bytes=56 << 20, dimension_semantics=("arbitrary",)),
        name="ffn",
    )(gate_s, up_s, down_s, normed, cot, wall)


MESH = pl.DeviceIdType.MESH
EVERY = slice(None)
GATHER_ROUTES = (
    ("z1", "z2", "z3", "x", "y", "core"),
    ("z1", "z2", "z3", "y", "x", "core"),
    ("x", "z1", "z2", "z3", "y", "core"),
    ("y", "z1", "z2", "z3", "x", "core"),
)


def position():
    dp = lax.axis_index("dp")
    return dp // 4, lax.rem(dp // 2, 2), lax.rem(dp, 2), lax.axis_index("fsdp")


def target(hop):
    y, x, c, z = position()
    if hop == "x":
        x = 1 - x
    elif hop == "y":
        y = 1 - y
    elif hop == "core":
        c = 1 - c
    elif hop == "back":
        z = lax.rem(z + 3, 4)
    else:
        z = lax.rem(z + 1, 4)
    return (y * 4 + x * 2 + c, z)


def enter(hops):
    barrier = pltpu.get_barrier_semaphore()
    for hop in hops:
        pl.semaphore_signal(barrier, inc=1, device_id=target(hop), device_id_type=MESH)
    pl.semaphore_wait(barrier, len(hops))


def split_slots(caps):
    small = caps // 6
    third = (caps - 2 * small) // 2
    counts = (small, small, third, caps - 2 * small - third)
    starts = (0, small, 2 * small, 2 * small + third)
    return counts, starts


GATHER_DELAYS = (0, 1, 0, 0)
SCATTER_DELAYS = (4, 4, 0, 0)


def round_count(counts, delays):
    return max(
        delay + (2 * count - 1 if route < 2 else count)
        for route, (count, delay) in enumerate(zip(counts, delays))
    )


def turn(route, at, counts, delays):
    at = at - delays[route]
    if route < 2:
        live = (at >= 0) & (lax.rem(at + 64, 2) == 0) & (at < 2 * counts[route])
        return live, at // 2
    return (at >= 0) & (at < counts[route]), at


def gather_kernel(mine_ref, gain_ref, wall_ref, gains_ref, own_sem, send_sem, recv_sem):
    y, x, c, z = position()
    counts, starts = split_slots(mine_ref.shape[0])
    rounds = round_count(counts, GATHER_DELAYS)
    own = pltpu.make_async_copy(mine_ref, wall_ref.at[y, x, c, z], own_sem.at[0])
    own_gain = pltpu.make_async_copy(gain_ref, gains_ref.at[y, x, c, z], own_sem.at[1])
    own.start()
    own_gain.start()
    enter(("x", "y", "core", "z", "back"))
    own.wait()
    own_gain.wait()

    def region(route, stage):
        hops = GATHER_ROUTES[route % 4]
        hop = hops[stage]
        done = hops[:stage]
        at_y = EVERY if "y" in done else y
        at_x = EVERY if "x" in done else x
        at_z = EVERY if "z3" in done else z
        if hop in ("z1", "z2", "z3"):
            at_z = lax.rem(z + 5 - int(hop[1]), 4)
        return at_y, at_x, c, at_z

    def copy(route, stage, index):
        if route == 4:
            view = gains_ref.at[region(route, stage)]
        else:
            view = wall_ref.at[region(route, stage) + (starts[route] + index,)]
        return pltpu.make_async_remote_copy(
            src_ref=view,
            dst_ref=view,
            send_sem=send_sem.at[route, stage],
            recv_sem=recv_sem.at[route, stage, index],
            device_id=target(GATHER_ROUTES[route % 4][stage]),
            device_id_type=MESH,
        )

    stages = len(GATHER_ROUTES[0])

    @pl.loop(0, rounds + stages)
    def _(t):
        for stage in range(stages + 1):
            for route in range(5):
                if route == 4:
                    live, index = t == stage, 0
                else:
                    live, index = turn(route, t - stage, counts, GATHER_DELAYS)

                @pl.when(live)
                def _(stage=stage, route=route, index=index):
                    if stage > 0:
                        copy(route, stage - 1, index).wait()
                    if stage < stages:
                        copy(route, stage, index).start()


def gather_slots(low_tiles, low_gains):
    caps, rows, width = low_tiles.shape
    counts, starts = split_slots(caps)
    kind = low_tiles.dtype
    vmem = pl.BlockSpec(memory_space=pltpu.VMEM)
    padded = jnp.pad(low_gains, ((0, 16 - low_gains.shape[0]), (0, 128 - low_gains.shape[1])))
    wall, gains = pl.pallas_call(
        gather_kernel,
        out_shape=[
            jax.ShapeDtypeStruct((2, 2, 2, 4, caps, rows, width), kind),
            jax.ShapeDtypeStruct((2, 2, 2, 4) + padded.shape, kind),
        ],
        in_specs=[vmem, vmem],
        out_specs=[pl.BlockSpec(memory_space=pl.ANY)] * 2,
        scratch_shapes=[
            pltpu.SemaphoreType.DMA((2,)),
            pltpu.SemaphoreType.DMA((5, 6)),
            pltpu.SemaphoreType.DMA((5, 6, max(counts))),
        ],
        compiler_params=pltpu.CompilerParams(
            collective_id=0, has_side_effects=True, vmem_limit_bytes=24 << 20
        ),
        name="gather_slots",
    )(low_tiles, padded)
    gains = gains.reshape((32,) + padded.shape)[:, : low_gains.shape[0], : low_gains.shape[1]]
    gains = gains.transpose(1, 0, 2).reshape(low_gains.shape[0], -1)
    return wall.reshape(32 * caps, rows, width), gains


SCATTER_ROUTES = (
    ("core", "y", "x", "z1", "z2", "z3", "end"),
    ("core", "x", "y", "z1", "z2", "z3", "end"),
    ("core", "y", "z1", "z2", "z3", "x", "end"),
    ("core", "x", "z1", "z2", "z3", "y", "end"),
)


SUM_HOPS = ("core", "x", "y", "z1", "z2", "z3")
SUM_START = 2


def scatter_extent(route, stage):
    hops = SCATTER_ROUTES[route]
    done = hops[1 : stage + 1] if hops[stage] in ("x", "y") else hops[1:stage]
    extent = []
    if "x" not in done or "y" not in done:
        extent.append(2)
    if not any(hop[0] == "z" for hop in hops[: stage + 1]):
        extent.append(4)
    return tuple(extent)


def scatter_terms(route, stage):
    hops = SCATTER_ROUTES[route]
    done = hops[1:stage]
    return 2 + ("x" in done) + ("y" in done) + ("z1" in done)


def scatter_kernel(look, wall_ref, gain_ref, out_ref, total_ref, core_ref, first_ref, second_ref, ring_ref, last_ref, *scratch):
    y, x, c, z = position()
    caps, rows, width = out_ref.shape
    counts, starts = split_slots(caps)
    rounds = round_count(counts, SCATTER_DELAYS)
    stages = len(SCATTER_ROUTES[0])
    held = {}
    made = {}
    scratch = list(scratch)
    for route in range(4):
        for stage in range(1, stages):
            held[route, stage] = scratch.pop(0)
            if stage < stages - 1:
                made[route, stage] = scratch.pop(0)
    load_sem, send_sem, recv_sem, sums, landed, sum_send, sum_recv = scratch
    enter(("x", "y", "core", "z", "back"))

    def pick(hop, mine, other):
        return other if hop else mine

    def landing(route, stage, slot):
        hops = SCATTER_ROUTES[route]
        hop = hops[stage]
        if hop == "core":
            return core_ref.at[:, :, :, slot]
        if hop[0] == "z":
            ring = ring_ref.at[int(hop[1]) - 1]
            return ring.at[0, slot] if route < 2 else ring.at[:, slot]
        if stage == 1:
            return first_ref.at[:, :, slot]
        if stage == 2:
            return second_ref.at[:, slot]
        return last_ref.at[slot]

    def terms(route, stage, slot):
        hops = SCATTER_ROUTES[route]
        hop = hops[stage]
        done = hops[1:stage]
        at_y = 1 - y if hop == "y" else (y if "y" in done else EVERY)
        at_x = 1 - x if hop == "x" else (x if "x" in done else EVERY)
        at_z = EVERY
        if hop[0] == "z":
            at_z = lax.rem(z + 4 - int(hop[1]), 4)
        elif "z3" in done:
            at_z = z
        views = [wall_ref.at[at_y, at_x, c, at_z, slot], core_ref.at[at_y, at_x, at_z, slot]]
        other = at_x if hops[1] == "y" else at_y
        if stage > 1:
            views.append(first_ref.at[other, at_z, slot])
        if route < 2 and stage > 2:
            views.append(second_ref.at[at_z, slot])
        if hop in ("z2", "z3"):
            ring = ring_ref.at[int(hop[1]) - 2]
            views.append(ring.at[0, slot] if route < 2 else ring.at[:, slot])
        elif "z3" in done:
            ring = ring_ref.at[2]
            views.append(ring.at[0, slot] if route < 2 else ring.at[other, slot])
        if route >= 2 and hop == "end":
            views.append(last_ref.at[slot])
        return views

    def send(route, stage, index):
        slot = starts[route] + index
        if stage == 0:
            source = wall_ref.at[:, :, 1 - c, :, slot]
        else:
            source = made[route, stage]
        return pltpu.make_async_remote_copy(
            src_ref=source,
            dst_ref=landing(route, stage, slot),
            send_sem=send_sem.at[route, stage],
            recv_sem=recv_sem.at[route, stage, index],
            device_id=target(SCATTER_ROUTES[route][stage]),
            device_id_type=MESH,
        )

    def early(route, stage, index):
        if stage > 0:
            for k, view in enumerate(terms(route, stage, starts[route] + index)[:-1]):
                pltpu.make_async_copy(view, held[route, stage].at[k], load_sem.at[route, stage]).start()

    def late(route, stage, index):
        if stage > 0:
            send(route, stage - 1, index).wait()
            view = terms(route, stage, starts[route] + index)[-1]
            last = held[route, stage].shape[0] - 1
            pltpu.make_async_copy(view, held[route, stage].at[last], load_sem.at[route, stage]).start()

    def finish(route, stage, index):
        if stage > 0:
            buf = held[route, stage]
            pltpu.make_async_copy(buf, buf, load_sem.at[route, stage]).wait()
            number = buf.shape[0]
            extent = buf.shape[1:-2]
            blocks = 1
            for size in extent:
                blocks *= size
            part = min(width, 512)

            @pl.loop(0, blocks)
            def _(block):
                if len(extent) == 2:
                    at = (block // extent[1], lax.rem(block, extent[1]))
                elif len(extent) == 1:
                    at = (block,)
                else:
                    at = ()
                for left in range(0, width, part):
                    cols = pl.ds(left, part)
                    total = buf[(0,) + at + (EVERY, cols)].astype(jnp.float32)
                    for k in range(1, number):
                        total += buf[(k,) + at + (EVERY, cols)].astype(jnp.float32)
                    if stage == stages - 1:
                        out_ref[starts[route] + index, :, cols] = total
                    else:
                        made[route, stage][at + (EVERY, cols)] = total.astype(made[route, stage].dtype)

        if stage < stages - 1:
            send(route, stage, index).start()

    def pass_sum(hop):
        return pltpu.make_async_remote_copy(
            src_ref=sums.at[hop] if hop < 4 else landed.at[hop - 1],
            dst_ref=landed.at[hop],
            send_sem=sum_send.at[hop],
            recv_sem=sum_recv.at[hop],
            device_id=target(SUM_HOPS[hop]),
            device_id_type=MESH,
        )

    def add_sums(step):
        if step > 0:
            pass_sum(step - 1).wait()
        if step == 0:
            sums[0] = gain_ref[...]
        elif step < 4:
            sums[step] = sums[step - 1] + landed[step - 1]
        elif step == len(SUM_HOPS):
            total_ref[...] = (sums[3] + landed[3]) + (landed[4] + landed[5])
        if step < len(SUM_HOPS):
            pass_sum(step).start()

    @pl.loop(0, rounds + stages - 1)
    def _(t):
        for step in range(len(SUM_HOPS) + 1):

            @pl.when(t == SUM_START + step)
            def _(step=step):
                add_sums(step)

        items = [(stage, route) for stage in range(stages - 1, -1, -1) for route in range(4)]

        def run(which, work):
            stage, route = items[which]
            live, index = turn(route, t - stage, counts, SCATTER_DELAYS)

            @pl.when(live)
            def _():
                work(route, stage, index)

        far, near = look
        for which in range(len(items) + far):
            if which < len(items):
                run(which, early)
            if far - near <= which < len(items) + far - near:
                run(which - far + near, late)
            if which >= far:
                run(which - far, finish)


def scatter_slots(grads_wall, gain_terms, caps, look=(4, 1)):
    rows, width = grads_wall.shape[1:]
    kind = grads_wall.dtype
    wall = grads_wall.reshape(2, 2, 2, 4, caps, rows, width)
    counts, starts = split_slots(caps)
    stages = len(SCATTER_ROUTES[0])
    scratch = []
    for route in range(4):
        for stage in range(1, stages):
            extent = scatter_extent(route, stage)
            scratch.append(pltpu.VMEM((scatter_terms(route, stage),) + extent + (rows, width), kind))
            if stage < stages - 1:
                scratch.append(pltpu.VMEM(extent + (rows, width), kind))
    tile = (caps, rows, width)
    out = pl.pallas_call(
        functools.partial(scatter_kernel, look),
        out_shape=[
            jax.ShapeDtypeStruct(tile, jnp.float32),
            jax.ShapeDtypeStruct(gain_terms.shape, jnp.float32),
            jax.ShapeDtypeStruct((2, 2, 4) + tile, kind),
            jax.ShapeDtypeStruct((2, 4) + tile, kind),
            jax.ShapeDtypeStruct((4,) + tile, kind),
            jax.ShapeDtypeStruct((3, 2) + tile, kind),
            jax.ShapeDtypeStruct(tile, kind),
        ],
        in_specs=[pl.BlockSpec(memory_space=pl.ANY), pl.BlockSpec(memory_space=pltpu.VMEM)],
        out_specs=[pl.BlockSpec(memory_space=pltpu.VMEM)] * 2 + [pl.BlockSpec(memory_space=pl.ANY)] * 5,
        scratch_shapes=scratch
        + [
            pltpu.SemaphoreType.DMA((4, stages)),
            pltpu.SemaphoreType.DMA((4, stages)),
            pltpu.SemaphoreType.DMA((4, stages, max(counts))),
            pltpu.VMEM((4,) + gain_terms.shape, jnp.float32),
            pltpu.VMEM((6,) + gain_terms.shape, jnp.float32),
            pltpu.SemaphoreType.DMA((6,)),
            pltpu.SemaphoreType.DMA((6,)),
        ],
        compiler_params=pltpu.CompilerParams(
            collective_id=1, has_side_effects=True, vmem_limit_bytes=56 << 20
        ),
        name="scatter_slots",
    )(wall, gain_terms)
    return out[0], out[1]


def shards(
    hidden_in,
    piece_starts,
    out_cotangent,
    owners,
    master,
    moment_one,
    moment_two,
    gain_master,
    gain_one,
    gain_two,
):
    devices = lax.axis_size("dp") * lax.axis_size("fsdp")
    caps, tile_rows, model_width = master.shape
    layout = section_layout(devices, tile_rows)
    slot_qkv, slot_out, slot_ffn, slot_down = slot_numbers(owners, layout, caps)
    query_tiles = model_width // tile_rows
    slot_query, slot_both = slot_qkv[:query_tiles], slot_qkv[query_tiles:]
    half = slot_ffn.shape[0] // 2
    wall, gains_low = gather_any(
        master.astype(jnp.bfloat16), gain_master.astype(jnp.bfloat16)
    )
    gains_low = gains_low.astype(jnp.float32)
    gain_attn = gains_low[0]
    gain_ffn = gains_low[1]
    tokens = hidden_in.astype(jnp.float32)
    local_len = tokens.shape[0]
    kv_width = KV_HEADS * HEAD
    first = lax.axis_index("fsdp") * local_len
    positions = first + jnp.arange(local_len, dtype=jnp.int32)
    places = jnp.concatenate([first[None].astype(jnp.int32), piece_starts[0]])
    cosine, sine = rope_tables(positions.astype(jnp.float32), 16 * tile_rows)
    inv_one = lax.rsqrt(jnp.mean(tokens * tokens, axis=1, keepdims=True) + norm_eps)
    normed = (tokens * inv_one * gain_attn).astype(jnp.bfloat16)
    both_local = project(slot_both, normed, cosine, sine, wall, turned=kv_width // (16 * tile_rows))
    both = lax.all_gather(both_local, "fsdp", axis=0, tiled=True)
    queries = project(slot_query, normed, cosine, sine, wall)
    attended, lse = attend(places, queries, both)
    middle, normed_two = mix(slot_out, attended, hidden_in, gain_ffn, wall)
    inv_two = lax.rsqrt(jnp.mean(middle * middle, axis=1, keepdims=True) + norm_eps)
    ffn_out, grad_normed_two, grads_wall = ffn_call(
        slot_ffn[:half], slot_ffn[half:], slot_down, normed_two, out_cotangent, wall
    )
    block_out = (middle + ffn_out).astype(jnp.bfloat16)
    scaled_two = grad_normed_two * gain_ffn
    grad_middle = (
        out_cotangent.astype(jnp.float32)
        + inv_two * scaled_two
        - middle * inv_two**3 * jnp.mean(scaled_two * middle, axis=1, keepdims=True)
    )
    gain_two_term = jnp.sum(grad_normed_two * middle * inv_two, axis=0)
    grad_branch = grad_middle.astype(jnp.bfloat16)
    grad_attended, grads_wall = mix_back(slot_out, attended, grad_branch, wall, grads_wall)
    grad_query, both_terms = attend_back(
        places, queries, both, grad_attended, lse, cosine, sine
    )
    both_sum = lax.psum_scatter(both_terms, "fsdp", scatter_dimension=0, tiled=True).astype(
        jnp.float32
    )
    grad_normed, grads_wall = project_back(slot_query, grad_query, normed, None, wall, grads_wall)
    both_sum = both_sum.reshape(local_len, KV_HEADS // PAIR, 2, PAIR * HEAD)
    grad_key = turn_back(both_sum[:, :, 0].reshape(local_len, kv_width), cosine, sine)
    grad_value = both_sum[:, :, 1].reshape(local_len, kv_width)
    grad_both = jnp.concatenate([grad_key, grad_value], axis=1).astype(jnp.bfloat16)
    grad_normed, grads_wall = project_back(
        slot_both, grad_both, normed, grad_normed, wall, grads_wall
    )
    keep_slot = filled_mask(owners, layout, lax.axis_index(("dp", "fsdp")))[:, None, None]
    gain_one_term = jnp.sum(grad_normed * tokens * inv_one, axis=0)
    weight_grad, gain_grad = scatter_any(
        grads_wall, jnp.stack([gain_one_term, gain_two_term]), caps
    )
    weight_grad = jnp.where(keep_slot, weight_grad, 0.0)
    scaled_one = grad_normed * gain_attn
    input_grad = (
        grad_middle
        + inv_one * scaled_one
        - tokens * inv_one**3 * jnp.mean(scaled_one * tokens, axis=1, keepdims=True)
    )
    step = float(STEP)
    new_one, new_two, new_weights = adam_step(
        master, moment_one, moment_two, weight_grad, step, decay_rate, learn_rate
    )
    new_one = jnp.where(keep_slot, new_one, 0.0)
    new_two = jnp.where(keep_slot, new_two, 0.0)
    new_weights = jnp.where(keep_slot, new_weights, 0.0)
    new_gain_one, new_gain_two, new_gains = adam_step(
        gain_master, gain_one, gain_two, gain_grad, step, 0.0, gain_rate
    )
    return (
        block_out,
        input_grad,
        weight_grad,
        new_weights,
        new_one,
        new_two,
        gain_grad,
        new_gains,
        new_gain_one,
        new_gain_two,
    )


def solution(mesh):
    return jax.shard_map(
        shards,
        mesh=mesh,
        in_specs=(
            P(("dp", "fsdp"), None),
            P("dp", None),
            P(("dp", "fsdp"), None),
            P(),
            P(("dp", "fsdp"), None, None),
            P(("dp", "fsdp"), None, None),
            P(("dp", "fsdp"), None, None),
            P(None, ("dp", "fsdp")),
            P(None, ("dp", "fsdp")),
            P(None, ("dp", "fsdp")),
        ),
        out_specs=(
            P(("dp", "fsdp"), None),
            P(("dp", "fsdp"), None),
            P(("dp", "fsdp"), None, None),
            P(("dp", "fsdp"), None, None),
            P(("dp", "fsdp"), None, None),
            P(("dp", "fsdp"), None, None),
            P(None, ("dp", "fsdp")),
            P(None, ("dp", "fsdp")),
            P(None, ("dp", "fsdp")),
            P(None, ("dp", "fsdp")),
        ),
        check_vma=False,
    )
```

```python
import functools

import jax
import jax.experimental.pallas as pl
import jax.experimental.pallas.tpu as pltpu
import jax.numpy as jnp
from jax import lax
from jax.sharding import PartitionSpec as P

D = 2048
HEADS = 32
KV_HEADS = 8
HEAD = 64
FF = 8192
PIECE = 256
STEP = 5


norm_eps = 1e-05
adam_eps = 1e-08
beta_one = 0.5
beta_two = 0.5
learn_rate = 0.02
gain_rate = 0.3
decay_rate = 0.1
rope_base = 500000.0
masked_score = -1e30


def section_layout(devices, tile_rows):
    counts = [
        (D + 2 * KV_HEADS * HEAD) // tile_rows,
        HEADS * HEAD // tile_rows,
        2 * FF // tile_rows,
        FF // tile_rows,
    ]
    layout = []
    first_tile = 0
    first_slot = 0
    for number in counts:
        capacity = 5 * number // (4 * devices) + 1
        layout.append((first_tile, number, capacity, first_slot))
        first_tile += number
        first_slot += capacity
    return layout


def adam_step(weights, first_moment, second_moment, grads, step, decay, rate):
    new_one = beta_one * first_moment + (1.0 - beta_one) * grads
    new_two = beta_two * second_moment + (1.0 - beta_two) * grads * grads
    correct_one = 1.0 - beta_one**step
    correct_two = 1.0 - beta_two**step
    update = -rate * (
        new_one / correct_one / (jnp.sqrt(new_two / correct_two) + adam_eps) + decay * weights
    )
    return (new_one, new_two, weights + update)


def slot_numbers(owners, layout, caps):
    placed = []
    for first_tile, number, capacity, first_slot in layout:
        mine = owners[first_tile : first_tile + number]
        order = jnp.arange(number, dtype=jnp.int32)
        earlier = (mine[:, None] == mine[None, :]) & (order[None, :] < order[:, None])
        ranked = jnp.sum(earlier.astype(jnp.int32), axis=1)
        placed.append(mine * caps + first_slot + ranked)
    return placed


def filled_mask(owners, layout, device):
    masks = []
    for first_tile, number, capacity, first_slot in layout:
        count = jnp.sum((owners[first_tile : first_tile + number] == device).astype(jnp.int32))
        masks.append(jnp.arange(capacity, dtype=jnp.int32) < count)
    return jnp.concatenate(masks)


def rope_tables(positions, block):
    half_dim = HEAD // 2
    inverse = rope_base ** (-(jnp.arange(half_dim, dtype=jnp.float32) * 2.0 / HEAD))
    angles = positions[:, None] * inverse[None, :]
    cosine = jnp.cos(angles)
    sine = jnp.sin(angles)
    return (
        jnp.tile(jnp.concatenate([cosine, cosine], axis=1), (1, block // HEAD)),
        jnp.tile(jnp.concatenate([-sine, sine], axis=1), (1, block // HEAD)),
    )


def turn_back(grads, cosine, sine):
    tokens, width = grads.shape
    half_dim = HEAD // 2
    heads = grads.reshape(tokens, width // HEAD, 2, half_dim)
    swapped = heads[:, :, ::-1].reshape(tokens, width)
    times = width // cosine.shape[1]
    return grads * jnp.tile(cosine, (1, times)) - swapped * jnp.tile(sine, (1, times))


def tuned_mesh():
    return (lax.axis_size("dp"), lax.axis_size("fsdp")) == (8, 4)


def forward_attention(low_tiles, low_gains, slots, places, hidden_in, cosine, sine, lead):
    caps, tile_rows, width = low_tiles.shape
    slot_query, slot_both, slot_out = slots
    if tuned_mesh():
        table = jnp.concatenate(slots)
        table = table // caps * lead + lax.rem(table, caps)
        (wall, weights, both, gains, normed, queries, attended, lse, middle, normed_two) = (
            gather_slots(low_tiles, low_gains, table, places, hidden_in, cosine, sine, lead)
        )
        return wall, gains, both, normed, queries, attended, lse, middle, normed_two
    wall = lax.all_gather(low_tiles, ("dp", "fsdp"), axis=0, tiled=True)
    gains = lax.all_gather(low_gains, ("dp", "fsdp"), axis=1, tiled=True).astype(jnp.float32)
    tokens = hidden_in.astype(jnp.float32)
    inv_one = lax.rsqrt(jnp.mean(tokens * tokens, axis=1, keepdims=True) + norm_eps)
    normed = (tokens * inv_one * gains[0]).astype(jnp.bfloat16)
    turned = KV_HEADS * HEAD // cosine.shape[1]
    both_local = project(slot_both, normed, cosine, sine, wall, turned=turned)
    both = lax.all_gather(both_local, "fsdp", axis=0, tiled=True)
    queries = project(slot_query, normed, cosine, sine, wall)
    attended, lse = attend(places, queries, both)
    middle, normed_two = mix(slot_out, attended, hidden_in, gains[1], wall)
    return wall, gains, both, normed, queries, attended, lse, middle, normed_two


def scatter_any(grads_wall, gain_terms, caps):
    number = gain_terms.shape[0]
    if tuned_mesh():
        padded = jnp.pad(gain_terms, ((0, 8 - number), (0, 0)))
        grads, total = scatter_slots(grads_wall, padded, caps)
        width = gain_terms.shape[1] // 32
        device = lax.axis_index(("dp", "fsdp"))
        return grads, lax.dynamic_slice_in_dim(total[:number], device * width, width, 1)
    grads = lax.psum_scatter(grads_wall, ("dp", "fsdp"), scatter_dimension=0, tiled=True)
    gain_grad = lax.psum_scatter(gain_terms, ("dp", "fsdp"), scatter_dimension=1, tiled=True)
    return grads.astype(jnp.float32), gain_grad


VMEM_ASK = 56 << 20
NT = (((1,), (1,)), ((), ()))
NN = (((1,), (0,)), ((), ()))
TN = (((0,), (0,)), ((), ()))


def dot(a, b, dims):
    return lax.dot_general(a, b, dims, preferred_element_type=jnp.float32)


def stream_tiles(table, wall_ref, held, sem, group):
    step = pl.program_id(0)
    steps = pl.num_programs(0)
    depth = held.shape[0]
    buf = lax.rem(step, depth)

    def fetch(at):
        into = lax.rem(at, depth)

        @pl.loop(0, group, unroll=True)
        def _(t):
            pltpu.make_async_copy(
                wall_ref.at[table[at * group + t]], held.at[into, t], sem.at[into]
            ).start()

    @pl.when(step == 0)
    def _():
        for ahead in range(depth - 1):

            @pl.when(ahead < steps)
            def _(ahead=ahead):
                fetch(jnp.int32(ahead))

    @pl.when(step + depth - 1 < steps)
    def _():
        fetch(step + depth - 1)

    pltpu.make_async_copy(held.at[buf], held.at[buf], sem.at[buf]).wait()
    rows = group * wall_ref.shape[1]
    return held[buf].reshape(rows, wall_ref.shape[2])


def store_tiles(table, grads_ref, made, sem, group, value):
    step = pl.program_id(0)
    steps = pl.num_programs(0)
    buf = lax.rem(step, 2)

    def drain(which):
        pltpu.make_async_copy(made.at[which], made.at[which], sem.at[which]).wait()

    @pl.when(step >= 2)
    def _():
        drain(buf)

    made[buf] = value.astype(made.dtype).reshape(made.shape[1:])

    @pl.loop(0, group, unroll=True)
    def _(t):
        pltpu.make_async_copy(
            made.at[buf, t], grads_ref.at[table[step * group + t]], sem.at[buf]
        ).start()

    @pl.when(step == steps - 1)
    def _():
        drain(1 - buf)
        drain(buf)


def swap_halves(u):
    width = u.shape[1]
    lane = lax.broadcasted_iota(jnp.int32, u.shape, 1)
    first = lax.rem(lane, HEAD) < HEAD // 2
    return jnp.where(
        first, pltpu.roll(u, width - HEAD // 2, 1), pltpu.roll(u, HEAD // 2, 1)
    )


def project_kernel(group, turned, table, normed_ref, cos_ref, sin_ref, wall_ref, out_ref, held, sem):
    weights = stream_tiles(table, wall_ref, held, sem, group)
    u = dot(normed_ref[...], weights, NT)
    if turned is None:
        out_ref[...] = (u * cos_ref[...] + swap_halves(u) * sin_ref[...]).astype(out_ref.dtype)
    else:

        @pl.when(pl.program_id(0) < turned)
        def _():
            out_ref[...] = (u * cos_ref[...] + swap_halves(u) * sin_ref[...]).astype(out_ref.dtype)

        @pl.when(pl.program_id(0) >= turned)
        def _():
            out_ref[...] = u.astype(out_ref.dtype)


def full_spec(shape):
    return pl.BlockSpec(shape, lambda i, *_: (0,) * len(shape))


def any_spec():
    return pl.BlockSpec(memory_space=pl.ANY)


AHEAD = 4


def held_tiles(depth, group, wall):
    return pltpu.VMEM((depth, group) + wall.shape[1:], wall.dtype)


def project(table, normed, cosine, sine, wall, turned=None, group=16):
    tokens = normed.shape[0]
    block = group * wall.shape[1]
    steps = table.shape[0] // group
    return pl.pallas_call(
        functools.partial(project_kernel, group, turned),
        grid_spec=pltpu.PrefetchScalarGridSpec(
            num_scalar_prefetch=1,
            grid=(steps,),
            in_specs=[full_spec(normed.shape), full_spec(cosine.shape), full_spec(sine.shape), any_spec()],
            out_specs=pl.BlockSpec((tokens, block), lambda i, *_: (0, i)),
            scratch_shapes=[held_tiles(AHEAD, group, wall), pltpu.SemaphoreType.DMA((AHEAD,))],
        ),
        out_shape=jax.ShapeDtypeStruct((tokens, steps * block), jnp.bfloat16),
        compiler_params=pltpu.CompilerParams(vmem_limit_bytes=VMEM_ASK),
        name="project",
    )(table, normed, cosine, sine, wall)


def mix_kernel(group, table, left_ref, hidden_ref, gain_ref, wall_ref, middle_ref, normed_ref, held, sem):
    step = pl.program_id(0)
    weights = stream_tiles(table, wall_ref, held, sem, group)

    @pl.when(step == 0)
    def _():
        middle_ref[...] = hidden_ref[...].astype(jnp.float32)

    middle_ref[...] += dot(left_ref[...], weights, NN)

    @pl.when(step == pl.num_programs(0) - 1)
    def _():
        middle = middle_ref[...]
        inv = lax.rsqrt(jnp.mean(middle * middle, axis=1, keepdims=True) + norm_eps)
        normed_ref[...] = (middle * inv * gain_ref[...]).astype(normed_ref.dtype)


def mix(table, left, hidden, gain, wall, group=16):
    tokens, width = hidden.shape
    block = group * wall.shape[1]
    return pl.pallas_call(
        functools.partial(mix_kernel, group),
        grid_spec=pltpu.PrefetchScalarGridSpec(
            num_scalar_prefetch=1,
            grid=(table.shape[0] // group,),
            in_specs=[
                pl.BlockSpec((tokens, block), lambda i, *_: (0, i)),
                full_spec(hidden.shape),
                full_spec((1, width)),
                any_spec(),
            ],
            out_specs=[full_spec(hidden.shape), full_spec(hidden.shape)],
            scratch_shapes=[held_tiles(AHEAD, group, wall), pltpu.SemaphoreType.DMA((AHEAD,))],
        ),
        out_shape=[
            jax.ShapeDtypeStruct(hidden.shape, jnp.float32),
            jax.ShapeDtypeStruct(hidden.shape, jnp.bfloat16),
        ],
        compiler_params=pltpu.CompilerParams(vmem_limit_bytes=VMEM_ASK),
        name="mix",
    )(table, left, hidden, gain.reshape(1, width), wall)


def mix_back_kernel(group, table, left_ref, right_ref, wall_ref, old_ref, out_ref, grads_ref, held, made, load_sem, store_sem):
    weights = stream_tiles(table, wall_ref, held, load_sem, group)
    right = right_ref[...]
    out_ref[...] = dot(right, weights, NT).astype(out_ref.dtype)
    store_tiles(table, grads_ref, made, store_sem, group, dot(left_ref[...], right, TN))


def mix_back(table, left, right, wall, grads, group=16):
    tokens, width = right.shape
    block = group * wall.shape[1]
    columns = pl.BlockSpec((tokens, block), lambda i, *_: (0, i))
    return pl.pallas_call(
        functools.partial(mix_back_kernel, group),
        grid_spec=pltpu.PrefetchScalarGridSpec(
            num_scalar_prefetch=1,
            grid=(table.shape[0] // group,),
            in_specs=[columns, full_spec(right.shape), any_spec(), any_spec()],
            out_specs=[columns, any_spec()],
            scratch_shapes=[
                held_tiles(AHEAD, group, wall),
                held_tiles(2, group, wall),
                pltpu.SemaphoreType.DMA((AHEAD,)),
                pltpu.SemaphoreType.DMA((2,)),
            ],
        ),
        out_shape=[
            jax.ShapeDtypeStruct(left.shape, jnp.bfloat16),
            jax.ShapeDtypeStruct(grads.shape, grads.dtype),
        ],
        input_output_aliases={4: 1},
        compiler_params=pltpu.CompilerParams(vmem_limit_bytes=VMEM_ASK),
        name="mix_back",
    )(table, left, right, wall, grads)


def project_back_kernel(group, fresh, table, left_ref, right_ref, wall_ref, old_ref, start_ref, out_ref, grads_ref, held, made, load_sem, store_sem):
    weights = stream_tiles(table, wall_ref, held, load_sem, group)

    @pl.when(pl.program_id(0) == 0)
    def _():
        out_ref[...] = jnp.zeros_like(out_ref) if fresh else start_ref[...]

    left = left_ref[...]
    out_ref[...] += dot(left, weights, NN)
    store_tiles(table, grads_ref, made, store_sem, group, dot(left, right_ref[...], TN))


def project_back(table, left, right, start, wall, grads, group=16):
    tokens, width = right.shape
    block = group * wall.shape[1]
    return pl.pallas_call(
        functools.partial(project_back_kernel, group, start is None),
        grid_spec=pltpu.PrefetchScalarGridSpec(
            num_scalar_prefetch=1,
            grid=(table.shape[0] // group,),
            in_specs=[
                pl.BlockSpec((tokens, block), lambda i, *_: (0, i)),
                full_spec(right.shape),
                any_spec(),
                any_spec(),
                any_spec() if start is None else full_spec(start.shape),
            ],
            out_specs=[full_spec(right.shape), any_spec()],
            scratch_shapes=[
                held_tiles(AHEAD, group, wall),
                held_tiles(2, group, wall),
                pltpu.SemaphoreType.DMA((AHEAD,)),
                pltpu.SemaphoreType.DMA((2,)),
            ],
        ),
        out_shape=[
            jax.ShapeDtypeStruct(right.shape, jnp.float32),
            jax.ShapeDtypeStruct(grads.shape, grads.dtype),
        ],
        input_output_aliases={4: 1},
        compiler_params=pltpu.CompilerParams(vmem_limit_bytes=VMEM_ASK),
        name="project_back",
    )(table, left, right, wall, grads, table if start is None else start)


def fill_mask(places, mask_ref):
    shape = mask_ref.shape
    query = lax.broadcasted_iota(jnp.int32, shape, 0) + places[0]
    key = lax.broadcasted_iota(jnp.int32, shape, 1)
    allowed = key <= query
    for piece in range(places.shape[0] - 1):
        low = places[1 + piece]
        inside_query = (query >= low) & (query < low + PIECE)
        inside_key = (key >= low) & (key < low + PIECE)
        allowed = allowed | (inside_query & inside_key)
    mask_ref[...] = jnp.where(allowed, 1.0, 0.0)


PAIR = 2
GROUP = HEADS // KV_HEADS


def attend_kernel(places, q_ref, k_ref, v_ref, out_ref, lse_ref, mask_ref):
    @pl.when(pl.program_id(0) == 0)
    def _():
        fill_mask(places, mask_ref)

    mask = mask_ref[...] > 0.5
    lane = lax.broadcasted_iota(jnp.int32, lse_ref.shape[1:], 1)
    logs = jnp.zeros(lse_ref.shape[1:], jnp.float32)
    scale = jnp.bfloat16(1.0 / HEAD**0.5)
    for side in range(PAIR):
        k = k_ref[:, side * HEAD : (side + 1) * HEAD]
        v = v_ref[:, side * HEAD : (side + 1) * HEAD]
        for h in range(GROUP):
            head = side * GROUP + h
            cols = slice(head * HEAD, (head + 1) * HEAD)
            scores = jnp.where(mask, dot(q_ref[:, cols] * scale, k, NT), masked_score)
            top = jnp.max(scores, axis=1, keepdims=True)
            raised = jnp.exp(scores - top)
            total = jnp.sum(raised, axis=1, keepdims=True)
            probs = (raised * (1.0 / total)).astype(jnp.bfloat16)
            out_ref[:, cols] = dot(probs, v, NN).astype(out_ref.dtype)
            logs = jnp.where(lane == head, top + jnp.log(total), logs)
    lse_ref[0] = logs


def attend(places, queries, both):
    tokens, width = queries.shape
    length = both.shape[0]
    steps = KV_HEADS // PAIR
    wide = PAIR * GROUP * HEAD
    narrow = PAIR * HEAD
    return pl.pallas_call(
        attend_kernel,
        grid_spec=pltpu.PrefetchScalarGridSpec(
            num_scalar_prefetch=1,
            grid=(steps,),
            in_specs=[
                pl.BlockSpec((tokens, wide), lambda i, *_: (0, i)),
                pl.BlockSpec((length, narrow), lambda i, *_: (0, i)),
                pl.BlockSpec((length, narrow), lambda i, *_: (0, steps + i)),
            ],
            out_specs=[
                pl.BlockSpec((tokens, wide), lambda i, *_: (0, i)),
                pl.BlockSpec((1, tokens, 128), lambda i, *_: (i, 0, 0)),
            ],
            scratch_shapes=[pltpu.VMEM((tokens, length), jnp.float32)],
        ),
        out_shape=[
            jax.ShapeDtypeStruct((tokens, width), jnp.bfloat16),
            jax.ShapeDtypeStruct((steps, tokens, 128), jnp.float32),
        ],
        compiler_params=pltpu.CompilerParams(vmem_limit_bytes=VMEM_ASK),
        name="attend",
    )(places, queries, both, both)


def attend_back_kernel(places, q_ref, k_ref, v_ref, grad_ref, lse_ref, cos_ref, sin_ref, out_ref, both_ref, mask_ref, turn_ref):
    @pl.when(pl.program_id(0) == 0)
    def _():
        fill_mask(places, mask_ref)

    mask = mask_ref[...] > 0.5
    scale = jnp.bfloat16(1.0 / HEAD**0.5)
    for side in range(PAIR):
        here = slice(side * HEAD, (side + 1) * HEAD)
        k = k_ref[:, here]
        v = v_ref[:, here]
        dk = None
        dv = None
        for h in range(GROUP):
            head = side * GROUP + h
            cols = slice(head * HEAD, (head + 1) * HEAD)
            q = q_ref[:, cols] * scale
            grad = grad_ref[:, cols]
            scores = jnp.where(mask, dot(q, k, NT), masked_score)
            probs = jnp.exp(scores - lse_ref[0, :, head : head + 1])
            grad_probs = dot(grad, v, NT)
            row_dot = jnp.sum(probs * grad_probs, axis=1, keepdims=True)
            grad_scores = (probs * (grad_probs - row_dot)).astype(jnp.bfloat16)
            turn_ref[:, cols] = dot(grad_scores, k, NN) * (1.0 / HEAD**0.5)
            dk_part = dot(q, grad_scores, TN)
            dv_part = dot(grad, probs.astype(jnp.bfloat16), TN)
            dk = dk_part if dk is None else dk + dk_part
            dv = dv_part if dv is None else dv + dv_part
        there = slice((PAIR + side) * HEAD, (PAIR + side + 1) * HEAD)
        both_ref[:, here] = dk.T.astype(both_ref.dtype)
        both_ref[:, there] = dv.T.astype(both_ref.dtype)
    wide = cos_ref.shape[1]
    for left in range(0, turn_ref.shape[1], wide):
        u = turn_ref[:, left : left + wide]
        out_ref[:, left : left + wide] = (u * cos_ref[...] - swap_halves(u) * sin_ref[...]).astype(out_ref.dtype)


def attend_back(places, queries, both, grad, lse, cosine, sine):
    tokens, width = queries.shape
    length = both.shape[0]
    steps = KV_HEADS // PAIR
    wide = PAIR * GROUP * HEAD
    narrow = PAIR * HEAD
    columns = pl.BlockSpec((tokens, wide), lambda i, *_: (0, i))
    keys = pl.BlockSpec((length, narrow), lambda i, *_: (0, i))
    return pl.pallas_call(
        attend_back_kernel,
        grid_spec=pltpu.PrefetchScalarGridSpec(
            num_scalar_prefetch=1,
            grid=(steps,),
            in_specs=[
                columns,
                keys,
                pl.BlockSpec((length, narrow), lambda i, *_: (0, steps + i)),
                columns,
                pl.BlockSpec((1, tokens, 128), lambda i, *_: (i, 0, 0)),
                full_spec(cosine.shape),
                full_spec(sine.shape),
            ],
            out_specs=[columns, pl.BlockSpec((length, 2 * narrow), lambda i, *_: (0, i))],
            scratch_shapes=[pltpu.VMEM((tokens, length), jnp.float32), pltpu.VMEM((tokens, wide), jnp.float32)],
        ),
        out_shape=[
            jax.ShapeDtypeStruct((tokens, width), jnp.bfloat16),
            jax.ShapeDtypeStruct((length, 2 * KV_HEADS * HEAD), jnp.bfloat16),
        ],
        compiler_params=pltpu.CompilerParams(vmem_limit_bytes=VMEM_ASK),
        name="attend_back",
    )(places, queries, both, both, grad, lse, cosine, sine)


def ffn_kernel(group, gate_s, up_s, down_s, normed_ref, cot_ref, wall_ref, out_ref, back_ref, grads_ref, held, made, load_sem, store_sem):
    step = pl.program_id(0)
    steps = pl.num_programs(0)
    tables = (gate_s, up_s, down_s)
    tile_rows = wall_ref.shape[1]
    width = wall_ref.shape[2]
    rows = group * tile_rows

    def fetch(at, buf):
        for kind in range(3):
            @pl.loop(0, group, unroll=True)
            def _(t, kind=kind):
                pltpu.make_async_copy(wall_ref.at[tables[kind][at * group + t]], held.at[buf, kind, t], load_sem.at[buf]).start()

    def drain(buf):
        pltpu.make_async_copy(made.at[buf], made.at[buf], store_sem.at[buf]).wait()

    buf = lax.rem(step, 2)

    @pl.when(step == 0)
    def _():
        fetch(0, 0)
        out_ref[...] = jnp.zeros_like(out_ref)
        back_ref[...] = jnp.zeros_like(back_ref)

    @pl.when(step + 1 < steps)
    def _():
        fetch(step + 1, 1 - buf)

    pltpu.make_async_copy(held.at[buf], held.at[buf], load_sem.at[buf]).wait()

    @pl.when(step >= 2)
    def _():
        drain(buf)

    normed = normed_ref[...]
    cot = cot_ref[...]
    w_gate = held[buf, 0].reshape(rows, width)
    w_up = held[buf, 1].reshape(rows, width)
    w_down = held[buf, 2].reshape(rows, width)
    nt = (((1,), (1,)), ((), ()))
    nn = (((1,), (0,)), ((), ()))
    tn = (((0,), (0,)), ((), ()))

    def dot(a, b, dims):
        return lax.dot_general(a, b, dims, preferred_element_type=jnp.float32)

    gate = dot(normed, w_gate, nt)
    up = dot(normed, w_up, nt)
    hidden = dot(cot, w_down, nt)
    sig = jax.nn.sigmoid(gate)
    silu = gate * sig
    act = (silu * up).astype(jnp.bfloat16)
    g_gate = (hidden * up * sig * (1.0 + gate * (1.0 - sig))).astype(jnp.bfloat16)
    g_up = (hidden * silu).astype(jnp.bfloat16)
    out_ref[...] += dot(act, w_down, nn)
    back_ref[...] += dot(g_gate, w_gate, nn) + dot(g_up, w_up, nn)
    made[buf, 0] = dot(g_gate, normed, tn).astype(jnp.bfloat16).reshape(group, tile_rows, width)
    made[buf, 1] = dot(g_up, normed, tn).astype(jnp.bfloat16).reshape(group, tile_rows, width)
    made[buf, 2] = dot(act, cot, tn).astype(jnp.bfloat16).reshape(group, tile_rows, width)
    for kind in range(3):
        @pl.loop(0, group, unroll=True)
        def _(t, kind=kind):
            pltpu.make_async_copy(made.at[buf, kind, t], grads_ref.at[tables[kind][step * group + t]], store_sem.at[buf]).start()

    @pl.when(step == steps - 1)
    def _():
        drain(1 - buf)
        drain(buf)

def ffn_call(gate_s, up_s, down_s, normed, cot, wall, group=16):
    tokens, width = normed.shape
    steps = gate_s.shape[0] // group
    tr = wall.shape[1]
    full = pl.BlockSpec((tokens, width), lambda i, *_: (0, 0))
    return pl.pallas_call(
        functools.partial(ffn_kernel, group),
        grid_spec=pltpu.PrefetchScalarGridSpec(
            num_scalar_prefetch=3, grid=(steps,),
            in_specs=[full, full, pl.BlockSpec(memory_space=pl.ANY)],
            out_specs=[full, full, pl.BlockSpec(memory_space=pl.ANY)],
            scratch_shapes=[pltpu.VMEM((2, 3, group, tr, width), jnp.bfloat16), pltpu.VMEM((2, 3, group, tr, width), jnp.bfloat16),
                pltpu.SemaphoreType.DMA((2,)), pltpu.SemaphoreType.DMA((2,))]),
        out_shape=[jax.ShapeDtypeStruct((tokens, width), jnp.float32), jax.ShapeDtypeStruct((tokens, width), jnp.float32), jax.ShapeDtypeStruct(wall.shape, jnp.bfloat16)],
        compiler_params=pltpu.CompilerParams(vmem_limit_bytes=56 << 20, dimension_semantics=("arbitrary",)),
        name="ffn",
    )(gate_s, up_s, down_s, normed, cot, wall)


MESH = pl.DeviceIdType.MESH
EVERY = slice(None)
GATHER_ROUTES = (
    ("z1", "z2", "z3", "x", "y", "core"),
    ("z1", "z2", "z3", "y", "x", "core"),
    ("x", "z1", "z2", "z3", "y", "core"),
    ("y", "z1", "z2", "z3", "x", "core"),
)


def position():
    dp = lax.axis_index("dp")
    return dp // 4, lax.rem(dp // 2, 2), lax.rem(dp, 2), lax.axis_index("fsdp")


def target(hop):
    y, x, c, z = position()
    if hop == "x":
        x = 1 - x
    elif hop == "y":
        y = 1 - y
    elif hop == "core":
        c = 1 - c
    elif hop == "back":
        z = lax.rem(z + 3, 4)
    else:
        z = lax.rem(z + 1, 4)
    return (y * 4 + x * 2 + c, z)


def enter(hops):
    barrier = pltpu.get_barrier_semaphore()
    for hop in hops:
        pl.semaphore_signal(barrier, inc=1, device_id=target(hop), device_id_type=MESH)
    pl.semaphore_wait(barrier, len(hops))


def split_slots(caps):
    small = caps // 6
    third = (caps - 2 * small) // 2
    counts = (small, small, third, caps - 2 * small - third)
    starts = (0, small, 2 * small, 2 * small + third)
    return counts, starts


GATHER_DELAYS = (0, 1, 0, 0)
SCATTER_DELAYS = (4, 4, 0, 0)


def round_count(counts, delays):
    return max(
        delay + (2 * count - 1 if route < 2 else count)
        for route, (count, delay) in enumerate(zip(counts, delays))
    )


def turn(route, at, counts, delays):
    at = at - delays[route]
    if route < 2:
        live = (at >= 0) & (lax.rem(at + 64, 2) == 0) & (at < 2 * counts[route])
        return live, at // 2
    return (at >= 0) & (at < counts[route]), at


def slot_of(route, index, counts, starts, lead, early):
    if route < 2:
        return 2 * lead + starts[route] + index
    here = 2 * lead + starts[route] - (route - 2) * lead
    count = counts[route]
    if early:
        later = (index + count - lead) // count
        return (route - 2) * lead + index + later * (here - route * lead + lead)
    final = index // (count - lead)
    return here + index - final * (here + count - lead - (route - 2) * lead)


def attend_side(side, q, k_pair, v_pair, mask, out_ref, logs):
    lane = lax.broadcasted_iota(jnp.int32, (q.shape[0], 128), 1)
    scale = jnp.bfloat16(1.0 / HEAD**0.5)
    k = k_pair[:, side * HEAD : (side + 1) * HEAD]
    v = v_pair[:, side * HEAD : (side + 1) * HEAD]
    for h in range(GROUP):
        cols = slice(h * HEAD, (h + 1) * HEAD)
        scores = jnp.where(mask, dot(q[:, cols] * scale, k, NT), masked_score)
        top = jnp.max(scores, axis=1, keepdims=True)
        raised = jnp.exp(scores - top)
        total = jnp.sum(raised, axis=1, keepdims=True)
        probs = (raised * (1.0 / total)).astype(jnp.bfloat16)
        out_ref[:, cols] = dot(probs, v, NN).astype(out_ref.dtype)
        logs = jnp.where(lane == side * GROUP + h, top + jnp.log(total), logs)
    return logs


GATHER_HOPS = ("z1", "z2", "z3")


def gather_kernel(
    lead,
    mine_ref,
    gain_ref,
    table,
    places,
    hidden_ref,
    cos_ref,
    sin_ref,
    wall_ref,
    gains_ref,
    weights_ref,
    both_ref,
    all_gains_ref,
    normed_ref,
    q_ref,
    att_ref,
    lse_ref,
    middle_ref,
    normed_two_ref,
    own_sem,
    send_sem,
    recv_sem,
    tiles,
    block,
    gain_tiles,
    keys,
    mask_ref,
    pair_ref,
    side_sem,
    hop_send,
    hop_recv,
):
    y, x, c, z = position()
    counts, starts = split_slots(mine_ref.shape[0])
    rounds = round_count(counts, GATHER_DELAYS)
    own = pltpu.make_async_copy(mine_ref, wall_ref.at[y, x, c, z], own_sem.at[0])
    own_gain = pltpu.make_async_copy(gain_ref, gains_ref.at[y, x, c, z], own_sem.at[1])
    own.start()
    own_gain.start()
    enter(("x", "y", "core", "z", "back"))
    own.wait()
    own_gain.wait()

    def region(route, stage):
        hops = GATHER_ROUTES[route % 4]
        hop = hops[stage]
        done = hops[:stage]
        at_y = EVERY if "y" in done else y
        at_x = EVERY if "x" in done else x
        at_z = EVERY if "z3" in done else z
        if hop in ("z1", "z2", "z3"):
            at_z = lax.rem(z + 5 - int(hop[1]), 4)
        return at_y, at_x, c, at_z

    def copy(route, stage, index):
        if route == 4:
            view = gains_ref.at[region(route, stage)]
        else:
            slot = slot_of(route, index, counts, starts, lead // 2, True)
            view = wall_ref.at[region(route, stage) + (slot,)]
        return pltpu.make_async_remote_copy(
            src_ref=view,
            dst_ref=view,
            send_sem=send_sem.at[route, stage],
            recv_sem=recv_sem.at[route, stage, index],
            device_id=target(GATHER_ROUTES[route % 4][stage]),
            device_id_type=MESH,
        )

    stages = len(GATHER_ROUTES[0])
    tokens, width = hidden_ref.shape
    number = block.shape[0]
    rows = number * block.shape[1]
    query_blocks = q_ref.shape[1] // rows
    key_blocks = keys.shape[1] // rows

    def take(at):
        @pl.loop(0, number, unroll=True)
        def _(t):
            block[t] = tiles[table[at * number + t]]

        pltpu.make_async_copy(
            block, weights_ref.at[pl.ds(at * number, number)], side_sem.at[1]
        ).start()
        return block[...].reshape(rows, width)

    def taken(at):
        pltpu.make_async_copy(
            block, weights_ref.at[pl.ds(at * number, number)], side_sem.at[1]
        ).wait()

    def load_tiles(d):
        return pltpu.make_async_copy(
            wall_ref.at[d // 16, lax.rem(d // 8, 2), lax.rem(d // 4, 2), lax.rem(d, 4), pl.ds(0, lead)],
            tiles.at[pl.ds(d * lead, lead)],
            side_sem.at[0],
        )

    load_gains = pltpu.make_async_copy(gains_ref, gain_tiles, side_sem.at[2])

    def pass_keys(part):
        hop = part // 2
        at = lax.rem(z + 4 - hop, 4)
        cols = KV_HEADS * HEAD
        view = keys.at[
            pl.ds(pl.multiple_of(at * tokens, tokens), tokens),
            pl.ds(part % 2 * cols, cols),
        ]
        return pltpu.make_async_remote_copy(
            src_ref=view,
            dst_ref=view,
            send_sem=hop_send.at[part],
            recv_sem=hop_recv.at[part],
            device_id=target(GATHER_HOPS[hop]),
            device_id_type=MESH,
        )

    def begin():
        @pl.loop(0, 32)
        def _(d):
            load_tiles(d).start()

        load_gains.start()

    def norm():
        load_gains.wait()
        lane = lax.broadcasted_iota(jnp.int32, (8, 128), 1)
        parts = []
        for d in range(0, 32, 2):
            even = gain_tiles[d // 16, (d // 8) % 2, (d // 4) % 2, d % 4].astype(jnp.float32)[:8]
            odd = gain_tiles[d // 16, (d // 8) % 2, (d // 4) % 2, d % 4 + 1].astype(jnp.float32)[:8]
            parts.append(jnp.where(lane < 64, even, pltpu.roll(odd, 64, 1)))
        all_gains_ref[...] = jnp.concatenate(parts, axis=1)
        hidden = hidden_ref[...].astype(jnp.float32)
        inv = lax.rsqrt(jnp.mean(hidden * hidden, axis=1, keepdims=True) + norm_eps)
        normed_ref[...] = (hidden * inv * all_gains_ref[0:1, :]).astype(normed_ref.dtype)
        fill_mask(places, mask_ref)

    def project_keys():
        pltpu.make_async_copy(tiles, tiles, side_sem.at[0]).wait()
        own_rows = pl.ds(pl.multiple_of(z * tokens, tokens), tokens)

        for b in range(key_blocks):
            at = query_blocks + b
            u = dot(normed_ref[...], take(at), NT)
            if b < key_blocks // 2:
                u = u * cos_ref[...] + swap_halves(u) * sin_ref[...]
            keys[own_rows, b * rows : (b + 1) * rows] = u.astype(keys.dtype)
            taken(at)

    def project_queries(low, high):
        @pl.loop(low, high)
        def _(b):
            u = dot(normed_ref[...], take(b), NT)
            u = u * cos_ref[...] + swap_halves(u) * sin_ref[...]
            q_ref[:, pl.ds(pl.multiple_of(b * rows, rows), rows)] = u.astype(q_ref.dtype)
            taken(b)

    def attend_step(pair, side):
        wide = GROUP * HEAD
        narrow = PAIR * HEAD
        here = pl.ds(pl.multiple_of((pair * PAIR + side) * wide, wide), wide)
        k_pair = keys[:, pl.ds(pl.multiple_of(pair * narrow, narrow), narrow)]
        v_pair = keys[:, pl.ds(pl.multiple_of(KV_HEADS * HEAD + pair * narrow, narrow), narrow)]
        logs = lse_ref[pair] if side else jnp.zeros((tokens, 128), jnp.float32)
        mask = mask_ref[...] > 0.5
        lse_ref[pair] = attend_side(side, q_ref[:, here], k_pair, v_pair, mask, pair_ref, logs)
        att_ref[:, here] = pair_ref[...]

    def mix_blocks(low):
        for more in range(4):
            b = low + more
            at = query_blocks + key_blocks + b
            left = att_ref[:, pl.ds(pl.multiple_of(b * rows, rows), rows)]
            middle_ref[...] += dot(left, take(at), NN)
            taken(at)

    def mix_end():
        middle = middle_ref[...]
        inv = lax.rsqrt(jnp.mean(middle * middle, axis=1, keepdims=True) + norm_eps)
        normed_two_ref[...] = (middle * inv * all_gains_ref[1:2, :]).astype(normed_two_ref.dtype)

    start = GATHER_DELAYS[3] + lead // 2 - 1 + stages
    keep_both = pltpu.make_async_copy(keys, both_ref, side_sem.at[3])

    @pl.loop(0, rounds + stages)
    def _(t):
        for stage in range(stages + 1):
            for route in range(5):
                if route == 4:
                    live, index = t == stage, 0
                else:
                    live, index = turn(route, t - stage, counts, GATHER_DELAYS)

                @pl.when(live)
                def _(stage=stage, route=route, index=index):
                    if stage > 0:
                        copy(route, stage - 1, index).wait()
                    if stage < stages:
                        copy(route, stage, index).start()

        @pl.when(t == start)
        def _():
            begin()
            norm()

        @pl.when(t == start + 1)
        def _():
            project_keys()

        parts = 2 * len(GATHER_HOPS)
        for part in range(parts + 1):

            @pl.when(t == start + 1 + part)
            def _(part=part):
                if part > 0:
                    pass_keys(part - 1).wait()
                if part < parts:
                    pass_keys(part).start()

        for third in range(4):

            @pl.when(t == start + 2 + third)
            def _(third=third):
                project_queries(third * query_blocks // 4, (third + 1) * query_blocks // 4)

        attending = start + 1 + parts

        @pl.when(t == attending)
        def _():
            keep_both.start()
            middle_ref[...] = hidden_ref[...].astype(jnp.float32)

        for side in range(PAIR):
            since = t - attending

            @pl.when((since >= 0) & (since < KV_HEADS) & (lax.rem(since + 64, 2) == side))
            def _(side=side, since=since):
                attend_step(since // 2, side)

        mixing = attending + KV_HEADS

        @pl.when((t >= mixing) & (t < mixing + query_blocks // 4))
        def _():
            mix_blocks((t - mixing) * 4)

        @pl.when(t == mixing + query_blocks // 4)
        def _():
            mix_end()
            keep_both.wait()


def gather_slots(low_tiles, low_gains, table, places, hidden, cosine, sine, lead):
    caps, rows, width = low_tiles.shape
    tokens = hidden.shape[0]
    length = tokens * 4
    counts, starts = split_slots(caps)
    kind = low_tiles.dtype
    vmem = pl.BlockSpec(memory_space=pltpu.VMEM)
    smem = pl.BlockSpec(memory_space=pltpu.SMEM)
    anyw = pl.BlockSpec(memory_space=pl.ANY)
    padded = jnp.pad(low_gains, ((0, 16 - low_gains.shape[0]), (0, 128 - low_gains.shape[1])))
    number = cosine.shape[1] // rows
    pairs = KV_HEADS // PAIR
    outs = pl.pallas_call(
        functools.partial(gather_kernel, lead),
        out_shape=[
            jax.ShapeDtypeStruct((2, 2, 2, 4, caps, rows, width), kind),
            jax.ShapeDtypeStruct((2, 2, 2, 4) + padded.shape, kind),
            jax.ShapeDtypeStruct((table.shape[0], rows, width), kind),
            jax.ShapeDtypeStruct((length, 2 * KV_HEADS * HEAD), kind),
            jax.ShapeDtypeStruct((8, width), jnp.float32),
            jax.ShapeDtypeStruct((tokens, width), kind),
            jax.ShapeDtypeStruct((tokens, width), kind),
            jax.ShapeDtypeStruct((tokens, width), kind),
            jax.ShapeDtypeStruct((pairs, tokens, 128), jnp.float32),
            jax.ShapeDtypeStruct((tokens, width), jnp.float32),
            jax.ShapeDtypeStruct((tokens, width), kind),
        ],
        in_specs=[vmem, vmem, smem, smem, vmem, vmem, vmem],
        out_specs=[anyw] * 4 + [vmem] * 7,
        scratch_shapes=[
            pltpu.SemaphoreType.DMA((2,)),
            pltpu.SemaphoreType.DMA((5, 6)),
            pltpu.SemaphoreType.DMA((5, 6, max(counts))),
            pltpu.VMEM((32 * lead, rows, width), kind),
            pltpu.VMEM((number, rows, width), kind),
            pltpu.VMEM((2, 2, 2, 4) + padded.shape, kind),
            pltpu.VMEM((length, 2 * KV_HEADS * HEAD), kind),
            pltpu.VMEM((tokens, length), jnp.float32),
            pltpu.VMEM((tokens, GROUP * HEAD), kind),
            pltpu.SemaphoreType.DMA((4,)),
            pltpu.SemaphoreType.DMA((6,)),
            pltpu.SemaphoreType.DMA((6,)),
        ],
        compiler_params=pltpu.CompilerParams(
            collective_id=0, has_side_effects=True, vmem_limit_bytes=62 << 20
        ),
        name="gather_slots",
    )(low_tiles, padded, table, places, hidden, cosine, sine)
    return [outs[0].reshape(32 * caps, rows, width)] + list(outs[2:])


SCATTER_ROUTES = (
    ("core", "y", "x", "z1", "z2", "z3", "end"),
    ("core", "x", "y", "z1", "z2", "z3", "end"),
    ("core", "y", "z1", "z2", "z3", "x", "end"),
    ("core", "x", "z1", "z2", "z3", "y", "end"),
)


SUM_HOPS = ("core", "x", "y", "z1", "z2", "z3")
SUM_START = 2


def scatter_extent(route, stage):
    hops = SCATTER_ROUTES[route]
    done = hops[1 : stage + 1] if hops[stage] in ("x", "y") else hops[1:stage]
    extent = []
    if "x" not in done or "y" not in done:
        extent.append(2)
    if not any(hop[0] == "z" for hop in hops[: stage + 1]):
        extent.append(4)
    return tuple(extent)


def scatter_terms(route, stage):
    hops = SCATTER_ROUTES[route]
    done = hops[1:stage]
    return 2 + ("x" in done) + ("y" in done) + ("z1" in done)


def scatter_kernel(look, wall_ref, gain_ref, out_ref, total_ref, core_ref, first_ref, second_ref, ring_ref, last_ref, *scratch):
    y, x, c, z = position()
    caps, rows, width = out_ref.shape
    counts, starts = split_slots(caps)
    rounds = round_count(counts, SCATTER_DELAYS)
    stages = len(SCATTER_ROUTES[0])
    held = {}
    made = {}
    scratch = list(scratch)
    for route in range(4):
        for stage in range(1, stages):
            held[route, stage] = scratch.pop(0)
            if stage < stages - 1:
                made[route, stage] = scratch.pop(0)
    load_sem, send_sem, recv_sem, sums, landed, sum_send, sum_recv = scratch
    enter(("x", "y", "core", "z", "back"))

    def pick(hop, mine, other):
        return other if hop else mine

    def landing(route, stage, slot):
        hops = SCATTER_ROUTES[route]
        hop = hops[stage]
        if hop == "core":
            return core_ref.at[:, :, :, slot]
        if hop[0] == "z":
            ring = ring_ref.at[int(hop[1]) - 1]
            return ring.at[0, slot] if route < 2 else ring.at[:, slot]
        if stage == 1:
            return first_ref.at[:, :, slot]
        if stage == 2:
            return second_ref.at[:, slot]
        return last_ref.at[slot]

    def terms(route, stage, slot):
        hops = SCATTER_ROUTES[route]
        hop = hops[stage]
        done = hops[1:stage]
        at_y = 1 - y if hop == "y" else (y if "y" in done else EVERY)
        at_x = 1 - x if hop == "x" else (x if "x" in done else EVERY)
        at_z = EVERY
        if hop[0] == "z":
            at_z = lax.rem(z + 4 - int(hop[1]), 4)
        elif "z3" in done:
            at_z = z
        views = [wall_ref.at[at_y, at_x, c, at_z, slot], core_ref.at[at_y, at_x, at_z, slot]]
        other = at_x if hops[1] == "y" else at_y
        if stage > 1:
            views.append(first_ref.at[other, at_z, slot])
        if route < 2 and stage > 2:
            views.append(second_ref.at[at_z, slot])
        if hop in ("z2", "z3"):
            ring = ring_ref.at[int(hop[1]) - 2]
            views.append(ring.at[0, slot] if route < 2 else ring.at[:, slot])
        elif "z3" in done:
            ring = ring_ref.at[2]
            views.append(ring.at[0, slot] if route < 2 else ring.at[other, slot])
        if route >= 2 and hop == "end":
            views.append(last_ref.at[slot])
        return views

    def send(route, stage, index):
        slot = starts[route] + index
        if stage == 0:
            source = wall_ref.at[:, :, 1 - c, :, slot]
        else:
            source = made[route, stage]
        return pltpu.make_async_remote_copy(
            src_ref=source,
            dst_ref=landing(route, stage, slot),
            send_sem=send_sem.at[route, stage],
            recv_sem=recv_sem.at[route, stage, index],
            device_id=target(SCATTER_ROUTES[route][stage]),
            device_id_type=MESH,
        )

    def early(route, stage, index):
        if stage > 0:
            for k, view in enumerate(terms(route, stage, starts[route] + index)[:-1]):
                pltpu.make_async_copy(view, held[route, stage].at[k], load_sem.at[route, stage]).start()

    def late(route, stage, index):
        if stage > 0:
            send(route, stage - 1, index).wait()
            view = terms(route, stage, starts[route] + index)[-1]
            last = held[route, stage].shape[0] - 1
            pltpu.make_async_copy(view, held[route, stage].at[last], load_sem.at[route, stage]).start()

    def finish(route, stage, index):
        if stage > 0:
            buf = held[route, stage]
            pltpu.make_async_copy(buf, buf, load_sem.at[route, stage]).wait()
            number = buf.shape[0]
            extent = buf.shape[1:-2]
            blocks = 1
            for size in extent:
                blocks *= size
            part = min(width, 512)

            @pl.loop(0, blocks)
            def _(block):
                if len(extent) == 2:
                    at = (block // extent[1], lax.rem(block, extent[1]))
                elif len(extent) == 1:
                    at = (block,)
                else:
                    at = ()
                for left in range(0, width, part):
                    cols = pl.ds(left, part)
                    total = buf[(0,) + at + (EVERY, cols)].astype(jnp.float32)
                    for k in range(1, number):
                        total += buf[(k,) + at + (EVERY, cols)].astype(jnp.float32)
                    if stage == stages - 1:
                        out_ref[starts[route] + index, :, cols] = total
                    else:
                        made[route, stage][at + (EVERY, cols)] = total.astype(made[route, stage].dtype)

        if stage < stages - 1:
            send(route, stage, index).start()

    def pass_sum(hop):
        return pltpu.make_async_remote_copy(
            src_ref=sums.at[hop] if hop < 4 else landed.at[hop - 1],
            dst_ref=landed.at[hop],
            send_sem=sum_send.at[hop],
            recv_sem=sum_recv.at[hop],
            device_id=target(SUM_HOPS[hop]),
            device_id_type=MESH,
        )

    def add_sums(step):
        if step > 0:
            pass_sum(step - 1).wait()
        if step == 0:
            sums[0] = gain_ref[...]
        elif step < 4:
            sums[step] = sums[step - 1] + landed[step - 1]
        elif step == len(SUM_HOPS):
            total_ref[...] = (sums[3] + landed[3]) + (landed[4] + landed[5])
        if step < len(SUM_HOPS):
            pass_sum(step).start()

    @pl.loop(0, rounds + stages - 1)
    def _(t):
        for step in range(len(SUM_HOPS) + 1):

            @pl.when(t == SUM_START + step)
            def _(step=step):
                add_sums(step)

        items = [(stage, route) for stage in range(stages - 1, -1, -1) for route in range(4)]

        def run(which, work):
            stage, route = items[which]
            live, index = turn(route, t - stage, counts, SCATTER_DELAYS)

            @pl.when(live)
            def _():
                work(route, stage, index)

        far, near = look
        for which in range(len(items) + far):
            if which < len(items):
                run(which, early)
            if far - near <= which < len(items) + far - near:
                run(which - far + near, late)
            if which >= far:
                run(which - far, finish)


def scatter_slots(grads_wall, gain_terms, caps, look=(4, 1)):
    rows, width = grads_wall.shape[1:]
    kind = grads_wall.dtype
    wall = grads_wall.reshape(2, 2, 2, 4, caps, rows, width)
    counts, starts = split_slots(caps)
    stages = len(SCATTER_ROUTES[0])
    scratch = []
    for route in range(4):
        for stage in range(1, stages):
            extent = scatter_extent(route, stage)
            scratch.append(pltpu.VMEM((scatter_terms(route, stage),) + extent + (rows, width), kind))
            if stage < stages - 1:
                scratch.append(pltpu.VMEM(extent + (rows, width), kind))
    tile = (caps, rows, width)
    out = pl.pallas_call(
        functools.partial(scatter_kernel, look),
        out_shape=[
            jax.ShapeDtypeStruct(tile, jnp.float32),
            jax.ShapeDtypeStruct(gain_terms.shape, jnp.float32),
            jax.ShapeDtypeStruct((2, 2, 4) + tile, kind),
            jax.ShapeDtypeStruct((2, 4) + tile, kind),
            jax.ShapeDtypeStruct((4,) + tile, kind),
            jax.ShapeDtypeStruct((3, 2) + tile, kind),
            jax.ShapeDtypeStruct(tile, kind),
        ],
        in_specs=[pl.BlockSpec(memory_space=pl.ANY), pl.BlockSpec(memory_space=pltpu.VMEM)],
        out_specs=[pl.BlockSpec(memory_space=pltpu.VMEM)] * 2 + [pl.BlockSpec(memory_space=pl.ANY)] * 5,
        scratch_shapes=scratch
        + [
            pltpu.SemaphoreType.DMA((4, stages)),
            pltpu.SemaphoreType.DMA((4, stages)),
            pltpu.SemaphoreType.DMA((4, stages, max(counts))),
            pltpu.VMEM((4,) + gain_terms.shape, jnp.float32),
            pltpu.VMEM((6,) + gain_terms.shape, jnp.float32),
            pltpu.SemaphoreType.DMA((6,)),
            pltpu.SemaphoreType.DMA((6,)),
        ],
        compiler_params=pltpu.CompilerParams(
            collective_id=1, has_side_effects=True, vmem_limit_bytes=56 << 20
        ),
        name="scatter_slots",
    )(wall, gain_terms)
    return out[0], out[1]


def shards(
    hidden_in,
    piece_starts,
    out_cotangent,
    owners,
    master,
    moment_one,
    moment_two,
    gain_master,
    gain_one,
    gain_two,
):
    devices = lax.axis_size("dp") * lax.axis_size("fsdp")
    caps, tile_rows, model_width = master.shape
    layout = section_layout(devices, tile_rows)
    slot_qkv, slot_out, slot_ffn, slot_down = slot_numbers(owners, layout, caps)
    query_tiles = model_width // tile_rows
    slot_query, slot_both = slot_qkv[:query_tiles], slot_qkv[query_tiles:]
    half = slot_ffn.shape[0] // 2
    lead = layout[2][3]
    tokens = hidden_in.astype(jnp.float32)
    local_len = tokens.shape[0]
    kv_width = KV_HEADS * HEAD
    first = lax.axis_index("fsdp") * local_len
    positions = first + jnp.arange(local_len, dtype=jnp.int32)
    places = jnp.concatenate([first[None].astype(jnp.int32), piece_starts[0]])
    cosine, sine = rope_tables(positions.astype(jnp.float32), 16 * tile_rows)
    wall, gains_low, both, normed, queries, attended, lse, middle, normed_two = forward_attention(
        master.astype(jnp.bfloat16),
        gain_master.astype(jnp.bfloat16),
        (slot_query, slot_both, slot_out),
        places,
        hidden_in,
        cosine,
        sine,
        lead,
    )
    gain_attn = gains_low[0]
    gain_ffn = gains_low[1]
    inv_one = lax.rsqrt(jnp.mean(tokens * tokens, axis=1, keepdims=True) + norm_eps)
    inv_two = lax.rsqrt(jnp.mean(middle * middle, axis=1, keepdims=True) + norm_eps)
    ffn_out, grad_normed_two, grads_wall = ffn_call(
        slot_ffn[:half], slot_ffn[half:], slot_down, normed_two, out_cotangent, wall
    )
    block_out = (middle + ffn_out).astype(jnp.bfloat16)
    scaled_two = grad_normed_two * gain_ffn
    grad_middle = (
        out_cotangent.astype(jnp.float32)
        + inv_two * scaled_two
        - middle * inv_two**3 * jnp.mean(scaled_two * middle, axis=1, keepdims=True)
    )
    gain_two_term = jnp.sum(grad_normed_two * middle * inv_two, axis=0)
    grad_branch = grad_middle.astype(jnp.bfloat16)
    grad_attended, grads_wall = mix_back(slot_out, attended, grad_branch, wall, grads_wall)
    grad_query, both_terms = attend_back(
        places, queries, both, grad_attended, lse, cosine, sine
    )
    both_sum = lax.psum_scatter(both_terms, "fsdp", scatter_dimension=0, tiled=True).astype(
        jnp.float32
    )
    grad_normed, grads_wall = project_back(slot_query, grad_query, normed, None, wall, grads_wall)
    both_sum = both_sum.reshape(local_len, KV_HEADS // PAIR, 2, PAIR * HEAD)
    grad_key = turn_back(both_sum[:, :, 0].reshape(local_len, kv_width), cosine, sine)
    grad_value = both_sum[:, :, 1].reshape(local_len, kv_width)
    grad_both = jnp.concatenate([grad_key, grad_value], axis=1).astype(jnp.bfloat16)
    grad_normed, grads_wall = project_back(
        slot_both, grad_both, normed, grad_normed, wall, grads_wall
    )
    keep_slot = filled_mask(owners, layout, lax.axis_index(("dp", "fsdp")))[:, None, None]
    gain_one_term = jnp.sum(grad_normed * tokens * inv_one, axis=0)
    weight_grad, gain_grad = scatter_any(
        grads_wall, jnp.stack([gain_one_term, gain_two_term]), caps
    )
    weight_grad = jnp.where(keep_slot, weight_grad, 0.0)
    scaled_one = grad_normed * gain_attn
    input_grad = (
        grad_middle
        + inv_one * scaled_one
        - tokens * inv_one**3 * jnp.mean(scaled_one * tokens, axis=1, keepdims=True)
    )
    step = float(STEP)
    new_one, new_two, new_weights = adam_step(
        master, moment_one, moment_two, weight_grad, step, decay_rate, learn_rate
    )
    new_one = jnp.where(keep_slot, new_one, 0.0)
    new_two = jnp.where(keep_slot, new_two, 0.0)
    new_weights = jnp.where(keep_slot, new_weights, 0.0)
    new_gain_one, new_gain_two, new_gains = adam_step(
        gain_master, gain_one, gain_two, gain_grad, step, 0.0, gain_rate
    )
    return (
        block_out,
        input_grad,
        weight_grad,
        new_weights,
        new_one,
        new_two,
        gain_grad,
        new_gains,
        new_gain_one,
        new_gain_two,
    )


def solution(mesh):
    return jax.shard_map(
        shards,
        mesh=mesh,
        in_specs=(
            P(("dp", "fsdp"), None),
            P("dp", None),
            P(("dp", "fsdp"), None),
            P(),
            P(("dp", "fsdp"), None, None),
            P(("dp", "fsdp"), None, None),
            P(("dp", "fsdp"), None, None),
            P(None, ("dp", "fsdp")),
            P(None, ("dp", "fsdp")),
            P(None, ("dp", "fsdp")),
        ),
        out_specs=(
            P(("dp", "fsdp"), None),
            P(("dp", "fsdp"), None),
            P(("dp", "fsdp"), None, None),
            P(("dp", "fsdp"), None, None),
            P(("dp", "fsdp"), None, None),
            P(("dp", "fsdp"), None, None),
            P(None, ("dp", "fsdp")),
            P(None, ("dp", "fsdp")),
            P(None, ("dp", "fsdp")),
            P(None, ("dp", "fsdp")),
        ),
        check_vma=False,
    )
```

```python
import functools

import jax
import jax.experimental.pallas as pl
import jax.experimental.pallas.tpu as pltpu
import jax.numpy as jnp
from jax import lax
from jax.sharding import PartitionSpec as P

D = 2048
HEADS = 32
KV_HEADS = 8
HEAD = 64
FF = 8192
PIECE = 256
STEP = 5


norm_eps = 1e-05
adam_eps = 1e-08
beta_one = 0.5
beta_two = 0.5
learn_rate = 0.02
gain_rate = 0.3
decay_rate = 0.1
rope_base = 500000.0
masked_score = -1e30


def section_layout(devices, tile_rows):
    counts = [
        (D + 2 * KV_HEADS * HEAD) // tile_rows,
        HEADS * HEAD // tile_rows,
        2 * FF // tile_rows,
        FF // tile_rows,
    ]
    layout = []
    first_tile = 0
    first_slot = 0
    for number in counts:
        capacity = 5 * number // (4 * devices) + 1
        layout.append((first_tile, number, capacity, first_slot))
        first_tile += number
        first_slot += capacity
    return layout


def adam_step(weights, first_moment, second_moment, grads, step, decay, rate):
    new_one = beta_one * first_moment + (1.0 - beta_one) * grads
    new_two = beta_two * second_moment + (1.0 - beta_two) * grads * grads
    correct_one = 1.0 - beta_one**step
    correct_two = 1.0 - beta_two**step
    update = -rate * (
        new_one / correct_one / (jnp.sqrt(new_two / correct_two) + adam_eps) + decay * weights
    )
    return (new_one, new_two, weights + update)


def slot_numbers(owners, layout, caps):
    placed = []
    for first_tile, number, capacity, first_slot in layout:
        mine = owners[first_tile : first_tile + number]
        order = jnp.arange(number, dtype=jnp.int32)
        earlier = (mine[:, None] == mine[None, :]) & (order[None, :] < order[:, None])
        ranked = jnp.sum(earlier.astype(jnp.int32), axis=1)
        placed.append(mine * caps + first_slot + ranked)
    return placed


def filled_mask(owners, layout, device):
    masks = []
    for first_tile, number, capacity, first_slot in layout:
        count = jnp.sum((owners[first_tile : first_tile + number] == device).astype(jnp.int32))
        masks.append(jnp.arange(capacity, dtype=jnp.int32) < count)
    return jnp.concatenate(masks)


def rope_tables(positions, block):
    half_dim = HEAD // 2
    inverse = rope_base ** (-(jnp.arange(half_dim, dtype=jnp.float32) * 2.0 / HEAD))
    angles = positions[:, None] * inverse[None, :]
    cosine = jnp.cos(angles)
    sine = jnp.sin(angles)
    return (
        jnp.tile(jnp.concatenate([cosine, cosine], axis=1), (1, block // HEAD)),
        jnp.tile(jnp.concatenate([-sine, sine], axis=1), (1, block // HEAD)),
    )


def turn_back(grads, cosine, sine):
    tokens, width = grads.shape
    half_dim = HEAD // 2
    heads = grads.reshape(tokens, width // HEAD, 2, half_dim)
    swapped = heads[:, :, ::-1].reshape(tokens, width)
    times = width // cosine.shape[1]
    return grads * jnp.tile(cosine, (1, times)) - swapped * jnp.tile(sine, (1, times))


def tuned_mesh():
    return (lax.axis_size("dp"), lax.axis_size("fsdp")) == (8, 4)


def forward_attention(low_tiles, low_gains, slots, places, hidden_in, cosine, sine, lead):
    caps, tile_rows, width = low_tiles.shape
    slot_query, slot_both, slot_out = slots
    if tuned_mesh():
        table = jnp.concatenate(slots)
        table = table // caps * lead + lax.rem(table, caps)
        (wall, weights, both, gains, normed, queries, attended, lse, middle, normed_two) = (
            gather_slots(low_tiles, low_gains, table, places, hidden_in, cosine, sine, lead)
        )
        return wall, weights, gains, both, normed, queries, attended, lse, middle, normed_two
    wall = lax.all_gather(low_tiles, ("dp", "fsdp"), axis=0, tiled=True)
    gains = lax.all_gather(low_gains, ("dp", "fsdp"), axis=1, tiled=True).astype(jnp.float32)
    tokens = hidden_in.astype(jnp.float32)
    inv_one = lax.rsqrt(jnp.mean(tokens * tokens, axis=1, keepdims=True) + norm_eps)
    normed = (tokens * inv_one * gains[0]).astype(jnp.bfloat16)
    turned = KV_HEADS * HEAD // cosine.shape[1]
    both_local = project(slot_both, normed, cosine, sine, wall, turned=turned)
    both = lax.all_gather(both_local, "fsdp", axis=0, tiled=True)
    queries = project(slot_query, normed, cosine, sine, wall)
    attended, lse = attend(places, queries, both)
    middle, normed_two = mix(slot_out, attended, hidden_in, gains[1], wall)
    return wall, wall, gains, both, normed, queries, attended, lse, middle, normed_two


def backward_attention(
    grads_wall,
    gain_two_term,
    weights,
    slots,
    places,
    branch,
    attended,
    queries,
    both,
    lse,
    normed,
    hidden_in,
    cosine,
    sine,
    layout,
    caps,
):
    slot_query, slot_both, slot_out = slots
    local_len, width = normed.shape
    kv_width = KV_HEADS * HEAD
    if tuned_mesh():
        lead = layout[2][3]
        table = jnp.concatenate(slots)
        table = table // caps * lead + lax.rem(table, caps)
        order = jnp.arange(table.shape[0], dtype=jnp.int32)
        here = jnp.arange(32 * lead, dtype=jnp.int32)
        tile_at = jnp.sum(jnp.where(table[None, :] == here[:, None], order[None, :], 0), axis=1)
        terms = jnp.pad(gain_two_term[None, :], ((1, 6), (0, 0)))
        grads, total, grad_normed = scatter_slots(
            grads_wall,
            terms,
            weights,
            tile_at,
            places,
            branch,
            attended,
            queries,
            both,
            lse,
            normed,
            hidden_in,
            cosine,
            sine,
            lead,
            layout[0][2],
            caps,
        )
        part = width // 32
        device = lax.axis_index(("dp", "fsdp"))
        return grads, lax.dynamic_slice_in_dim(total[:2], device * part, part, 1), grad_normed
    grad_attended, grads_wall = mix_back(slot_out, attended, branch, weights, grads_wall)
    grad_query, both_terms = attend_back(
        places, queries, both, grad_attended, lse, cosine, sine
    )
    both_sum = lax.psum_scatter(both_terms, "fsdp", scatter_dimension=0, tiled=True).astype(
        jnp.float32
    )
    grad_normed, grads_wall = project_back(slot_query, grad_query, normed, None, weights, grads_wall)
    both_sum = both_sum.reshape(local_len, KV_HEADS // PAIR, 2, PAIR * HEAD)
    grad_key = turn_back(both_sum[:, :, 0].reshape(local_len, kv_width), cosine, sine)
    grad_value = both_sum[:, :, 1].reshape(local_len, kv_width)
    grad_both = jnp.concatenate([grad_key, grad_value], axis=1).astype(jnp.bfloat16)
    grad_normed, grads_wall = project_back(
        slot_both, grad_both, normed, grad_normed, weights, grads_wall
    )
    tokens = hidden_in.astype(jnp.float32)
    inv_one = lax.rsqrt(jnp.mean(tokens * tokens, axis=1, keepdims=True) + norm_eps)
    gain_one_term = jnp.sum(grad_normed * tokens * inv_one, axis=0)
    gain_terms = jnp.stack([gain_one_term, gain_two_term])
    grads = lax.psum_scatter(grads_wall, ("dp", "fsdp"), scatter_dimension=0, tiled=True)
    gain_grad = lax.psum_scatter(gain_terms, ("dp", "fsdp"), scatter_dimension=1, tiled=True)
    return grads.astype(jnp.float32), gain_grad, grad_normed


VMEM_ASK = 56 << 20
NT = (((1,), (1,)), ((), ()))
NN = (((1,), (0,)), ((), ()))
TN = (((0,), (0,)), ((), ()))


def dot(a, b, dims):
    return lax.dot_general(a, b, dims, preferred_element_type=jnp.float32)


def stream_tiles(table, wall_ref, held, sem, group):
    step = pl.program_id(0)
    steps = pl.num_programs(0)
    depth = held.shape[0]
    buf = lax.rem(step, depth)

    def fetch(at):
        into = lax.rem(at, depth)

        @pl.loop(0, group, unroll=True)
        def _(t):
            pltpu.make_async_copy(
                wall_ref.at[table[at * group + t]], held.at[into, t], sem.at[into]
            ).start()

    @pl.when(step == 0)
    def _():
        for ahead in range(depth - 1):

            @pl.when(ahead < steps)
            def _(ahead=ahead):
                fetch(jnp.int32(ahead))

    @pl.when(step + depth - 1 < steps)
    def _():
        fetch(step + depth - 1)

    pltpu.make_async_copy(held.at[buf], held.at[buf], sem.at[buf]).wait()
    rows = group * wall_ref.shape[1]
    return held[buf].reshape(rows, wall_ref.shape[2])


def store_tiles(table, grads_ref, made, sem, group, value):
    step = pl.program_id(0)
    steps = pl.num_programs(0)
    buf = lax.rem(step, 2)

    def drain(which):
        pltpu.make_async_copy(made.at[which], made.at[which], sem.at[which]).wait()

    @pl.when(step >= 2)
    def _():
        drain(buf)

    made[buf] = value.astype(made.dtype).reshape(made.shape[1:])

    @pl.loop(0, group, unroll=True)
    def _(t):
        pltpu.make_async_copy(
            made.at[buf, t], grads_ref.at[table[step * group + t]], sem.at[buf]
        ).start()

    @pl.when(step == steps - 1)
    def _():
        drain(1 - buf)
        drain(buf)


def swap_halves(u):
    width = u.shape[1]
    lane = lax.broadcasted_iota(jnp.int32, u.shape, 1)
    first = lax.rem(lane, HEAD) < HEAD // 2
    return jnp.where(
        first, pltpu.roll(u, width - HEAD // 2, 1), pltpu.roll(u, HEAD // 2, 1)
    )


def project_kernel(group, turned, table, normed_ref, cos_ref, sin_ref, wall_ref, out_ref, held, sem):
    weights = stream_tiles(table, wall_ref, held, sem, group)
    u = dot(normed_ref[...], weights, NT)
    if turned is None:
        out_ref[...] = (u * cos_ref[...] + swap_halves(u) * sin_ref[...]).astype(out_ref.dtype)
    else:

        @pl.when(pl.program_id(0) < turned)
        def _():
            out_ref[...] = (u * cos_ref[...] + swap_halves(u) * sin_ref[...]).astype(out_ref.dtype)

        @pl.when(pl.program_id(0) >= turned)
        def _():
            out_ref[...] = u.astype(out_ref.dtype)


def full_spec(shape):
    return pl.BlockSpec(shape, lambda i, *_: (0,) * len(shape))


def any_spec():
    return pl.BlockSpec(memory_space=pl.ANY)


AHEAD = 4


def held_tiles(depth, group, wall):
    return pltpu.VMEM((depth, group) + wall.shape[1:], wall.dtype)


def project(table, normed, cosine, sine, wall, turned=None, group=16):
    tokens = normed.shape[0]
    block = group * wall.shape[1]
    steps = table.shape[0] // group
    return pl.pallas_call(
        functools.partial(project_kernel, group, turned),
        grid_spec=pltpu.PrefetchScalarGridSpec(
            num_scalar_prefetch=1,
            grid=(steps,),
            in_specs=[full_spec(normed.shape), full_spec(cosine.shape), full_spec(sine.shape), any_spec()],
            out_specs=pl.BlockSpec((tokens, block), lambda i, *_: (0, i)),
            scratch_shapes=[held_tiles(AHEAD, group, wall), pltpu.SemaphoreType.DMA((AHEAD,))],
        ),
        out_shape=jax.ShapeDtypeStruct((tokens, steps * block), jnp.bfloat16),
        compiler_params=pltpu.CompilerParams(vmem_limit_bytes=VMEM_ASK),
        name="project",
    )(table, normed, cosine, sine, wall)


def mix_kernel(group, table, left_ref, hidden_ref, gain_ref, wall_ref, middle_ref, normed_ref, held, sem):
    step = pl.program_id(0)
    weights = stream_tiles(table, wall_ref, held, sem, group)

    @pl.when(step == 0)
    def _():
        middle_ref[...] = hidden_ref[...].astype(jnp.float32)

    middle_ref[...] += dot(left_ref[...], weights, NN)

    @pl.when(step == pl.num_programs(0) - 1)
    def _():
        middle = middle_ref[...]
        inv = lax.rsqrt(jnp.mean(middle * middle, axis=1, keepdims=True) + norm_eps)
        normed_ref[...] = (middle * inv * gain_ref[...]).astype(normed_ref.dtype)


def mix(table, left, hidden, gain, wall, group=16):
    tokens, width = hidden.shape
    block = group * wall.shape[1]
    return pl.pallas_call(
        functools.partial(mix_kernel, group),
        grid_spec=pltpu.PrefetchScalarGridSpec(
            num_scalar_prefetch=1,
            grid=(table.shape[0] // group,),
            in_specs=[
                pl.BlockSpec((tokens, block), lambda i, *_: (0, i)),
                full_spec(hidden.shape),
                full_spec((1, width)),
                any_spec(),
            ],
            out_specs=[full_spec(hidden.shape), full_spec(hidden.shape)],
            scratch_shapes=[held_tiles(AHEAD, group, wall), pltpu.SemaphoreType.DMA((AHEAD,))],
        ),
        out_shape=[
            jax.ShapeDtypeStruct(hidden.shape, jnp.float32),
            jax.ShapeDtypeStruct(hidden.shape, jnp.bfloat16),
        ],
        compiler_params=pltpu.CompilerParams(vmem_limit_bytes=VMEM_ASK),
        name="mix",
    )(table, left, hidden, gain.reshape(1, width), wall)


def mix_back_kernel(group, table, left_ref, right_ref, wall_ref, old_ref, out_ref, grads_ref, held, made, load_sem, store_sem):
    weights = stream_tiles(table, wall_ref, held, load_sem, group)
    right = right_ref[...]
    out_ref[...] = dot(right, weights, NT).astype(out_ref.dtype)
    store_tiles(table, grads_ref, made, store_sem, group, dot(left_ref[...], right, TN))


def mix_back(table, left, right, wall, grads, group=16):
    tokens, width = right.shape
    block = group * wall.shape[1]
    columns = pl.BlockSpec((tokens, block), lambda i, *_: (0, i))
    return pl.pallas_call(
        functools.partial(mix_back_kernel, group),
        grid_spec=pltpu.PrefetchScalarGridSpec(
            num_scalar_prefetch=1,
            grid=(table.shape[0] // group,),
            in_specs=[columns, full_spec(right.shape), any_spec(), any_spec()],
            out_specs=[columns, any_spec()],
            scratch_shapes=[
                held_tiles(AHEAD, group, wall),
                held_tiles(2, group, wall),
                pltpu.SemaphoreType.DMA((AHEAD,)),
                pltpu.SemaphoreType.DMA((2,)),
            ],
        ),
        out_shape=[
            jax.ShapeDtypeStruct(left.shape, jnp.bfloat16),
            jax.ShapeDtypeStruct(grads.shape, grads.dtype),
        ],
        input_output_aliases={4: 1},
        compiler_params=pltpu.CompilerParams(vmem_limit_bytes=VMEM_ASK),
        name="mix_back",
    )(table, left, right, wall, grads)


def project_back_kernel(group, fresh, table, left_ref, right_ref, wall_ref, old_ref, start_ref, out_ref, grads_ref, held, made, load_sem, store_sem):
    weights = stream_tiles(table, wall_ref, held, load_sem, group)

    @pl.when(pl.program_id(0) == 0)
    def _():
        out_ref[...] = jnp.zeros_like(out_ref) if fresh else start_ref[...]

    left = left_ref[...]
    out_ref[...] += dot(left, weights, NN)
    store_tiles(table, grads_ref, made, store_sem, group, dot(left, right_ref[...], TN))


def project_back(table, left, right, start, wall, grads, group=16):
    tokens, width = right.shape
    block = group * wall.shape[1]
    return pl.pallas_call(
        functools.partial(project_back_kernel, group, start is None),
        grid_spec=pltpu.PrefetchScalarGridSpec(
            num_scalar_prefetch=1,
            grid=(table.shape[0] // group,),
            in_specs=[
                pl.BlockSpec((tokens, block), lambda i, *_: (0, i)),
                full_spec(right.shape),
                any_spec(),
                any_spec(),
                any_spec() if start is None else full_spec(start.shape),
            ],
            out_specs=[full_spec(right.shape), any_spec()],
            scratch_shapes=[
                held_tiles(AHEAD, group, wall),
                held_tiles(2, group, wall),
                pltpu.SemaphoreType.DMA((AHEAD,)),
                pltpu.SemaphoreType.DMA((2,)),
            ],
        ),
        out_shape=[
            jax.ShapeDtypeStruct(right.shape, jnp.float32),
            jax.ShapeDtypeStruct(grads.shape, grads.dtype),
        ],
        input_output_aliases={4: 1},
        compiler_params=pltpu.CompilerParams(vmem_limit_bytes=VMEM_ASK),
        name="project_back",
    )(table, left, right, wall, grads, table if start is None else start)


def fill_mask(places, mask_ref):
    shape = mask_ref.shape
    query = lax.broadcasted_iota(jnp.int32, shape, 0) + places[0]
    key = lax.broadcasted_iota(jnp.int32, shape, 1)
    allowed = key <= query
    for piece in range(places.shape[0] - 1):
        low = places[1 + piece]
        inside_query = (query >= low) & (query < low + PIECE)
        inside_key = (key >= low) & (key < low + PIECE)
        allowed = allowed | (inside_query & inside_key)
    mask_ref[...] = jnp.where(allowed, 1.0, 0.0)


PAIR = 2
GROUP = HEADS // KV_HEADS


def attend_kernel(places, q_ref, k_ref, v_ref, out_ref, lse_ref, mask_ref):
    @pl.when(pl.program_id(0) == 0)
    def _():
        fill_mask(places, mask_ref)

    mask = mask_ref[...] > 0.5
    lane = lax.broadcasted_iota(jnp.int32, lse_ref.shape[1:], 1)
    logs = jnp.zeros(lse_ref.shape[1:], jnp.float32)
    scale = jnp.bfloat16(1.0 / HEAD**0.5)
    for side in range(PAIR):
        k = k_ref[:, side * HEAD : (side + 1) * HEAD]
        v = v_ref[:, side * HEAD : (side + 1) * HEAD]
        for h in range(GROUP):
            head = side * GROUP + h
            cols = slice(head * HEAD, (head + 1) * HEAD)
            scores = jnp.where(mask, dot(q_ref[:, cols] * scale, k, NT), masked_score)
            top = jnp.max(scores, axis=1, keepdims=True)
            raised = jnp.exp(scores - top)
            total = jnp.sum(raised, axis=1, keepdims=True)
            probs = (raised * (1.0 / total)).astype(jnp.bfloat16)
            out_ref[:, cols] = dot(probs, v, NN).astype(out_ref.dtype)
            logs = jnp.where(lane == head, top + jnp.log(total), logs)
    lse_ref[0] = logs


def attend(places, queries, both):
    tokens, width = queries.shape
    length = both.shape[0]
    steps = KV_HEADS // PAIR
    wide = PAIR * GROUP * HEAD
    narrow = PAIR * HEAD
    return pl.pallas_call(
        attend_kernel,
        grid_spec=pltpu.PrefetchScalarGridSpec(
            num_scalar_prefetch=1,
            grid=(steps,),
            in_specs=[
                pl.BlockSpec((tokens, wide), lambda i, *_: (0, i)),
                pl.BlockSpec((length, narrow), lambda i, *_: (0, i)),
                pl.BlockSpec((length, narrow), lambda i, *_: (0, steps + i)),
            ],
            out_specs=[
                pl.BlockSpec((tokens, wide), lambda i, *_: (0, i)),
                pl.BlockSpec((1, tokens, 128), lambda i, *_: (i, 0, 0)),
            ],
            scratch_shapes=[pltpu.VMEM((tokens, length), jnp.float32)],
        ),
        out_shape=[
            jax.ShapeDtypeStruct((tokens, width), jnp.bfloat16),
            jax.ShapeDtypeStruct((steps, tokens, 128), jnp.float32),
        ],
        compiler_params=pltpu.CompilerParams(vmem_limit_bytes=VMEM_ASK),
        name="attend",
    )(places, queries, both, both)


def attend_back_kernel(places, q_ref, k_ref, v_ref, grad_ref, lse_ref, cos_ref, sin_ref, out_ref, both_ref, mask_ref, turn_ref):
    @pl.when(pl.program_id(0) == 0)
    def _():
        fill_mask(places, mask_ref)

    mask = mask_ref[...] > 0.5
    scale = jnp.bfloat16(1.0 / HEAD**0.5)
    for side in range(PAIR):
        here = slice(side * HEAD, (side + 1) * HEAD)
        k = k_ref[:, here]
        v = v_ref[:, here]
        dk = None
        dv = None
        for h in range(GROUP):
            head = side * GROUP + h
            cols = slice(head * HEAD, (head + 1) * HEAD)
            q = q_ref[:, cols] * scale
            grad = grad_ref[:, cols]
            scores = jnp.where(mask, dot(q, k, NT), masked_score)
            probs = jnp.exp(scores - lse_ref[0, :, head : head + 1])
            grad_probs = dot(grad, v, NT)
            row_dot = jnp.sum(probs * grad_probs, axis=1, keepdims=True)
            grad_scores = (probs * (grad_probs - row_dot)).astype(jnp.bfloat16)
            turn_ref[:, cols] = dot(grad_scores, k, NN) * (1.0 / HEAD**0.5)
            dk_part = dot(q, grad_scores, TN)
            dv_part = dot(grad, probs.astype(jnp.bfloat16), TN)
            dk = dk_part if dk is None else dk + dk_part
            dv = dv_part if dv is None else dv + dv_part
        there = slice((PAIR + side) * HEAD, (PAIR + side + 1) * HEAD)
        both_ref[:, here] = dk.T.astype(both_ref.dtype)
        both_ref[:, there] = dv.T.astype(both_ref.dtype)
    wide = cos_ref.shape[1]
    for left in range(0, turn_ref.shape[1], wide):
        u = turn_ref[:, left : left + wide]
        out_ref[:, left : left + wide] = (u * cos_ref[...] - swap_halves(u) * sin_ref[...]).astype(out_ref.dtype)


def attend_back(places, queries, both, grad, lse, cosine, sine):
    tokens, width = queries.shape
    length = both.shape[0]
    steps = KV_HEADS // PAIR
    wide = PAIR * GROUP * HEAD
    narrow = PAIR * HEAD
    columns = pl.BlockSpec((tokens, wide), lambda i, *_: (0, i))
    keys = pl.BlockSpec((length, narrow), lambda i, *_: (0, i))
    return pl.pallas_call(
        attend_back_kernel,
        grid_spec=pltpu.PrefetchScalarGridSpec(
            num_scalar_prefetch=1,
            grid=(steps,),
            in_specs=[
                columns,
                keys,
                pl.BlockSpec((length, narrow), lambda i, *_: (0, steps + i)),
                columns,
                pl.BlockSpec((1, tokens, 128), lambda i, *_: (i, 0, 0)),
                full_spec(cosine.shape),
                full_spec(sine.shape),
            ],
            out_specs=[columns, pl.BlockSpec((length, 2 * narrow), lambda i, *_: (0, i))],
            scratch_shapes=[pltpu.VMEM((tokens, length), jnp.float32), pltpu.VMEM((tokens, wide), jnp.float32)],
        ),
        out_shape=[
            jax.ShapeDtypeStruct((tokens, width), jnp.bfloat16),
            jax.ShapeDtypeStruct((length, 2 * KV_HEADS * HEAD), jnp.bfloat16),
        ],
        compiler_params=pltpu.CompilerParams(vmem_limit_bytes=VMEM_ASK),
        name="attend_back",
    )(places, queries, both, both, grad, lse, cosine, sine)


def ffn_kernel(group, gate_s, up_s, down_s, normed_ref, cot_ref, wall_ref, out_ref, back_ref, grads_ref, held, made, load_sem, store_sem):
    step = pl.program_id(0)
    steps = pl.num_programs(0)
    tables = (gate_s, up_s, down_s)
    tile_rows = wall_ref.shape[1]
    width = wall_ref.shape[2]
    rows = group * tile_rows

    def fetch(at, buf):
        for kind in range(3):
            @pl.loop(0, group, unroll=True)
            def _(t, kind=kind):
                pltpu.make_async_copy(wall_ref.at[tables[kind][at * group + t]], held.at[buf, kind, t], load_sem.at[buf]).start()

    def drain(buf):
        pltpu.make_async_copy(made.at[buf], made.at[buf], store_sem.at[buf]).wait()

    buf = lax.rem(step, 2)

    @pl.when(step == 0)
    def _():
        fetch(0, 0)
        out_ref[...] = jnp.zeros_like(out_ref)
        back_ref[...] = jnp.zeros_like(back_ref)

    @pl.when(step + 1 < steps)
    def _():
        fetch(step + 1, 1 - buf)

    pltpu.make_async_copy(held.at[buf], held.at[buf], load_sem.at[buf]).wait()

    @pl.when(step >= 2)
    def _():
        drain(buf)

    normed = normed_ref[...]
    cot = cot_ref[...]
    w_gate = held[buf, 0].reshape(rows, width)
    w_up = held[buf, 1].reshape(rows, width)
    w_down = held[buf, 2].reshape(rows, width)
    nt = (((1,), (1,)), ((), ()))
    nn = (((1,), (0,)), ((), ()))
    tn = (((0,), (0,)), ((), ()))

    def dot(a, b, dims):
        return lax.dot_general(a, b, dims, preferred_element_type=jnp.float32)

    gate = dot(normed, w_gate, nt)
    up = dot(normed, w_up, nt)
    hidden = dot(cot, w_down, nt)
    sig = jax.nn.sigmoid(gate)
    silu = gate * sig
    act = (silu * up).astype(jnp.bfloat16)
    g_gate = (hidden * up * sig * (1.0 + gate * (1.0 - sig))).astype(jnp.bfloat16)
    g_up = (hidden * silu).astype(jnp.bfloat16)
    out_ref[...] += dot(act, w_down, nn)
    back_ref[...] += dot(g_gate, w_gate, nn) + dot(g_up, w_up, nn)
    made[buf, 0] = dot(g_gate, normed, tn).astype(jnp.bfloat16).reshape(group, tile_rows, width)
    made[buf, 1] = dot(g_up, normed, tn).astype(jnp.bfloat16).reshape(group, tile_rows, width)
    made[buf, 2] = dot(act, cot, tn).astype(jnp.bfloat16).reshape(group, tile_rows, width)
    for kind in range(3):
        @pl.loop(0, group, unroll=True)
        def _(t, kind=kind):
            pltpu.make_async_copy(made.at[buf, kind, t], grads_ref.at[tables[kind][step * group + t]], store_sem.at[buf]).start()

    @pl.when(step == steps - 1)
    def _():
        drain(1 - buf)
        drain(buf)

def ffn_call(gate_s, up_s, down_s, normed, cot, wall, group=16):
    tokens, width = normed.shape
    steps = gate_s.shape[0] // group
    tr = wall.shape[1]
    full = pl.BlockSpec((tokens, width), lambda i, *_: (0, 0))
    return pl.pallas_call(
        functools.partial(ffn_kernel, group),
        grid_spec=pltpu.PrefetchScalarGridSpec(
            num_scalar_prefetch=3, grid=(steps,),
            in_specs=[full, full, pl.BlockSpec(memory_space=pl.ANY)],
            out_specs=[full, full, pl.BlockSpec(memory_space=pl.ANY)],
            scratch_shapes=[pltpu.VMEM((2, 3, group, tr, width), jnp.bfloat16), pltpu.VMEM((2, 3, group, tr, width), jnp.bfloat16),
                pltpu.SemaphoreType.DMA((2,)), pltpu.SemaphoreType.DMA((2,))]),
        out_shape=[jax.ShapeDtypeStruct((tokens, width), jnp.float32), jax.ShapeDtypeStruct((tokens, width), jnp.float32), jax.ShapeDtypeStruct(wall.shape, jnp.bfloat16)],
        compiler_params=pltpu.CompilerParams(vmem_limit_bytes=56 << 20, dimension_semantics=("arbitrary",)),
        name="ffn",
    )(gate_s, up_s, down_s, normed, cot, wall)


MESH = pl.DeviceIdType.MESH
EVERY = slice(None)
GATHER_ROUTES = (
    ("z1", "z2", "z3", "x", "y", "core"),
    ("z1", "z2", "z3", "y", "x", "core"),
    ("x", "z1", "z2", "z3", "y", "core"),
    ("y", "z1", "z2", "z3", "x", "core"),
)


def position():
    dp = lax.axis_index("dp")
    return dp // 4, lax.rem(dp // 2, 2), lax.rem(dp, 2), lax.axis_index("fsdp")


def target(hop):
    y, x, c, z = position()
    if hop == "x":
        x = 1 - x
    elif hop == "y":
        y = 1 - y
    elif hop == "core":
        c = 1 - c
    elif hop == "back":
        z = lax.rem(z + 3, 4)
    else:
        z = lax.rem(z + 1, 4)
    return (y * 4 + x * 2 + c, z)


def enter(hops):
    barrier = pltpu.get_barrier_semaphore()
    for hop in hops:
        pl.semaphore_signal(barrier, inc=1, device_id=target(hop), device_id_type=MESH)
    pl.semaphore_wait(barrier, len(hops))


def split_slots(caps):
    small = caps // 6
    third = (caps - 2 * small) // 2
    counts = (small, small, third, caps - 2 * small - third)
    starts = (0, small, 2 * small, 2 * small + third)
    return counts, starts


GATHER_DELAYS = (0, 1, 0, 0)
SCATTER_DELAYS = (4, 4, 0, 0)


def round_count(counts, delays):
    return max(
        delay + (2 * count - 1 if route < 2 else count)
        for route, (count, delay) in enumerate(zip(counts, delays))
    )


def turn(route, at, counts, delays):
    at = at - delays[route]
    if route < 2:
        live = (at >= 0) & (lax.rem(at + 64, 2) == 0) & (at < 2 * counts[route])
        return live, at // 2
    return (at >= 0) & (at < counts[route]), at


def slot_of(route, index, counts, starts, lead, early):
    if route < 2:
        return 2 * lead + starts[route] + index
    here = 2 * lead + starts[route] - (route - 2) * lead
    count = counts[route]
    if early:
        later = (index + count - lead) // count
        return (route - 2) * lead + index + later * (here - route * lead + lead)
    final = index // (count - lead)
    return here + index - final * (here + count - lead - (route - 2) * lead)


def attend_side(side, q, k_pair, v_pair, mask, out_ref, logs):
    lane = lax.broadcasted_iota(jnp.int32, (q.shape[0], 128), 1)
    scale = jnp.bfloat16(1.0 / HEAD**0.5)
    k = k_pair[:, side * HEAD : (side + 1) * HEAD]
    v = v_pair[:, side * HEAD : (side + 1) * HEAD]
    for h in range(GROUP):
        cols = slice(h * HEAD, (h + 1) * HEAD)
        scores = jnp.where(mask, dot(q[:, cols] * scale, k, NT), masked_score)
        top = jnp.max(scores, axis=1, keepdims=True)
        raised = jnp.exp(scores - top)
        total = jnp.sum(raised, axis=1, keepdims=True)
        probs = (raised * (1.0 / total)).astype(jnp.bfloat16)
        out_ref[:, cols] = dot(probs, v, NN).astype(out_ref.dtype)
        logs = jnp.where(lane == side * GROUP + h, top + jnp.log(total), logs)
    return logs


GATHER_HOPS = ("z1", "z2", "z3")


def gather_kernel(
    lead,
    mine_ref,
    gain_ref,
    table,
    places,
    hidden_ref,
    cos_ref,
    sin_ref,
    wall_ref,
    gains_ref,
    weights_ref,
    both_ref,
    all_gains_ref,
    normed_ref,
    q_ref,
    att_ref,
    lse_ref,
    middle_ref,
    normed_two_ref,
    own_sem,
    send_sem,
    recv_sem,
    tiles,
    block,
    gain_tiles,
    keys,
    mask_ref,
    pair_ref,
    side_sem,
    hop_send,
    hop_recv,
):
    y, x, c, z = position()
    counts, starts = split_slots(mine_ref.shape[0])
    rounds = round_count(counts, GATHER_DELAYS)
    own = pltpu.make_async_copy(mine_ref, wall_ref.at[y, x, c, z], own_sem.at[0])
    own_gain = pltpu.make_async_copy(gain_ref, gains_ref.at[y, x, c, z], own_sem.at[1])
    own.start()
    own_gain.start()
    enter(("x", "y", "core", "z", "back"))
    own.wait()
    own_gain.wait()

    def region(route, stage):
        hops = GATHER_ROUTES[route % 4]
        hop = hops[stage]
        done = hops[:stage]
        at_y = EVERY if "y" in done else y
        at_x = EVERY if "x" in done else x
        at_z = EVERY if "z3" in done else z
        if hop in ("z1", "z2", "z3"):
            at_z = lax.rem(z + 5 - int(hop[1]), 4)
        return at_y, at_x, c, at_z

    def copy(route, stage, index):
        if route == 4:
            view = gains_ref.at[region(route, stage)]
        else:
            slot = slot_of(route, index, counts, starts, lead // 2, True)
            view = wall_ref.at[region(route, stage) + (slot,)]
        return pltpu.make_async_remote_copy(
            src_ref=view,
            dst_ref=view,
            send_sem=send_sem.at[route, stage],
            recv_sem=recv_sem.at[route, stage, index],
            device_id=target(GATHER_ROUTES[route % 4][stage]),
            device_id_type=MESH,
        )

    stages = len(GATHER_ROUTES[0])
    tokens, width = hidden_ref.shape
    number = block.shape[0]
    rows = number * block.shape[1]
    query_blocks = q_ref.shape[1] // rows
    key_blocks = keys.shape[1] // rows

    def take(at):
        @pl.loop(0, number, unroll=True)
        def _(t):
            block[t] = tiles[table[at * number + t]]

        pltpu.make_async_copy(
            block, weights_ref.at[pl.ds(at * number, number)], side_sem.at[1]
        ).start()
        return block[...].reshape(rows, width)

    def taken(at):
        pltpu.make_async_copy(
            block, weights_ref.at[pl.ds(at * number, number)], side_sem.at[1]
        ).wait()

    def load_tiles(d):
        return pltpu.make_async_copy(
            wall_ref.at[d // 16, lax.rem(d // 8, 2), lax.rem(d // 4, 2), lax.rem(d, 4), pl.ds(0, lead)],
            tiles.at[pl.ds(d * lead, lead)],
            side_sem.at[0],
        )

    load_gains = pltpu.make_async_copy(gains_ref, gain_tiles, side_sem.at[2])

    def pass_keys(part):
        hop = part // 2
        at = lax.rem(z + 4 - hop, 4)
        cols = KV_HEADS * HEAD
        view = keys.at[
            pl.ds(pl.multiple_of(at * tokens, tokens), tokens),
            pl.ds(part % 2 * cols, cols),
        ]
        return pltpu.make_async_remote_copy(
            src_ref=view,
            dst_ref=view,
            send_sem=hop_send.at[part],
            recv_sem=hop_recv.at[part],
            device_id=target(GATHER_HOPS[hop]),
            device_id_type=MESH,
        )

    def begin():
        @pl.loop(0, 32)
        def _(d):
            load_tiles(d).start()

        load_gains.start()

    def norm():
        load_gains.wait()
        lane = lax.broadcasted_iota(jnp.int32, (8, 128), 1)
        parts = []
        for d in range(0, 32, 2):
            even = gain_tiles[d // 16, (d // 8) % 2, (d // 4) % 2, d % 4].astype(jnp.float32)[:8]
            odd = gain_tiles[d // 16, (d // 8) % 2, (d // 4) % 2, d % 4 + 1].astype(jnp.float32)[:8]
            parts.append(jnp.where(lane < 64, even, pltpu.roll(odd, 64, 1)))
        all_gains_ref[...] = jnp.concatenate(parts, axis=1)
        hidden = hidden_ref[...].astype(jnp.float32)
        inv = lax.rsqrt(jnp.mean(hidden * hidden, axis=1, keepdims=True) + norm_eps)
        normed_ref[...] = (hidden * inv * all_gains_ref[0:1, :]).astype(normed_ref.dtype)
        fill_mask(places, mask_ref)

    def project_keys():
        pltpu.make_async_copy(tiles, tiles, side_sem.at[0]).wait()
        own_rows = pl.ds(pl.multiple_of(z * tokens, tokens), tokens)

        for b in range(key_blocks):
            at = query_blocks + b
            u = dot(normed_ref[...], take(at), NT)
            if b < key_blocks // 2:
                u = u * cos_ref[...] + swap_halves(u) * sin_ref[...]
            keys[own_rows, b * rows : (b + 1) * rows] = u.astype(keys.dtype)
            taken(at)

    def project_queries(low, high):
        @pl.loop(low, high)
        def _(b):
            u = dot(normed_ref[...], take(b), NT)
            u = u * cos_ref[...] + swap_halves(u) * sin_ref[...]
            q_ref[:, pl.ds(pl.multiple_of(b * rows, rows), rows)] = u.astype(q_ref.dtype)
            taken(b)

    def attend_step(pair, side):
        wide = GROUP * HEAD
        narrow = PAIR * HEAD
        here = pl.ds(pl.multiple_of((pair * PAIR + side) * wide, wide), wide)
        k_pair = keys[:, pl.ds(pl.multiple_of(pair * narrow, narrow), narrow)]
        v_pair = keys[:, pl.ds(pl.multiple_of(KV_HEADS * HEAD + pair * narrow, narrow), narrow)]
        logs = lse_ref[pair] if side else jnp.zeros((tokens, 128), jnp.float32)
        mask = mask_ref[...] > 0.5
        lse_ref[pair] = attend_side(side, q_ref[:, here], k_pair, v_pair, mask, pair_ref, logs)
        att_ref[:, here] = pair_ref[...]

    def mix_blocks(low):
        for more in range(4):
            b = low + more
            at = query_blocks + key_blocks + b
            left = att_ref[:, pl.ds(pl.multiple_of(b * rows, rows), rows)]
            middle_ref[...] += dot(left, take(at), NN)
            taken(at)

    def mix_end():
        middle = middle_ref[...]
        inv = lax.rsqrt(jnp.mean(middle * middle, axis=1, keepdims=True) + norm_eps)
        normed_two_ref[...] = (middle * inv * all_gains_ref[1:2, :]).astype(normed_two_ref.dtype)

    start = GATHER_DELAYS[3] + lead // 2 - 1 + stages
    keep_both = pltpu.make_async_copy(keys, both_ref, side_sem.at[3])

    @pl.loop(0, rounds + stages)
    def _(t):
        for stage in range(stages + 1):
            for route in range(5):
                if route == 4:
                    live, index = t == stage, 0
                else:
                    live, index = turn(route, t - stage, counts, GATHER_DELAYS)

                @pl.when(live)
                def _(stage=stage, route=route, index=index):
                    if stage > 0:
                        copy(route, stage - 1, index).wait()
                    if stage < stages:
                        copy(route, stage, index).start()

        @pl.when(t == start)
        def _():
            begin()
            norm()

        @pl.when(t == start + 1)
        def _():
            project_keys()

        parts = 2 * len(GATHER_HOPS)
        for part in range(parts + 1):

            @pl.when(t == start + 1 + part)
            def _(part=part):
                if part > 0:
                    pass_keys(part - 1).wait()
                if part < parts:
                    pass_keys(part).start()

        for third in range(4):

            @pl.when(t == start + 2 + third)
            def _(third=third):
                project_queries(third * query_blocks // 4, (third + 1) * query_blocks // 4)

        attending = start + 1 + parts

        @pl.when(t == attending)
        def _():
            keep_both.start()
            middle_ref[...] = hidden_ref[...].astype(jnp.float32)

        for side in range(PAIR):
            since = t - attending

            @pl.when((since >= 0) & (since < KV_HEADS) & (lax.rem(since + 64, 2) == side))
            def _(side=side, since=since):
                attend_step(since // 2, side)

        mixing = attending + KV_HEADS

        @pl.when((t >= mixing) & (t < mixing + query_blocks // 4))
        def _():
            mix_blocks((t - mixing) * 4)

        @pl.when(t == mixing + query_blocks // 4)
        def _():
            mix_end()
            keep_both.wait()


def gather_slots(low_tiles, low_gains, table, places, hidden, cosine, sine, lead):
    caps, rows, width = low_tiles.shape
    tokens = hidden.shape[0]
    length = tokens * 4
    counts, starts = split_slots(caps)
    kind = low_tiles.dtype
    vmem = pl.BlockSpec(memory_space=pltpu.VMEM)
    smem = pl.BlockSpec(memory_space=pltpu.SMEM)
    anyw = pl.BlockSpec(memory_space=pl.ANY)
    padded = jnp.pad(low_gains, ((0, 16 - low_gains.shape[0]), (0, 128 - low_gains.shape[1])))
    number = cosine.shape[1] // rows
    pairs = KV_HEADS // PAIR
    outs = pl.pallas_call(
        functools.partial(gather_kernel, lead),
        out_shape=[
            jax.ShapeDtypeStruct((2, 2, 2, 4, caps, rows, width), kind),
            jax.ShapeDtypeStruct((2, 2, 2, 4) + padded.shape, kind),
            jax.ShapeDtypeStruct((table.shape[0], rows, width), kind),
            jax.ShapeDtypeStruct((length, 2 * KV_HEADS * HEAD), kind),
            jax.ShapeDtypeStruct((8, width), jnp.float32),
            jax.ShapeDtypeStruct((tokens, width), kind),
            jax.ShapeDtypeStruct((tokens, width), kind),
            jax.ShapeDtypeStruct((tokens, width), kind),
            jax.ShapeDtypeStruct((pairs, tokens, 128), jnp.float32),
            jax.ShapeDtypeStruct((tokens, width), jnp.float32),
            jax.ShapeDtypeStruct((tokens, width), kind),
        ],
        in_specs=[vmem, vmem, smem, smem, vmem, vmem, vmem],
        out_specs=[anyw] * 4 + [vmem] * 7,
        scratch_shapes=[
            pltpu.SemaphoreType.DMA((2,)),
            pltpu.SemaphoreType.DMA((5, 6)),
            pltpu.SemaphoreType.DMA((5, 6, max(counts))),
            pltpu.VMEM((32 * lead, rows, width), kind),
            pltpu.VMEM((number, rows, width), kind),
            pltpu.VMEM((2, 2, 2, 4) + padded.shape, kind),
            pltpu.VMEM((length, 2 * KV_HEADS * HEAD), kind),
            pltpu.VMEM((tokens, length), jnp.float32),
            pltpu.VMEM((tokens, GROUP * HEAD), kind),
            pltpu.SemaphoreType.DMA((4,)),
            pltpu.SemaphoreType.DMA((6,)),
            pltpu.SemaphoreType.DMA((6,)),
        ],
        compiler_params=pltpu.CompilerParams(
            collective_id=0, has_side_effects=True, vmem_limit_bytes=62 << 20
        ),
        name="gather_slots",
    )(low_tiles, padded, table, places, hidden, cosine, sine)
    return [outs[0].reshape(32 * caps, rows, width)] + list(outs[2:])


SCATTER_ROUTES = (
    ("core", "y", "x", "z1", "z2", "z3", "end"),
    ("core", "x", "y", "z1", "z2", "z3", "end"),
    ("core", "y", "z1", "z2", "z3", "x", "end"),
    ("core", "x", "z1", "z2", "z3", "y", "end"),
)


SUM_HOPS = ("core", "x", "y", "z1", "z2", "z3")
SUM_START = 2


def scatter_extent(route, stage):
    hops = SCATTER_ROUTES[route]
    done = hops[1 : stage + 1] if hops[stage] in ("x", "y") else hops[1:stage]
    extent = []
    if "x" not in done or "y" not in done:
        extent.append(2)
    if not any(hop[0] == "z" for hop in hops[: stage + 1]):
        extent.append(4)
    return tuple(extent)


def scatter_terms(route, stage):
    hops = SCATTER_ROUTES[route]
    done = hops[1:stage]
    return 2 + ("x" in done) + ("y" in done) + ("z1" in done)


def attend_back_side(side, q, k_pair, v_pair, grad, mask, logs, turn_ref, k_out, v_out):
    scale = jnp.bfloat16(1.0 / HEAD**0.5)
    here = slice(side * HEAD, (side + 1) * HEAD)
    k = k_pair[:, here]
    v = v_pair[:, here]
    dk = None
    dv = None
    for h in range(GROUP):
        cols = slice(h * HEAD, (h + 1) * HEAD)
        head = side * GROUP + h
        q_head = q[:, cols] * scale
        scores = jnp.where(mask, dot(q_head, k, NT), masked_score)
        probs = jnp.exp(scores - logs[:, head : head + 1])
        grad_probs = dot(grad[:, cols], v, NT)
        row_dot = jnp.sum(probs * grad_probs, axis=1, keepdims=True)
        grad_scores = (probs * (grad_probs - row_dot)).astype(jnp.bfloat16)
        turn_ref[:, cols] = dot(grad_scores, k, NN) * (1.0 / HEAD**0.5)
        dk_part = dot(q_head, grad_scores, TN)
        dv_part = dot(grad[:, cols], probs.astype(jnp.bfloat16), TN)
        dk = dk_part if dk is None else dk + dk_part
        dv = dv_part if dv is None else dv + dv_part
    k_out[:, here] = dk.T.astype(k_out.dtype)
    v_out[:, here] = dv.T.astype(v_out.dtype)


def scatter_kernel(
    look,
    lead,
    first_group,
    old_ref,
    gain_ref,
    weights_ref,
    table,
    places,
    branch_ref,
    att_ref,
    q_ref,
    both_ref,
    lse_ref,
    normed_ref,
    hidden_ref,
    cos_ref,
    sin_ref,
    wall_ref,
    out_ref,
    total_ref,
    back_ref,
    core_ref,
    first_ref,
    second_ref,
    ring_ref,
    last_ref,
    *scratch,
):
    y, x, c, z = position()
    caps, rows, width = out_ref.shape
    counts, starts = split_slots(caps)
    rounds = round_count(counts, SCATTER_DELAYS)
    stages = len(SCATTER_ROUTES[0])
    held = {}
    made = {}
    scratch = list(scratch)
    for route in range(4):
        for stage in range(1, stages):
            held[route, stage] = scratch.pop(0)
            made[route, stage] = scratch.pop(0)
    load_sem, send_sem, recv_sem, out_sem, sums, landed, sum_send, sum_recv = scratch[:8]
    (
        streamed,
        grad_att,
        grad_q,
        grad_kv,
        grad_both,
        k_pair_ref,
        v_pair_ref,
        turn_ref,
        hop_out,
        hop_in,
        turned,
        left_ref,
        built,
        mask_ref,
        stream_sem,
        hop_send,
        hop_recv,
        built_sem,
    ) = scratch[8:]
    enter(("x", "y", "core", "z", "back"))

    def landing(route, stage, slot):
        hops = SCATTER_ROUTES[route]
        hop = hops[stage]
        if hop == "core":
            return core_ref.at[:, :, :, slot]
        if hop[0] == "z":
            ring = ring_ref.at[int(hop[1]) - 1]
            return ring.at[0, slot] if route < 2 else ring.at[:, slot]
        if stage == 1:
            return first_ref.at[:, :, slot]
        if stage == 2:
            return second_ref.at[:, slot]
        return last_ref.at[slot]

    def terms(route, stage, slot):
        hops = SCATTER_ROUTES[route]
        hop = hops[stage]
        done = hops[1:stage]
        at_y = 1 - y if hop == "y" else (y if "y" in done else EVERY)
        at_x = 1 - x if hop == "x" else (x if "x" in done else EVERY)
        at_z = EVERY
        if hop[0] == "z":
            at_z = lax.rem(z + 4 - int(hop[1]), 4)
        elif "z3" in done:
            at_z = z
        views = [wall_ref.at[at_y, at_x, c, at_z, slot], core_ref.at[at_y, at_x, at_z, slot]]
        other = at_x if hops[1] == "y" else at_y
        if stage > 1:
            views.append(first_ref.at[other, at_z, slot])
        if route < 2 and stage > 2:
            views.append(second_ref.at[at_z, slot])
        if hop in ("z2", "z3"):
            ring = ring_ref.at[int(hop[1]) - 2]
            views.append(ring.at[0, slot] if route < 2 else ring.at[:, slot])
        elif "z3" in done:
            ring = ring_ref.at[2]
            views.append(ring.at[0, slot] if route < 2 else ring.at[other, slot])
        if route >= 2 and hop == "end":
            views.append(last_ref.at[slot])
        return views

    def slot_at(route, index):
        return slot_of(route, index, counts, starts, lead // 2, False)

    def send(route, stage, index):
        slot = slot_at(route, index)
        if stage == 0:
            source = wall_ref.at[:, :, 1 - c, :, slot]
        else:
            source = made[route, stage]
        return pltpu.make_async_remote_copy(
            src_ref=source,
            dst_ref=landing(route, stage, slot),
            send_sem=send_sem.at[route, stage],
            recv_sem=recv_sem.at[route, stage, index],
            device_id=target(SCATTER_ROUTES[route][stage]),
            device_id_type=MESH,
        )

    def keep(route, index):
        return pltpu.make_async_copy(
            made[route, stages - 1], out_ref.at[slot_at(route, index)], out_sem.at[route]
        )

    def early(route, stage, index):
        if stage > 0:
            for k, view in enumerate(terms(route, stage, slot_at(route, index))[:-1]):
                pltpu.make_async_copy(view, held[route, stage].at[k], load_sem.at[route, stage]).start()

    def late(route, stage, index):
        if stage > 0:
            send(route, stage - 1, index).wait()
            view = terms(route, stage, slot_at(route, index))[-1]
            last = held[route, stage].shape[0] - 1
            pltpu.make_async_copy(view, held[route, stage].at[last], load_sem.at[route, stage]).start()

    def finish(route, stage, index):
        if stage > 0:
            buf = held[route, stage]
            pltpu.make_async_copy(buf, buf, load_sem.at[route, stage]).wait()
            number = buf.shape[0]
            extent = buf.shape[1:-2]
            blocks = 1
            for size in extent:
                blocks *= size
            part = min(width, 512)
            if stage == stages - 1:

                @pl.when(index > 0)
                def _():
                    keep(route, index - 1).wait()

            @pl.loop(0, blocks)
            def _(block):
                if len(extent) == 2:
                    at = (block // extent[1], lax.rem(block, extent[1]))
                elif len(extent) == 1:
                    at = (block,)
                else:
                    at = ()
                for left in range(0, width, part):
                    cols = pl.ds(left, part)
                    total = buf[(0,) + at + (EVERY, cols)].astype(jnp.float32)
                    for k in range(1, number):
                        total += buf[(k,) + at + (EVERY, cols)].astype(jnp.float32)
                    made[route, stage][at + (EVERY, cols)] = total.astype(made[route, stage].dtype)

        if stage < stages - 1:
            send(route, stage, index).start()
        else:
            keep(route, index).start()

    def pass_sum(hop):
        return pltpu.make_async_remote_copy(
            src_ref=sums.at[hop] if hop < 4 else landed.at[hop - 1],
            dst_ref=landed.at[hop],
            send_sem=sum_send.at[hop],
            recv_sem=sum_recv.at[hop],
            device_id=target(SUM_HOPS[hop]),
            device_id_type=MESH,
        )

    def add_sums(step):
        if step > 0:
            pass_sum(step - 1).wait()
        if step == 0:
            hidden = hidden_ref[...].astype(jnp.float32)
            inv = lax.rsqrt(jnp.mean(hidden * hidden, axis=1, keepdims=True) + norm_eps)
            term = jnp.sum(back_ref[...] * hidden * inv, axis=0, keepdims=True)
            line = lax.broadcasted_iota(jnp.int32, gain_ref.shape, 0)
            sums[0] = jnp.where(line == 0, term, gain_ref[...])
        elif step < 4:
            sums[step] = sums[step - 1] + landed[step - 1]
        elif step == len(SUM_HOPS):
            total_ref[...] = (sums[3] + landed[3]) + (landed[4] + landed[5])
        if step < len(SUM_HOPS):
            pass_sum(step).start()

    tokens = hidden_ref.shape[0]
    number = cos_ref.shape[1] // rows
    block = number * rows
    query_blocks = q_ref.shape[1] // block
    key_blocks = both_ref.shape[1] // block
    out_blocks = att_ref.shape[1] // block
    all_blocks = query_blocks + key_blocks + out_blocks
    kv_width = KV_HEADS * HEAD

    def stream(n):
        at = lax.rem(n + query_blocks + key_blocks, all_blocks)
        return pltpu.make_async_copy(
            weights_ref.at[pl.ds(at * number, number)],
            streamed.at[lax.rem(n, 2)],
            stream_sem.at[lax.rem(n, 2)],
        )

    def streamed_block(n):
        stream(n).wait()

        @pl.when(n + 1 < all_blocks)
        def _():
            stream(n + 1).start()

        return streamed[lax.rem(n, 2)].reshape(block, width)

    def column(b):
        return pl.ds(pl.multiple_of(b * block, block), block)

    def turn_tiles(at, value):
        flipped = value.astype(jnp.float32).T.astype(turned.dtype)
        turned[pl.ds(at * number, number)] = flipped.reshape(number, rows, tokens)

    def out_back(low, high):
        @pl.loop(low, high)
        def _(b):
            grad_att[:, column(b)] = dot(branch_ref[...], streamed_block(b), NT).astype(
                grad_att.dtype
            )
            turn_tiles(query_blocks + key_blocks + b, att_ref[:, column(b)])

    def query_back(low, high):
        @pl.loop(low, high)
        def _(b):
            left = grad_q[:, column(b)]
            back_ref[...] += dot(left, streamed_block(out_blocks + b), NN)
            turn_tiles(b, left)

    def key_back():
        @pl.loop(0, key_blocks)
        def _(b):
            left = grad_both[:, column(b)]
            back_ref[...] += dot(left, streamed_block(out_blocks + query_blocks + b), NN)
            turn_tiles(query_blocks + b, left)

    def attend_back_step(pair, side):
        wide = GROUP * HEAD
        narrow = PAIR * HEAD
        here = pl.ds(pl.multiple_of((pair * PAIR + side) * wide, wide), wide)
        k_cols = pl.ds(pl.multiple_of(pair * narrow, narrow), narrow)
        v_cols = pl.ds(pl.multiple_of(kv_width + pair * narrow, narrow), narrow)
        attend_back_side(
            side,
            q_ref[:, here],
            both_ref[:, k_cols],
            both_ref[:, v_cols],
            grad_att[:, here],
            mask_ref[...] > 0.5,
            lse_ref[pair],
            turn_ref,
            k_pair_ref,
            v_pair_ref,
        )
        u = turn_ref[...]
        grad_q[:, here] = (u * cos_ref[...] - swap_halves(u) * sin_ref[...]).astype(grad_q.dtype)
        if side == PAIR - 1:
            grad_kv[:, k_cols] = k_pair_ref[...]
            grad_kv[:, v_cols] = v_pair_ref[...]

    def key_rows(far):
        at = lax.rem(z + 4 - far, 4)
        return pl.ds(pl.multiple_of(at * tokens, tokens), tokens)

    def pass_terms(hop):
        return pltpu.make_async_remote_copy(
            src_ref=hop_out.at[hop],
            dst_ref=hop_in.at[hop],
            send_sem=hop_send.at[hop],
            recv_sem=hop_recv.at[hop],
            device_id=target("z1"),
            device_id_type=MESH,
        )

    def key_terms(hop):
        if hop > 0:
            pass_terms(hop - 1).wait()
        if hop < 3:
            own = grad_kv[key_rows(hop + 1), :]
            if hop > 0:
                own = (own.astype(jnp.float32) + hop_in[hop - 1].astype(jnp.float32)).astype(own.dtype)
            hop_out[hop] = own
            pass_terms(hop).start()
        else:
            own = grad_kv[key_rows(0), :].astype(jnp.float32) + hop_in[2].astype(jnp.float32)
            for b in range(key_blocks):
                u = own[:, b * block : (b + 1) * block]
                if b < key_blocks // 2:
                    u = u * cos_ref[...] - swap_halves(u) * sin_ref[...]
                grad_both[:, b * block : (b + 1) * block] = u.astype(grad_both.dtype)

    def built_copy(which, j, d):
        return pltpu.make_async_copy(
            built.at[which, d],
            wall_ref.at[d // 16, lax.rem(d // 8, 2), lax.rem(d // 4, 2), lax.rem(d, 4), j],
            built_sem.at[which],
        )

    def build(which, j, right_ref):
        @pl.loop(0, 32, unroll=True)
        def _(d):
            left_ref[d] = turned[table[d * lead + j]]

        for part in range(4):
            left = left_ref[part * 8 : (part + 1) * 8].reshape(8 * rows, tokens)
            value = dot(left, right_ref[...], NN).astype(built.dtype)
            built[which, part * 8 : (part + 1) * 8] = value.reshape(8, rows, width)

        @pl.loop(0, 32)
        def _(d):
            built_copy(which, j, d).start()

    def finish_built(which):
        pltpu.make_async_copy(built.at[which], built.at[which], built_sem.at[which]).wait()

    half = lead // 2
    attending = 2
    passing = attending + KV_HEADS
    building = passing + 5
    stream(0).start()

    @pl.loop(0, rounds + stages - 1)
    def _(t):
        for step in range(2):

            @pl.when(t == step)
            def _(step=step):
                if step == 0:
                    fill_mask(places, mask_ref)
                    back_ref[...] = jnp.zeros_like(back_ref)
                out_back(step * out_blocks // 2, (step + 1) * out_blocks // 2)

        for side in range(PAIR):
            since = t - attending

            @pl.when((since >= 0) & (since < KV_HEADS) & (lax.rem(since + 64, 2) == side))
            def _(side=side, since=since):
                attend_back_step(since // 2, side)

        for hop in range(4):

            @pl.when(t == passing + hop)
            def _(hop=hop):
                key_terms(hop)
                query_back(hop * query_blocks // 4, (hop + 1) * query_blocks // 4)

        @pl.when(t == passing + 4)
        def _():
            key_back()

        pair = t - building

        @pl.when((pair >= 1) & (pair <= half))
        def _():
            finish_built(0)
            finish_built(1)

        @pl.when((pair >= 0) & (pair < half))
        def _():
            build(0, pair, normed_ref)

        split = first_group - half

        @pl.when((pair >= 0) & (pair < split))
        def _():
            build(1, half + pair, normed_ref)

        @pl.when((pair >= split) & (pair < half))
        def _():
            build(1, half + pair, branch_ref)

        for step in range(len(SUM_HOPS) + 1):

            @pl.when(t == building + step)
            def _(step=step):
                add_sums(step)

        items = [(stage, route) for stage in range(stages - 1, -1, -1) for route in range(4)]

        def run(which, work):
            stage, route = items[which]
            live, index = turn(route, t - stage, counts, SCATTER_DELAYS)

            @pl.when(live)
            def _():
                work(route, stage, index)

        far, near = look
        for which in range(len(items) + far):
            if which < len(items):
                run(which, early)
            if far - near <= which < len(items) + far - near:
                run(which - far + near, late)
            if which >= far:
                run(which - far, finish)

    for route in range(4):
        keep(route, counts[route] - 1).wait()


def scatter_slots(
    grads_wall,
    gain_terms,
    weights,
    table,
    places,
    branch,
    attended,
    queries,
    both,
    lse,
    normed,
    hidden,
    cosine,
    sine,
    lead,
    first_group,
    caps,
    look=(4, 1),
):
    rows, width = grads_wall.shape[1:]
    kind = grads_wall.dtype
    wall = grads_wall.reshape(2, 2, 2, 4, caps, rows, width)
    counts, starts = split_slots(caps)
    stages = len(SCATTER_ROUTES[0])
    scratch = []
    for route in range(4):
        for stage in range(1, stages):
            extent = scatter_extent(route, stage)
            scratch.append(pltpu.VMEM((scatter_terms(route, stage),) + extent + (rows, width), kind))
            last = stage == stages - 1
            scratch.append(pltpu.VMEM(extent + (rows, width), jnp.float32 if last else kind))
    tile = (caps, rows, width)
    tokens = hidden.shape[0]
    number = cosine.shape[1] // rows
    length, both_width = both.shape
    dma = pltpu.SemaphoreType.DMA
    scratch += [
        dma((4, stages)),
        dma((4, stages)),
        dma((4, stages, max(counts))),
        dma((4,)),
        pltpu.VMEM((4,) + gain_terms.shape, jnp.float32),
        pltpu.VMEM((6,) + gain_terms.shape, jnp.float32),
        dma((6,)),
        dma((6,)),
        pltpu.VMEM((2, number, rows, width), kind),
        pltpu.VMEM((tokens, width), kind),
        pltpu.VMEM((tokens, width), kind),
        pltpu.VMEM((length, both_width), kind),
        pltpu.VMEM((tokens, both_width), kind),
        pltpu.VMEM((length, PAIR * HEAD), kind),
        pltpu.VMEM((length, PAIR * HEAD), kind),
        pltpu.VMEM((tokens, GROUP * HEAD), jnp.float32),
        pltpu.VMEM((3, tokens, both_width), kind),
        pltpu.VMEM((3, tokens, both_width), kind),
        pltpu.VMEM((weights.shape[0], rows, tokens), kind),
        pltpu.VMEM((32, rows, tokens), kind),
        pltpu.VMEM((2, 32, rows, width), kind),
        pltpu.VMEM((tokens, length), jnp.float32),
        dma((2,)),
        dma((3,)),
        dma((3,)),
        dma((2,)),
    ]
    vmem = pl.BlockSpec(memory_space=pltpu.VMEM)
    smem = pl.BlockSpec(memory_space=pltpu.SMEM)
    anyw = pl.BlockSpec(memory_space=pl.ANY)
    out = pl.pallas_call(
        functools.partial(scatter_kernel, look, lead, first_group),
        out_shape=[
            jax.ShapeDtypeStruct(wall.shape, kind),
            jax.ShapeDtypeStruct(tile, jnp.float32),
            jax.ShapeDtypeStruct(gain_terms.shape, jnp.float32),
            jax.ShapeDtypeStruct((tokens, width), jnp.float32),
            jax.ShapeDtypeStruct((2, 2, 4) + tile, kind),
            jax.ShapeDtypeStruct((2, 4) + tile, kind),
            jax.ShapeDtypeStruct((4,) + tile, kind),
            jax.ShapeDtypeStruct((3, 2) + tile, kind),
            jax.ShapeDtypeStruct(tile, kind),
        ],
        in_specs=[anyw, vmem, anyw, smem, smem] + [vmem] * 9,
        out_specs=[anyw, anyw, vmem, vmem] + [anyw] * 5,
        scratch_shapes=scratch,
        input_output_aliases={0: 0},
        compiler_params=pltpu.CompilerParams(
            collective_id=1, has_side_effects=True, vmem_limit_bytes=62 << 20
        ),
        name="scatter_slots",
    )(
        wall, gain_terms, weights, table, places, branch, attended, queries, both, lse, normed,
        hidden, cosine, sine,
    )
    return out[1], out[2], out[3]


def shards(
    hidden_in,
    piece_starts,
    out_cotangent,
    owners,
    master,
    moment_one,
    moment_two,
    gain_master,
    gain_one,
    gain_two,
):
    devices = lax.axis_size("dp") * lax.axis_size("fsdp")
    caps, tile_rows, model_width = master.shape
    layout = section_layout(devices, tile_rows)
    slot_qkv, slot_out, slot_ffn, slot_down = slot_numbers(owners, layout, caps)
    query_tiles = model_width // tile_rows
    slot_query, slot_both = slot_qkv[:query_tiles], slot_qkv[query_tiles:]
    half = slot_ffn.shape[0] // 2
    lead = layout[2][3]
    tokens = hidden_in.astype(jnp.float32)
    local_len = tokens.shape[0]
    first = lax.axis_index("fsdp") * local_len
    positions = first + jnp.arange(local_len, dtype=jnp.int32)
    places = jnp.concatenate([first[None].astype(jnp.int32), piece_starts[0]])
    cosine, sine = rope_tables(positions.astype(jnp.float32), 16 * tile_rows)
    (
        wall, weights, gains_low, both, normed, queries, attended, lse, middle, normed_two
    ) = forward_attention(
        master.astype(jnp.bfloat16),
        gain_master.astype(jnp.bfloat16),
        (slot_query, slot_both, slot_out),
        places,
        hidden_in,
        cosine,
        sine,
        lead,
    )
    gain_attn = gains_low[0]
    gain_ffn = gains_low[1]
    inv_one = lax.rsqrt(jnp.mean(tokens * tokens, axis=1, keepdims=True) + norm_eps)
    inv_two = lax.rsqrt(jnp.mean(middle * middle, axis=1, keepdims=True) + norm_eps)
    ffn_out, grad_normed_two, grads_wall = ffn_call(
        slot_ffn[:half], slot_ffn[half:], slot_down, normed_two, out_cotangent, wall
    )
    block_out = (middle + ffn_out).astype(jnp.bfloat16)
    scaled_two = grad_normed_two * gain_ffn
    grad_middle = (
        out_cotangent.astype(jnp.float32)
        + inv_two * scaled_two
        - middle * inv_two**3 * jnp.mean(scaled_two * middle, axis=1, keepdims=True)
    )
    gain_two_term = jnp.sum(grad_normed_two * middle * inv_two, axis=0)
    grad_branch = grad_middle.astype(jnp.bfloat16)
    weight_grad, gain_grad, grad_normed = backward_attention(
        grads_wall,
        gain_two_term,
        weights,
        (slot_query, slot_both, slot_out),
        places,
        grad_branch,
        attended,
        queries,
        both,
        lse,
        normed,
        hidden_in,
        cosine,
        sine,
        layout,
        caps,
    )
    keep_slot = filled_mask(owners, layout, lax.axis_index(("dp", "fsdp")))[:, None, None]
    weight_grad = jnp.where(keep_slot, weight_grad, 0.0)
    scaled_one = grad_normed * gain_attn
    input_grad = (
        grad_middle
        + inv_one * scaled_one
        - tokens * inv_one**3 * jnp.mean(scaled_one * tokens, axis=1, keepdims=True)
    )
    step = float(STEP)
    new_one, new_two, new_weights = adam_step(
        master, moment_one, moment_two, weight_grad, step, decay_rate, learn_rate
    )
    new_one = jnp.where(keep_slot, new_one, 0.0)
    new_two = jnp.where(keep_slot, new_two, 0.0)
    new_weights = jnp.where(keep_slot, new_weights, 0.0)
    new_gain_one, new_gain_two, new_gains = adam_step(
        gain_master, gain_one, gain_two, gain_grad, step, 0.0, gain_rate
    )
    return (
        block_out,
        input_grad,
        weight_grad,
        new_weights,
        new_one,
        new_two,
        gain_grad,
        new_gains,
        new_gain_one,
        new_gain_two,
    )


def solution(mesh):
    return jax.shard_map(
        shards,
        mesh=mesh,
        in_specs=(
            P(("dp", "fsdp"), None),
            P("dp", None),
            P(("dp", "fsdp"), None),
            P(),
            P(("dp", "fsdp"), None, None),
            P(("dp", "fsdp"), None, None),
            P(("dp", "fsdp"), None, None),
            P(None, ("dp", "fsdp")),
            P(None, ("dp", "fsdp")),
            P(None, ("dp", "fsdp")),
        ),
        out_specs=(
            P(("dp", "fsdp"), None),
            P(("dp", "fsdp"), None),
            P(("dp", "fsdp"), None, None),
            P(("dp", "fsdp"), None, None),
            P(("dp", "fsdp"), None, None),
            P(("dp", "fsdp"), None, None),
            P(None, ("dp", "fsdp")),
            P(None, ("dp", "fsdp")),
            P(None, ("dp", "fsdp")),
            P(None, ("dp", "fsdp")),
        ),
        check_vma=False,
    )
```

```python
import functools

import jax
import jax.experimental.pallas as pl
import jax.experimental.pallas.tpu as pltpu
import jax.numpy as jnp
from jax import lax
from jax.sharding import PartitionSpec as P

D = 2048
HEADS = 32
KV_HEADS = 8
HEAD = 64
FF = 8192
PIECE = 256
STEP = 5


norm_eps = 1e-05
adam_eps = 1e-08
beta_one = 0.5
beta_two = 0.5
learn_rate = 0.02
gain_rate = 0.3
decay_rate = 0.1
rope_base = 500000.0
masked_score = -1e30


def section_layout(devices, tile_rows):
    counts = [
        (D + 2 * KV_HEADS * HEAD) // tile_rows,
        HEADS * HEAD // tile_rows,
        2 * FF // tile_rows,
        FF // tile_rows,
    ]
    layout = []
    first_tile = 0
    first_slot = 0
    for number in counts:
        capacity = 5 * number // (4 * devices) + 1
        layout.append((first_tile, number, capacity, first_slot))
        first_tile += number
        first_slot += capacity
    return layout


def adam_step(weights, first_moment, second_moment, grads, step, decay, rate):
    new_one = beta_one * first_moment + (1.0 - beta_one) * grads
    new_two = beta_two * second_moment + (1.0 - beta_two) * grads * grads
    correct_one = 1.0 - beta_one**step
    correct_two = 1.0 - beta_two**step
    update = -rate * (
        new_one / correct_one / (jnp.sqrt(new_two / correct_two) + adam_eps) + decay * weights
    )
    return (new_one, new_two, weights + update)


def slot_numbers(owners, layout, caps):
    placed = []
    for first_tile, number, capacity, first_slot in layout:
        mine = owners[first_tile : first_tile + number]
        order = jnp.arange(number, dtype=jnp.int32)
        earlier = (mine[:, None] == mine[None, :]) & (order[None, :] < order[:, None])
        ranked = jnp.sum(earlier.astype(jnp.int32), axis=1)
        placed.append(mine * caps + first_slot + ranked)
    return placed


def filled_mask(owners, layout, device):
    masks = []
    for first_tile, number, capacity, first_slot in layout:
        count = jnp.sum((owners[first_tile : first_tile + number] == device).astype(jnp.int32))
        masks.append(jnp.arange(capacity, dtype=jnp.int32) < count)
    return jnp.concatenate(masks)


def rope_tables(positions, block):
    half_dim = HEAD // 2
    inverse = rope_base ** (-(jnp.arange(half_dim, dtype=jnp.float32) * 2.0 / HEAD))
    angles = positions[:, None] * inverse[None, :]
    cosine = jnp.cos(angles)
    sine = jnp.sin(angles)
    return (
        jnp.tile(jnp.concatenate([cosine, cosine], axis=1), (1, block // HEAD)),
        jnp.tile(jnp.concatenate([-sine, sine], axis=1), (1, block // HEAD)),
    )


def turn_back(grads, cosine, sine):
    tokens, width = grads.shape
    half_dim = HEAD // 2
    heads = grads.reshape(tokens, width // HEAD, 2, half_dim)
    swapped = heads[:, :, ::-1].reshape(tokens, width)
    times = width // cosine.shape[1]
    return grads * jnp.tile(cosine, (1, times)) - swapped * jnp.tile(sine, (1, times))


def tuned_mesh():
    return (lax.axis_size("dp"), lax.axis_size("fsdp")) == (8, 4)


def forward_attention(low_tiles, low_gains, slots, places, hidden_in, cosine, sine, lead):
    caps, tile_rows, width = low_tiles.shape
    slot_query, slot_both, slot_out = slots
    if tuned_mesh():
        table = jnp.concatenate(slots)
        table = table // caps * lead + lax.rem(table, caps)
        (wall, weights, both, gains, normed, queries, attended, lse, middle, normed_two) = (
            gather_slots(low_tiles, low_gains, table, places, hidden_in, cosine, sine, lead)
        )
        return wall, weights, gains, both, normed, queries, attended, lse, middle, normed_two
    wall = lax.all_gather(low_tiles, ("dp", "fsdp"), axis=0, tiled=True)
    gains = lax.all_gather(low_gains, ("dp", "fsdp"), axis=1, tiled=True).astype(jnp.float32)
    tokens = hidden_in.astype(jnp.float32)
    inv_one = lax.rsqrt(jnp.mean(tokens * tokens, axis=1, keepdims=True) + norm_eps)
    normed = (tokens * inv_one * gains[0]).astype(jnp.bfloat16)
    turned = KV_HEADS * HEAD // cosine.shape[1]
    both_local = project(slot_both, normed, cosine, sine, wall, turned=turned)
    both = lax.all_gather(both_local, "fsdp", axis=0, tiled=True)
    queries = project(slot_query, normed, cosine, sine, wall)
    attended, lse = attend(places, queries, both)
    middle, normed_two = mix(slot_out, attended, hidden_in, gains[1], wall)
    return wall, wall, gains, both, normed, queries, attended, lse, middle, normed_two


def backward_attention(
    grads_wall,
    gain_two_term,
    weights,
    slots,
    places,
    branch,
    attended,
    queries,
    both,
    lse,
    normed,
    hidden_in,
    cosine,
    sine,
    layout,
    caps,
):
    slot_query, slot_both, slot_out = slots
    local_len, width = normed.shape
    kv_width = KV_HEADS * HEAD
    if tuned_mesh():
        lead = layout[2][3]
        table = jnp.concatenate(slots)
        table = table // caps * lead + lax.rem(table, caps)
        order = jnp.arange(table.shape[0], dtype=jnp.int32)
        here = jnp.arange(32 * lead, dtype=jnp.int32)
        tile_at = jnp.sum(jnp.where(table[None, :] == here[:, None], order[None, :], 0), axis=1)
        terms = jnp.pad(gain_two_term[None, :], ((1, 6), (0, 0)))
        grads, total, grad_normed = scatter_slots(
            grads_wall,
            terms,
            weights,
            tile_at,
            places,
            branch,
            attended,
            queries,
            both,
            lse,
            normed,
            hidden_in,
            cosine,
            sine,
            lead,
            layout[0][2],
            caps,
        )
        part = width // 32
        device = lax.axis_index(("dp", "fsdp"))
        return grads, lax.dynamic_slice_in_dim(total[:2], device * part, part, 1), grad_normed
    grad_attended, grads_wall = mix_back(slot_out, attended, branch, weights, grads_wall)
    grad_query, both_terms = attend_back(
        places, queries, both, grad_attended, lse, cosine, sine
    )
    both_sum = lax.psum_scatter(both_terms, "fsdp", scatter_dimension=0, tiled=True).astype(
        jnp.float32
    )
    grad_normed, grads_wall = project_back(slot_query, grad_query, normed, None, weights, grads_wall)
    both_sum = both_sum.reshape(local_len, KV_HEADS // PAIR, 2, PAIR * HEAD)
    grad_key = turn_back(both_sum[:, :, 0].reshape(local_len, kv_width), cosine, sine)
    grad_value = both_sum[:, :, 1].reshape(local_len, kv_width)
    grad_both = jnp.concatenate([grad_key, grad_value], axis=1).astype(jnp.bfloat16)
    grad_normed, grads_wall = project_back(
        slot_both, grad_both, normed, grad_normed, weights, grads_wall
    )
    tokens = hidden_in.astype(jnp.float32)
    inv_one = lax.rsqrt(jnp.mean(tokens * tokens, axis=1, keepdims=True) + norm_eps)
    gain_one_term = jnp.sum(grad_normed * tokens * inv_one, axis=0)
    gain_terms = jnp.stack([gain_one_term, gain_two_term])
    grads = lax.psum_scatter(grads_wall, ("dp", "fsdp"), scatter_dimension=0, tiled=True)
    gain_grad = lax.psum_scatter(gain_terms, ("dp", "fsdp"), scatter_dimension=1, tiled=True)
    return grads.astype(jnp.float32), gain_grad, grad_normed


VMEM_ASK = 56 << 20
NT = (((1,), (1,)), ((), ()))
NN = (((1,), (0,)), ((), ()))
TN = (((0,), (0,)), ((), ()))


def dot(a, b, dims):
    return lax.dot_general(a, b, dims, preferred_element_type=jnp.float32)


def stream_tiles(table, wall_ref, held, sem, group):
    step = pl.program_id(0)
    steps = pl.num_programs(0)
    depth = held.shape[0]
    buf = lax.rem(step, depth)

    def fetch(at):
        into = lax.rem(at, depth)

        @pl.loop(0, group, unroll=True)
        def _(t):
            pltpu.make_async_copy(
                wall_ref.at[table[at * group + t]], held.at[into, t], sem.at[into]
            ).start()

    @pl.when(step == 0)
    def _():
        for ahead in range(depth - 1):

            @pl.when(ahead < steps)
            def _(ahead=ahead):
                fetch(jnp.int32(ahead))

    @pl.when(step + depth - 1 < steps)
    def _():
        fetch(step + depth - 1)

    pltpu.make_async_copy(held.at[buf], held.at[buf], sem.at[buf]).wait()
    rows = group * wall_ref.shape[1]
    return held[buf].reshape(rows, wall_ref.shape[2])


def store_tiles(table, grads_ref, made, sem, group, value):
    step = pl.program_id(0)
    steps = pl.num_programs(0)
    buf = lax.rem(step, 2)

    def drain(which):
        pltpu.make_async_copy(made.at[which], made.at[which], sem.at[which]).wait()

    @pl.when(step >= 2)
    def _():
        drain(buf)

    made[buf] = value.astype(made.dtype).reshape(made.shape[1:])

    @pl.loop(0, group, unroll=True)
    def _(t):
        pltpu.make_async_copy(
            made.at[buf, t], grads_ref.at[table[step * group + t]], sem.at[buf]
        ).start()

    @pl.when(step == steps - 1)
    def _():
        drain(1 - buf)
        drain(buf)


def swap_halves(u):
    width = u.shape[1]
    lane = lax.broadcasted_iota(jnp.int32, u.shape, 1)
    first = lax.rem(lane, HEAD) < HEAD // 2
    return jnp.where(
        first, pltpu.roll(u, width - HEAD // 2, 1), pltpu.roll(u, HEAD // 2, 1)
    )


def project_kernel(group, turned, table, normed_ref, cos_ref, sin_ref, wall_ref, out_ref, held, sem):
    weights = stream_tiles(table, wall_ref, held, sem, group)
    u = dot(normed_ref[...], weights, NT)
    if turned is None:
        out_ref[...] = (u * cos_ref[...] + swap_halves(u) * sin_ref[...]).astype(out_ref.dtype)
    else:

        @pl.when(pl.program_id(0) < turned)
        def _():
            out_ref[...] = (u * cos_ref[...] + swap_halves(u) * sin_ref[...]).astype(out_ref.dtype)

        @pl.when(pl.program_id(0) >= turned)
        def _():
            out_ref[...] = u.astype(out_ref.dtype)


def full_spec(shape):
    return pl.BlockSpec(shape, lambda i, *_: (0,) * len(shape))


def any_spec():
    return pl.BlockSpec(memory_space=pl.ANY)


AHEAD = 4


def held_tiles(depth, group, wall):
    return pltpu.VMEM((depth, group) + wall.shape[1:], wall.dtype)


def project(table, normed, cosine, sine, wall, turned=None, group=16):
    tokens = normed.shape[0]
    block = group * wall.shape[1]
    steps = table.shape[0] // group
    return pl.pallas_call(
        functools.partial(project_kernel, group, turned),
        grid_spec=pltpu.PrefetchScalarGridSpec(
            num_scalar_prefetch=1,
            grid=(steps,),
            in_specs=[full_spec(normed.shape), full_spec(cosine.shape), full_spec(sine.shape), any_spec()],
            out_specs=pl.BlockSpec((tokens, block), lambda i, *_: (0, i)),
            scratch_shapes=[held_tiles(AHEAD, group, wall), pltpu.SemaphoreType.DMA((AHEAD,))],
        ),
        out_shape=jax.ShapeDtypeStruct((tokens, steps * block), jnp.bfloat16),
        compiler_params=pltpu.CompilerParams(vmem_limit_bytes=VMEM_ASK),
        name="project",
    )(table, normed, cosine, sine, wall)


def mix_kernel(group, table, left_ref, hidden_ref, gain_ref, wall_ref, middle_ref, normed_ref, held, sem):
    step = pl.program_id(0)
    weights = stream_tiles(table, wall_ref, held, sem, group)

    @pl.when(step == 0)
    def _():
        middle_ref[...] = hidden_ref[...].astype(jnp.float32)

    middle_ref[...] += dot(left_ref[...], weights, NN)

    @pl.when(step == pl.num_programs(0) - 1)
    def _():
        middle = middle_ref[...]
        inv = lax.rsqrt(jnp.mean(middle * middle, axis=1, keepdims=True) + norm_eps)
        normed_ref[...] = (middle * inv * gain_ref[...]).astype(normed_ref.dtype)


def mix(table, left, hidden, gain, wall, group=16):
    tokens, width = hidden.shape
    block = group * wall.shape[1]
    return pl.pallas_call(
        functools.partial(mix_kernel, group),
        grid_spec=pltpu.PrefetchScalarGridSpec(
            num_scalar_prefetch=1,
            grid=(table.shape[0] // group,),
            in_specs=[
                pl.BlockSpec((tokens, block), lambda i, *_: (0, i)),
                full_spec(hidden.shape),
                full_spec((1, width)),
                any_spec(),
            ],
            out_specs=[full_spec(hidden.shape), full_spec(hidden.shape)],
            scratch_shapes=[held_tiles(AHEAD, group, wall), pltpu.SemaphoreType.DMA((AHEAD,))],
        ),
        out_shape=[
            jax.ShapeDtypeStruct(hidden.shape, jnp.float32),
            jax.ShapeDtypeStruct(hidden.shape, jnp.bfloat16),
        ],
        compiler_params=pltpu.CompilerParams(vmem_limit_bytes=VMEM_ASK),
        name="mix",
    )(table, left, hidden, gain.reshape(1, width), wall)


def mix_back_kernel(group, table, left_ref, right_ref, wall_ref, old_ref, out_ref, grads_ref, held, made, load_sem, store_sem):
    weights = stream_tiles(table, wall_ref, held, load_sem, group)
    right = right_ref[...]
    out_ref[...] = dot(right, weights, NT).astype(out_ref.dtype)
    store_tiles(table, grads_ref, made, store_sem, group, dot(left_ref[...], right, TN))


def mix_back(table, left, right, wall, grads, group=16):
    tokens, width = right.shape
    block = group * wall.shape[1]
    columns = pl.BlockSpec((tokens, block), lambda i, *_: (0, i))
    return pl.pallas_call(
        functools.partial(mix_back_kernel, group),
        grid_spec=pltpu.PrefetchScalarGridSpec(
            num_scalar_prefetch=1,
            grid=(table.shape[0] // group,),
            in_specs=[columns, full_spec(right.shape), any_spec(), any_spec()],
            out_specs=[columns, any_spec()],
            scratch_shapes=[
                held_tiles(AHEAD, group, wall),
                held_tiles(2, group, wall),
                pltpu.SemaphoreType.DMA((AHEAD,)),
                pltpu.SemaphoreType.DMA((2,)),
            ],
        ),
        out_shape=[
            jax.ShapeDtypeStruct(left.shape, jnp.bfloat16),
            jax.ShapeDtypeStruct(grads.shape, grads.dtype),
        ],
        input_output_aliases={4: 1},
        compiler_params=pltpu.CompilerParams(vmem_limit_bytes=VMEM_ASK),
        name="mix_back",
    )(table, left, right, wall, grads)


def project_back_kernel(group, fresh, table, left_ref, right_ref, wall_ref, old_ref, start_ref, out_ref, grads_ref, held, made, load_sem, store_sem):
    weights = stream_tiles(table, wall_ref, held, load_sem, group)

    @pl.when(pl.program_id(0) == 0)
    def _():
        out_ref[...] = jnp.zeros_like(out_ref) if fresh else start_ref[...]

    left = left_ref[...]
    out_ref[...] += dot(left, weights, NN)
    store_tiles(table, grads_ref, made, store_sem, group, dot(left, right_ref[...], TN))


def project_back(table, left, right, start, wall, grads, group=16):
    tokens, width = right.shape
    block = group * wall.shape[1]
    return pl.pallas_call(
        functools.partial(project_back_kernel, group, start is None),
        grid_spec=pltpu.PrefetchScalarGridSpec(
            num_scalar_prefetch=1,
            grid=(table.shape[0] // group,),
            in_specs=[
                pl.BlockSpec((tokens, block), lambda i, *_: (0, i)),
                full_spec(right.shape),
                any_spec(),
                any_spec(),
                any_spec() if start is None else full_spec(start.shape),
            ],
            out_specs=[full_spec(right.shape), any_spec()],
            scratch_shapes=[
                held_tiles(AHEAD, group, wall),
                held_tiles(2, group, wall),
                pltpu.SemaphoreType.DMA((AHEAD,)),
                pltpu.SemaphoreType.DMA((2,)),
            ],
        ),
        out_shape=[
            jax.ShapeDtypeStruct(right.shape, jnp.float32),
            jax.ShapeDtypeStruct(grads.shape, grads.dtype),
        ],
        input_output_aliases={4: 1},
        compiler_params=pltpu.CompilerParams(vmem_limit_bytes=VMEM_ASK),
        name="project_back",
    )(table, left, right, wall, grads, table if start is None else start)


def fill_mask(places, mask_ref):
    shape = mask_ref.shape
    query = lax.broadcasted_iota(jnp.int32, shape, 0) + places[0]
    key = lax.broadcasted_iota(jnp.int32, shape, 1)
    allowed = key <= query
    for piece in range(places.shape[0] - 1):
        low = places[1 + piece]
        inside_query = (query >= low) & (query < low + PIECE)
        inside_key = (key >= low) & (key < low + PIECE)
        allowed = allowed | (inside_query & inside_key)
    mask_ref[...] = jnp.where(allowed, 1.0, 0.0)


PAIR = 2
GROUP = HEADS // KV_HEADS


def attend_kernel(places, q_ref, k_ref, v_ref, out_ref, lse_ref, mask_ref):
    @pl.when(pl.program_id(0) == 0)
    def _():
        fill_mask(places, mask_ref)

    mask = mask_ref[...] > 0.5
    lane = lax.broadcasted_iota(jnp.int32, lse_ref.shape[1:], 1)
    logs = jnp.zeros(lse_ref.shape[1:], jnp.float32)
    scale = jnp.bfloat16(1.0 / HEAD**0.5)
    for side in range(PAIR):
        k = k_ref[:, side * HEAD : (side + 1) * HEAD]
        v = v_ref[:, side * HEAD : (side + 1) * HEAD]
        for h in range(GROUP):
            head = side * GROUP + h
            cols = slice(head * HEAD, (head + 1) * HEAD)
            scores = jnp.where(mask, dot(q_ref[:, cols] * scale, k, NT), masked_score)
            top = jnp.max(scores, axis=1, keepdims=True)
            raised = jnp.exp(scores - top)
            total = jnp.sum(raised, axis=1, keepdims=True)
            probs = (raised * (1.0 / total)).astype(jnp.bfloat16)
            out_ref[:, cols] = dot(probs, v, NN).astype(out_ref.dtype)
            logs = jnp.where(lane == head, top + jnp.log(total), logs)
    lse_ref[0] = logs


def attend(places, queries, both):
    tokens, width = queries.shape
    length = both.shape[0]
    steps = KV_HEADS // PAIR
    wide = PAIR * GROUP * HEAD
    narrow = PAIR * HEAD
    return pl.pallas_call(
        attend_kernel,
        grid_spec=pltpu.PrefetchScalarGridSpec(
            num_scalar_prefetch=1,
            grid=(steps,),
            in_specs=[
                pl.BlockSpec((tokens, wide), lambda i, *_: (0, i)),
                pl.BlockSpec((length, narrow), lambda i, *_: (0, i)),
                pl.BlockSpec((length, narrow), lambda i, *_: (0, steps + i)),
            ],
            out_specs=[
                pl.BlockSpec((tokens, wide), lambda i, *_: (0, i)),
                pl.BlockSpec((1, tokens, 128), lambda i, *_: (i, 0, 0)),
            ],
            scratch_shapes=[pltpu.VMEM((tokens, length), jnp.float32)],
        ),
        out_shape=[
            jax.ShapeDtypeStruct((tokens, width), jnp.bfloat16),
            jax.ShapeDtypeStruct((steps, tokens, 128), jnp.float32),
        ],
        compiler_params=pltpu.CompilerParams(vmem_limit_bytes=VMEM_ASK),
        name="attend",
    )(places, queries, both, both)


def attend_back_kernel(places, q_ref, k_ref, v_ref, grad_ref, lse_ref, cos_ref, sin_ref, out_ref, both_ref, mask_ref, turn_ref):
    @pl.when(pl.program_id(0) == 0)
    def _():
        fill_mask(places, mask_ref)

    mask = mask_ref[...] > 0.5
    scale = jnp.bfloat16(1.0 / HEAD**0.5)
    for side in range(PAIR):
        here = slice(side * HEAD, (side + 1) * HEAD)
        k = k_ref[:, here]
        v = v_ref[:, here]
        dk = None
        dv = None
        for h in range(GROUP):
            head = side * GROUP + h
            cols = slice(head * HEAD, (head + 1) * HEAD)
            q = q_ref[:, cols] * scale
            grad = grad_ref[:, cols]
            scores = jnp.where(mask, dot(q, k, NT), masked_score)
            probs = jnp.exp(scores - lse_ref[0, :, head : head + 1])
            grad_probs = dot(grad, v, NT)
            row_dot = jnp.sum(probs * grad_probs, axis=1, keepdims=True)
            grad_scores = (probs * (grad_probs - row_dot)).astype(jnp.bfloat16)
            turn_ref[:, cols] = dot(grad_scores, k, NN) * (1.0 / HEAD**0.5)
            dk_part = dot(q, grad_scores, TN)
            dv_part = dot(grad, probs.astype(jnp.bfloat16), TN)
            dk = dk_part if dk is None else dk + dk_part
            dv = dv_part if dv is None else dv + dv_part
        there = slice((PAIR + side) * HEAD, (PAIR + side + 1) * HEAD)
        both_ref[:, here] = dk.T.astype(both_ref.dtype)
        both_ref[:, there] = dv.T.astype(both_ref.dtype)
    wide = cos_ref.shape[1]
    for left in range(0, turn_ref.shape[1], wide):
        u = turn_ref[:, left : left + wide]
        out_ref[:, left : left + wide] = (u * cos_ref[...] - swap_halves(u) * sin_ref[...]).astype(out_ref.dtype)


def attend_back(places, queries, both, grad, lse, cosine, sine):
    tokens, width = queries.shape
    length = both.shape[0]
    steps = KV_HEADS // PAIR
    wide = PAIR * GROUP * HEAD
    narrow = PAIR * HEAD
    columns = pl.BlockSpec((tokens, wide), lambda i, *_: (0, i))
    keys = pl.BlockSpec((length, narrow), lambda i, *_: (0, i))
    return pl.pallas_call(
        attend_back_kernel,
        grid_spec=pltpu.PrefetchScalarGridSpec(
            num_scalar_prefetch=1,
            grid=(steps,),
            in_specs=[
                columns,
                keys,
                pl.BlockSpec((length, narrow), lambda i, *_: (0, steps + i)),
                columns,
                pl.BlockSpec((1, tokens, 128), lambda i, *_: (i, 0, 0)),
                full_spec(cosine.shape),
                full_spec(sine.shape),
            ],
            out_specs=[columns, pl.BlockSpec((length, 2 * narrow), lambda i, *_: (0, i))],
            scratch_shapes=[pltpu.VMEM((tokens, length), jnp.float32), pltpu.VMEM((tokens, wide), jnp.float32)],
        ),
        out_shape=[
            jax.ShapeDtypeStruct((tokens, width), jnp.bfloat16),
            jax.ShapeDtypeStruct((length, 2 * KV_HEADS * HEAD), jnp.bfloat16),
        ],
        compiler_params=pltpu.CompilerParams(vmem_limit_bytes=VMEM_ASK),
        name="attend_back",
    )(places, queries, both, both, grad, lse, cosine, sine)


def ffn_kernel(group, gate_s, up_s, down_s, normed_ref, cot_ref, wall_ref, out_ref, back_ref, grads_ref, held, made, load_sem, store_sem):
    step = pl.program_id(0)
    steps = pl.num_programs(0)
    tables = (gate_s, up_s, down_s)
    tile_rows = wall_ref.shape[1]
    width = wall_ref.shape[2]
    rows = group * tile_rows

    def fetch(at, buf):
        for kind in range(3):
            @pl.loop(0, group, unroll=True)
            def _(t, kind=kind):
                pltpu.make_async_copy(wall_ref.at[tables[kind][at * group + t]], held.at[buf, kind, t], load_sem.at[buf]).start()

    def drain(buf):
        pltpu.make_async_copy(made.at[buf], made.at[buf], store_sem.at[buf]).wait()

    buf = lax.rem(step, 2)

    @pl.when(step == 0)
    def _():
        fetch(0, 0)
        out_ref[...] = jnp.zeros_like(out_ref)
        back_ref[...] = jnp.zeros_like(back_ref)

    @pl.when(step + 1 < steps)
    def _():
        fetch(step + 1, 1 - buf)

    pltpu.make_async_copy(held.at[buf], held.at[buf], load_sem.at[buf]).wait()

    @pl.when(step >= 2)
    def _():
        drain(buf)

    normed = normed_ref[...]
    cot = cot_ref[...]
    w_gate = held[buf, 0].reshape(rows, width)
    w_up = held[buf, 1].reshape(rows, width)
    w_down = held[buf, 2].reshape(rows, width)
    nt = (((1,), (1,)), ((), ()))
    nn = (((1,), (0,)), ((), ()))
    tn = (((0,), (0,)), ((), ()))

    def dot(a, b, dims):
        return lax.dot_general(a, b, dims, preferred_element_type=jnp.float32)

    gate = dot(normed, w_gate, nt)
    up = dot(normed, w_up, nt)
    hidden = dot(cot, w_down, nt)
    sig = jax.nn.sigmoid(gate)
    silu = gate * sig
    act = (silu * up).astype(jnp.bfloat16)
    g_gate = (hidden * up * sig * (1.0 + gate * (1.0 - sig))).astype(jnp.bfloat16)
    g_up = (hidden * silu).astype(jnp.bfloat16)
    out_ref[...] += dot(act, w_down, nn)
    back_ref[...] += dot(g_gate, w_gate, nn) + dot(g_up, w_up, nn)
    made[buf, 0] = dot(g_gate, normed, tn).astype(jnp.bfloat16).reshape(group, tile_rows, width)
    made[buf, 1] = dot(g_up, normed, tn).astype(jnp.bfloat16).reshape(group, tile_rows, width)
    made[buf, 2] = dot(act, cot, tn).astype(jnp.bfloat16).reshape(group, tile_rows, width)
    for kind in range(3):
        @pl.loop(0, group, unroll=True)
        def _(t, kind=kind):
            pltpu.make_async_copy(made.at[buf, kind, t], grads_ref.at[tables[kind][step * group + t]], store_sem.at[buf]).start()

    @pl.when(step == steps - 1)
    def _():
        drain(1 - buf)
        drain(buf)

def ffn_call(gate_s, up_s, down_s, normed, cot, wall, group=16):
    tokens, width = normed.shape
    steps = gate_s.shape[0] // group
    tr = wall.shape[1]
    full = pl.BlockSpec((tokens, width), lambda i, *_: (0, 0))
    return pl.pallas_call(
        functools.partial(ffn_kernel, group),
        grid_spec=pltpu.PrefetchScalarGridSpec(
            num_scalar_prefetch=3, grid=(steps,),
            in_specs=[full, full, pl.BlockSpec(memory_space=pl.ANY)],
            out_specs=[full, full, pl.BlockSpec(memory_space=pl.ANY)],
            scratch_shapes=[pltpu.VMEM((2, 3, group, tr, width), jnp.bfloat16), pltpu.VMEM((2, 3, group, tr, width), jnp.bfloat16),
                pltpu.SemaphoreType.DMA((2,)), pltpu.SemaphoreType.DMA((2,))]),
        out_shape=[jax.ShapeDtypeStruct((tokens, width), jnp.float32), jax.ShapeDtypeStruct((tokens, width), jnp.float32), jax.ShapeDtypeStruct(wall.shape, jnp.bfloat16)],
        compiler_params=pltpu.CompilerParams(vmem_limit_bytes=56 << 20, dimension_semantics=("arbitrary",)),
        name="ffn",
    )(gate_s, up_s, down_s, normed, cot, wall)


MESH = pl.DeviceIdType.MESH
EVERY = slice(None)
GATHER_ROUTES = (
    ("z1", "z2", "z3", "x", "y", "core"),
    ("z1", "z2", "z3", "y", "x", "core"),
    ("x", "z1", "z2", "z3", "y", "core"),
    ("y", "z1", "z2", "z3", "x", "core"),
)


def position():
    dp = lax.axis_index("dp")
    return dp // 4, lax.rem(dp // 2, 2), lax.rem(dp, 2), lax.axis_index("fsdp")


def target(hop):
    y, x, c, z = position()
    if hop == "x":
        x = 1 - x
    elif hop == "y":
        y = 1 - y
    elif hop == "core":
        c = 1 - c
    elif hop == "back":
        z = lax.rem(z + 3, 4)
    else:
        z = lax.rem(z + 1, 4)
    return (y * 4 + x * 2 + c, z)


def enter(hops):
    barrier = pltpu.get_barrier_semaphore()
    for hop in hops:
        pl.semaphore_signal(barrier, inc=1, device_id=target(hop), device_id_type=MESH)
    pl.semaphore_wait(barrier, len(hops))


GATHER_PLAN = (3, (0, 0, 0, 0), (10, 6), (11, 3))
SCATTER_PLAN = (3, (4, 4, 0, 0), (4, 6), (40, 0))


def split_slots(caps, plan):
    small = caps * plan[0] // 16
    third = (caps - 2 * small) // 2
    counts = (small, small, third, caps - 2 * small - third)
    starts = (0, small, 2 * small, 2 * small + third)
    return counts, starts


def round_count(counts, plan):
    share, delays, (dense, extra), (gap, pause) = plan
    ends = []
    for route in range(4):
        at = [
            t
            for t in range(200)
            if (t % 2 == 0 or dense <= t < dense + extra if route < 2 else not gap <= t < gap + pause)
        ]
        ends.append(delays[route] + at[counts[route] - 1] + 1)
    return max(ends)


def passed(at, edge):
    return (at - edge + 64) // 64


def turn(route, at, counts, plan):
    share, delays, (dense, extra), (gap, pause) = plan
    at = at - delays[route]
    if route < 2:
        begun = passed(at, dense)
        over = passed(at, dense + extra)
        slow = at // 2
        quick = dense // 2 + at - dense
        late = dense // 2 + extra + (at - dense - extra) // 2
        index = (1 - begun) * slow + (begun - over) * quick + over * late
        even = lax.rem(at + 64, 2) == 0
        live = (at >= 0) & (even | (begun - over == 1)) & (index < counts[route])
        return live, index
    index = at - pause * passed(at, gap)
    live = (at >= 0) & ((at < gap) | (at >= gap + pause)) & (index < counts[route])
    return live, index


def slot_of(route, index, counts, starts, lead, early):
    if route < 2:
        return 2 * lead + starts[route] + index
    here = 2 * lead + starts[route] - (route - 2) * lead
    count = counts[route]
    if early:
        later = (index + count - lead) // count
        return (route - 2) * lead + index + later * (here - route * lead + lead)
    final = index // (count - lead)
    return here + index - final * (here + count - lead - (route - 2) * lead)


def attend_side(side, q, k_pair, v_pair, mask, out_ref, logs):
    lane = lax.broadcasted_iota(jnp.int32, (q.shape[0], 128), 1)
    scale = jnp.bfloat16(1.0 / HEAD**0.5)
    k = k_pair[:, side * HEAD : (side + 1) * HEAD]
    v = v_pair[:, side * HEAD : (side + 1) * HEAD]
    for h in range(GROUP):
        cols = slice(h * HEAD, (h + 1) * HEAD)
        scores = jnp.where(mask, dot(q[:, cols] * scale, k, NT), masked_score)
        top = jnp.max(scores, axis=1, keepdims=True)
        raised = jnp.exp(scores - top)
        total = jnp.sum(raised, axis=1, keepdims=True)
        probs = (raised * (1.0 / total)).astype(jnp.bfloat16)
        out_ref[:, cols] = dot(probs, v, NN).astype(out_ref.dtype)
        logs = jnp.where(lane == side * GROUP + h, top + jnp.log(total), logs)
    return logs


GATHER_HOPS = ("z1", "z2", "z3")


def gather_kernel(
    lead,
    mine_ref,
    gain_ref,
    table,
    places,
    hidden_ref,
    cos_ref,
    sin_ref,
    wall_ref,
    gains_ref,
    weights_ref,
    both_ref,
    all_gains_ref,
    normed_ref,
    q_ref,
    att_ref,
    lse_ref,
    middle_ref,
    normed_two_ref,
    own_sem,
    send_sem,
    recv_sem,
    tiles,
    block,
    gain_tiles,
    keys,
    mask_ref,
    pair_ref,
    side_sem,
    hop_send,
    hop_recv,
):
    y, x, c, z = position()
    counts, starts = split_slots(mine_ref.shape[0], GATHER_PLAN)
    rounds = round_count(counts, GATHER_PLAN)
    own = pltpu.make_async_copy(mine_ref, wall_ref.at[y, x, c, z], own_sem.at[0])
    own_gain = pltpu.make_async_copy(gain_ref, gains_ref.at[y, x, c, z], own_sem.at[1])
    own.start()
    own_gain.start()
    enter(("x", "y", "core", "z", "back"))
    own.wait()
    own_gain.wait()

    def region(route, stage):
        hops = GATHER_ROUTES[route % 4]
        hop = hops[stage]
        done = hops[:stage]
        at_y = EVERY if "y" in done else y
        at_x = EVERY if "x" in done else x
        at_z = EVERY if "z3" in done else z
        if hop in ("z1", "z2", "z3"):
            at_z = lax.rem(z + 5 - int(hop[1]), 4)
        return at_y, at_x, c, at_z

    def copy(route, stage, index):
        if route == 4:
            view = gains_ref.at[region(route, stage)]
        else:
            slot = slot_of(route, index, counts, starts, lead // 2, True)
            view = wall_ref.at[region(route, stage) + (slot,)]
        return pltpu.make_async_remote_copy(
            src_ref=view,
            dst_ref=view,
            send_sem=send_sem.at[route, stage],
            recv_sem=recv_sem.at[route, stage, index],
            device_id=target(GATHER_ROUTES[route % 4][stage]),
            device_id_type=MESH,
        )

    stages = len(GATHER_ROUTES[0])
    tokens, width = hidden_ref.shape
    number = block.shape[0]
    rows = number * block.shape[1]
    query_blocks = q_ref.shape[1] // rows
    key_blocks = keys.shape[1] // rows

    def take(at):
        @pl.loop(0, number, unroll=True)
        def _(t):
            block[t] = tiles[table[at * number + t]]

        pltpu.make_async_copy(
            block, weights_ref.at[pl.ds(at * number, number)], side_sem.at[1]
        ).start()
        return block[...].reshape(rows, width)

    def taken(at):
        pltpu.make_async_copy(
            block, weights_ref.at[pl.ds(at * number, number)], side_sem.at[1]
        ).wait()

    def load_tiles(d):
        return pltpu.make_async_copy(
            wall_ref.at[d // 16, lax.rem(d // 8, 2), lax.rem(d // 4, 2), lax.rem(d, 4), pl.ds(0, lead)],
            tiles.at[pl.ds(d * lead, lead)],
            side_sem.at[0],
        )

    load_gains = pltpu.make_async_copy(gains_ref, gain_tiles, side_sem.at[2])

    def pass_keys(part):
        hop = part // 2
        at = lax.rem(z + 4 - hop, 4)
        cols = KV_HEADS * HEAD
        view = keys.at[
            pl.ds(pl.multiple_of(at * tokens, tokens), tokens),
            pl.ds(part % 2 * cols, cols),
        ]
        return pltpu.make_async_remote_copy(
            src_ref=view,
            dst_ref=view,
            send_sem=hop_send.at[part],
            recv_sem=hop_recv.at[part],
            device_id=target(GATHER_HOPS[hop]),
            device_id_type=MESH,
        )

    def begin():
        @pl.loop(0, 32)
        def _(d):
            load_tiles(d).start()

        load_gains.start()

    def norm():
        load_gains.wait()
        lane = lax.broadcasted_iota(jnp.int32, (8, 128), 1)
        parts = []
        for d in range(0, 32, 2):
            even = gain_tiles[d // 16, (d // 8) % 2, (d // 4) % 2, d % 4].astype(jnp.float32)[:8]
            odd = gain_tiles[d // 16, (d // 8) % 2, (d // 4) % 2, d % 4 + 1].astype(jnp.float32)[:8]
            parts.append(jnp.where(lane < 64, even, pltpu.roll(odd, 64, 1)))
        all_gains_ref[...] = jnp.concatenate(parts, axis=1)
        hidden = hidden_ref[...].astype(jnp.float32)
        inv = lax.rsqrt(jnp.mean(hidden * hidden, axis=1, keepdims=True) + norm_eps)
        normed_ref[...] = (hidden * inv * all_gains_ref[0:1, :]).astype(normed_ref.dtype)
        fill_mask(places, mask_ref)

    def project_keys():
        pltpu.make_async_copy(tiles, tiles, side_sem.at[0]).wait()
        own_rows = pl.ds(pl.multiple_of(z * tokens, tokens), tokens)

        for b in range(key_blocks):
            at = query_blocks + b
            u = dot(normed_ref[...], take(at), NT)
            if b < key_blocks // 2:
                u = u * cos_ref[...] + swap_halves(u) * sin_ref[...]
            keys[own_rows, b * rows : (b + 1) * rows] = u.astype(keys.dtype)
            taken(at)

    def project_queries(low, high):
        @pl.loop(low, high)
        def _(b):
            u = dot(normed_ref[...], take(b), NT)
            u = u * cos_ref[...] + swap_halves(u) * sin_ref[...]
            q_ref[:, pl.ds(pl.multiple_of(b * rows, rows), rows)] = u.astype(q_ref.dtype)
            taken(b)

    def attend_step(pair, side):
        wide = GROUP * HEAD
        narrow = PAIR * HEAD
        here = pl.ds(pl.multiple_of((pair * PAIR + side) * wide, wide), wide)
        k_pair = keys[:, pl.ds(pl.multiple_of(pair * narrow, narrow), narrow)]
        v_pair = keys[:, pl.ds(pl.multiple_of(KV_HEADS * HEAD + pair * narrow, narrow), narrow)]
        logs = lse_ref[pair] if side else jnp.zeros((tokens, 128), jnp.float32)
        mask = mask_ref[...] > 0.5
        lse_ref[pair] = attend_side(side, q_ref[:, here], k_pair, v_pair, mask, pair_ref, logs)
        att_ref[:, here] = pair_ref[...]

    def mix_blocks(low):
        for more in range(4):
            b = low + more
            at = query_blocks + key_blocks + b
            left = att_ref[:, pl.ds(pl.multiple_of(b * rows, rows), rows)]
            middle_ref[...] += dot(left, take(at), NN)
            taken(at)

    def mix_end():
        middle = middle_ref[...]
        inv = lax.rsqrt(jnp.mean(middle * middle, axis=1, keepdims=True) + norm_eps)
        normed_two_ref[...] = (middle * inv * all_gains_ref[1:2, :]).astype(normed_two_ref.dtype)

    start = GATHER_PLAN[1][3] + lead // 2 - 1 + stages
    keep_both = pltpu.make_async_copy(keys, both_ref, side_sem.at[3])

    @pl.loop(0, rounds + stages)
    def _(t):
        for stage in range(stages + 1):
            for route in range(5):
                if route == 4:
                    live, index = t == stage, 0
                else:
                    live, index = turn(route, t - stage, counts, GATHER_PLAN)

                @pl.when(live)
                def _(stage=stage, route=route, index=index):
                    if stage > 0:
                        copy(route, stage - 1, index).wait()
                    if stage < stages:
                        copy(route, stage, index).start()

        @pl.when(t == start)
        def _():
            begin()
            norm()

        @pl.when(t == start + 1)
        def _():
            project_keys()

        parts = 2 * len(GATHER_HOPS)
        for part in range(parts + 1):

            @pl.when(t == start + 1 + part)
            def _(part=part):
                if part > 0:
                    pass_keys(part - 1).wait()
                if part < parts:
                    pass_keys(part).start()

        for third in range(4):

            @pl.when(t == start + 2 + third)
            def _(third=third):
                project_queries(third * query_blocks // 4, (third + 1) * query_blocks // 4)

        attending = start + 1 + parts

        @pl.when(t == attending)
        def _():
            keep_both.start()
            middle_ref[...] = hidden_ref[...].astype(jnp.float32)

        for side in range(PAIR):
            since = t - attending

            @pl.when((since >= 0) & (since < KV_HEADS) & (lax.rem(since + 64, 2) == side))
            def _(side=side, since=since):
                attend_step(since // 2, side)

        mixing = attending + KV_HEADS

        @pl.when((t >= mixing) & (t < mixing + query_blocks // 4))
        def _():
            mix_blocks((t - mixing) * 4)

        @pl.when(t == mixing + query_blocks // 4)
        def _():
            mix_end()
            keep_both.wait()


def gather_slots(low_tiles, low_gains, table, places, hidden, cosine, sine, lead):
    caps, rows, width = low_tiles.shape
    tokens = hidden.shape[0]
    length = tokens * 4
    counts, starts = split_slots(caps, GATHER_PLAN)
    kind = low_tiles.dtype
    vmem = pl.BlockSpec(memory_space=pltpu.VMEM)
    smem = pl.BlockSpec(memory_space=pltpu.SMEM)
    anyw = pl.BlockSpec(memory_space=pl.ANY)
    padded = jnp.pad(low_gains, ((0, 16 - low_gains.shape[0]), (0, 128 - low_gains.shape[1])))
    number = cosine.shape[1] // rows
    pairs = KV_HEADS // PAIR
    outs = pl.pallas_call(
        functools.partial(gather_kernel, lead),
        out_shape=[
            jax.ShapeDtypeStruct((2, 2, 2, 4, caps, rows, width), kind),
            jax.ShapeDtypeStruct((2, 2, 2, 4) + padded.shape, kind),
            jax.ShapeDtypeStruct((table.shape[0], rows, width), kind),
            jax.ShapeDtypeStruct((length, 2 * KV_HEADS * HEAD), kind),
            jax.ShapeDtypeStruct((8, width), jnp.float32),
            jax.ShapeDtypeStruct((tokens, width), kind),
            jax.ShapeDtypeStruct((tokens, width), kind),
            jax.ShapeDtypeStruct((tokens, width), kind),
            jax.ShapeDtypeStruct((pairs, tokens, 128), jnp.float32),
            jax.ShapeDtypeStruct((tokens, width), jnp.float32),
            jax.ShapeDtypeStruct((tokens, width), kind),
        ],
        in_specs=[vmem, vmem, smem, smem, vmem, vmem, vmem],
        out_specs=[anyw] * 4 + [vmem] * 7,
        scratch_shapes=[
            pltpu.SemaphoreType.DMA((2,)),
            pltpu.SemaphoreType.DMA((5, 6)),
            pltpu.SemaphoreType.DMA((5, 6, max(counts))),
            pltpu.VMEM((32 * lead, rows, width), kind),
            pltpu.VMEM((number, rows, width), kind),
            pltpu.VMEM((2, 2, 2, 4) + padded.shape, kind),
            pltpu.VMEM((length, 2 * KV_HEADS * HEAD), kind),
            pltpu.VMEM((tokens, length), jnp.float32),
            pltpu.VMEM((tokens, GROUP * HEAD), kind),
            pltpu.SemaphoreType.DMA((4,)),
            pltpu.SemaphoreType.DMA((6,)),
            pltpu.SemaphoreType.DMA((6,)),
        ],
        compiler_params=pltpu.CompilerParams(
            collective_id=0, has_side_effects=True, vmem_limit_bytes=62 << 20
        ),
        name="gather_slots",
    )(low_tiles, padded, table, places, hidden, cosine, sine)
    return [outs[0].reshape(32 * caps, rows, width)] + list(outs[2:])


SCATTER_ROUTES = (
    ("core", "y", "x", "z1", "z2", "z3", "end"),
    ("core", "x", "y", "z1", "z2", "z3", "end"),
    ("core", "y", "z1", "z2", "z3", "x", "end"),
    ("core", "x", "z1", "z2", "z3", "y", "end"),
)


SUM_HOPS = ("core", "x", "y", "z1", "z2", "z3")
SUM_START = 2


def scatter_extent(route, stage):
    hops = SCATTER_ROUTES[route]
    done = hops[1 : stage + 1] if hops[stage] in ("x", "y") else hops[1:stage]
    extent = []
    if "x" not in done or "y" not in done:
        extent.append(2)
    if not any(hop[0] == "z" for hop in hops[: stage + 1]):
        extent.append(4)
    return tuple(extent)


def scatter_terms(route, stage):
    hops = SCATTER_ROUTES[route]
    done = hops[1:stage]
    return 2 + ("x" in done) + ("y" in done) + ("z1" in done)


def attend_back_side(side, q, k_pair, v_pair, grad, mask, logs, turn_ref, k_out, v_out):
    scale = jnp.bfloat16(1.0 / HEAD**0.5)
    here = slice(side * HEAD, (side + 1) * HEAD)
    k = k_pair[:, here]
    v = v_pair[:, here]
    dk = None
    dv = None
    for h in range(GROUP):
        cols = slice(h * HEAD, (h + 1) * HEAD)
        head = side * GROUP + h
        q_head = q[:, cols] * scale
        scores = jnp.where(mask, dot(q_head, k, NT), masked_score)
        probs = jnp.exp(scores - logs[:, head : head + 1])
        grad_probs = dot(grad[:, cols], v, NT)
        row_dot = jnp.sum(probs * grad_probs, axis=1, keepdims=True)
        grad_scores = (probs * (grad_probs - row_dot)).astype(jnp.bfloat16)
        turn_ref[:, cols] = dot(grad_scores, k, NN) * (1.0 / HEAD**0.5)
        dk_part = dot(q_head, grad_scores, TN)
        dv_part = dot(grad[:, cols], probs.astype(jnp.bfloat16), TN)
        dk = dk_part if dk is None else dk + dk_part
        dv = dv_part if dv is None else dv + dv_part
    k_out[:, here] = dk.T.astype(k_out.dtype)
    v_out[:, here] = dv.T.astype(v_out.dtype)


def scatter_kernel(
    look,
    lead,
    first_group,
    old_ref,
    gain_ref,
    weights_ref,
    table,
    places,
    branch_ref,
    att_ref,
    q_ref,
    both_ref,
    lse_ref,
    normed_ref,
    hidden_ref,
    cos_ref,
    sin_ref,
    wall_ref,
    out_ref,
    total_ref,
    back_ref,
    core_ref,
    first_ref,
    second_ref,
    ring_ref,
    last_ref,
    *scratch,
):
    y, x, c, z = position()
    caps, rows, width = out_ref.shape
    counts, starts = split_slots(caps, SCATTER_PLAN)
    rounds = round_count(counts, SCATTER_PLAN)
    stages = len(SCATTER_ROUTES[0])
    held = {}
    made = {}
    scratch = list(scratch)
    for route in range(4):
        for stage in range(1, stages):
            held[route, stage] = scratch.pop(0)
            made[route, stage] = scratch.pop(0)
    load_sem, send_sem, recv_sem, out_sem, sums, landed, sum_send, sum_recv = scratch[:8]
    (
        streamed,
        grad_att,
        grad_q,
        grad_kv,
        grad_both,
        k_pair_ref,
        v_pair_ref,
        turn_ref,
        hop_out,
        hop_in,
        turned,
        left_ref,
        built,
        mask_ref,
        stream_sem,
        hop_send,
        hop_recv,
        built_sem,
    ) = scratch[8:]
    enter(("x", "y", "core", "z", "back"))

    def landing(route, stage, slot):
        hops = SCATTER_ROUTES[route]
        hop = hops[stage]
        if hop == "core":
            return core_ref.at[:, :, :, slot]
        if hop[0] == "z":
            ring = ring_ref.at[int(hop[1]) - 1]
            return ring.at[0, slot] if route < 2 else ring.at[:, slot]
        if stage == 1:
            return first_ref.at[:, :, slot]
        if stage == 2:
            return second_ref.at[:, slot]
        return last_ref.at[slot]

    def terms(route, stage, slot):
        hops = SCATTER_ROUTES[route]
        hop = hops[stage]
        done = hops[1:stage]
        at_y = 1 - y if hop == "y" else (y if "y" in done else EVERY)
        at_x = 1 - x if hop == "x" else (x if "x" in done else EVERY)
        at_z = EVERY
        if hop[0] == "z":
            at_z = lax.rem(z + 4 - int(hop[1]), 4)
        elif "z3" in done:
            at_z = z
        views = [wall_ref.at[at_y, at_x, c, at_z, slot], core_ref.at[at_y, at_x, at_z, slot]]
        other = at_x if hops[1] == "y" else at_y
        if stage > 1:
            views.append(first_ref.at[other, at_z, slot])
        if route < 2 and stage > 2:
            views.append(second_ref.at[at_z, slot])
        if hop in ("z2", "z3"):
            ring = ring_ref.at[int(hop[1]) - 2]
            views.append(ring.at[0, slot] if route < 2 else ring.at[:, slot])
        elif "z3" in done:
            ring = ring_ref.at[2]
            views.append(ring.at[0, slot] if route < 2 else ring.at[other, slot])
        if route >= 2 and hop == "end":
            views.append(last_ref.at[slot])
        return views

    def slot_at(route, index):
        return slot_of(route, index, counts, starts, lead // 2, False)

    def send(route, stage, index):
        slot = slot_at(route, index)
        if stage == 0:
            source = wall_ref.at[:, :, 1 - c, :, slot]
        else:
            source = made[route, stage]
        return pltpu.make_async_remote_copy(
            src_ref=source,
            dst_ref=landing(route, stage, slot),
            send_sem=send_sem.at[route, stage],
            recv_sem=recv_sem.at[route, stage, index],
            device_id=target(SCATTER_ROUTES[route][stage]),
            device_id_type=MESH,
        )

    def keep(route, index):
        return pltpu.make_async_copy(
            made[route, stages - 1], out_ref.at[slot_at(route, index)], out_sem.at[route]
        )

    def early(route, stage, index):
        if stage > 0:
            for k, view in enumerate(terms(route, stage, slot_at(route, index))[:-1]):
                pltpu.make_async_copy(view, held[route, stage].at[k], load_sem.at[route, stage]).start()

    def late(route, stage, index):
        if stage > 0:
            send(route, stage - 1, index).wait()
            view = terms(route, stage, slot_at(route, index))[-1]
            last = held[route, stage].shape[0] - 1
            pltpu.make_async_copy(view, held[route, stage].at[last], load_sem.at[route, stage]).start()

    def finish(route, stage, index):
        if stage > 0:
            buf = held[route, stage]
            pltpu.make_async_copy(buf, buf, load_sem.at[route, stage]).wait()
            number = buf.shape[0]
            extent = buf.shape[1:-2]
            blocks = 1
            for size in extent:
                blocks *= size
            part = min(width, 512)
            if stage == stages - 1:

                @pl.when(index > 0)
                def _():
                    keep(route, index - 1).wait()

            @pl.loop(0, blocks)
            def _(block):
                if len(extent) == 2:
                    at = (block // extent[1], lax.rem(block, extent[1]))
                elif len(extent) == 1:
                    at = (block,)
                else:
                    at = ()
                for left in range(0, width, part):
                    cols = pl.ds(left, part)
                    total = buf[(0,) + at + (EVERY, cols)].astype(jnp.float32)
                    for k in range(1, number):
                        total += buf[(k,) + at + (EVERY, cols)].astype(jnp.float32)
                    made[route, stage][at + (EVERY, cols)] = total.astype(made[route, stage].dtype)

        if stage < stages - 1:
            send(route, stage, index).start()
        else:
            keep(route, index).start()

    def pass_sum(hop):
        return pltpu.make_async_remote_copy(
            src_ref=sums.at[hop] if hop < 4 else landed.at[hop - 1],
            dst_ref=landed.at[hop],
            send_sem=sum_send.at[hop],
            recv_sem=sum_recv.at[hop],
            device_id=target(SUM_HOPS[hop]),
            device_id_type=MESH,
        )

    def add_sums(step):
        if step > 0:
            pass_sum(step - 1).wait()
        if step == 0:
            hidden = hidden_ref[...].astype(jnp.float32)
            inv = lax.rsqrt(jnp.mean(hidden * hidden, axis=1, keepdims=True) + norm_eps)
            term = jnp.sum(back_ref[...] * hidden * inv, axis=0, keepdims=True)
            line = lax.broadcasted_iota(jnp.int32, gain_ref.shape, 0)
            sums[0] = jnp.where(line == 0, term, gain_ref[...])
        elif step < 4:
            sums[step] = sums[step - 1] + landed[step - 1]
        elif step == len(SUM_HOPS):
            total_ref[...] = (sums[3] + landed[3]) + (landed[4] + landed[5])
        if step < len(SUM_HOPS):
            pass_sum(step).start()

    tokens = hidden_ref.shape[0]
    number = cos_ref.shape[1] // rows
    block = number * rows
    query_blocks = q_ref.shape[1] // block
    key_blocks = both_ref.shape[1] // block
    out_blocks = att_ref.shape[1] // block
    all_blocks = query_blocks + key_blocks + out_blocks
    kv_width = KV_HEADS * HEAD

    def stream(n):
        at = lax.rem(n + query_blocks + key_blocks, all_blocks)
        return pltpu.make_async_copy(
            weights_ref.at[pl.ds(at * number, number)],
            streamed.at[lax.rem(n, 2)],
            stream_sem.at[lax.rem(n, 2)],
        )

    def streamed_block(n):
        stream(n).wait()

        @pl.when(n + 1 < all_blocks)
        def _():
            stream(n + 1).start()

        return streamed[lax.rem(n, 2)].reshape(block, width)

    def column(b):
        return pl.ds(pl.multiple_of(b * block, block), block)

    def turn_tiles(at, value):
        flipped = value.astype(jnp.float32).T.astype(turned.dtype)
        turned[pl.ds(at * number, number)] = flipped.reshape(number, rows, tokens)

    def out_back(low, high):
        @pl.loop(low, high)
        def _(b):
            grad_att[:, column(b)] = dot(branch_ref[...], streamed_block(b), NT).astype(
                grad_att.dtype
            )
            turn_tiles(query_blocks + key_blocks + b, att_ref[:, column(b)])

    def query_back(low, high):
        @pl.loop(low, high)
        def _(b):
            left = grad_q[:, column(b)]
            back_ref[...] += dot(left, streamed_block(out_blocks + b), NN)
            turn_tiles(b, left)

    def key_back():
        @pl.loop(0, key_blocks)
        def _(b):
            left = grad_both[:, column(b)]
            back_ref[...] += dot(left, streamed_block(out_blocks + query_blocks + b), NN)
            turn_tiles(query_blocks + b, left)

    def attend_back_step(pair, side):
        wide = GROUP * HEAD
        narrow = PAIR * HEAD
        here = pl.ds(pl.multiple_of((pair * PAIR + side) * wide, wide), wide)
        k_cols = pl.ds(pl.multiple_of(pair * narrow, narrow), narrow)
        v_cols = pl.ds(pl.multiple_of(kv_width + pair * narrow, narrow), narrow)
        attend_back_side(
            side,
            q_ref[:, here],
            both_ref[:, k_cols],
            both_ref[:, v_cols],
            grad_att[:, here],
            mask_ref[...] > 0.5,
            lse_ref[pair],
            turn_ref,
            k_pair_ref,
            v_pair_ref,
        )
        u = turn_ref[...]
        grad_q[:, here] = (u * cos_ref[...] - swap_halves(u) * sin_ref[...]).astype(grad_q.dtype)
        if side == PAIR - 1:
            grad_kv[:, k_cols] = k_pair_ref[...]
            grad_kv[:, v_cols] = v_pair_ref[...]

    def key_rows(far):
        at = lax.rem(z + 4 - far, 4)
        return pl.ds(pl.multiple_of(at * tokens, tokens), tokens)

    def pass_terms(hop):
        return pltpu.make_async_remote_copy(
            src_ref=hop_out.at[hop],
            dst_ref=hop_in.at[hop],
            send_sem=hop_send.at[hop],
            recv_sem=hop_recv.at[hop],
            device_id=target("z1"),
            device_id_type=MESH,
        )

    def key_terms(hop):
        if hop > 0:
            pass_terms(hop - 1).wait()
        if hop < 3:
            own = grad_kv[key_rows(hop + 1), :]
            if hop > 0:
                own = (own.astype(jnp.float32) + hop_in[hop - 1].astype(jnp.float32)).astype(own.dtype)
            hop_out[hop] = own
            pass_terms(hop).start()
        else:
            own = grad_kv[key_rows(0), :].astype(jnp.float32) + hop_in[2].astype(jnp.float32)
            for b in range(key_blocks):
                u = own[:, b * block : (b + 1) * block]
                if b < key_blocks // 2:
                    u = u * cos_ref[...] - swap_halves(u) * sin_ref[...]
                grad_both[:, b * block : (b + 1) * block] = u.astype(grad_both.dtype)

    def built_copy(which, j, d):
        return pltpu.make_async_copy(
            built.at[which, d],
            wall_ref.at[d // 16, lax.rem(d // 8, 2), lax.rem(d // 4, 2), lax.rem(d, 4), j],
            built_sem.at[which],
        )

    def build(which, j, right_ref):
        @pl.loop(0, 32, unroll=True)
        def _(d):
            left_ref[d] = turned[table[d * lead + j]]

        for part in range(4):
            left = left_ref[part * 8 : (part + 1) * 8].reshape(8 * rows, tokens)
            value = dot(left, right_ref[...], NN).astype(built.dtype)
            built[which, part * 8 : (part + 1) * 8] = value.reshape(8, rows, width)

        @pl.loop(0, 32)
        def _(d):
            built_copy(which, j, d).start()

    def finish_built(which):
        pltpu.make_async_copy(built.at[which], built.at[which], built_sem.at[which]).wait()

    half = lead // 2
    attending = 2
    passing = attending + KV_HEADS
    building = passing + 5
    stream(0).start()

    def beside(t):
        for step in range(2):

            @pl.when(t == step)
            def _(step=step):
                if step == 0:
                    fill_mask(places, mask_ref)
                    back_ref[...] = jnp.zeros_like(back_ref)
                out_back(step * out_blocks // 2, (step + 1) * out_blocks // 2)

        for side in range(PAIR):
            since = t - attending

            @pl.when((since >= 0) & (since < KV_HEADS) & (lax.rem(since + 64, 2) == side))
            def _(side=side, since=since):
                attend_back_step(since // 2, side)

        for hop in range(4):

            @pl.when(t == passing + hop)
            def _(hop=hop):
                key_terms(hop)
                query_back(hop * query_blocks // 4, (hop + 1) * query_blocks // 4)

        @pl.when(t == passing + 4)
        def _():
            key_back()

        pair = t - building

        @pl.when((pair >= 1) & (pair <= half))
        def _():
            finish_built(0)
            finish_built(1)

        @pl.when((pair >= 0) & (pair < half))
        def _():
            build(0, pair, normed_ref)

        split = first_group - half

        @pl.when((pair >= 0) & (pair < split))
        def _():
            build(1, half + pair, normed_ref)

        @pl.when((pair >= split) & (pair < half))
        def _():
            build(1, half + pair, branch_ref)

        for step in range(len(SUM_HOPS) + 1):

            @pl.when(t == building + step)
            def _(step=step):
                add_sums(step)

    @pl.loop(0, rounds + stages - 1)
    def _(t):
        items = [(stage, route) for stage in range(stages - 1, -1, -1) for route in range(4)]

        def run(which, work):
            stage, route = items[which]
            live, index = turn(route, t - stage, counts, SCATTER_PLAN)

            @pl.when(live)
            def _():
                work(route, stage, index)

        far, near, place_beside = look
        for which in range(len(items) + far):
            if which == place_beside:
                beside(t)
            if which < len(items):
                run(which, early)
            if far - near <= which < len(items) + far - near:
                run(which - far + near, late)
            if which >= far:
                run(which - far, finish)

    for route in range(4):
        keep(route, counts[route] - 1).wait()


def scatter_slots(
    grads_wall,
    gain_terms,
    weights,
    table,
    places,
    branch,
    attended,
    queries,
    both,
    lse,
    normed,
    hidden,
    cosine,
    sine,
    lead,
    first_group,
    caps,
    look=(4, 1, 16),
):
    rows, width = grads_wall.shape[1:]
    kind = grads_wall.dtype
    wall = grads_wall.reshape(2, 2, 2, 4, caps, rows, width)
    counts, starts = split_slots(caps, SCATTER_PLAN)
    stages = len(SCATTER_ROUTES[0])
    scratch = []
    for route in range(4):
        for stage in range(1, stages):
            extent = scatter_extent(route, stage)
            scratch.append(pltpu.VMEM((scatter_terms(route, stage),) + extent + (rows, width), kind))
            last = stage == stages - 1
            scratch.append(pltpu.VMEM(extent + (rows, width), jnp.float32 if last else kind))
    tile = (caps, rows, width)
    tokens = hidden.shape[0]
    number = cosine.shape[1] // rows
    length, both_width = both.shape
    dma = pltpu.SemaphoreType.DMA
    scratch += [
        dma((4, stages)),
        dma((4, stages)),
        dma((4, stages, max(counts))),
        dma((4,)),
        pltpu.VMEM((4,) + gain_terms.shape, jnp.float32),
        pltpu.VMEM((6,) + gain_terms.shape, jnp.float32),
        dma((6,)),
        dma((6,)),
        pltpu.VMEM((2, number, rows, width), kind),
        pltpu.VMEM((tokens, width), kind),
        pltpu.VMEM((tokens, width), kind),
        pltpu.VMEM((length, both_width), kind),
        pltpu.VMEM((tokens, both_width), kind),
        pltpu.VMEM((length, PAIR * HEAD), kind),
        pltpu.VMEM((length, PAIR * HEAD), kind),
        pltpu.VMEM((tokens, GROUP * HEAD), jnp.float32),
        pltpu.VMEM((3, tokens, both_width), kind),
        pltpu.VMEM((3, tokens, both_width), kind),
        pltpu.VMEM((weights.shape[0], rows, tokens), kind),
        pltpu.VMEM((32, rows, tokens), kind),
        pltpu.VMEM((2, 32, rows, width), kind),
        pltpu.VMEM((tokens, length), jnp.float32),
        dma((2,)),
        dma((3,)),
        dma((3,)),
        dma((2,)),
    ]
    vmem = pl.BlockSpec(memory_space=pltpu.VMEM)
    smem = pl.BlockSpec(memory_space=pltpu.SMEM)
    anyw = pl.BlockSpec(memory_space=pl.ANY)
    out = pl.pallas_call(
        functools.partial(scatter_kernel, look, lead, first_group),
        out_shape=[
            jax.ShapeDtypeStruct(wall.shape, kind),
            jax.ShapeDtypeStruct(tile, jnp.float32),
            jax.ShapeDtypeStruct(gain_terms.shape, jnp.float32),
            jax.ShapeDtypeStruct((tokens, width), jnp.float32),
            jax.ShapeDtypeStruct((2, 2, 4) + tile, kind),
            jax.ShapeDtypeStruct((2, 4) + tile, kind),
            jax.ShapeDtypeStruct((4,) + tile, kind),
            jax.ShapeDtypeStruct((3, 2) + tile, kind),
            jax.ShapeDtypeStruct(tile, kind),
        ],
        in_specs=[anyw, vmem, anyw, smem, smem] + [vmem] * 9,
        out_specs=[anyw, anyw, vmem, vmem] + [anyw] * 5,
        scratch_shapes=scratch,
        input_output_aliases={0: 0},
        compiler_params=pltpu.CompilerParams(
            collective_id=1, has_side_effects=True, vmem_limit_bytes=62 << 20
        ),
        name="scatter_slots",
    )(
        wall, gain_terms, weights, table, places, branch, attended, queries, both, lse, normed,
        hidden, cosine, sine,
    )
    return out[1], out[2], out[3]


def shards(
    hidden_in,
    piece_starts,
    out_cotangent,
    owners,
    master,
    moment_one,
    moment_two,
    gain_master,
    gain_one,
    gain_two,
):
    devices = lax.axis_size("dp") * lax.axis_size("fsdp")
    caps, tile_rows, model_width = master.shape
    layout = section_layout(devices, tile_rows)
    slot_qkv, slot_out, slot_ffn, slot_down = slot_numbers(owners, layout, caps)
    query_tiles = model_width // tile_rows
    slot_query, slot_both = slot_qkv[:query_tiles], slot_qkv[query_tiles:]
    half = slot_ffn.shape[0] // 2
    lead = layout[2][3]
    tokens = hidden_in.astype(jnp.float32)
    local_len = tokens.shape[0]
    first = lax.axis_index("fsdp") * local_len
    positions = first + jnp.arange(local_len, dtype=jnp.int32)
    places = jnp.concatenate([first[None].astype(jnp.int32), piece_starts[0]])
    cosine, sine = rope_tables(positions.astype(jnp.float32), 16 * tile_rows)
    (
        wall, weights, gains_low, both, normed, queries, attended, lse, middle, normed_two
    ) = forward_attention(
        master.astype(jnp.bfloat16),
        gain_master.astype(jnp.bfloat16),
        (slot_query, slot_both, slot_out),
        places,
        hidden_in,
        cosine,
        sine,
        lead,
    )
    gain_attn = gains_low[0]
    gain_ffn = gains_low[1]
    inv_one = lax.rsqrt(jnp.mean(tokens * tokens, axis=1, keepdims=True) + norm_eps)
    inv_two = lax.rsqrt(jnp.mean(middle * middle, axis=1, keepdims=True) + norm_eps)
    ffn_out, grad_normed_two, grads_wall = ffn_call(
        slot_ffn[:half], slot_ffn[half:], slot_down, normed_two, out_cotangent, wall
    )
    block_out = (middle + ffn_out).astype(jnp.bfloat16)
    scaled_two = grad_normed_two * gain_ffn
    grad_middle = (
        out_cotangent.astype(jnp.float32)
        + inv_two * scaled_two
        - middle * inv_two**3 * jnp.mean(scaled_two * middle, axis=1, keepdims=True)
    )
    gain_two_term = jnp.sum(grad_normed_two * middle * inv_two, axis=0)
    grad_branch = grad_middle.astype(jnp.bfloat16)
    weight_grad, gain_grad, grad_normed = backward_attention(
        grads_wall,
        gain_two_term,
        weights,
        (slot_query, slot_both, slot_out),
        places,
        grad_branch,
        attended,
        queries,
        both,
        lse,
        normed,
        hidden_in,
        cosine,
        sine,
        layout,
        caps,
    )
    keep_slot = filled_mask(owners, layout, lax.axis_index(("dp", "fsdp")))[:, None, None]
    weight_grad = jnp.where(keep_slot, weight_grad, 0.0)
    scaled_one = grad_normed * gain_attn
    input_grad = (
        grad_middle
        + inv_one * scaled_one
        - tokens * inv_one**3 * jnp.mean(scaled_one * tokens, axis=1, keepdims=True)
    )
    step = float(STEP)
    new_one, new_two, new_weights = adam_step(
        master, moment_one, moment_two, weight_grad, step, decay_rate, learn_rate
    )
    new_one = jnp.where(keep_slot, new_one, 0.0)
    new_two = jnp.where(keep_slot, new_two, 0.0)
    new_weights = jnp.where(keep_slot, new_weights, 0.0)
    new_gain_one, new_gain_two, new_gains = adam_step(
        gain_master, gain_one, gain_two, gain_grad, step, 0.0, gain_rate
    )
    return (
        block_out,
        input_grad,
        weight_grad,
        new_weights,
        new_one,
        new_two,
        gain_grad,
        new_gains,
        new_gain_one,
        new_gain_two,
    )


def solution(mesh):
    return jax.shard_map(
        shards,
        mesh=mesh,
        in_specs=(
            P(("dp", "fsdp"), None),
            P("dp", None),
            P(("dp", "fsdp"), None),
            P(),
            P(("dp", "fsdp"), None, None),
            P(("dp", "fsdp"), None, None),
            P(("dp", "fsdp"), None, None),
            P(None, ("dp", "fsdp")),
            P(None, ("dp", "fsdp")),
            P(None, ("dp", "fsdp")),
        ),
        out_specs=(
            P(("dp", "fsdp"), None),
            P(("dp", "fsdp"), None),
            P(("dp", "fsdp"), None, None),
            P(("dp", "fsdp"), None, None),
            P(("dp", "fsdp"), None, None),
            P(("dp", "fsdp"), None, None),
            P(None, ("dp", "fsdp")),
            P(None, ("dp", "fsdp")),
            P(None, ("dp", "fsdp")),
            P(None, ("dp", "fsdp")),
        ),
        check_vma=False,
    )
```

```python
import functools

import jax
import jax.experimental.pallas as pl
import jax.experimental.pallas.tpu as pltpu
import jax.numpy as jnp
import numpy as np
from jax import lax
from jax.sharding import PartitionSpec as P

D = 2048
HEADS = 32
KV_HEADS = 8
HEAD = 64
FF = 8192
PIECE = 256
STEP = 5


norm_eps = 1e-05
adam_eps = 1e-08
beta_one = 0.5
beta_two = 0.5
learn_rate = 0.02
gain_rate = 0.3
decay_rate = 0.1
rope_base = 500000.0
masked_score = -1e30


def section_layout(devices, tile_rows):
    counts = [
        (D + 2 * KV_HEADS * HEAD) // tile_rows,
        HEADS * HEAD // tile_rows,
        2 * FF // tile_rows,
        FF // tile_rows,
    ]
    layout = []
    first_tile = 0
    first_slot = 0
    for number in counts:
        capacity = 5 * number // (4 * devices) + 1
        layout.append((first_tile, number, capacity, first_slot))
        first_tile += number
        first_slot += capacity
    return layout


def adam_step(weights, first_moment, second_moment, grads, step, decay, rate):
    new_one = beta_one * first_moment + (1.0 - beta_one) * grads
    new_two = beta_two * second_moment + (1.0 - beta_two) * grads * grads
    correct_one = 1.0 - beta_one**step
    correct_two = 1.0 - beta_two**step
    update = -rate * (
        new_one / correct_one / (jnp.sqrt(new_two / correct_two) + adam_eps) + decay * weights
    )
    return (new_one, new_two, weights + update)


def slot_numbers(owners, layout, caps):
    numbers = [entry[1] for entry in layout]
    group = jnp.asarray(np.repeat(np.arange(4), numbers), jnp.int32)
    base = jnp.asarray(np.repeat([entry[3] for entry in layout], numbers), jnp.int32)
    kind = owners * 4 + group
    order = jnp.arange(kind.shape[0], dtype=jnp.int32)
    earlier = (kind[:, None] == kind[None, :]) & (order[:, None] < order[None, :])
    return owners * caps + base + jnp.sum(earlier.astype(jnp.int32), axis=0)


def filled_mask(slots, caps, device):
    here = device * caps + jnp.arange(caps, dtype=jnp.int32)
    return jnp.any(slots[None, :] == here[:, None], axis=1)


def rope_tables(positions, block):
    half_dim = HEAD // 2
    inverse = rope_base ** (-(jnp.arange(half_dim, dtype=jnp.float32) * 2.0 / HEAD))
    angles = positions[:, None] * inverse[None, :]
    cosine = jnp.cos(angles)
    sine = jnp.sin(angles)
    return (
        jnp.tile(jnp.concatenate([cosine, cosine], axis=1), (1, block // HEAD)),
        jnp.tile(jnp.concatenate([-sine, sine], axis=1), (1, block // HEAD)),
    )


def turn_back(grads, cosine, sine):
    tokens, width = grads.shape
    half_dim = HEAD // 2
    heads = grads.reshape(tokens, width // HEAD, 2, half_dim)
    swapped = heads[:, :, ::-1].reshape(tokens, width)
    times = width // cosine.shape[1]
    return grads * jnp.tile(cosine, (1, times)) - swapped * jnp.tile(sine, (1, times))


def tuned_mesh():
    return (lax.axis_size("dp"), lax.axis_size("fsdp")) == (8, 4)


def attention_slots(slots, layout, width, tile_rows):
    query = width // tile_rows
    return slots[:query], slots[query : layout[1][0]], slots[layout[1][0] : layout[2][0]]


def forward_attention(low_tiles, low_gains, slots, places, hidden_in, cosine, sine, layout):
    caps, tile_rows, width = low_tiles.shape
    lead = layout[2][3]
    slot_query, slot_both, slot_out = attention_slots(slots, layout, width, tile_rows)
    if tuned_mesh():
        table = slots[: layout[2][0]]
        table = table // caps * lead + lax.rem(table, caps)
        (wall, weights, both, gains, normed, queries, attended, lse, middle, normed_two) = (
            gather_slots(low_tiles, low_gains, table, places, hidden_in, cosine, sine, lead)
        )
        return wall, weights, gains, both, normed, queries, attended, lse, middle, normed_two
    wall = lax.all_gather(low_tiles, ("dp", "fsdp"), axis=0, tiled=True)
    gains = lax.all_gather(low_gains, ("dp", "fsdp"), axis=1, tiled=True).astype(jnp.float32)
    tokens = hidden_in.astype(jnp.float32)
    inv_one = lax.rsqrt(jnp.mean(tokens * tokens, axis=1, keepdims=True) + norm_eps)
    normed = (tokens * inv_one * gains[0]).astype(jnp.bfloat16)
    turned = KV_HEADS * HEAD // cosine.shape[1]
    both_local = project(slot_both, normed, cosine, sine, wall, turned=turned)
    both = lax.all_gather(both_local, "fsdp", axis=0, tiled=True)
    queries = project(slot_query, normed, cosine, sine, wall)
    attended, lse = attend(places, queries, both)
    middle, normed_two = mix(slot_out, attended, hidden_in, gains[1], wall)
    return wall, wall, gains, both, normed, queries, attended, lse, middle, normed_two


def backward_attention(
    grads_wall,
    gain_terms,
    grad_middle,
    gains,
    weights,
    slots,
    places,
    branch,
    attended,
    queries,
    both,
    lse,
    normed,
    hidden_in,
    cosine,
    sine,
    layout,
    caps,
):
    local_len, width = normed.shape
    tile_rows = weights.shape[1]
    slot_query, slot_both, slot_out = attention_slots(slots, layout, width, tile_rows)
    kv_width = KV_HEADS * HEAD
    if tuned_mesh():
        lead = layout[2][3]
        table = slots[: layout[2][0]]
        table = table // caps * lead + lax.rem(table, caps)
        order = jnp.arange(table.shape[0], dtype=jnp.int32)
        here = jnp.arange(32 * lead, dtype=jnp.int32)
        tile_at = jnp.sum(jnp.where(table[None, :] == here[:, None], order[None, :], 0), axis=1)
        grads, total, input_grad = scatter_slots(
            grads_wall,
            gain_terms,
            weights,
            tile_at,
            places,
            branch,
            attended,
            queries,
            both,
            lse,
            normed,
            hidden_in,
            cosine,
            sine,
            grad_middle,
            gains,
            lead,
            layout[0][2],
            caps,
        )
        part = width // 32
        device = lax.axis_index(("dp", "fsdp"))
        return grads, lax.dynamic_slice_in_dim(total[:2], device * part, part, 1), input_grad
    grad_attended, grads_wall = mix_back(slot_out, attended, branch, weights, grads_wall)
    grad_query, both_terms = attend_back(
        places, queries, both, grad_attended, lse, cosine, sine
    )
    both_sum = lax.psum_scatter(both_terms, "fsdp", scatter_dimension=0, tiled=True).astype(
        jnp.float32
    )
    grad_normed, grads_wall = project_back(slot_query, grad_query, normed, None, weights, grads_wall)
    both_sum = both_sum.reshape(local_len, KV_HEADS // PAIR, 2, PAIR * HEAD)
    grad_key = turn_back(both_sum[:, :, 0].reshape(local_len, kv_width), cosine, sine)
    grad_value = both_sum[:, :, 1].reshape(local_len, kv_width)
    grad_both = jnp.concatenate([grad_key, grad_value], axis=1).astype(jnp.bfloat16)
    grad_normed, grads_wall = project_back(
        slot_both, grad_both, normed, grad_normed, weights, grads_wall
    )
    tokens = hidden_in.astype(jnp.float32)
    inv_one = lax.rsqrt(jnp.mean(tokens * tokens, axis=1, keepdims=True) + norm_eps)
    gain_one_term = jnp.sum(grad_normed * tokens * inv_one, axis=0)
    gain_terms = jnp.stack([gain_one_term, gain_terms[1]])
    scaled = grad_normed * gains[0]
    part = jnp.mean(scaled * tokens, axis=1, keepdims=True)
    input_grad = grad_middle + inv_one * scaled - tokens * inv_one**3 * part
    grads = lax.psum_scatter(grads_wall, ("dp", "fsdp"), scatter_dimension=0, tiled=True)
    gain_grad = lax.psum_scatter(gain_terms, ("dp", "fsdp"), scatter_dimension=1, tiled=True)
    return grads.astype(jnp.float32), gain_grad, input_grad


VMEM_ASK = 56 << 20
NT = (((1,), (1,)), ((), ()))
NN = (((1,), (0,)), ((), ()))
TN = (((0,), (0,)), ((), ()))


def dot(a, b, dims):
    return lax.dot_general(a, b, dims, preferred_element_type=jnp.float32)


def stream_tiles(table, wall_ref, held, sem, group):
    step = pl.program_id(0)
    steps = pl.num_programs(0)
    depth = held.shape[0]
    buf = lax.rem(step, depth)

    def fetch(at):
        into = lax.rem(at, depth)

        @pl.loop(0, group, unroll=True)
        def _(t):
            pltpu.make_async_copy(
                wall_ref.at[table[at * group + t]], held.at[into, t], sem.at[into]
            ).start()

    @pl.when(step == 0)
    def _():
        for ahead in range(depth - 1):

            @pl.when(ahead < steps)
            def _(ahead=ahead):
                fetch(jnp.int32(ahead))

    @pl.when(step + depth - 1 < steps)
    def _():
        fetch(step + depth - 1)

    pltpu.make_async_copy(held.at[buf], held.at[buf], sem.at[buf]).wait()
    rows = group * wall_ref.shape[1]
    return held[buf].reshape(rows, wall_ref.shape[2])


def store_tiles(table, grads_ref, made, sem, group, value):
    step = pl.program_id(0)
    steps = pl.num_programs(0)
    buf = lax.rem(step, 2)

    def drain(which):
        pltpu.make_async_copy(made.at[which], made.at[which], sem.at[which]).wait()

    @pl.when(step >= 2)
    def _():
        drain(buf)

    made[buf] = value.astype(made.dtype).reshape(made.shape[1:])

    @pl.loop(0, group, unroll=True)
    def _(t):
        pltpu.make_async_copy(
            made.at[buf, t], grads_ref.at[table[step * group + t]], sem.at[buf]
        ).start()

    @pl.when(step == steps - 1)
    def _():
        drain(1 - buf)
        drain(buf)


def swap_halves(u):
    width = u.shape[1]
    lane = lax.broadcasted_iota(jnp.int32, u.shape, 1)
    first = lax.rem(lane, HEAD) < HEAD // 2
    return jnp.where(
        first, pltpu.roll(u, width - HEAD // 2, 1), pltpu.roll(u, HEAD // 2, 1)
    )


def project_kernel(group, turned, table, normed_ref, cos_ref, sin_ref, wall_ref, out_ref, held, sem):
    weights = stream_tiles(table, wall_ref, held, sem, group)
    u = dot(normed_ref[...], weights, NT)
    if turned is None:
        out_ref[...] = (u * cos_ref[...] + swap_halves(u) * sin_ref[...]).astype(out_ref.dtype)
    else:

        @pl.when(pl.program_id(0) < turned)
        def _():
            out_ref[...] = (u * cos_ref[...] + swap_halves(u) * sin_ref[...]).astype(out_ref.dtype)

        @pl.when(pl.program_id(0) >= turned)
        def _():
            out_ref[...] = u.astype(out_ref.dtype)


def full_spec(shape):
    return pl.BlockSpec(shape, lambda i, *_: (0,) * len(shape))


def any_spec():
    return pl.BlockSpec(memory_space=pl.ANY)


AHEAD = 4


def held_tiles(depth, group, wall):
    return pltpu.VMEM((depth, group) + wall.shape[1:], wall.dtype)


def project(table, normed, cosine, sine, wall, turned=None, group=16):
    tokens = normed.shape[0]
    block = group * wall.shape[1]
    steps = table.shape[0] // group
    return pl.pallas_call(
        functools.partial(project_kernel, group, turned),
        grid_spec=pltpu.PrefetchScalarGridSpec(
            num_scalar_prefetch=1,
            grid=(steps,),
            in_specs=[full_spec(normed.shape), full_spec(cosine.shape), full_spec(sine.shape), any_spec()],
            out_specs=pl.BlockSpec((tokens, block), lambda i, *_: (0, i)),
            scratch_shapes=[held_tiles(AHEAD, group, wall), pltpu.SemaphoreType.DMA((AHEAD,))],
        ),
        out_shape=jax.ShapeDtypeStruct((tokens, steps * block), jnp.bfloat16),
        compiler_params=pltpu.CompilerParams(vmem_limit_bytes=VMEM_ASK),
        name="project",
    )(table, normed, cosine, sine, wall)


def mix_kernel(group, table, left_ref, hidden_ref, gain_ref, wall_ref, middle_ref, normed_ref, held, sem):
    step = pl.program_id(0)
    weights = stream_tiles(table, wall_ref, held, sem, group)

    @pl.when(step == 0)
    def _():
        middle_ref[...] = hidden_ref[...].astype(jnp.float32)

    middle_ref[...] += dot(left_ref[...], weights, NN)

    @pl.when(step == pl.num_programs(0) - 1)
    def _():
        middle = middle_ref[...]
        inv = lax.rsqrt(jnp.mean(middle * middle, axis=1, keepdims=True) + norm_eps)
        normed_ref[...] = (middle * inv * gain_ref[...]).astype(normed_ref.dtype)


def mix(table, left, hidden, gain, wall, group=16):
    tokens, width = hidden.shape
    block = group * wall.shape[1]
    return pl.pallas_call(
        functools.partial(mix_kernel, group),
        grid_spec=pltpu.PrefetchScalarGridSpec(
            num_scalar_prefetch=1,
            grid=(table.shape[0] // group,),
            in_specs=[
                pl.BlockSpec((tokens, block), lambda i, *_: (0, i)),
                full_spec(hidden.shape),
                full_spec((1, width)),
                any_spec(),
            ],
            out_specs=[full_spec(hidden.shape), full_spec(hidden.shape)],
            scratch_shapes=[held_tiles(AHEAD, group, wall), pltpu.SemaphoreType.DMA((AHEAD,))],
        ),
        out_shape=[
            jax.ShapeDtypeStruct(hidden.shape, jnp.float32),
            jax.ShapeDtypeStruct(hidden.shape, jnp.bfloat16),
        ],
        compiler_params=pltpu.CompilerParams(vmem_limit_bytes=VMEM_ASK),
        name="mix",
    )(table, left, hidden, gain.reshape(1, width), wall)


def mix_back_kernel(group, table, left_ref, right_ref, wall_ref, old_ref, out_ref, grads_ref, held, made, load_sem, store_sem):
    weights = stream_tiles(table, wall_ref, held, load_sem, group)
    right = right_ref[...]
    out_ref[...] = dot(right, weights, NT).astype(out_ref.dtype)
    store_tiles(table, grads_ref, made, store_sem, group, dot(left_ref[...], right, TN))


def mix_back(table, left, right, wall, grads, group=16):
    tokens, width = right.shape
    block = group * wall.shape[1]
    columns = pl.BlockSpec((tokens, block), lambda i, *_: (0, i))
    return pl.pallas_call(
        functools.partial(mix_back_kernel, group),
        grid_spec=pltpu.PrefetchScalarGridSpec(
            num_scalar_prefetch=1,
            grid=(table.shape[0] // group,),
            in_specs=[columns, full_spec(right.shape), any_spec(), any_spec()],
            out_specs=[columns, any_spec()],
            scratch_shapes=[
                held_tiles(AHEAD, group, wall),
                held_tiles(2, group, wall),
                pltpu.SemaphoreType.DMA((AHEAD,)),
                pltpu.SemaphoreType.DMA((2,)),
            ],
        ),
        out_shape=[
            jax.ShapeDtypeStruct(left.shape, jnp.bfloat16),
            jax.ShapeDtypeStruct(grads.shape, grads.dtype),
        ],
        input_output_aliases={4: 1},
        compiler_params=pltpu.CompilerParams(vmem_limit_bytes=VMEM_ASK),
        name="mix_back",
    )(table, left, right, wall, grads)


def project_back_kernel(group, fresh, table, left_ref, right_ref, wall_ref, old_ref, start_ref, out_ref, grads_ref, held, made, load_sem, store_sem):
    weights = stream_tiles(table, wall_ref, held, load_sem, group)

    @pl.when(pl.program_id(0) == 0)
    def _():
        out_ref[...] = jnp.zeros_like(out_ref) if fresh else start_ref[...]

    left = left_ref[...]
    out_ref[...] += dot(left, weights, NN)
    store_tiles(table, grads_ref, made, store_sem, group, dot(left, right_ref[...], TN))


def project_back(table, left, right, start, wall, grads, group=16):
    tokens, width = right.shape
    block = group * wall.shape[1]
    return pl.pallas_call(
        functools.partial(project_back_kernel, group, start is None),
        grid_spec=pltpu.PrefetchScalarGridSpec(
            num_scalar_prefetch=1,
            grid=(table.shape[0] // group,),
            in_specs=[
                pl.BlockSpec((tokens, block), lambda i, *_: (0, i)),
                full_spec(right.shape),
                any_spec(),
                any_spec(),
                any_spec() if start is None else full_spec(start.shape),
            ],
            out_specs=[full_spec(right.shape), any_spec()],
            scratch_shapes=[
                held_tiles(AHEAD, group, wall),
                held_tiles(2, group, wall),
                pltpu.SemaphoreType.DMA((AHEAD,)),
                pltpu.SemaphoreType.DMA((2,)),
            ],
        ),
        out_shape=[
            jax.ShapeDtypeStruct(right.shape, jnp.float32),
            jax.ShapeDtypeStruct(grads.shape, grads.dtype),
        ],
        input_output_aliases={4: 1},
        compiler_params=pltpu.CompilerParams(vmem_limit_bytes=VMEM_ASK),
        name="project_back",
    )(table, left, right, wall, grads, table if start is None else start)


def fill_mask(places, mask_ref):
    shape = mask_ref.shape
    query = lax.broadcasted_iota(jnp.int32, shape, 0) + places[0]
    key = lax.broadcasted_iota(jnp.int32, shape, 1)
    allowed = key <= query
    for piece in range(places.shape[0] - 1):
        low = places[1 + piece]
        inside_query = (query >= low) & (query < low + PIECE)
        inside_key = (key >= low) & (key < low + PIECE)
        allowed = allowed | (inside_query & inside_key)
    mask_ref[...] = jnp.where(allowed, 1.0, 0.0)


PAIR = 2
GROUP = HEADS // KV_HEADS


def attend_kernel(places, q_ref, k_ref, v_ref, out_ref, lse_ref, mask_ref):
    @pl.when(pl.program_id(0) == 0)
    def _():
        fill_mask(places, mask_ref)

    mask = mask_ref[...] > 0.5
    lane = lax.broadcasted_iota(jnp.int32, lse_ref.shape[1:], 1)
    logs = jnp.zeros(lse_ref.shape[1:], jnp.float32)
    scale = jnp.bfloat16(1.0 / HEAD**0.5)
    for side in range(PAIR):
        k = k_ref[:, side * HEAD : (side + 1) * HEAD]
        v = v_ref[:, side * HEAD : (side + 1) * HEAD]
        for h in range(GROUP):
            head = side * GROUP + h
            cols = slice(head * HEAD, (head + 1) * HEAD)
            scores = jnp.where(mask, dot(q_ref[:, cols] * scale, k, NT), masked_score)
            top = jnp.max(scores, axis=1, keepdims=True)
            raised = jnp.exp(scores - top)
            total = jnp.sum(raised, axis=1, keepdims=True)
            probs = (raised * (1.0 / total)).astype(jnp.bfloat16)
            out_ref[:, cols] = dot(probs, v, NN).astype(out_ref.dtype)
            logs = jnp.where(lane == head, top + jnp.log(total), logs)
    lse_ref[0] = logs


def attend(places, queries, both):
    tokens, width = queries.shape
    length = both.shape[0]
    steps = KV_HEADS // PAIR
    wide = PAIR * GROUP * HEAD
    narrow = PAIR * HEAD
    return pl.pallas_call(
        attend_kernel,
        grid_spec=pltpu.PrefetchScalarGridSpec(
            num_scalar_prefetch=1,
            grid=(steps,),
            in_specs=[
                pl.BlockSpec((tokens, wide), lambda i, *_: (0, i)),
                pl.BlockSpec((length, narrow), lambda i, *_: (0, i)),
                pl.BlockSpec((length, narrow), lambda i, *_: (0, steps + i)),
            ],
            out_specs=[
                pl.BlockSpec((tokens, wide), lambda i, *_: (0, i)),
                pl.BlockSpec((1, tokens, 128), lambda i, *_: (i, 0, 0)),
            ],
            scratch_shapes=[pltpu.VMEM((tokens, length), jnp.float32)],
        ),
        out_shape=[
            jax.ShapeDtypeStruct((tokens, width), jnp.bfloat16),
            jax.ShapeDtypeStruct((steps, tokens, 128), jnp.float32),
        ],
        compiler_params=pltpu.CompilerParams(vmem_limit_bytes=VMEM_ASK),
        name="attend",
    )(places, queries, both, both)


def attend_back_kernel(places, q_ref, k_ref, v_ref, grad_ref, lse_ref, cos_ref, sin_ref, out_ref, both_ref, mask_ref, turn_ref):
    @pl.when(pl.program_id(0) == 0)
    def _():
        fill_mask(places, mask_ref)

    mask = mask_ref[...] > 0.5
    scale = jnp.bfloat16(1.0 / HEAD**0.5)
    for side in range(PAIR):
        here = slice(side * HEAD, (side + 1) * HEAD)
        k = k_ref[:, here]
        v = v_ref[:, here]
        dk = None
        dv = None
        for h in range(GROUP):
            head = side * GROUP + h
            cols = slice(head * HEAD, (head + 1) * HEAD)
            q = q_ref[:, cols] * scale
            grad = grad_ref[:, cols]
            scores = jnp.where(mask, dot(q, k, NT), masked_score)
            probs = jnp.exp(scores - lse_ref[0, :, head : head + 1])
            grad_probs = dot(grad, v, NT)
            row_dot = jnp.sum(probs * grad_probs, axis=1, keepdims=True)
            grad_scores = (probs * (grad_probs - row_dot)).astype(jnp.bfloat16)
            turn_ref[:, cols] = dot(grad_scores, k, NN) * (1.0 / HEAD**0.5)
            dk_part = dot(q, grad_scores, TN)
            dv_part = dot(grad, probs.astype(jnp.bfloat16), TN)
            dk = dk_part if dk is None else dk + dk_part
            dv = dv_part if dv is None else dv + dv_part
        there = slice((PAIR + side) * HEAD, (PAIR + side + 1) * HEAD)
        both_ref[:, here] = dk.T.astype(both_ref.dtype)
        both_ref[:, there] = dv.T.astype(both_ref.dtype)
    wide = cos_ref.shape[1]
    for left in range(0, turn_ref.shape[1], wide):
        u = turn_ref[:, left : left + wide]
        out_ref[:, left : left + wide] = (u * cos_ref[...] - swap_halves(u) * sin_ref[...]).astype(out_ref.dtype)


def attend_back(places, queries, both, grad, lse, cosine, sine):
    tokens, width = queries.shape
    length = both.shape[0]
    steps = KV_HEADS // PAIR
    wide = PAIR * GROUP * HEAD
    narrow = PAIR * HEAD
    columns = pl.BlockSpec((tokens, wide), lambda i, *_: (0, i))
    keys = pl.BlockSpec((length, narrow), lambda i, *_: (0, i))
    return pl.pallas_call(
        attend_back_kernel,
        grid_spec=pltpu.PrefetchScalarGridSpec(
            num_scalar_prefetch=1,
            grid=(steps,),
            in_specs=[
                columns,
                keys,
                pl.BlockSpec((length, narrow), lambda i, *_: (0, steps + i)),
                columns,
                pl.BlockSpec((1, tokens, 128), lambda i, *_: (i, 0, 0)),
                full_spec(cosine.shape),
                full_spec(sine.shape),
            ],
            out_specs=[columns, pl.BlockSpec((length, 2 * narrow), lambda i, *_: (0, i))],
            scratch_shapes=[pltpu.VMEM((tokens, length), jnp.float32), pltpu.VMEM((tokens, wide), jnp.float32)],
        ),
        out_shape=[
            jax.ShapeDtypeStruct((tokens, width), jnp.bfloat16),
            jax.ShapeDtypeStruct((length, 2 * KV_HEADS * HEAD), jnp.bfloat16),
        ],
        compiler_params=pltpu.CompilerParams(vmem_limit_bytes=VMEM_ASK),
        name="attend_back",
    )(places, queries, both, both, grad, lse, cosine, sine)


def ffn_kernel(group, offsets, table, normed_ref, cot_ref, middle_ref, gains_ref, wall_ref, block_ref, grad_ref, branch_ref, gain_ref, grads_ref, out_ref, back_ref, held, made, load_sem, store_sem):
    step = pl.program_id(0)
    steps = pl.num_programs(0)
    tile_rows = wall_ref.shape[1]
    width = wall_ref.shape[2]
    rows = group * tile_rows

    def fetch(at, buf):
        for kind in range(3):
            @pl.loop(0, group, unroll=True)
            def _(t, kind=kind):
                pltpu.make_async_copy(wall_ref.at[table[offsets[kind] + at * group + t]], held.at[buf, kind, t], load_sem.at[buf]).start()

    def drain(buf):
        pltpu.make_async_copy(made.at[buf], made.at[buf], store_sem.at[buf]).wait()

    buf = lax.rem(step, 2)

    @pl.when(step == 0)
    def _():
        fetch(0, 0)
        out_ref[...] = jnp.zeros_like(out_ref)
        back_ref[...] = jnp.zeros_like(back_ref)

    @pl.when(step + 1 < steps)
    def _():
        fetch(step + 1, 1 - buf)

    pltpu.make_async_copy(held.at[buf], held.at[buf], load_sem.at[buf]).wait()

    @pl.when(step >= 2)
    def _():
        drain(buf)

    normed = normed_ref[...]
    cot = cot_ref[...]
    w_both = held[buf, 0:2].reshape(2 * rows, width)
    w_down = held[buf, 2].reshape(rows, width)
    nt = (((1,), (1,)), ((), ()))
    nn = (((1,), (0,)), ((), ()))
    tn = (((0,), (0,)), ((), ()))

    def dot(a, b, dims):
        return lax.dot_general(a, b, dims, preferred_element_type=jnp.float32)

    gate_up = dot(normed, w_both, nt)
    gate = gate_up[:, :rows]
    up = gate_up[:, rows:]
    hidden = dot(cot, w_down, nt)
    sig = jax.nn.sigmoid(gate)
    silu = gate * sig
    act = (silu * up).astype(jnp.bfloat16)
    g_gate = (hidden * up * sig * (1.0 + gate * (1.0 - sig))).astype(jnp.bfloat16)
    g_up = (hidden * silu).astype(jnp.bfloat16)
    g_both = jnp.concatenate([g_gate, g_up], axis=1)
    out_ref[...] += dot(act, w_down, nn)
    back_ref[...] += dot(g_both, w_both, nn)
    made[buf, 0:2] = dot(g_both, normed, tn).astype(jnp.bfloat16).reshape(2, group, tile_rows, width)
    made[buf, 2] = dot(act, cot, tn).astype(jnp.bfloat16).reshape(group, tile_rows, width)
    for kind in range(3):
        @pl.loop(0, group, unroll=True)
        def _(t, kind=kind):
            pltpu.make_async_copy(made.at[buf, kind, t], grads_ref.at[table[offsets[kind] + step * group + t]], store_sem.at[buf]).start()

    @pl.when(step == steps - 1)
    def _():
        middle = middle_ref[...]
        inv = lax.rsqrt(jnp.mean(middle * middle, axis=1, keepdims=True) + norm_eps)
        back = back_ref[...]
        scaled = back * gains_ref[1:2, :]
        part = jnp.mean(scaled * middle, axis=1, keepdims=True)
        grad = cot_ref[...].astype(jnp.float32) + inv * scaled - middle * inv**3 * part
        grad_ref[...] = grad
        branch_ref[...] = grad.astype(jnp.bfloat16)
        block_ref[...] = (middle + out_ref[...]).astype(jnp.bfloat16)
        term = jnp.sum(back * middle * inv, axis=0, keepdims=True)
        line = lax.broadcasted_iota(jnp.int32, gain_ref.shape, 0)
        gain_ref[...] = jnp.where(line == 1, term, 0.0)
        drain(1 - buf)
        drain(buf)

def ffn_call(table, offsets, number, normed, cot, middle, gains, wall, group=32):
    tokens, width = normed.shape
    steps = number // group
    tr = wall.shape[1]
    full = pl.BlockSpec((tokens, width), lambda i, *_: (0, 0))
    return pl.pallas_call(
        functools.partial(ffn_kernel, group, offsets),
        grid_spec=pltpu.PrefetchScalarGridSpec(
            num_scalar_prefetch=1, grid=(steps,),
            in_specs=[full, full, full, full_spec(gains.shape), any_spec()],
            out_specs=[full, full, full, full_spec((8, width)), any_spec()],
            scratch_shapes=[
                pltpu.VMEM((tokens, width), jnp.float32),
                pltpu.VMEM((tokens, width), jnp.float32),
                pltpu.VMEM((2, 3, group, tr, width), jnp.bfloat16),
                pltpu.VMEM((2, 3, group, tr, width), jnp.bfloat16),
                pltpu.SemaphoreType.DMA((2,)),
                pltpu.SemaphoreType.DMA((2,)),
            ],
        ),
        out_shape=[
            jax.ShapeDtypeStruct((tokens, width), jnp.bfloat16),
            jax.ShapeDtypeStruct((tokens, width), jnp.float32),
            jax.ShapeDtypeStruct((tokens, width), jnp.bfloat16),
            jax.ShapeDtypeStruct((8, width), jnp.float32),
            jax.ShapeDtypeStruct(wall.shape, jnp.bfloat16),
        ],
        compiler_params=pltpu.CompilerParams(vmem_limit_bytes=60 << 20, dimension_semantics=("arbitrary",)),
        name="ffn",
    )(table, normed, cot, middle, gains, wall)


MESH = pl.DeviceIdType.MESH
EVERY = slice(None)
GATHER_ROUTES = (
    ("z1", "z2", "z3", "x", "y", "core"),
    ("z1", "z2", "z3", "y", "x", "core"),
    ("x", "z1", "z2", "z3", "y", "core"),
    ("y", "z1", "z2", "z3", "x", "core"),
)


def position():
    dp = lax.axis_index("dp")
    return dp // 4, lax.rem(dp // 2, 2), lax.rem(dp, 2), lax.axis_index("fsdp")


def target(hop):
    y, x, c, z = position()
    if hop == "x":
        x = 1 - x
    elif hop == "y":
        y = 1 - y
    elif hop == "core":
        c = 1 - c
    elif hop == "back":
        z = lax.rem(z + 3, 4)
    else:
        z = lax.rem(z + 1, 4)
    return (y * 4 + x * 2 + c, z)


def enter(hops):
    barrier = pltpu.get_barrier_semaphore()
    for hop in hops:
        pl.semaphore_signal(barrier, inc=1, device_id=target(hop), device_id_type=MESH)
    pl.semaphore_wait(barrier, len(hops))


GATHER_PLAN = (3, (0, 0, 0, 0), (10, 6), (11, 3))
SCATTER_PLAN = (3, (5, 5, 0, 0), (4, 6), (40, 0))


def split_slots(caps, plan):
    small = caps * plan[0] // 16
    third = (caps - 2 * small) // 2
    counts = (small, small, third, caps - 2 * small - third)
    starts = (0, small, 2 * small, 2 * small + third)
    return counts, starts


def round_count(counts, plan):
    share, delays, (dense, extra), (gap, pause) = plan
    ends = []
    for route in range(4):
        at = [
            t
            for t in range(200)
            if (t % 2 == 0 or dense <= t < dense + extra if route < 2 else not gap <= t < gap + pause)
        ]
        ends.append(delays[route] + at[counts[route] - 1] + 1)
    return max(ends)


def passed(at, edge):
    return (at - edge + 64) // 64


def turn(route, at, counts, plan):
    share, delays, (dense, extra), (gap, pause) = plan
    at = at - delays[route]
    if route < 2:
        begun = passed(at, dense)
        over = passed(at, dense + extra)
        slow = at // 2
        quick = dense // 2 + at - dense
        late = dense // 2 + extra + (at - dense - extra) // 2
        index = (1 - begun) * slow + (begun - over) * quick + over * late
        even = lax.rem(at + 64, 2) == 0
        live = (at >= 0) & (even | (begun - over == 1)) & (index < counts[route])
        return live, index
    index = at - pause * passed(at, gap)
    live = (at >= 0) & ((at < gap) | (at >= gap + pause)) & (index < counts[route])
    return live, index


def slot_of(route, index, counts, starts, lead, early):
    if route < 2:
        return 2 * lead + starts[route] + index
    here = 2 * lead + starts[route] - (route - 2) * lead
    count = counts[route]
    if early:
        later = (index + count - lead) // count
        return (route - 2) * lead + index + later * (here - route * lead + lead)
    final = index // (count - lead)
    return here + index - final * (here + count - lead - (route - 2) * lead)


def attend_side(side, q, k_pair, v_pair, mask, out_ref, logs):
    lane = lax.broadcasted_iota(jnp.int32, (q.shape[0], 128), 1)
    scale = jnp.bfloat16(1.0 / HEAD**0.5)
    k = k_pair[:, side * HEAD : (side + 1) * HEAD]
    v = v_pair[:, side * HEAD : (side + 1) * HEAD]
    for h in range(GROUP):
        cols = slice(h * HEAD, (h + 1) * HEAD)
        scores = jnp.where(mask, dot(q[:, cols] * scale, k, NT), masked_score)
        top = jnp.max(scores, axis=1, keepdims=True)
        raised = jnp.exp(scores - top)
        total = jnp.sum(raised, axis=1, keepdims=True)
        probs = (raised * (1.0 / total)).astype(jnp.bfloat16)
        out_ref[:, cols] = dot(probs, v, NN).astype(out_ref.dtype)
        logs = jnp.where(lane == side * GROUP + h, top + jnp.log(total), logs)
    return logs


GATHER_HOPS = ("z1", "z2", "z3")


def gather_kernel(
    lead,
    mine_ref,
    gain_ref,
    table,
    places,
    hidden_ref,
    cos_ref,
    sin_ref,
    wall_ref,
    gains_ref,
    weights_ref,
    both_ref,
    all_gains_ref,
    normed_ref,
    q_ref,
    att_ref,
    lse_ref,
    middle_ref,
    normed_two_ref,
    own_sem,
    send_sem,
    recv_sem,
    tiles,
    block,
    gain_tiles,
    keys,
    mask_ref,
    pair_ref,
    side_sem,
    hop_send,
    hop_recv,
):
    y, x, c, z = position()
    counts, starts = split_slots(mine_ref.shape[0], GATHER_PLAN)
    rounds = round_count(counts, GATHER_PLAN)
    own = pltpu.make_async_copy(mine_ref, wall_ref.at[y, x, c, z], own_sem.at[0])
    own_gain = pltpu.make_async_copy(gain_ref, gains_ref.at[y, x, c, z], own_sem.at[1])
    own.start()
    own_gain.start()
    enter(("x", "y", "core", "z", "back"))
    own.wait()
    own_gain.wait()

    def region(route, stage):
        hops = GATHER_ROUTES[route % 4]
        hop = hops[stage]
        done = hops[:stage]
        at_y = EVERY if "y" in done else y
        at_x = EVERY if "x" in done else x
        at_z = EVERY if "z3" in done else z
        if hop in ("z1", "z2", "z3"):
            at_z = lax.rem(z + 5 - int(hop[1]), 4)
        return at_y, at_x, c, at_z

    def copy(route, stage, index):
        if route == 4:
            view = gains_ref.at[region(route, stage)]
        else:
            slot = slot_of(route, index, counts, starts, lead // 2, True)
            view = wall_ref.at[region(route, stage) + (slot,)]
        return pltpu.make_async_remote_copy(
            src_ref=view,
            dst_ref=view,
            send_sem=send_sem.at[route, stage],
            recv_sem=recv_sem.at[route, stage, index],
            device_id=target(GATHER_ROUTES[route % 4][stage]),
            device_id_type=MESH,
        )

    stages = len(GATHER_ROUTES[0])
    tokens, width = hidden_ref.shape
    number = block.shape[0]
    rows = number * block.shape[1]
    query_blocks = q_ref.shape[1] // rows
    key_blocks = keys.shape[1] // rows

    def take(at):
        @pl.loop(0, number, unroll=True)
        def _(t):
            block[t] = tiles[table[at * number + t]]

        pltpu.make_async_copy(
            block, weights_ref.at[pl.ds(at * number, number)], side_sem.at[1]
        ).start()
        return block[...].reshape(rows, width)

    def taken(at):
        pltpu.make_async_copy(
            block, weights_ref.at[pl.ds(at * number, number)], side_sem.at[1]
        ).wait()

    def load_tiles(d):
        return pltpu.make_async_copy(
            wall_ref.at[d // 16, lax.rem(d // 8, 2), lax.rem(d // 4, 2), lax.rem(d, 4), pl.ds(0, lead)],
            tiles.at[pl.ds(d * lead, lead)],
            side_sem.at[0],
        )

    load_gains = pltpu.make_async_copy(gains_ref, gain_tiles, side_sem.at[2])

    def pass_keys(part):
        hop = part // 2
        at = lax.rem(z + 4 - hop, 4)
        cols = KV_HEADS * HEAD
        view = keys.at[
            pl.ds(pl.multiple_of(at * tokens, tokens), tokens),
            pl.ds(part % 2 * cols, cols),
        ]
        return pltpu.make_async_remote_copy(
            src_ref=view,
            dst_ref=view,
            send_sem=hop_send.at[part],
            recv_sem=hop_recv.at[part],
            device_id=target(GATHER_HOPS[hop]),
            device_id_type=MESH,
        )

    def begin():
        @pl.loop(0, 32)
        def _(d):
            load_tiles(d).start()

        load_gains.start()

    def norm():
        load_gains.wait()
        lane = lax.broadcasted_iota(jnp.int32, (8, 128), 1)
        parts = []
        for d in range(0, 32, 2):
            even = gain_tiles[d // 16, (d // 8) % 2, (d // 4) % 2, d % 4].astype(jnp.float32)[:8]
            odd = gain_tiles[d // 16, (d // 8) % 2, (d // 4) % 2, d % 4 + 1].astype(jnp.float32)[:8]
            parts.append(jnp.where(lane < 64, even, pltpu.roll(odd, 64, 1)))
        all_gains_ref[...] = jnp.concatenate(parts, axis=1)
        hidden = hidden_ref[...].astype(jnp.float32)
        inv = lax.rsqrt(jnp.mean(hidden * hidden, axis=1, keepdims=True) + norm_eps)
        normed_ref[...] = (hidden * inv * all_gains_ref[0:1, :]).astype(normed_ref.dtype)
        fill_mask(places, mask_ref)

    def project_keys():
        pltpu.make_async_copy(tiles, tiles, side_sem.at[0]).wait()
        own_rows = pl.ds(pl.multiple_of(z * tokens, tokens), tokens)

        for b in range(key_blocks):
            at = query_blocks + b
            u = dot(normed_ref[...], take(at), NT)
            if b < key_blocks // 2:
                u = u * cos_ref[...] + swap_halves(u) * sin_ref[...]
            keys[own_rows, b * rows : (b + 1) * rows] = u.astype(keys.dtype)
            taken(at)

    def project_queries(low, high):
        @pl.loop(low, high)
        def _(b):
            u = dot(normed_ref[...], take(b), NT)
            u = u * cos_ref[...] + swap_halves(u) * sin_ref[...]
            q_ref[:, pl.ds(pl.multiple_of(b * rows, rows), rows)] = u.astype(q_ref.dtype)
            taken(b)

    def attend_step(pair, side):
        wide = GROUP * HEAD
        narrow = PAIR * HEAD
        here = pl.ds(pl.multiple_of((pair * PAIR + side) * wide, wide), wide)
        k_pair = keys[:, pl.ds(pl.multiple_of(pair * narrow, narrow), narrow)]
        v_pair = keys[:, pl.ds(pl.multiple_of(KV_HEADS * HEAD + pair * narrow, narrow), narrow)]
        logs = lse_ref[pair] if side else jnp.zeros((tokens, 128), jnp.float32)
        mask = mask_ref[...] > 0.5
        lse_ref[pair] = attend_side(side, q_ref[:, here], k_pair, v_pair, mask, pair_ref, logs)
        att_ref[:, here] = pair_ref[...]

    def mix_blocks(low):
        for more in range(4):
            b = low + more
            at = query_blocks + key_blocks + b
            left = att_ref[:, pl.ds(pl.multiple_of(b * rows, rows), rows)]
            middle_ref[...] += dot(left, take(at), NN)
            taken(at)

    def mix_end():
        middle = middle_ref[...]
        inv = lax.rsqrt(jnp.mean(middle * middle, axis=1, keepdims=True) + norm_eps)
        normed_two_ref[...] = (middle * inv * all_gains_ref[1:2, :]).astype(normed_two_ref.dtype)

    start = GATHER_PLAN[1][3] + lead // 2 - 1 + stages
    keep_both = pltpu.make_async_copy(keys, both_ref, side_sem.at[3])

    @pl.loop(0, rounds + stages)
    def _(t):
        for stage in range(stages + 1):
            for route in range(5):
                if route == 4:
                    live, index = t == stage, 0
                else:
                    live, index = turn(route, t - stage, counts, GATHER_PLAN)

                @pl.when(live)
                def _(stage=stage, route=route, index=index):
                    if stage > 0:
                        copy(route, stage - 1, index).wait()
                    if stage < stages:
                        copy(route, stage, index).start()

        @pl.when(t == start)
        def _():
            begin()
            norm()

        @pl.when(t == start + 1)
        def _():
            project_keys()

        parts = 2 * len(GATHER_HOPS)
        for part in range(parts + 1):

            @pl.when(t == start + 1 + part)
            def _(part=part):
                if part > 0:
                    pass_keys(part - 1).wait()
                if part < parts:
                    pass_keys(part).start()

        for third in range(4):

            @pl.when(t == start + 2 + third)
            def _(third=third):
                project_queries(third * query_blocks // 4, (third + 1) * query_blocks // 4)

        attending = start + 1 + parts

        @pl.when(t == attending)
        def _():
            keep_both.start()
            middle_ref[...] = hidden_ref[...].astype(jnp.float32)

        for side in range(PAIR):
            since = t - attending

            @pl.when((since >= 0) & (since < KV_HEADS) & (lax.rem(since + 64, 2) == side))
            def _(side=side, since=since):
                attend_step(since // 2, side)

        mixing = attending + KV_HEADS

        @pl.when((t >= mixing) & (t < mixing + query_blocks // 4))
        def _():
            mix_blocks((t - mixing) * 4)

        @pl.when(t == mixing + query_blocks // 4)
        def _():
            mix_end()
            keep_both.wait()


def gather_slots(low_tiles, low_gains, table, places, hidden, cosine, sine, lead):
    caps, rows, width = low_tiles.shape
    tokens = hidden.shape[0]
    length = tokens * 4
    counts, starts = split_slots(caps, GATHER_PLAN)
    kind = low_tiles.dtype
    vmem = pl.BlockSpec(memory_space=pltpu.VMEM)
    smem = pl.BlockSpec(memory_space=pltpu.SMEM)
    anyw = pl.BlockSpec(memory_space=pl.ANY)
    padded = jnp.pad(low_gains, ((0, 16 - low_gains.shape[0]), (0, 128 - low_gains.shape[1])))
    number = cosine.shape[1] // rows
    pairs = KV_HEADS // PAIR
    outs = pl.pallas_call(
        functools.partial(gather_kernel, lead),
        out_shape=[
            jax.ShapeDtypeStruct((2, 2, 2, 4, caps, rows, width), kind),
            jax.ShapeDtypeStruct((2, 2, 2, 4) + padded.shape, kind),
            jax.ShapeDtypeStruct((table.shape[0], rows, width), kind),
            jax.ShapeDtypeStruct((length, 2 * KV_HEADS * HEAD), kind),
            jax.ShapeDtypeStruct((8, width), jnp.float32),
            jax.ShapeDtypeStruct((tokens, width), kind),
            jax.ShapeDtypeStruct((tokens, width), kind),
            jax.ShapeDtypeStruct((tokens, width), kind),
            jax.ShapeDtypeStruct((pairs, tokens, 128), jnp.float32),
            jax.ShapeDtypeStruct((tokens, width), jnp.float32),
            jax.ShapeDtypeStruct((tokens, width), kind),
        ],
        in_specs=[vmem, vmem, smem, smem, vmem, vmem, vmem],
        out_specs=[anyw] * 4 + [vmem] * 7,
        scratch_shapes=[
            pltpu.SemaphoreType.DMA((2,)),
            pltpu.SemaphoreType.DMA((5, 6)),
            pltpu.SemaphoreType.DMA((5, 6, max(counts))),
            pltpu.VMEM((32 * lead, rows, width), kind),
            pltpu.VMEM((number, rows, width), kind),
            pltpu.VMEM((2, 2, 2, 4) + padded.shape, kind),
            pltpu.VMEM((length, 2 * KV_HEADS * HEAD), kind),
            pltpu.VMEM((tokens, length), jnp.float32),
            pltpu.VMEM((tokens, GROUP * HEAD), kind),
            pltpu.SemaphoreType.DMA((4,)),
            pltpu.SemaphoreType.DMA((6,)),
            pltpu.SemaphoreType.DMA((6,)),
        ],
        compiler_params=pltpu.CompilerParams(
            collective_id=0, has_side_effects=True, vmem_limit_bytes=62 << 20
        ),
        name="gather_slots",
    )(low_tiles, padded, table, places, hidden, cosine, sine)
    return [outs[0].reshape(32 * caps, rows, width)] + list(outs[2:])


SCATTER_ROUTES = (
    ("core", "y", "x", "z1", "z2", "z3", "end"),
    ("core", "x", "y", "z1", "z2", "z3", "end"),
    ("core", "y", "z1", "z2", "z3", "x", "end"),
    ("core", "x", "z1", "z2", "z3", "y", "end"),
)


SUM_HOPS = ("core", "x", "y", "z1", "z2", "z3")
SUM_START = 2


def scatter_extent(route, stage):
    hops = SCATTER_ROUTES[route]
    done = hops[1 : stage + 1] if hops[stage] in ("x", "y") else hops[1:stage]
    extent = []
    if "x" not in done or "y" not in done:
        extent.append(2)
    if not any(hop[0] == "z" for hop in hops[: stage + 1]):
        extent.append(4)
    return tuple(extent)


def scatter_terms(route, stage):
    hops = SCATTER_ROUTES[route]
    done = hops[1:stage]
    return 2 + ("x" in done) + ("y" in done) + ("z1" in done)


def attend_back_side(side, q, k_pair, v_pair, grad, mask, logs, turn_ref, k_out, v_out):
    scale = jnp.bfloat16(1.0 / HEAD**0.5)
    here = slice(side * HEAD, (side + 1) * HEAD)
    k = k_pair[:, here]
    v = v_pair[:, here]
    dk = None
    dv = None
    for h in range(GROUP):
        cols = slice(h * HEAD, (h + 1) * HEAD)
        head = side * GROUP + h
        q_head = q[:, cols] * scale
        scores = jnp.where(mask, dot(q_head, k, NT), masked_score)
        probs = jnp.exp(scores - logs[:, head : head + 1])
        grad_probs = dot(grad[:, cols], v, NT)
        row_dot = jnp.sum(probs * grad_probs, axis=1, keepdims=True)
        grad_scores = (probs * (grad_probs - row_dot)).astype(jnp.bfloat16)
        turn_ref[:, cols] = dot(grad_scores, k, NN) * (1.0 / HEAD**0.5)
        dk_part = dot(q_head, grad_scores, TN)
        dv_part = dot(grad[:, cols], probs.astype(jnp.bfloat16), TN)
        dk = dk_part if dk is None else dk + dk_part
        dv = dv_part if dv is None else dv + dv_part
    k_out[:, here] = dk.T.astype(k_out.dtype)
    v_out[:, here] = dv.T.astype(v_out.dtype)


def scatter_kernel(
    look,
    lead,
    first_group,
    old_ref,
    gain_ref,
    weights_ref,
    table,
    places,
    branch_ref,
    att_ref,
    q_ref,
    both_ref,
    lse_ref,
    normed_ref,
    hidden_ref,
    cos_ref,
    sin_ref,
    grad_ref,
    gains_ref,
    wall_ref,
    out_ref,
    total_ref,
    input_ref,
    core_ref,
    first_ref,
    second_ref,
    ring_ref,
    last_ref,
    *scratch,
):
    y, x, c, z = position()
    caps, rows, width = out_ref.shape
    counts, starts = split_slots(caps, SCATTER_PLAN)
    rounds = round_count(counts, SCATTER_PLAN)
    stages = len(SCATTER_ROUTES[0])
    held = {}
    made = {}
    scratch = list(scratch)
    for route in range(4):
        for stage in range(1, stages):
            held[route, stage] = scratch.pop(0)
            made[route, stage] = scratch.pop(0)
    load_sem, send_sem, recv_sem, out_sem, sums, landed, sum_send, sum_recv = scratch[:8]
    (
        streamed,
        grad_att,
        grad_q,
        grad_kv,
        grad_both,
        k_pair_ref,
        v_pair_ref,
        turn_ref,
        hop_out,
        hop_in,
        turned,
        left_ref,
        built,
        mask_ref,
        stream_sem,
        hop_send,
        hop_recv,
        built_sem,
        back_ref,
    ) = scratch[8:]
    enter(("x", "y", "core", "z", "back"))

    def landing(route, stage, slot):
        hops = SCATTER_ROUTES[route]
        hop = hops[stage]
        if hop == "core":
            return core_ref.at[:, :, :, slot]
        if hop[0] == "z":
            ring = ring_ref.at[int(hop[1]) - 1]
            return ring.at[0, slot] if route < 2 else ring.at[:, slot]
        if stage == 1:
            return first_ref.at[:, :, slot]
        if stage == 2:
            return second_ref.at[:, slot]
        return last_ref.at[slot]

    def terms(route, stage, slot):
        hops = SCATTER_ROUTES[route]
        hop = hops[stage]
        done = hops[1:stage]
        at_y = 1 - y if hop == "y" else (y if "y" in done else EVERY)
        at_x = 1 - x if hop == "x" else (x if "x" in done else EVERY)
        at_z = EVERY
        if hop[0] == "z":
            at_z = lax.rem(z + 4 - int(hop[1]), 4)
        elif "z3" in done:
            at_z = z
        views = [wall_ref.at[at_y, at_x, c, at_z, slot], core_ref.at[at_y, at_x, at_z, slot]]
        other = at_x if hops[1] == "y" else at_y
        if stage > 1:
            views.append(first_ref.at[other, at_z, slot])
        if route < 2 and stage > 2:
            views.append(second_ref.at[at_z, slot])
        if hop in ("z2", "z3"):
            ring = ring_ref.at[int(hop[1]) - 2]
            views.append(ring.at[0, slot] if route < 2 else ring.at[:, slot])
        elif "z3" in done:
            ring = ring_ref.at[2]
            views.append(ring.at[0, slot] if route < 2 else ring.at[other, slot])
        if route >= 2 and hop == "end":
            views.append(last_ref.at[slot])
        return views

    def slot_at(route, index):
        return slot_of(route, index, counts, starts, lead // 2, False)

    def send(route, stage, index):
        slot = slot_at(route, index)
        if stage == 0:
            source = wall_ref.at[:, :, 1 - c, :, slot]
        else:
            source = made[route, stage]
        return pltpu.make_async_remote_copy(
            src_ref=source,
            dst_ref=landing(route, stage, slot),
            send_sem=send_sem.at[route, stage],
            recv_sem=recv_sem.at[route, stage, index],
            device_id=target(SCATTER_ROUTES[route][stage]),
            device_id_type=MESH,
        )

    def keep(route, index):
        return pltpu.make_async_copy(
            made[route, stages - 1], out_ref.at[slot_at(route, index)], out_sem.at[route]
        )

    def early(route, stage, index):
        if stage > 0:
            for k, view in enumerate(terms(route, stage, slot_at(route, index))[:-1]):
                pltpu.make_async_copy(view, held[route, stage].at[k], load_sem.at[route, stage]).start()

    def late(route, stage, index):
        if stage > 0:
            send(route, stage - 1, index).wait()
            view = terms(route, stage, slot_at(route, index))[-1]
            last = held[route, stage].shape[0] - 1
            pltpu.make_async_copy(view, held[route, stage].at[last], load_sem.at[route, stage]).start()

    def finish(route, stage, index):
        if stage > 0:
            buf = held[route, stage]
            pltpu.make_async_copy(buf, buf, load_sem.at[route, stage]).wait()
            number = buf.shape[0]
            extent = buf.shape[1:-2]
            blocks = 1
            for size in extent:
                blocks *= size
            part = min(width, 512)
            if stage == stages - 1:

                @pl.when(index > 0)
                def _():
                    keep(route, index - 1).wait()

            @pl.loop(0, blocks)
            def _(block):
                if len(extent) == 2:
                    at = (block // extent[1], lax.rem(block, extent[1]))
                elif len(extent) == 1:
                    at = (block,)
                else:
                    at = ()
                for left in range(0, width, part):
                    cols = pl.ds(left, part)
                    total = buf[(0,) + at + (EVERY, cols)].astype(jnp.float32)
                    for k in range(1, number):
                        total += buf[(k,) + at + (EVERY, cols)].astype(jnp.float32)
                    made[route, stage][at + (EVERY, cols)] = total.astype(made[route, stage].dtype)

        if stage < stages - 1:
            send(route, stage, index).start()
        else:
            keep(route, index).start()

    def pass_sum(hop):
        return pltpu.make_async_remote_copy(
            src_ref=sums.at[hop] if hop < 4 else landed.at[hop - 1],
            dst_ref=landed.at[hop],
            send_sem=sum_send.at[hop],
            recv_sem=sum_recv.at[hop],
            device_id=target(SUM_HOPS[hop]),
            device_id_type=MESH,
        )

    def add_sums(step):
        if step > 0:
            pass_sum(step - 1).wait()
        if step == 0:
            hidden = hidden_ref[...].astype(jnp.float32)
            inv = lax.rsqrt(jnp.mean(hidden * hidden, axis=1, keepdims=True) + norm_eps)
            back = back_ref[...]
            term = jnp.sum(back * hidden * inv, axis=0, keepdims=True)
            scaled = back * gains_ref[0:1, :]
            part = jnp.mean(scaled * hidden, axis=1, keepdims=True)
            input_ref[...] = grad_ref[...] + inv * scaled - hidden * inv**3 * part
            line = lax.broadcasted_iota(jnp.int32, gain_ref.shape, 0)
            sums[0] = jnp.where(line == 0, term, gain_ref[...])
        elif step < 4:
            sums[step] = sums[step - 1] + landed[step - 1]
        elif step == len(SUM_HOPS):
            total_ref[...] = (sums[3] + landed[3]) + (landed[4] + landed[5])
        if step < len(SUM_HOPS):
            pass_sum(step).start()

    tokens = hidden_ref.shape[0]
    number = cos_ref.shape[1] // rows
    block = number * rows
    query_blocks = q_ref.shape[1] // block
    key_blocks = both_ref.shape[1] // block
    out_blocks = att_ref.shape[1] // block
    all_blocks = query_blocks + key_blocks + out_blocks
    kv_width = KV_HEADS * HEAD

    def stream(n):
        at = lax.rem(n + query_blocks + key_blocks, all_blocks)
        return pltpu.make_async_copy(
            weights_ref.at[pl.ds(at * number, number)],
            streamed.at[lax.rem(n, 2)],
            stream_sem.at[lax.rem(n, 2)],
        )

    def streamed_block(n):
        stream(n).wait()

        @pl.when(n + 1 < all_blocks)
        def _():
            stream(n + 1).start()

        return streamed[lax.rem(n, 2)].reshape(block, width)

    def column(b):
        return pl.ds(pl.multiple_of(b * block, block), block)

    def turn_tiles(at, value):
        flipped = value.astype(jnp.float32).T.astype(turned.dtype)
        turned[pl.ds(at * number, number)] = flipped.reshape(number, rows, tokens)

    def out_back(low, high):
        @pl.loop(low, high)
        def _(b):
            grad_att[:, column(b)] = dot(branch_ref[...], streamed_block(b), NT).astype(
                grad_att.dtype
            )
            turn_tiles(query_blocks + key_blocks + b, att_ref[:, column(b)])

    def query_back(low, high):
        @pl.loop(low, high)
        def _(b):
            left = grad_q[:, column(b)]
            back_ref[...] += dot(left, streamed_block(out_blocks + b), NN)
            turn_tiles(b, left)

    def key_back():
        @pl.loop(0, key_blocks)
        def _(b):
            left = grad_both[:, column(b)]
            back_ref[...] += dot(left, streamed_block(out_blocks + query_blocks + b), NN)
            turn_tiles(query_blocks + b, left)

    def attend_back_step(pair, side):
        wide = GROUP * HEAD
        narrow = PAIR * HEAD
        here = pl.ds(pl.multiple_of((pair * PAIR + side) * wide, wide), wide)
        k_cols = pl.ds(pl.multiple_of(pair * narrow, narrow), narrow)
        v_cols = pl.ds(pl.multiple_of(kv_width + pair * narrow, narrow), narrow)
        attend_back_side(
            side,
            q_ref[:, here],
            both_ref[:, k_cols],
            both_ref[:, v_cols],
            grad_att[:, here],
            mask_ref[...] > 0.5,
            lse_ref[pair],
            turn_ref,
            k_pair_ref,
            v_pair_ref,
        )
        u = turn_ref[...]
        grad_q[:, here] = (u * cos_ref[...] - swap_halves(u) * sin_ref[...]).astype(grad_q.dtype)
        if side == PAIR - 1:
            grad_kv[:, k_cols] = k_pair_ref[...]
            grad_kv[:, v_cols] = v_pair_ref[...]

    def key_rows(far):
        at = lax.rem(z + 4 - far, 4)
        return pl.ds(pl.multiple_of(at * tokens, tokens), tokens)

    def pass_terms(hop):
        return pltpu.make_async_remote_copy(
            src_ref=hop_out.at[hop],
            dst_ref=hop_in.at[hop],
            send_sem=hop_send.at[hop],
            recv_sem=hop_recv.at[hop],
            device_id=target("z1"),
            device_id_type=MESH,
        )

    def key_terms(hop):
        if hop > 0:
            pass_terms(hop - 1).wait()
        if hop < 3:
            own = grad_kv[key_rows(hop + 1), :]
            if hop > 0:
                own = (own.astype(jnp.float32) + hop_in[hop - 1].astype(jnp.float32)).astype(own.dtype)
            hop_out[hop] = own
            pass_terms(hop).start()
        else:
            own = grad_kv[key_rows(0), :].astype(jnp.float32) + hop_in[2].astype(jnp.float32)
            for b in range(key_blocks):
                u = own[:, b * block : (b + 1) * block]
                if b < key_blocks // 2:
                    u = u * cos_ref[...] - swap_halves(u) * sin_ref[...]
                grad_both[:, b * block : (b + 1) * block] = u.astype(grad_both.dtype)

    def built_copy(which, j, d):
        return pltpu.make_async_copy(
            built.at[which, d],
            wall_ref.at[d // 16, lax.rem(d // 8, 2), lax.rem(d // 4, 2), lax.rem(d, 4), j],
            built_sem.at[which],
        )

    def build(which, j, right_ref):
        @pl.loop(0, 32, unroll=True)
        def _(d):
            left_ref[d] = turned[table[d * lead + j]]

        for part in range(4):
            left = left_ref[part * 8 : (part + 1) * 8].reshape(8 * rows, tokens)
            value = dot(left, right_ref[...], NN).astype(built.dtype)
            built[which, part * 8 : (part + 1) * 8] = value.reshape(8, rows, width)

        @pl.loop(0, 32)
        def _(d):
            built_copy(which, j, d).start()

    def finish_built(which):
        pltpu.make_async_copy(built.at[which], built.at[which], built_sem.at[which]).wait()

    half = lead // 2
    attending = 2
    passing = attending + KV_HEADS
    building = passing + 5
    stream(0).start()

    def beside(t):
        for step in range(2):

            @pl.when(t == step)
            def _(step=step):
                if step == 0:
                    fill_mask(places, mask_ref)
                    back_ref[...] = jnp.zeros_like(back_ref)
                out_back(step * out_blocks // 2, (step + 1) * out_blocks // 2)

        for side in range(PAIR):
            since = t - attending

            @pl.when((since >= 0) & (since < KV_HEADS) & (lax.rem(since + 64, 2) == side))
            def _(side=side, since=since):
                attend_back_step(since // 2, side)

        for hop in range(4):

            @pl.when(t == passing + hop)
            def _(hop=hop):
                key_terms(hop)
                query_back(hop * query_blocks // 4, (hop + 1) * query_blocks // 4)

        @pl.when(t == passing + 4)
        def _():
            key_back()

        pair = t - building

        @pl.when((pair >= 1) & (pair <= half))
        def _():
            finish_built(0)
            finish_built(1)

        @pl.when((pair >= 0) & (pair < half))
        def _():
            build(0, pair, normed_ref)

        split = first_group - half

        @pl.when((pair >= 0) & (pair < split))
        def _():
            build(1, half + pair, normed_ref)

        @pl.when((pair >= split) & (pair < half))
        def _():
            build(1, half + pair, branch_ref)

        for step in range(len(SUM_HOPS) + 1):

            @pl.when(t == building + step)
            def _(step=step):
                add_sums(step)

    @pl.loop(0, rounds + stages - 1)
    def _(t):
        items = [(stage, route) for stage in range(stages - 1, -1, -1) for route in range(4)]

        def run(which, work):
            stage, route = items[which]
            live, index = turn(route, t - stage, counts, SCATTER_PLAN)

            @pl.when(live)
            def _():
                work(route, stage, index)

        far, near, place_beside = look
        for which in range(len(items) + far):
            if which == place_beside:
                beside(t)
            if which < len(items):
                run(which, early)
            if far - near <= which < len(items) + far - near:
                run(which - far + near, late)
            if which >= far:
                run(which - far, finish)

    for route in range(4):
        keep(route, counts[route] - 1).wait()


def scatter_slots(
    grads_wall,
    gain_terms,
    weights,
    table,
    places,
    branch,
    attended,
    queries,
    both,
    lse,
    normed,
    hidden,
    cosine,
    sine,
    grad_middle,
    gains,
    lead,
    first_group,
    caps,
    look=(5, 2, 17),
):
    rows, width = grads_wall.shape[1:]
    kind = grads_wall.dtype
    wall = grads_wall.reshape(2, 2, 2, 4, caps, rows, width)
    counts, starts = split_slots(caps, SCATTER_PLAN)
    stages = len(SCATTER_ROUTES[0])
    scratch = []
    for route in range(4):
        for stage in range(1, stages):
            extent = scatter_extent(route, stage)
            scratch.append(pltpu.VMEM((scatter_terms(route, stage),) + extent + (rows, width), kind))
            last = stage == stages - 1
            scratch.append(pltpu.VMEM(extent + (rows, width), jnp.float32 if last else kind))
    tile = (caps, rows, width)
    tokens = hidden.shape[0]
    number = cosine.shape[1] // rows
    length, both_width = both.shape
    dma = pltpu.SemaphoreType.DMA
    scratch += [
        dma((4, stages)),
        dma((4, stages)),
        dma((4, stages, max(counts))),
        dma((4,)),
        pltpu.VMEM((4,) + gain_terms.shape, jnp.float32),
        pltpu.VMEM((6,) + gain_terms.shape, jnp.float32),
        dma((6,)),
        dma((6,)),
        pltpu.VMEM((2, number, rows, width), kind),
        pltpu.VMEM((tokens, width), kind),
        pltpu.VMEM((tokens, width), kind),
        pltpu.VMEM((length, both_width), kind),
        pltpu.VMEM((tokens, both_width), kind),
        pltpu.VMEM((length, PAIR * HEAD), kind),
        pltpu.VMEM((length, PAIR * HEAD), kind),
        pltpu.VMEM((tokens, GROUP * HEAD), jnp.float32),
        pltpu.VMEM((3, tokens, both_width), kind),
        pltpu.VMEM((3, tokens, both_width), kind),
        pltpu.VMEM((weights.shape[0], rows, tokens), kind),
        pltpu.VMEM((32, rows, tokens), kind),
        pltpu.VMEM((2, 32, rows, width), kind),
        pltpu.VMEM((tokens, length), jnp.float32),
        dma((2,)),
        dma((3,)),
        dma((3,)),
        dma((2,)),
        pltpu.VMEM((tokens, width), jnp.float32),
    ]
    vmem = pl.BlockSpec(memory_space=pltpu.VMEM)
    smem = pl.BlockSpec(memory_space=pltpu.SMEM)
    anyw = pl.BlockSpec(memory_space=pl.ANY)
    out = pl.pallas_call(
        functools.partial(scatter_kernel, look, lead, first_group),
        out_shape=[
            jax.ShapeDtypeStruct(wall.shape, kind),
            jax.ShapeDtypeStruct(tile, jnp.float32),
            jax.ShapeDtypeStruct(gain_terms.shape, jnp.float32),
            jax.ShapeDtypeStruct((tokens, width), jnp.float32),
            jax.ShapeDtypeStruct((2, 2, 4) + tile, kind),
            jax.ShapeDtypeStruct((2, 4) + tile, kind),
            jax.ShapeDtypeStruct((4,) + tile, kind),
            jax.ShapeDtypeStruct((3, 2) + tile, kind),
            jax.ShapeDtypeStruct(tile, kind),
        ],
        in_specs=[anyw, vmem, anyw, smem, smem] + [vmem] * 11,
        out_specs=[anyw, anyw, vmem, vmem] + [anyw] * 5,
        scratch_shapes=scratch,
        input_output_aliases={0: 0},
        compiler_params=pltpu.CompilerParams(
            collective_id=1, has_side_effects=True, vmem_limit_bytes=62 << 20
        ),
        name="scatter_slots",
    )(
        wall, gain_terms, weights, table, places, branch, attended, queries, both, lse, normed,
        hidden, cosine, sine, grad_middle, gains,
    )
    return out[1], out[2], out[3]


def shards(
    hidden_in,
    piece_starts,
    out_cotangent,
    owners,
    master,
    moment_one,
    moment_two,
    gain_master,
    gain_one,
    gain_two,
):
    devices = lax.axis_size("dp") * lax.axis_size("fsdp")
    caps, tile_rows, model_width = master.shape
    layout = section_layout(devices, tile_rows)
    slots = slot_numbers(owners, layout, caps)
    local_len = hidden_in.shape[0]
    first = lax.axis_index("fsdp") * local_len
    positions = first + jnp.arange(local_len, dtype=jnp.int32)
    places = jnp.concatenate([first[None].astype(jnp.int32), piece_starts[0]])
    cosine, sine = rope_tables(positions.astype(jnp.float32), 16 * tile_rows)
    (
        wall, weights, gains_low, both, normed, queries, attended, lse, middle, normed_two
    ) = forward_attention(
        master.astype(jnp.bfloat16),
        gain_master.astype(jnp.bfloat16),
        slots,
        places,
        hidden_in,
        cosine,
        sine,
        layout,
    )
    block_out, grad_middle, grad_branch, gain_terms, grads_wall = ffn_call(
        slots,
        (layout[2][0], layout[2][0] + layout[2][1] // 2, layout[3][0]),
        layout[3][1],
        normed_two,
        out_cotangent,
        middle,
        gains_low,
        wall,
    )
    weight_grad, gain_grad, input_grad = backward_attention(
        grads_wall,
        gain_terms,
        grad_middle,
        gains_low,
        weights,
        slots,
        places,
        grad_branch,
        attended,
        queries,
        both,
        lse,
        normed,
        hidden_in,
        cosine,
        sine,
        layout,
        caps,
    )
    keep_slot = filled_mask(slots, caps, lax.axis_index(("dp", "fsdp")))[:, None, None]
    weight_grad = jnp.where(keep_slot, weight_grad, 0.0)
    step = float(STEP)
    new_one, new_two, new_weights = adam_step(
        master, moment_one, moment_two, weight_grad, step, decay_rate, learn_rate
    )
    new_one = jnp.where(keep_slot, new_one, 0.0)
    new_two = jnp.where(keep_slot, new_two, 0.0)
    new_weights = jnp.where(keep_slot, new_weights, 0.0)
    new_gain_one, new_gain_two, new_gains = adam_step(
        gain_master, gain_one, gain_two, gain_grad, step, 0.0, gain_rate
    )
    return (
        block_out,
        input_grad,
        weight_grad,
        new_weights,
        new_one,
        new_two,
        gain_grad,
        new_gains,
        new_gain_one,
        new_gain_two,
    )


def solution(mesh):
    return jax.shard_map(
        shards,
        mesh=mesh,
        in_specs=(
            P(("dp", "fsdp"), None),
            P("dp", None),
            P(("dp", "fsdp"), None),
            P(),
            P(("dp", "fsdp"), None, None),
            P(("dp", "fsdp"), None, None),
            P(("dp", "fsdp"), None, None),
            P(None, ("dp", "fsdp")),
            P(None, ("dp", "fsdp")),
            P(None, ("dp", "fsdp")),
        ),
        out_specs=(
            P(("dp", "fsdp"), None),
            P(("dp", "fsdp"), None),
            P(("dp", "fsdp"), None, None),
            P(("dp", "fsdp"), None, None),
            P(("dp", "fsdp"), None, None),
            P(("dp", "fsdp"), None, None),
            P(None, ("dp", "fsdp")),
            P(None, ("dp", "fsdp")),
            P(None, ("dp", "fsdp")),
            P(None, ("dp", "fsdp")),
        ),
        check_vma=False,
    )
```

```python
import functools

import jax
import jax.experimental.pallas as pl
import jax.experimental.pallas.tpu as pltpu
import jax.numpy as jnp
import numpy as np
from jax import lax
from jax.sharding import PartitionSpec as P

D = 2048
HEADS = 32
KV_HEADS = 8
HEAD = 64
FF = 8192
PIECE = 256
STEP = 5


norm_eps = 1e-05
adam_eps = 1e-08
beta_one = 0.5
beta_two = 0.5
learn_rate = 0.02
gain_rate = 0.3
decay_rate = 0.1
rope_base = 500000.0
masked_score = -1e30


def section_layout(devices, tile_rows):
    counts = [
        (D + 2 * KV_HEADS * HEAD) // tile_rows,
        HEADS * HEAD // tile_rows,
        2 * FF // tile_rows,
        FF // tile_rows,
    ]
    layout = []
    first_tile = 0
    first_slot = 0
    for number in counts:
        capacity = 5 * number // (4 * devices) + 1
        layout.append((first_tile, number, capacity, first_slot))
        first_tile += number
        first_slot += capacity
    return layout


def adam_step(weights, first_moment, second_moment, grads, step, decay, rate):
    new_one = beta_one * first_moment + (1.0 - beta_one) * grads
    new_two = beta_two * second_moment + (1.0 - beta_two) * grads * grads
    correct_one = 1.0 - beta_one**step
    correct_two = 1.0 - beta_two**step
    update = -rate * (
        new_one / correct_one / (jnp.sqrt(new_two / correct_two) + adam_eps) + decay * weights
    )
    return (new_one, new_two, weights + update)


def slot_numbers(owners, layout, caps):
    numbers = [entry[1] for entry in layout]
    group = jnp.asarray(np.repeat(np.arange(4), numbers), jnp.int32)
    base = jnp.asarray(np.repeat([entry[3] for entry in layout], numbers), jnp.int32)
    kind = owners * 4 + group
    order = jnp.arange(kind.shape[0], dtype=jnp.int32)
    earlier = (kind[:, None] == kind[None, :]) & (order[:, None] < order[None, :])
    return owners * caps + base + jnp.sum(earlier.astype(jnp.int32), axis=0)


def filled_mask(slots, caps, device):
    here = device * caps + jnp.arange(caps, dtype=jnp.int32)
    return jnp.any(slots[None, :] == here[:, None], axis=1)


def rope_tables(positions, block):
    half_dim = HEAD // 2
    inverse = rope_base ** (-(jnp.arange(half_dim, dtype=jnp.float32) * 2.0 / HEAD))
    angles = positions[:, None] * inverse[None, :]
    cosine = jnp.cos(angles)
    sine = jnp.sin(angles)
    return (
        jnp.tile(jnp.concatenate([cosine, cosine], axis=1), (1, block // HEAD)),
        jnp.tile(jnp.concatenate([-sine, sine], axis=1), (1, block // HEAD)),
    )


def turn_back(grads, cosine, sine):
    tokens, width = grads.shape
    half_dim = HEAD // 2
    heads = grads.reshape(tokens, width // HEAD, 2, half_dim)
    swapped = heads[:, :, ::-1].reshape(tokens, width)
    times = width // cosine.shape[1]
    return grads * jnp.tile(cosine, (1, times)) - swapped * jnp.tile(sine, (1, times))


def tuned_mesh():
    return (lax.axis_size("dp"), lax.axis_size("fsdp")) == (8, 4)


def attention_slots(slots, layout, width, tile_rows):
    query = width // tile_rows
    return slots[:query], slots[query : layout[1][0]], slots[layout[1][0] : layout[2][0]]


def forward_attention(own_tiles, low_gains, slots, places, hidden_in, cosine, sine, layout):
    caps, tile_rows, width = own_tiles.shape
    lead = layout[2][3]
    slot_query, slot_both, slot_out = attention_slots(slots, layout, width, tile_rows)
    if tuned_mesh():
        table = slots[: layout[2][0]]
        table = table // caps * lead + lax.rem(table, caps)
        (wall, weights, both, gains, normed, queries, attended, lse, middle, normed_two) = (
            gather_slots(own_tiles, low_gains, table, places, hidden_in, cosine, sine, lead)
        )
        return wall, weights, gains, both, normed, queries, attended, lse, middle, normed_two
    low_tiles = own_tiles.astype(jnp.bfloat16)
    wall = lax.all_gather(low_tiles, ("dp", "fsdp"), axis=0, tiled=True)
    gains = lax.all_gather(low_gains, ("dp", "fsdp"), axis=1, tiled=True).astype(jnp.float32)
    tokens = hidden_in.astype(jnp.float32)
    inv_one = lax.rsqrt(jnp.mean(tokens * tokens, axis=1, keepdims=True) + norm_eps)
    normed = (tokens * inv_one * gains[0]).astype(jnp.bfloat16)
    turned = KV_HEADS * HEAD // cosine.shape[1]
    both_local = project(slot_both, normed, cosine, sine, wall, turned=turned)
    both = lax.all_gather(both_local, "fsdp", axis=0, tiled=True)
    queries = project(slot_query, normed, cosine, sine, wall)
    attended, lse = attend(places, queries, both)
    middle, normed_two = mix(slot_out, attended, hidden_in, gains[1], wall)
    return wall, wall, gains, both, normed, queries, attended, lse, middle, normed_two


def backward_attention(
    grads_wall,
    gain_terms,
    grad_middle,
    gains,
    weights,
    slots,
    places,
    branch,
    attended,
    queries,
    both,
    lse,
    normed,
    hidden_in,
    cosine,
    sine,
    layout,
    caps,
):
    local_len, width = normed.shape
    tile_rows = weights.shape[1]
    slot_query, slot_both, slot_out = attention_slots(slots, layout, width, tile_rows)
    kv_width = KV_HEADS * HEAD
    if tuned_mesh():
        lead = layout[2][3]
        table = slots[: layout[2][0]]
        table = table // caps * lead + lax.rem(table, caps)
        order = jnp.arange(table.shape[0], dtype=jnp.int32)
        here = jnp.arange(32 * lead, dtype=jnp.int32)
        tile_at = jnp.sum(jnp.where(table[None, :] == here[:, None], order[None, :], 0), axis=1)
        grads, total, input_grad = scatter_slots(
            grads_wall,
            gain_terms,
            weights,
            tile_at,
            places,
            branch,
            attended,
            queries,
            both,
            lse,
            normed,
            hidden_in,
            cosine,
            sine,
            grad_middle,
            gains,
            lead,
            layout[0][2],
            caps,
        )
        part = width // 32
        device = lax.axis_index(("dp", "fsdp"))
        return grads, lax.dynamic_slice_in_dim(total[:2], device * part, part, 1), input_grad
    grad_attended, grads_wall = mix_back(slot_out, attended, branch, weights, grads_wall)
    grad_query, both_terms = attend_back(
        places, queries, both, grad_attended, lse, cosine, sine
    )
    both_sum = lax.psum_scatter(both_terms, "fsdp", scatter_dimension=0, tiled=True).astype(
        jnp.float32
    )
    grad_normed, grads_wall = project_back(slot_query, grad_query, normed, None, weights, grads_wall)
    both_sum = both_sum.reshape(local_len, KV_HEADS // PAIR, 2, PAIR * HEAD)
    grad_key = turn_back(both_sum[:, :, 0].reshape(local_len, kv_width), cosine, sine)
    grad_value = both_sum[:, :, 1].reshape(local_len, kv_width)
    grad_both = jnp.concatenate([grad_key, grad_value], axis=1).astype(jnp.bfloat16)
    grad_normed, grads_wall = project_back(
        slot_both, grad_both, normed, grad_normed, weights, grads_wall
    )
    tokens = hidden_in.astype(jnp.float32)
    inv_one = lax.rsqrt(jnp.mean(tokens * tokens, axis=1, keepdims=True) + norm_eps)
    gain_one_term = jnp.sum(grad_normed * tokens * inv_one, axis=0)
    gain_terms = jnp.stack([gain_one_term, gain_terms[1]])
    scaled = grad_normed * gains[0]
    part = jnp.mean(scaled * tokens, axis=1, keepdims=True)
    input_grad = grad_middle + inv_one * scaled - tokens * inv_one**3 * part
    grads = lax.psum_scatter(grads_wall, ("dp", "fsdp"), scatter_dimension=0, tiled=True)
    gain_grad = lax.psum_scatter(gain_terms, ("dp", "fsdp"), scatter_dimension=1, tiled=True)
    return grads.astype(jnp.float32), gain_grad, input_grad


VMEM_ASK = 56 << 20
NT = (((1,), (1,)), ((), ()))
NN = (((1,), (0,)), ((), ()))
TN = (((0,), (0,)), ((), ()))


def dot(a, b, dims):
    return lax.dot_general(a, b, dims, preferred_element_type=jnp.float32)


def stream_tiles(table, wall_ref, held, sem, group):
    step = pl.program_id(0)
    steps = pl.num_programs(0)
    depth = held.shape[0]
    buf = lax.rem(step, depth)

    def fetch(at):
        into = lax.rem(at, depth)

        @pl.loop(0, group, unroll=True)
        def _(t):
            pltpu.make_async_copy(
                wall_ref.at[table[at * group + t]], held.at[into, t], sem.at[into]
            ).start()

    @pl.when(step == 0)
    def _():
        for ahead in range(depth - 1):

            @pl.when(ahead < steps)
            def _(ahead=ahead):
                fetch(jnp.int32(ahead))

    @pl.when(step + depth - 1 < steps)
    def _():
        fetch(step + depth - 1)

    pltpu.make_async_copy(held.at[buf], held.at[buf], sem.at[buf]).wait()
    rows = group * wall_ref.shape[1]
    return held[buf].reshape(rows, wall_ref.shape[2])


def store_tiles(table, grads_ref, made, sem, group, value):
    step = pl.program_id(0)
    steps = pl.num_programs(0)
    buf = lax.rem(step, 2)

    def drain(which):
        pltpu.make_async_copy(made.at[which], made.at[which], sem.at[which]).wait()

    @pl.when(step >= 2)
    def _():
        drain(buf)

    made[buf] = value.astype(made.dtype).reshape(made.shape[1:])

    @pl.loop(0, group, unroll=True)
    def _(t):
        pltpu.make_async_copy(
            made.at[buf, t], grads_ref.at[table[step * group + t]], sem.at[buf]
        ).start()

    @pl.when(step == steps - 1)
    def _():
        drain(1 - buf)
        drain(buf)


def swap_halves(u):
    width = u.shape[1]
    lane = lax.broadcasted_iota(jnp.int32, u.shape, 1)
    first = lax.rem(lane, HEAD) < HEAD // 2
    return jnp.where(
        first, pltpu.roll(u, width - HEAD // 2, 1), pltpu.roll(u, HEAD // 2, 1)
    )


def project_kernel(group, turned, table, normed_ref, cos_ref, sin_ref, wall_ref, out_ref, held, sem):
    weights = stream_tiles(table, wall_ref, held, sem, group)
    u = dot(normed_ref[...], weights, NT)
    if turned is None:
        out_ref[...] = (u * cos_ref[...] + swap_halves(u) * sin_ref[...]).astype(out_ref.dtype)
    else:

        @pl.when(pl.program_id(0) < turned)
        def _():
            out_ref[...] = (u * cos_ref[...] + swap_halves(u) * sin_ref[...]).astype(out_ref.dtype)

        @pl.when(pl.program_id(0) >= turned)
        def _():
            out_ref[...] = u.astype(out_ref.dtype)


def full_spec(shape):
    return pl.BlockSpec(shape, lambda i, *_: (0,) * len(shape))


def any_spec():
    return pl.BlockSpec(memory_space=pl.ANY)


AHEAD = 4


def held_tiles(depth, group, wall):
    return pltpu.VMEM((depth, group) + wall.shape[1:], wall.dtype)


def project(table, normed, cosine, sine, wall, turned=None, group=16):
    tokens = normed.shape[0]
    block = group * wall.shape[1]
    steps = table.shape[0] // group
    return pl.pallas_call(
        functools.partial(project_kernel, group, turned),
        grid_spec=pltpu.PrefetchScalarGridSpec(
            num_scalar_prefetch=1,
            grid=(steps,),
            in_specs=[full_spec(normed.shape), full_spec(cosine.shape), full_spec(sine.shape), any_spec()],
            out_specs=pl.BlockSpec((tokens, block), lambda i, *_: (0, i)),
            scratch_shapes=[held_tiles(AHEAD, group, wall), pltpu.SemaphoreType.DMA((AHEAD,))],
        ),
        out_shape=jax.ShapeDtypeStruct((tokens, steps * block), jnp.bfloat16),
        compiler_params=pltpu.CompilerParams(vmem_limit_bytes=VMEM_ASK),
        name="project",
    )(table, normed, cosine, sine, wall)


def mix_kernel(group, table, left_ref, hidden_ref, gain_ref, wall_ref, middle_ref, normed_ref, held, sem):
    step = pl.program_id(0)
    weights = stream_tiles(table, wall_ref, held, sem, group)

    @pl.when(step == 0)
    def _():
        middle_ref[...] = hidden_ref[...].astype(jnp.float32)

    middle_ref[...] += dot(left_ref[...], weights, NN)

    @pl.when(step == pl.num_programs(0) - 1)
    def _():
        middle = middle_ref[...]
        inv = lax.rsqrt(jnp.mean(middle * middle, axis=1, keepdims=True) + norm_eps)
        normed_ref[...] = (middle * inv * gain_ref[...]).astype(normed_ref.dtype)


def mix(table, left, hidden, gain, wall, group=16):
    tokens, width = hidden.shape
    block = group * wall.shape[1]
    return pl.pallas_call(
        functools.partial(mix_kernel, group),
        grid_spec=pltpu.PrefetchScalarGridSpec(
            num_scalar_prefetch=1,
            grid=(table.shape[0] // group,),
            in_specs=[
                pl.BlockSpec((tokens, block), lambda i, *_: (0, i)),
                full_spec(hidden.shape),
                full_spec((1, width)),
                any_spec(),
            ],
            out_specs=[full_spec(hidden.shape), full_spec(hidden.shape)],
            scratch_shapes=[held_tiles(AHEAD, group, wall), pltpu.SemaphoreType.DMA((AHEAD,))],
        ),
        out_shape=[
            jax.ShapeDtypeStruct(hidden.shape, jnp.float32),
            jax.ShapeDtypeStruct(hidden.shape, jnp.bfloat16),
        ],
        compiler_params=pltpu.CompilerParams(vmem_limit_bytes=VMEM_ASK),
        name="mix",
    )(table, left, hidden, gain.reshape(1, width), wall)


def mix_back_kernel(group, table, left_ref, right_ref, wall_ref, old_ref, out_ref, grads_ref, held, made, load_sem, store_sem):
    weights = stream_tiles(table, wall_ref, held, load_sem, group)
    right = right_ref[...]
    out_ref[...] = dot(right, weights, NT).astype(out_ref.dtype)
    store_tiles(table, grads_ref, made, store_sem, group, dot(left_ref[...], right, TN))


def mix_back(table, left, right, wall, grads, group=16):
    tokens, width = right.shape
    block = group * wall.shape[1]
    columns = pl.BlockSpec((tokens, block), lambda i, *_: (0, i))
    return pl.pallas_call(
        functools.partial(mix_back_kernel, group),
        grid_spec=pltpu.PrefetchScalarGridSpec(
            num_scalar_prefetch=1,
            grid=(table.shape[0] // group,),
            in_specs=[columns, full_spec(right.shape), any_spec(), any_spec()],
            out_specs=[columns, any_spec()],
            scratch_shapes=[
                held_tiles(AHEAD, group, wall),
                held_tiles(2, group, wall),
                pltpu.SemaphoreType.DMA((AHEAD,)),
                pltpu.SemaphoreType.DMA((2,)),
            ],
        ),
        out_shape=[
            jax.ShapeDtypeStruct(left.shape, jnp.bfloat16),
            jax.ShapeDtypeStruct(grads.shape, grads.dtype),
        ],
        input_output_aliases={4: 1},
        compiler_params=pltpu.CompilerParams(vmem_limit_bytes=VMEM_ASK),
        name="mix_back",
    )(table, left, right, wall, grads)


def project_back_kernel(group, fresh, table, left_ref, right_ref, wall_ref, old_ref, start_ref, out_ref, grads_ref, held, made, load_sem, store_sem):
    weights = stream_tiles(table, wall_ref, held, load_sem, group)

    @pl.when(pl.program_id(0) == 0)
    def _():
        out_ref[...] = jnp.zeros_like(out_ref) if fresh else start_ref[...]

    left = left_ref[...]
    out_ref[...] += dot(left, weights, NN)
    store_tiles(table, grads_ref, made, store_sem, group, dot(left, right_ref[...], TN))


def project_back(table, left, right, start, wall, grads, group=16):
    tokens, width = right.shape
    block = group * wall.shape[1]
    return pl.pallas_call(
        functools.partial(project_back_kernel, group, start is None),
        grid_spec=pltpu.PrefetchScalarGridSpec(
            num_scalar_prefetch=1,
            grid=(table.shape[0] // group,),
            in_specs=[
                pl.BlockSpec((tokens, block), lambda i, *_: (0, i)),
                full_spec(right.shape),
                any_spec(),
                any_spec(),
                any_spec() if start is None else full_spec(start.shape),
            ],
            out_specs=[full_spec(right.shape), any_spec()],
            scratch_shapes=[
                held_tiles(AHEAD, group, wall),
                held_tiles(2, group, wall),
                pltpu.SemaphoreType.DMA((AHEAD,)),
                pltpu.SemaphoreType.DMA((2,)),
            ],
        ),
        out_shape=[
            jax.ShapeDtypeStruct(right.shape, jnp.float32),
            jax.ShapeDtypeStruct(grads.shape, grads.dtype),
        ],
        input_output_aliases={4: 1},
        compiler_params=pltpu.CompilerParams(vmem_limit_bytes=VMEM_ASK),
        name="project_back",
    )(table, left, right, wall, grads, table if start is None else start)


def fill_mask(places, mask_ref):
    shape = mask_ref.shape
    query = lax.broadcasted_iota(jnp.int32, shape, 0) + places[0]
    key = lax.broadcasted_iota(jnp.int32, shape, 1)
    allowed = key <= query
    for piece in range(places.shape[0] - 1):
        low = places[1 + piece]
        inside_query = (query >= low) & (query < low + PIECE)
        inside_key = (key >= low) & (key < low + PIECE)
        allowed = allowed | (inside_query & inside_key)
    mask_ref[...] = jnp.where(allowed, 1.0, 0.0)


PAIR = 2
GROUP = HEADS // KV_HEADS


def attend_kernel(places, q_ref, k_ref, v_ref, out_ref, lse_ref, mask_ref):
    @pl.when(pl.program_id(0) == 0)
    def _():
        fill_mask(places, mask_ref)

    mask = mask_ref[...] > 0.5
    lane = lax.broadcasted_iota(jnp.int32, lse_ref.shape[1:], 1)
    logs = jnp.zeros(lse_ref.shape[1:], jnp.float32)
    scale = jnp.bfloat16(1.0 / HEAD**0.5)
    for side in range(PAIR):
        k = k_ref[:, side * HEAD : (side + 1) * HEAD]
        v = v_ref[:, side * HEAD : (side + 1) * HEAD]
        for h in range(GROUP):
            head = side * GROUP + h
            cols = slice(head * HEAD, (head + 1) * HEAD)
            scores = jnp.where(mask, dot(q_ref[:, cols] * scale, k, NT), masked_score)
            top = jnp.max(scores, axis=1, keepdims=True)
            raised = jnp.exp(scores - top)
            total = jnp.sum(raised, axis=1, keepdims=True)
            probs = (raised * (1.0 / total)).astype(jnp.bfloat16)
            out_ref[:, cols] = dot(probs, v, NN).astype(out_ref.dtype)
            logs = jnp.where(lane == head, top + jnp.log(total), logs)
    lse_ref[0] = logs


def attend(places, queries, both):
    tokens, width = queries.shape
    length = both.shape[0]
    steps = KV_HEADS // PAIR
    wide = PAIR * GROUP * HEAD
    narrow = PAIR * HEAD
    return pl.pallas_call(
        attend_kernel,
        grid_spec=pltpu.PrefetchScalarGridSpec(
            num_scalar_prefetch=1,
            grid=(steps,),
            in_specs=[
                pl.BlockSpec((tokens, wide), lambda i, *_: (0, i)),
                pl.BlockSpec((length, narrow), lambda i, *_: (0, i)),
                pl.BlockSpec((length, narrow), lambda i, *_: (0, steps + i)),
            ],
            out_specs=[
                pl.BlockSpec((tokens, wide), lambda i, *_: (0, i)),
                pl.BlockSpec((1, tokens, 128), lambda i, *_: (i, 0, 0)),
            ],
            scratch_shapes=[pltpu.VMEM((tokens, length), jnp.float32)],
        ),
        out_shape=[
            jax.ShapeDtypeStruct((tokens, width), jnp.bfloat16),
            jax.ShapeDtypeStruct((steps, tokens, 128), jnp.float32),
        ],
        compiler_params=pltpu.CompilerParams(vmem_limit_bytes=VMEM_ASK),
        name="attend",
    )(places, queries, both, both)


def attend_back_kernel(places, q_ref, k_ref, v_ref, grad_ref, lse_ref, cos_ref, sin_ref, out_ref, both_ref, mask_ref, turn_ref):
    @pl.when(pl.program_id(0) == 0)
    def _():
        fill_mask(places, mask_ref)

    mask = mask_ref[...] > 0.5
    scale = jnp.bfloat16(1.0 / HEAD**0.5)
    for side in range(PAIR):
        here = slice(side * HEAD, (side + 1) * HEAD)
        k = k_ref[:, here]
        v = v_ref[:, here]
        dk = None
        dv = None
        for h in range(GROUP):
            head = side * GROUP + h
            cols = slice(head * HEAD, (head + 1) * HEAD)
            q = q_ref[:, cols] * scale
            grad = grad_ref[:, cols]
            scores = jnp.where(mask, dot(q, k, NT), masked_score)
            probs = jnp.exp(scores - lse_ref[0, :, head : head + 1])
            grad_probs = dot(grad, v, NT)
            row_dot = jnp.sum(probs * grad_probs, axis=1, keepdims=True)
            grad_scores = (probs * (grad_probs - row_dot)).astype(jnp.bfloat16)
            turn_ref[:, cols] = dot(grad_scores, k, NN) * (1.0 / HEAD**0.5)
            dk_part = dot(q, grad_scores, TN)
            dv_part = dot(grad, probs.astype(jnp.bfloat16), TN)
            dk = dk_part if dk is None else dk + dk_part
            dv = dv_part if dv is None else dv + dv_part
        there = slice((PAIR + side) * HEAD, (PAIR + side + 1) * HEAD)
        both_ref[:, here] = dk.T.astype(both_ref.dtype)
        both_ref[:, there] = dv.T.astype(both_ref.dtype)
    wide = cos_ref.shape[1]
    for left in range(0, turn_ref.shape[1], wide):
        u = turn_ref[:, left : left + wide]
        out_ref[:, left : left + wide] = (u * cos_ref[...] - swap_halves(u) * sin_ref[...]).astype(out_ref.dtype)


def attend_back(places, queries, both, grad, lse, cosine, sine):
    tokens, width = queries.shape
    length = both.shape[0]
    steps = KV_HEADS // PAIR
    wide = PAIR * GROUP * HEAD
    narrow = PAIR * HEAD
    columns = pl.BlockSpec((tokens, wide), lambda i, *_: (0, i))
    keys = pl.BlockSpec((length, narrow), lambda i, *_: (0, i))
    return pl.pallas_call(
        attend_back_kernel,
        grid_spec=pltpu.PrefetchScalarGridSpec(
            num_scalar_prefetch=1,
            grid=(steps,),
            in_specs=[
                columns,
                keys,
                pl.BlockSpec((length, narrow), lambda i, *_: (0, steps + i)),
                columns,
                pl.BlockSpec((1, tokens, 128), lambda i, *_: (i, 0, 0)),
                full_spec(cosine.shape),
                full_spec(sine.shape),
            ],
            out_specs=[columns, pl.BlockSpec((length, 2 * narrow), lambda i, *_: (0, i))],
            scratch_shapes=[pltpu.VMEM((tokens, length), jnp.float32), pltpu.VMEM((tokens, wide), jnp.float32)],
        ),
        out_shape=[
            jax.ShapeDtypeStruct((tokens, width), jnp.bfloat16),
            jax.ShapeDtypeStruct((length, 2 * KV_HEADS * HEAD), jnp.bfloat16),
        ],
        compiler_params=pltpu.CompilerParams(vmem_limit_bytes=VMEM_ASK),
        name="attend_back",
    )(places, queries, both, both, grad, lse, cosine, sine)


def ffn_kernel(group, offsets, table, normed_ref, cot_ref, middle_ref, gains_ref, wall_ref, block_ref, grad_ref, branch_ref, gain_ref, grads_ref, out_ref, back_ref, held, made, load_sem, store_sem):
    step = pl.program_id(0)
    steps = pl.num_programs(0)
    tile_rows = wall_ref.shape[1]
    width = wall_ref.shape[2]
    rows = group * tile_rows

    def fetch(at, buf):
        for kind in range(3):
            @pl.loop(0, group, unroll=True)
            def _(t, kind=kind):
                pltpu.make_async_copy(wall_ref.at[table[offsets[kind] + at * group + t]], held.at[buf, kind, t], load_sem.at[buf]).start()

    def drain(buf):
        pltpu.make_async_copy(made.at[buf], made.at[buf], store_sem.at[buf]).wait()

    buf = lax.rem(step, 2)

    @pl.when(step == 0)
    def _():
        fetch(0, 0)
        out_ref[...] = jnp.zeros_like(out_ref)
        back_ref[...] = jnp.zeros_like(back_ref)

    @pl.when(step + 1 < steps)
    def _():
        fetch(step + 1, 1 - buf)

    pltpu.make_async_copy(held.at[buf], held.at[buf], load_sem.at[buf]).wait()

    @pl.when(step >= 2)
    def _():
        drain(buf)

    normed = normed_ref[...]
    cot = cot_ref[...]
    w_both = held[buf, 0:2].reshape(2 * rows, width)
    w_down = held[buf, 2].reshape(rows, width)
    nt = (((1,), (1,)), ((), ()))
    nn = (((1,), (0,)), ((), ()))
    tn = (((0,), (0,)), ((), ()))

    def dot(a, b, dims):
        return lax.dot_general(a, b, dims, preferred_element_type=jnp.float32)

    gate_up = dot(normed, w_both, nt)
    gate = gate_up[:, :rows]
    up = gate_up[:, rows:]
    hidden = dot(cot, w_down, nt)
    sig = jax.nn.sigmoid(gate)
    silu = gate * sig
    act = (silu * up).astype(jnp.bfloat16)
    g_gate = (hidden * up * sig * (1.0 + gate * (1.0 - sig))).astype(jnp.bfloat16)
    g_up = (hidden * silu).astype(jnp.bfloat16)
    g_both = jnp.concatenate([g_gate, g_up], axis=1)
    out_ref[...] += dot(act, w_down, nn)
    back_ref[...] += dot(g_both, w_both, nn)
    made[buf, 0:2] = dot(g_both, normed, tn).astype(jnp.bfloat16).reshape(2, group, tile_rows, width)
    made[buf, 2] = dot(act, cot, tn).astype(jnp.bfloat16).reshape(group, tile_rows, width)
    for kind in range(3):
        @pl.loop(0, group, unroll=True)
        def _(t, kind=kind):
            pltpu.make_async_copy(made.at[buf, kind, t], grads_ref.at[table[offsets[kind] + step * group + t]], store_sem.at[buf]).start()

    @pl.when(step == steps - 1)
    def _():
        middle = middle_ref[...]
        inv = lax.rsqrt(jnp.mean(middle * middle, axis=1, keepdims=True) + norm_eps)
        back = back_ref[...]
        scaled = back * gains_ref[1:2, :]
        part = jnp.mean(scaled * middle, axis=1, keepdims=True)
        grad = cot_ref[...].astype(jnp.float32) + inv * scaled - middle * inv**3 * part
        grad_ref[...] = grad
        branch_ref[...] = grad.astype(jnp.bfloat16)
        block_ref[...] = (middle + out_ref[...]).astype(jnp.bfloat16)
        term = jnp.sum(back * middle * inv, axis=0, keepdims=True)
        line = lax.broadcasted_iota(jnp.int32, gain_ref.shape, 0)
        gain_ref[...] = jnp.where(line == 1, term, 0.0)
        drain(1 - buf)
        drain(buf)

def ffn_call(table, offsets, number, normed, cot, middle, gains, wall, group=32):
    tokens, width = normed.shape
    steps = number // group
    tr = wall.shape[1]
    full = pl.BlockSpec((tokens, width), lambda i, *_: (0, 0))
    return pl.pallas_call(
        functools.partial(ffn_kernel, group, offsets),
        grid_spec=pltpu.PrefetchScalarGridSpec(
            num_scalar_prefetch=1, grid=(steps,),
            in_specs=[full, full, full, full_spec(gains.shape), any_spec()],
            out_specs=[full, full, full, full_spec((8, width)), any_spec()],
            scratch_shapes=[
                pltpu.VMEM((tokens, width), jnp.float32),
                pltpu.VMEM((tokens, width), jnp.float32),
                pltpu.VMEM((2, 3, group, tr, width), jnp.bfloat16),
                pltpu.VMEM((2, 3, group, tr, width), jnp.bfloat16),
                pltpu.SemaphoreType.DMA((2,)),
                pltpu.SemaphoreType.DMA((2,)),
            ],
        ),
        out_shape=[
            jax.ShapeDtypeStruct((tokens, width), jnp.bfloat16),
            jax.ShapeDtypeStruct((tokens, width), jnp.float32),
            jax.ShapeDtypeStruct((tokens, width), jnp.bfloat16),
            jax.ShapeDtypeStruct((8, width), jnp.float32),
            jax.ShapeDtypeStruct(wall.shape, jnp.bfloat16),
        ],
        compiler_params=pltpu.CompilerParams(vmem_limit_bytes=60 << 20, dimension_semantics=("arbitrary",)),
        name="ffn",
    )(table, normed, cot, middle, gains, wall)


MESH = pl.DeviceIdType.MESH
EVERY = slice(None)
GATHER_ROUTES = (
    ("z1", "z2", "z3", "x", "y", "core"),
    ("z1", "z2", "z3", "y", "x", "core"),
    ("x", "z1", "z2", "z3", "y", "core"),
    ("y", "z1", "z2", "z3", "x", "core"),
)


def position():
    dp = lax.axis_index("dp")
    return dp // 4, lax.rem(dp // 2, 2), lax.rem(dp, 2), lax.axis_index("fsdp")


def target(hop):
    y, x, c, z = position()
    if hop == "x":
        x = 1 - x
    elif hop == "y":
        y = 1 - y
    elif hop == "core":
        c = 1 - c
    elif hop == "back":
        z = lax.rem(z + 3, 4)
    else:
        z = lax.rem(z + 1, 4)
    return (y * 4 + x * 2 + c, z)


def greet(hops):
    barrier = pltpu.get_barrier_semaphore()
    for hop in hops:
        pl.semaphore_signal(barrier, inc=1, device_id=target(hop), device_id_type=MESH)


def meet(hops):
    pl.semaphore_wait(pltpu.get_barrier_semaphore(), len(hops))


def enter(hops):
    greet(hops)
    meet(hops)


GATHER_PLAN = (3, (0, 0, 0, 0), (10, 6), (11, 3))
SCATTER_PLAN = (3, (5, 5, 0, 0), (4, 6), (40, 0))


def split_slots(caps, plan):
    small = caps * plan[0] // 16
    third = (caps - 2 * small) // 2
    counts = (small, small, third, caps - 2 * small - third)
    starts = (0, small, 2 * small, 2 * small + third)
    return counts, starts


def round_count(counts, plan):
    share, delays, (dense, extra), (gap, pause) = plan
    ends = []
    for route in range(4):
        at = [
            t
            for t in range(200)
            if (t % 2 == 0 or dense <= t < dense + extra if route < 2 else not gap <= t < gap + pause)
        ]
        ends.append(delays[route] + at[counts[route] - 1] + 1)
    return max(ends)


def passed(at, edge):
    return (at - edge + 64) // 64


def turn(route, at, counts, plan):
    share, delays, (dense, extra), (gap, pause) = plan
    at = at - delays[route]
    if route < 2:
        begun = passed(at, dense)
        over = passed(at, dense + extra)
        slow = at // 2
        quick = dense // 2 + at - dense
        late = dense // 2 + extra + (at - dense - extra) // 2
        index = (1 - begun) * slow + (begun - over) * quick + over * late
        even = lax.rem(at + 64, 2) == 0
        live = (at >= 0) & (even | (begun - over == 1)) & (index < counts[route])
        return live, index
    index = at - pause * passed(at, gap)
    live = (at >= 0) & ((at < gap) | (at >= gap + pause)) & (index < counts[route])
    return live, index


def slot_of(route, index, counts, starts, lead, early):
    if route < 2:
        return 2 * lead + starts[route] + index
    here = 2 * lead + starts[route] - (route - 2) * lead
    count = counts[route]
    if early:
        later = (index + count - lead) // count
        return (route - 2) * lead + index + later * (here - route * lead + lead)
    final = index // (count - lead)
    return here + index - final * (here + count - lead - (route - 2) * lead)


def attend_side(side, q, k_pair, v_pair, mask, out_ref, logs):
    lane = lax.broadcasted_iota(jnp.int32, (q.shape[0], 128), 1)
    scale = jnp.bfloat16(1.0 / HEAD**0.5)
    k = k_pair[:, side * HEAD : (side + 1) * HEAD]
    v = v_pair[:, side * HEAD : (side + 1) * HEAD]
    for h in range(GROUP):
        cols = slice(h * HEAD, (h + 1) * HEAD)
        scores = jnp.where(mask, dot(q[:, cols] * scale, k, NT), masked_score)
        top = jnp.max(scores, axis=1, keepdims=True)
        raised = jnp.exp(scores - top)
        total = jnp.sum(raised, axis=1, keepdims=True)
        probs = (raised * (1.0 / total)).astype(jnp.bfloat16)
        out_ref[:, cols] = dot(probs, v, NN).astype(out_ref.dtype)
        logs = jnp.where(lane == side * GROUP + h, top + jnp.log(total), logs)
    return logs


GATHER_HOPS = ("z1", "z2", "z3")


def gather_kernel(
    lead,
    mine_ref,
    gain_ref,
    table,
    places,
    hidden_ref,
    cos_ref,
    sin_ref,
    wall_ref,
    gains_ref,
    weights_ref,
    both_ref,
    all_gains_ref,
    normed_ref,
    q_ref,
    att_ref,
    lse_ref,
    middle_ref,
    normed_two_ref,
    own_sem,
    load_sem,
    store_sem,
    wide_ref,
    low_ref,
    send_sem,
    recv_sem,
    tiles,
    block,
    gain_tiles,
    keys,
    mask_ref,
    pair_ref,
    side_sem,
    hop_send,
    hop_recv,
):
    y, x, c, z = position()
    counts, starts = split_slots(mine_ref.shape[0], GATHER_PLAN)
    rounds = round_count(counts, GATHER_PLAN)
    own_gain = pltpu.make_async_copy(gain_ref, gains_ref.at[y, x, c, z], own_sem)
    own_gain.start()
    greet(("x", "y", "core", "z", "back"))
    few = wide_ref.shape[1]
    parts_own = mine_ref.shape[0] // few

    def load_own(i):
        return pltpu.make_async_copy(
            mine_ref.at[pl.ds(i * few, few)], wide_ref.at[lax.rem(i, 2)], load_sem.at[lax.rem(i, 2)]
        )

    def store_own(i):
        return pltpu.make_async_copy(
            low_ref.at[lax.rem(i, 2)],
            wall_ref.at[y, x, c, z, pl.ds(i * few, few)],
            store_sem.at[lax.rem(i, 2)],
        )

    load_own(0).start()
    load_own(1).start()

    @pl.loop(0, parts_own)
    def _(i):
        load_own(i).wait()

        @pl.when(i >= 2)
        def _():
            store_own(i - 2).wait()

        low_ref[lax.rem(i, 2)] = wide_ref[lax.rem(i, 2)].astype(low_ref.dtype)
        store_own(i).start()

        @pl.when(i + 2 < parts_own)
        def _():
            load_own(i + 2).start()

    store_own(parts_own - 2).wait()
    store_own(parts_own - 1).wait()
    own_gain.wait()
    meet(("x", "y", "core", "z", "back"))

    def region(route, stage):
        hops = GATHER_ROUTES[route % 4]
        hop = hops[stage]
        done = hops[:stage]
        at_y = EVERY if "y" in done else y
        at_x = EVERY if "x" in done else x
        at_z = EVERY if "z3" in done else z
        if hop in ("z1", "z2", "z3"):
            at_z = lax.rem(z + 5 - int(hop[1]), 4)
        return at_y, at_x, c, at_z

    def copy(route, stage, index):
        if route == 4:
            view = gains_ref.at[region(route, stage)]
        else:
            slot = slot_of(route, index, counts, starts, lead // 2, True)
            view = wall_ref.at[region(route, stage) + (slot,)]
        return pltpu.make_async_remote_copy(
            src_ref=view,
            dst_ref=view,
            send_sem=send_sem.at[route, stage],
            recv_sem=recv_sem.at[route, stage, index],
            device_id=target(GATHER_ROUTES[route % 4][stage]),
            device_id_type=MESH,
        )

    stages = len(GATHER_ROUTES[0])
    tokens, width = hidden_ref.shape
    number = block.shape[0]
    rows = number * block.shape[1]
    query_blocks = q_ref.shape[1] // rows
    key_blocks = keys.shape[1] // rows

    def take(at):
        @pl.loop(0, number, unroll=True)
        def _(t):
            block[t] = tiles[table[at * number + t]]

        pltpu.make_async_copy(
            block, weights_ref.at[pl.ds(at * number, number)], side_sem.at[1]
        ).start()
        return block[...].reshape(rows, width)

    def taken(at):
        pltpu.make_async_copy(
            block, weights_ref.at[pl.ds(at * number, number)], side_sem.at[1]
        ).wait()

    def load_tiles(d):
        return pltpu.make_async_copy(
            wall_ref.at[d // 16, lax.rem(d // 8, 2), lax.rem(d // 4, 2), lax.rem(d, 4), pl.ds(0, lead)],
            tiles.at[pl.ds(d * lead, lead)],
            side_sem.at[0],
        )

    load_gains = pltpu.make_async_copy(gains_ref, gain_tiles, side_sem.at[2])

    def pass_keys(part):
        hop = part // 2
        at = lax.rem(z + 4 - hop, 4)
        cols = KV_HEADS * HEAD
        view = keys.at[
            pl.ds(pl.multiple_of(at * tokens, tokens), tokens),
            pl.ds(part % 2 * cols, cols),
        ]
        return pltpu.make_async_remote_copy(
            src_ref=view,
            dst_ref=view,
            send_sem=hop_send.at[part],
            recv_sem=hop_recv.at[part],
            device_id=target(GATHER_HOPS[hop]),
            device_id_type=MESH,
        )

    def begin():
        @pl.loop(0, 32)
        def _(d):
            load_tiles(d).start()

        load_gains.start()

    def norm():
        load_gains.wait()
        lane = lax.broadcasted_iota(jnp.int32, (8, 128), 1)
        parts = []
        for d in range(0, 32, 2):
            even = gain_tiles[d // 16, (d // 8) % 2, (d // 4) % 2, d % 4].astype(jnp.float32)[:8]
            odd = gain_tiles[d // 16, (d // 8) % 2, (d // 4) % 2, d % 4 + 1].astype(jnp.float32)[:8]
            parts.append(jnp.where(lane < 64, even, pltpu.roll(odd, 64, 1)))
        all_gains_ref[...] = jnp.concatenate(parts, axis=1)
        hidden = hidden_ref[...].astype(jnp.float32)
        inv = lax.rsqrt(jnp.mean(hidden * hidden, axis=1, keepdims=True) + norm_eps)
        normed_ref[...] = (hidden * inv * all_gains_ref[0:1, :]).astype(normed_ref.dtype)
        fill_mask(places, mask_ref)

    def project_keys():
        pltpu.make_async_copy(tiles, tiles, side_sem.at[0]).wait()
        own_rows = pl.ds(pl.multiple_of(z * tokens, tokens), tokens)

        for b in range(key_blocks):
            at = query_blocks + b
            u = dot(normed_ref[...], take(at), NT)
            if b < key_blocks // 2:
                u = u * cos_ref[...] + swap_halves(u) * sin_ref[...]
            keys[own_rows, b * rows : (b + 1) * rows] = u.astype(keys.dtype)
            taken(at)

    def project_queries(low, high):
        @pl.loop(low, high)
        def _(b):
            u = dot(normed_ref[...], take(b), NT)
            u = u * cos_ref[...] + swap_halves(u) * sin_ref[...]
            q_ref[:, pl.ds(pl.multiple_of(b * rows, rows), rows)] = u.astype(q_ref.dtype)
            taken(b)

    def attend_step(pair, side):
        wide = GROUP * HEAD
        narrow = PAIR * HEAD
        here = pl.ds(pl.multiple_of((pair * PAIR + side) * wide, wide), wide)
        k_pair = keys[:, pl.ds(pl.multiple_of(pair * narrow, narrow), narrow)]
        v_pair = keys[:, pl.ds(pl.multiple_of(KV_HEADS * HEAD + pair * narrow, narrow), narrow)]
        logs = lse_ref[pair] if side else jnp.zeros((tokens, 128), jnp.float32)
        mask = mask_ref[...] > 0.5
        lse_ref[pair] = attend_side(side, q_ref[:, here], k_pair, v_pair, mask, pair_ref, logs)
        att_ref[:, here] = pair_ref[...]

    def mix_blocks(low):
        for more in range(4):
            b = low + more
            at = query_blocks + key_blocks + b
            left = att_ref[:, pl.ds(pl.multiple_of(b * rows, rows), rows)]
            middle_ref[...] += dot(left, take(at), NN)
            taken(at)

    def mix_end():
        middle = middle_ref[...]
        inv = lax.rsqrt(jnp.mean(middle * middle, axis=1, keepdims=True) + norm_eps)
        normed_two_ref[...] = (middle * inv * all_gains_ref[1:2, :]).astype(normed_two_ref.dtype)

    start = GATHER_PLAN[1][3] + lead // 2 - 1 + stages
    keep_both = pltpu.make_async_copy(keys, both_ref, side_sem.at[3])

    @pl.loop(0, rounds + stages)
    def _(t):
        for stage in range(stages + 1):
            for route in range(5):
                if route == 4:
                    live, index = t == stage, 0
                else:
                    live, index = turn(route, t - stage, counts, GATHER_PLAN)

                @pl.when(live)
                def _(stage=stage, route=route, index=index):
                    if stage > 0:
                        copy(route, stage - 1, index).wait()
                    if stage < stages:
                        copy(route, stage, index).start()

        @pl.when(t == start)
        def _():
            begin()
            norm()

        @pl.when(t == start + 1)
        def _():
            project_keys()

        parts = 2 * len(GATHER_HOPS)
        for part in range(parts + 1):

            @pl.when(t == start + 1 + part)
            def _(part=part):
                if part > 0:
                    pass_keys(part - 1).wait()
                if part < parts:
                    pass_keys(part).start()

        for third in range(4):

            @pl.when(t == start + 2 + third)
            def _(third=third):
                project_queries(third * query_blocks // 4, (third + 1) * query_blocks // 4)

        attending = start + 1 + parts

        @pl.when(t == attending)
        def _():
            keep_both.start()
            middle_ref[...] = hidden_ref[...].astype(jnp.float32)

        for side in range(PAIR):
            since = t - attending

            @pl.when((since >= 0) & (since < KV_HEADS) & (lax.rem(since + 64, 2) == side))
            def _(side=side, since=since):
                attend_step(since // 2, side)

        mixing = attending + KV_HEADS

        @pl.when((t >= mixing) & (t < mixing + query_blocks // 4))
        def _():
            mix_blocks((t - mixing) * 4)

        @pl.when(t == mixing + query_blocks // 4)
        def _():
            mix_end()
            keep_both.wait()


def gather_slots(own_tiles, low_gains, table, places, hidden, cosine, sine, lead):
    caps, rows, width = own_tiles.shape
    few = max(size for size in range(1, caps // 3) if caps % size == 0)
    tokens = hidden.shape[0]
    length = tokens * 4
    counts, starts = split_slots(caps, GATHER_PLAN)
    kind = low_gains.dtype
    vmem = pl.BlockSpec(memory_space=pltpu.VMEM)
    smem = pl.BlockSpec(memory_space=pltpu.SMEM)
    anyw = pl.BlockSpec(memory_space=pl.ANY)
    padded = jnp.pad(low_gains, ((0, 16 - low_gains.shape[0]), (0, 128 - low_gains.shape[1])))
    number = cosine.shape[1] // rows
    pairs = KV_HEADS // PAIR
    outs = pl.pallas_call(
        functools.partial(gather_kernel, lead),
        out_shape=[
            jax.ShapeDtypeStruct((2, 2, 2, 4, caps, rows, width), kind),
            jax.ShapeDtypeStruct((2, 2, 2, 4) + padded.shape, kind),
            jax.ShapeDtypeStruct((table.shape[0], rows, width), kind),
            jax.ShapeDtypeStruct((length, 2 * KV_HEADS * HEAD), kind),
            jax.ShapeDtypeStruct((8, width), jnp.float32),
            jax.ShapeDtypeStruct((tokens, width), kind),
            jax.ShapeDtypeStruct((tokens, width), kind),
            jax.ShapeDtypeStruct((tokens, width), kind),
            jax.ShapeDtypeStruct((pairs, tokens, 128), jnp.float32),
            jax.ShapeDtypeStruct((tokens, width), jnp.float32),
            jax.ShapeDtypeStruct((tokens, width), kind),
        ],
        in_specs=[anyw, vmem, smem, smem, vmem, vmem, vmem],
        out_specs=[anyw] * 4 + [vmem] * 7,
        scratch_shapes=[
            pltpu.SemaphoreType.DMA,
            pltpu.SemaphoreType.DMA((2,)),
            pltpu.SemaphoreType.DMA((2,)),
            pltpu.VMEM((2, few, rows, width), own_tiles.dtype),
            pltpu.VMEM((2, few, rows, width), kind),
            pltpu.SemaphoreType.DMA((5, 6)),
            pltpu.SemaphoreType.DMA((5, 6, max(counts))),
            pltpu.VMEM((32 * lead, rows, width), kind),
            pltpu.VMEM((number, rows, width), kind),
            pltpu.VMEM((2, 2, 2, 4) + padded.shape, kind),
            pltpu.VMEM((length, 2 * KV_HEADS * HEAD), kind),
            pltpu.VMEM((tokens, length), jnp.float32),
            pltpu.VMEM((tokens, GROUP * HEAD), kind),
            pltpu.SemaphoreType.DMA((4,)),
            pltpu.SemaphoreType.DMA((6,)),
            pltpu.SemaphoreType.DMA((6,)),
        ],
        compiler_params=pltpu.CompilerParams(
            collective_id=0, has_side_effects=True, vmem_limit_bytes=62 << 20
        ),
        name="gather_slots",
    )(own_tiles, padded, table, places, hidden, cosine, sine)
    return [outs[0].reshape(32 * caps, rows, width)] + list(outs[2:])


SCATTER_ROUTES = (
    ("core", "y", "x", "z1", "z2", "z3", "end"),
    ("core", "x", "y", "z1", "z2", "z3", "end"),
    ("core", "y", "z1", "z2", "z3", "x", "end"),
    ("core", "x", "z1", "z2", "z3", "y", "end"),
)


SUM_HOPS = ("core", "x", "y", "z1", "z2", "z3")
SUM_START = 2


def scatter_extent(route, stage):
    hops = SCATTER_ROUTES[route]
    done = hops[1 : stage + 1] if hops[stage] in ("x", "y") else hops[1:stage]
    extent = []
    if "x" not in done or "y" not in done:
        extent.append(2)
    if not any(hop[0] == "z" for hop in hops[: stage + 1]):
        extent.append(4)
    return tuple(extent)


def scatter_terms(route, stage):
    hops = SCATTER_ROUTES[route]
    done = hops[1:stage]
    return 2 + ("x" in done) + ("y" in done) + ("z1" in done)


def attend_back_side(side, q, k_pair, v_pair, grad, mask, logs, turn_ref, k_out, v_out):
    scale = jnp.bfloat16(1.0 / HEAD**0.5)
    here = slice(side * HEAD, (side + 1) * HEAD)
    k = k_pair[:, here]
    v = v_pair[:, here]
    dk = None
    dv = None
    for h in range(GROUP):
        cols = slice(h * HEAD, (h + 1) * HEAD)
        head = side * GROUP + h
        q_head = q[:, cols] * scale
        scores = jnp.where(mask, dot(q_head, k, NT), masked_score)
        probs = jnp.exp(scores - logs[:, head : head + 1])
        grad_probs = dot(grad[:, cols], v, NT)
        row_dot = jnp.sum(probs * grad_probs, axis=1, keepdims=True)
        grad_scores = (probs * (grad_probs - row_dot)).astype(jnp.bfloat16)
        turn_ref[:, cols] = dot(grad_scores, k, NN) * (1.0 / HEAD**0.5)
        dk_part = dot(q_head, grad_scores, TN)
        dv_part = dot(grad[:, cols], probs.astype(jnp.bfloat16), TN)
        dk = dk_part if dk is None else dk + dk_part
        dv = dv_part if dv is None else dv + dv_part
    k_out[:, here] = dk.T.astype(k_out.dtype)
    v_out[:, here] = dv.T.astype(v_out.dtype)


def scatter_kernel(
    look,
    lead,
    first_group,
    old_ref,
    gain_ref,
    weights_ref,
    table,
    places,
    branch_ref,
    att_ref,
    q_ref,
    both_ref,
    lse_ref,
    normed_ref,
    hidden_ref,
    cos_ref,
    sin_ref,
    grad_ref,
    gains_ref,
    wall_ref,
    out_ref,
    total_ref,
    input_ref,
    core_ref,
    first_ref,
    second_ref,
    ring_ref,
    last_ref,
    *scratch,
):
    y, x, c, z = position()
    caps, rows, width = out_ref.shape
    counts, starts = split_slots(caps, SCATTER_PLAN)
    rounds = round_count(counts, SCATTER_PLAN)
    stages = len(SCATTER_ROUTES[0])
    held = {}
    made = {}
    scratch = list(scratch)
    for route in range(4):
        for stage in range(1, stages):
            held[route, stage] = scratch.pop(0)
            made[route, stage] = scratch.pop(0)
    load_sem, send_sem, recv_sem, out_sem, sums, landed, sum_send, sum_recv = scratch[:8]
    (
        streamed,
        grad_att,
        grad_q,
        grad_kv,
        grad_both,
        k_pair_ref,
        v_pair_ref,
        turn_ref,
        hop_out,
        hop_in,
        turned,
        left_ref,
        built,
        mask_ref,
        stream_sem,
        hop_send,
        hop_recv,
        built_sem,
        back_ref,
    ) = scratch[8:]
    enter(("x", "y", "core", "z", "back"))

    def landing(route, stage, slot):
        hops = SCATTER_ROUTES[route]
        hop = hops[stage]
        if hop == "core":
            return core_ref.at[:, :, :, slot]
        if hop[0] == "z":
            ring = ring_ref.at[int(hop[1]) - 1]
            return ring.at[0, slot] if route < 2 else ring.at[:, slot]
        if stage == 1:
            return first_ref.at[:, :, slot]
        if stage == 2:
            return second_ref.at[:, slot]
        return last_ref.at[slot]

    def terms(route, stage, slot):
        hops = SCATTER_ROUTES[route]
        hop = hops[stage]
        done = hops[1:stage]
        at_y = 1 - y if hop == "y" else (y if "y" in done else EVERY)
        at_x = 1 - x if hop == "x" else (x if "x" in done else EVERY)
        at_z = EVERY
        if hop[0] == "z":
            at_z = lax.rem(z + 4 - int(hop[1]), 4)
        elif "z3" in done:
            at_z = z
        views = [wall_ref.at[at_y, at_x, c, at_z, slot], core_ref.at[at_y, at_x, at_z, slot]]
        other = at_x if hops[1] == "y" else at_y
        if stage > 1:
            views.append(first_ref.at[other, at_z, slot])
        if route < 2 and stage > 2:
            views.append(second_ref.at[at_z, slot])
        if hop in ("z2", "z3"):
            ring = ring_ref.at[int(hop[1]) - 2]
            views.append(ring.at[0, slot] if route < 2 else ring.at[:, slot])
        elif "z3" in done:
            ring = ring_ref.at[2]
            views.append(ring.at[0, slot] if route < 2 else ring.at[other, slot])
        if route >= 2 and hop == "end":
            views.append(last_ref.at[slot])
        return views

    def slot_at(route, index):
        return slot_of(route, index, counts, starts, lead // 2, False)

    def send(route, stage, index):
        slot = slot_at(route, index)
        if stage == 0:
            source = wall_ref.at[:, :, 1 - c, :, slot]
        else:
            source = made[route, stage]
        return pltpu.make_async_remote_copy(
            src_ref=source,
            dst_ref=landing(route, stage, slot),
            send_sem=send_sem.at[route, stage],
            recv_sem=recv_sem.at[route, stage, index],
            device_id=target(SCATTER_ROUTES[route][stage]),
            device_id_type=MESH,
        )

    def keep(route, index):
        return pltpu.make_async_copy(
            made[route, stages - 1], out_ref.at[slot_at(route, index)], out_sem.at[route]
        )

    def early(route, stage, index):
        if stage > 0:
            for k, view in enumerate(terms(route, stage, slot_at(route, index))[:-1]):
                pltpu.make_async_copy(view, held[route, stage].at[k], load_sem.at[route, stage]).start()

    def late(route, stage, index):
        if stage > 0:
            send(route, stage - 1, index).wait()
            view = terms(route, stage, slot_at(route, index))[-1]
            last = held[route, stage].shape[0] - 1
            pltpu.make_async_copy(view, held[route, stage].at[last], load_sem.at[route, stage]).start()

    def finish(route, stage, index):
        if stage > 0:
            buf = held[route, stage]
            pltpu.make_async_copy(buf, buf, load_sem.at[route, stage]).wait()
            number = buf.shape[0]
            extent = buf.shape[1:-2]
            blocks = 1
            for size in extent:
                blocks *= size
            part = min(width, 512)
            if stage == stages - 1:

                @pl.when(index > 0)
                def _():
                    keep(route, index - 1).wait()

            @pl.loop(0, blocks)
            def _(block):
                if len(extent) == 2:
                    at = (block // extent[1], lax.rem(block, extent[1]))
                elif len(extent) == 1:
                    at = (block,)
                else:
                    at = ()
                for left in range(0, width, part):
                    cols = pl.ds(left, part)
                    total = buf[(0,) + at + (EVERY, cols)].astype(jnp.float32)
                    for k in range(1, number):
                        total += buf[(k,) + at + (EVERY, cols)].astype(jnp.float32)
                    made[route, stage][at + (EVERY, cols)] = total.astype(made[route, stage].dtype)

        if stage < stages - 1:
            send(route, stage, index).start()
        else:
            keep(route, index).start()

    def pass_sum(hop):
        return pltpu.make_async_remote_copy(
            src_ref=sums.at[hop] if hop < 4 else landed.at[hop - 1],
            dst_ref=landed.at[hop],
            send_sem=sum_send.at[hop],
            recv_sem=sum_recv.at[hop],
            device_id=target(SUM_HOPS[hop]),
            device_id_type=MESH,
        )

    def add_sums(step):
        if step > 0:
            pass_sum(step - 1).wait()
        if step == 0:
            hidden = hidden_ref[...].astype(jnp.float32)
            inv = lax.rsqrt(jnp.mean(hidden * hidden, axis=1, keepdims=True) + norm_eps)
            back = back_ref[...]
            term = jnp.sum(back * hidden * inv, axis=0, keepdims=True)
            scaled = back * gains_ref[0:1, :]
            part = jnp.mean(scaled * hidden, axis=1, keepdims=True)
            input_ref[...] = grad_ref[...] + inv * scaled - hidden * inv**3 * part
            line = lax.broadcasted_iota(jnp.int32, gain_ref.shape, 0)
            sums[0] = jnp.where(line == 0, term, gain_ref[...])
        elif step < 4:
            sums[step] = sums[step - 1] + landed[step - 1]
        elif step == len(SUM_HOPS):
            total_ref[...] = (sums[3] + landed[3]) + (landed[4] + landed[5])
        if step < len(SUM_HOPS):
            pass_sum(step).start()

    tokens = hidden_ref.shape[0]
    number = cos_ref.shape[1] // rows
    block = number * rows
    query_blocks = q_ref.shape[1] // block
    key_blocks = both_ref.shape[1] // block
    out_blocks = att_ref.shape[1] // block
    all_blocks = query_blocks + key_blocks + out_blocks
    kv_width = KV_HEADS * HEAD

    def stream(n):
        at = lax.rem(n + query_blocks + key_blocks, all_blocks)
        return pltpu.make_async_copy(
            weights_ref.at[pl.ds(at * number, number)],
            streamed.at[lax.rem(n, 2)],
            stream_sem.at[lax.rem(n, 2)],
        )

    def streamed_block(n):
        stream(n).wait()

        @pl.when(n + 1 < all_blocks)
        def _():
            stream(n + 1).start()

        return streamed[lax.rem(n, 2)].reshape(block, width)

    def column(b):
        return pl.ds(pl.multiple_of(b * block, block), block)

    def turn_tiles(at, value):
        flipped = value.astype(jnp.float32).T.astype(turned.dtype)
        turned[pl.ds(at * number, number)] = flipped.reshape(number, rows, tokens)

    def out_back(low, high):
        @pl.loop(low, high)
        def _(b):
            grad_att[:, column(b)] = dot(branch_ref[...], streamed_block(b), NT).astype(
                grad_att.dtype
            )
            turn_tiles(query_blocks + key_blocks + b, att_ref[:, column(b)])

    def query_back(low, high):
        @pl.loop(low, high)
        def _(b):
            left = grad_q[:, column(b)]
            back_ref[...] += dot(left, streamed_block(out_blocks + b), NN)
            turn_tiles(b, left)

    def key_back():
        @pl.loop(0, key_blocks)
        def _(b):
            left = grad_both[:, column(b)]
            back_ref[...] += dot(left, streamed_block(out_blocks + query_blocks + b), NN)
            turn_tiles(query_blocks + b, left)

    def attend_back_step(pair, side):
        wide = GROUP * HEAD
        narrow = PAIR * HEAD
        here = pl.ds(pl.multiple_of((pair * PAIR + side) * wide, wide), wide)
        k_cols = pl.ds(pl.multiple_of(pair * narrow, narrow), narrow)
        v_cols = pl.ds(pl.multiple_of(kv_width + pair * narrow, narrow), narrow)
        attend_back_side(
            side,
            q_ref[:, here],
            both_ref[:, k_cols],
            both_ref[:, v_cols],
            grad_att[:, here],
            mask_ref[...] > 0.5,
            lse_ref[pair],
            turn_ref,
            k_pair_ref,
            v_pair_ref,
        )
        u = turn_ref[...]
        grad_q[:, here] = (u * cos_ref[...] - swap_halves(u) * sin_ref[...]).astype(grad_q.dtype)
        if side == PAIR - 1:
            grad_kv[:, k_cols] = k_pair_ref[...]
            grad_kv[:, v_cols] = v_pair_ref[...]

    def key_rows(far):
        at = lax.rem(z + 4 - far, 4)
        return pl.ds(pl.multiple_of(at * tokens, tokens), tokens)

    def pass_terms(hop):
        return pltpu.make_async_remote_copy(
            src_ref=hop_out.at[hop],
            dst_ref=hop_in.at[hop],
            send_sem=hop_send.at[hop],
            recv_sem=hop_recv.at[hop],
            device_id=target("z1"),
            device_id_type=MESH,
        )

    def key_terms(hop):
        if hop > 0:
            pass_terms(hop - 1).wait()
        if hop < 3:
            own = grad_kv[key_rows(hop + 1), :]
            if hop > 0:
                own = (own.astype(jnp.float32) + hop_in[hop - 1].astype(jnp.float32)).astype(own.dtype)
            hop_out[hop] = own
            pass_terms(hop).start()
        else:
            own = grad_kv[key_rows(0), :].astype(jnp.float32) + hop_in[2].astype(jnp.float32)
            for b in range(key_blocks):
                u = own[:, b * block : (b + 1) * block]
                if b < key_blocks // 2:
                    u = u * cos_ref[...] - swap_halves(u) * sin_ref[...]
                grad_both[:, b * block : (b + 1) * block] = u.astype(grad_both.dtype)

    def built_copy(which, j, d):
        return pltpu.make_async_copy(
            built.at[which, d],
            wall_ref.at[d // 16, lax.rem(d // 8, 2), lax.rem(d // 4, 2), lax.rem(d, 4), j],
            built_sem.at[which],
        )

    def build(which, j, right_ref):
        @pl.loop(0, 32, unroll=True)
        def _(d):
            left_ref[d] = turned[table[d * lead + j]]

        for part in range(4):
            left = left_ref[part * 8 : (part + 1) * 8].reshape(8 * rows, tokens)
            value = dot(left, right_ref[...], NN).astype(built.dtype)
            built[which, part * 8 : (part + 1) * 8] = value.reshape(8, rows, width)

        @pl.loop(0, 32)
        def _(d):
            built_copy(which, j, d).start()

    def finish_built(which):
        pltpu.make_async_copy(built.at[which], built.at[which], built_sem.at[which]).wait()

    half = lead // 2
    attending = 2
    passing = attending + KV_HEADS
    building = passing + 5
    stream(0).start()

    def beside(t):
        for step in range(2):

            @pl.when(t == step)
            def _(step=step):
                if step == 0:
                    fill_mask(places, mask_ref)
                    back_ref[...] = jnp.zeros_like(back_ref)
                out_back(step * out_blocks // 2, (step + 1) * out_blocks // 2)

        for side in range(PAIR):
            since = t - attending

            @pl.when((since >= 0) & (since < KV_HEADS) & (lax.rem(since + 64, 2) == side))
            def _(side=side, since=since):
                attend_back_step(since // 2, side)

        for hop in range(4):

            @pl.when(t == passing + hop)
            def _(hop=hop):
                key_terms(hop)
                query_back(hop * query_blocks // 4, (hop + 1) * query_blocks // 4)

        @pl.when(t == passing + 4)
        def _():
            key_back()

        pair = t - building

        @pl.when((pair >= 1) & (pair <= half))
        def _():
            finish_built(0)
            finish_built(1)

        @pl.when((pair >= 0) & (pair < half))
        def _():
            build(0, pair, normed_ref)

        split = first_group - half

        @pl.when((pair >= 0) & (pair < split))
        def _():
            build(1, half + pair, normed_ref)

        @pl.when((pair >= split) & (pair < half))
        def _():
            build(1, half + pair, branch_ref)

        for step in range(len(SUM_HOPS) + 1):

            @pl.when(t == building + step)
            def _(step=step):
                add_sums(step)

    @pl.loop(0, rounds + stages - 1)
    def _(t):
        items = [(stage, route) for stage in range(stages - 1, -1, -1) for route in range(4)]

        def run(which, work):
            stage, route = items[which]
            live, index = turn(route, t - stage, counts, SCATTER_PLAN)

            @pl.when(live)
            def _():
                work(route, stage, index)

        far, near, place_beside = look
        for which in range(len(items) + far):
            if which == place_beside:
                beside(t)
            if which < len(items):
                run(which, early)
            if far - near <= which < len(items) + far - near:
                run(which - far + near, late)
            if which >= far:
                run(which - far, finish)

    for route in range(4):
        keep(route, counts[route] - 1).wait()


def scatter_slots(
    grads_wall,
    gain_terms,
    weights,
    table,
    places,
    branch,
    attended,
    queries,
    both,
    lse,
    normed,
    hidden,
    cosine,
    sine,
    grad_middle,
    gains,
    lead,
    first_group,
    caps,
    look=(5, 2, 17),
):
    rows, width = grads_wall.shape[1:]
    kind = grads_wall.dtype
    wall = grads_wall.reshape(2, 2, 2, 4, caps, rows, width)
    counts, starts = split_slots(caps, SCATTER_PLAN)
    stages = len(SCATTER_ROUTES[0])
    scratch = []
    for route in range(4):
        for stage in range(1, stages):
            extent = scatter_extent(route, stage)
            scratch.append(pltpu.VMEM((scatter_terms(route, stage),) + extent + (rows, width), kind))
            last = stage == stages - 1
            scratch.append(pltpu.VMEM(extent + (rows, width), jnp.float32 if last else kind))
    tile = (caps, rows, width)
    tokens = hidden.shape[0]
    number = cosine.shape[1] // rows
    length, both_width = both.shape
    dma = pltpu.SemaphoreType.DMA
    scratch += [
        dma((4, stages)),
        dma((4, stages)),
        dma((4, stages, max(counts))),
        dma((4,)),
        pltpu.VMEM((4,) + gain_terms.shape, jnp.float32),
        pltpu.VMEM((6,) + gain_terms.shape, jnp.float32),
        dma((6,)),
        dma((6,)),
        pltpu.VMEM((2, number, rows, width), kind),
        pltpu.VMEM((tokens, width), kind),
        pltpu.VMEM((tokens, width), kind),
        pltpu.VMEM((length, both_width), kind),
        pltpu.VMEM((tokens, both_width), kind),
        pltpu.VMEM((length, PAIR * HEAD), kind),
        pltpu.VMEM((length, PAIR * HEAD), kind),
        pltpu.VMEM((tokens, GROUP * HEAD), jnp.float32),
        pltpu.VMEM((3, tokens, both_width), kind),
        pltpu.VMEM((3, tokens, both_width), kind),
        pltpu.VMEM((weights.shape[0], rows, tokens), kind),
        pltpu.VMEM((32, rows, tokens), kind),
        pltpu.VMEM((2, 32, rows, width), kind),
        pltpu.VMEM((tokens, length), jnp.float32),
        dma((2,)),
        dma((3,)),
        dma((3,)),
        dma((2,)),
        pltpu.VMEM((tokens, width), jnp.float32),
    ]
    vmem = pl.BlockSpec(memory_space=pltpu.VMEM)
    smem = pl.BlockSpec(memory_space=pltpu.SMEM)
    anyw = pl.BlockSpec(memory_space=pl.ANY)
    out = pl.pallas_call(
        functools.partial(scatter_kernel, look, lead, first_group),
        out_shape=[
            jax.ShapeDtypeStruct(wall.shape, kind),
            jax.ShapeDtypeStruct(tile, jnp.float32),
            jax.ShapeDtypeStruct(gain_terms.shape, jnp.float32),
            jax.ShapeDtypeStruct((tokens, width), jnp.float32),
            jax.ShapeDtypeStruct((2, 2, 4) + tile, kind),
            jax.ShapeDtypeStruct((2, 4) + tile, kind),
            jax.ShapeDtypeStruct((4,) + tile, kind),
            jax.ShapeDtypeStruct((3, 2) + tile, kind),
            jax.ShapeDtypeStruct(tile, kind),
        ],
        in_specs=[anyw, vmem, anyw, smem, smem] + [vmem] * 11,
        out_specs=[anyw, anyw, vmem, vmem] + [anyw] * 5,
        scratch_shapes=scratch,
        input_output_aliases={0: 0},
        compiler_params=pltpu.CompilerParams(
            collective_id=1, has_side_effects=True, vmem_limit_bytes=62 << 20
        ),
        name="scatter_slots",
    )(
        wall, gain_terms, weights, table, places, branch, attended, queries, both, lse, normed,
        hidden, cosine, sine, grad_middle, gains,
    )
    return out[1], out[2], out[3]


def shards(
    hidden_in,
    piece_starts,
    out_cotangent,
    owners,
    master,
    moment_one,
    moment_two,
    gain_master,
    gain_one,
    gain_two,
):
    devices = lax.axis_size("dp") * lax.axis_size("fsdp")
    caps, tile_rows, model_width = master.shape
    layout = section_layout(devices, tile_rows)
    slots = slot_numbers(owners, layout, caps)
    local_len = hidden_in.shape[0]
    first = lax.axis_index("fsdp") * local_len
    positions = first + jnp.arange(local_len, dtype=jnp.int32)
    places = jnp.concatenate([first[None].astype(jnp.int32), piece_starts[0]])
    cosine, sine = rope_tables(positions.astype(jnp.float32), 16 * tile_rows)
    (
        wall, weights, gains_low, both, normed, queries, attended, lse, middle, normed_two
    ) = forward_attention(
        master,
        gain_master.astype(jnp.bfloat16),
        slots,
        places,
        hidden_in,
        cosine,
        sine,
        layout,
    )
    block_out, grad_middle, grad_branch, gain_terms, grads_wall = ffn_call(
        slots,
        (layout[2][0], layout[2][0] + layout[2][1] // 2, layout[3][0]),
        layout[3][1],
        normed_two,
        out_cotangent,
        middle,
        gains_low,
        wall,
    )
    weight_grad, gain_grad, input_grad = backward_attention(
        grads_wall,
        gain_terms,
        grad_middle,
        gains_low,
        weights,
        slots,
        places,
        grad_branch,
        attended,
        queries,
        both,
        lse,
        normed,
        hidden_in,
        cosine,
        sine,
        layout,
        caps,
    )
    keep_slot = filled_mask(slots, caps, lax.axis_index(("dp", "fsdp")))[:, None, None]
    weight_grad = jnp.where(keep_slot, weight_grad, 0.0)
    step = float(STEP)
    new_one, new_two, new_weights = adam_step(
        master, moment_one, moment_two, weight_grad, step, decay_rate, learn_rate
    )
    new_one = jnp.where(keep_slot, new_one, 0.0)
    new_two = jnp.where(keep_slot, new_two, 0.0)
    new_weights = jnp.where(keep_slot, new_weights, 0.0)
    new_gain_one, new_gain_two, new_gains = adam_step(
        gain_master, gain_one, gain_two, gain_grad, step, 0.0, gain_rate
    )
    return (
        block_out,
        input_grad,
        weight_grad,
        new_weights,
        new_one,
        new_two,
        gain_grad,
        new_gains,
        new_gain_one,
        new_gain_two,
    )


def solution(mesh):
    return jax.shard_map(
        shards,
        mesh=mesh,
        in_specs=(
            P(("dp", "fsdp"), None),
            P("dp", None),
            P(("dp", "fsdp"), None),
            P(),
            P(("dp", "fsdp"), None, None),
            P(("dp", "fsdp"), None, None),
            P(("dp", "fsdp"), None, None),
            P(None, ("dp", "fsdp")),
            P(None, ("dp", "fsdp")),
            P(None, ("dp", "fsdp")),
        ),
        out_specs=(
            P(("dp", "fsdp"), None),
            P(("dp", "fsdp"), None),
            P(("dp", "fsdp"), None, None),
            P(("dp", "fsdp"), None, None),
            P(("dp", "fsdp"), None, None),
            P(("dp", "fsdp"), None, None),
            P(None, ("dp", "fsdp")),
            P(None, ("dp", "fsdp")),
            P(None, ("dp", "fsdp")),
            P(None, ("dp", "fsdp")),
        ),
        check_vma=False,
    )
```

```python
import functools

import jax
import jax.experimental.pallas as pl
import jax.experimental.pallas.tpu as pltpu
import jax.numpy as jnp
import numpy as np
from jax import lax
from jax.sharding import PartitionSpec as P

D = 2048
HEADS = 32
KV_HEADS = 8
HEAD = 64
FF = 8192
PIECE = 256
STEP = 5


norm_eps = 1e-05
adam_eps = 1e-08
beta_one = 0.5
beta_two = 0.5
learn_rate = 0.02
gain_rate = 0.3
decay_rate = 0.1
rope_base = 500000.0
masked_score = -1e30


def section_layout(devices, tile_rows):
    counts = [
        (D + 2 * KV_HEADS * HEAD) // tile_rows,
        HEADS * HEAD // tile_rows,
        2 * FF // tile_rows,
        FF // tile_rows,
    ]
    layout = []
    first_tile = 0
    first_slot = 0
    for number in counts:
        capacity = 5 * number // (4 * devices) + 1
        layout.append((first_tile, number, capacity, first_slot))
        first_tile += number
        first_slot += capacity
    return layout


def adam_step(weights, first_moment, second_moment, grads, step, decay, rate):
    new_one = beta_one * first_moment + (1.0 - beta_one) * grads
    new_two = beta_two * second_moment + (1.0 - beta_two) * grads * grads
    correct_one = 1.0 - beta_one**step
    correct_two = 1.0 - beta_two**step
    update = -rate * (
        new_one / correct_one / (jnp.sqrt(new_two / correct_two) + adam_eps) + decay * weights
    )
    return (new_one, new_two, weights + update)


def slot_numbers(owners, layout, caps):
    numbers = [entry[1] for entry in layout]
    group = jnp.asarray(np.repeat(np.arange(4), numbers), jnp.int32)
    base = jnp.asarray(np.repeat([entry[3] for entry in layout], numbers), jnp.int32)
    kind = owners * 4 + group
    order = jnp.arange(kind.shape[0], dtype=jnp.int32)
    earlier = (kind[:, None] == kind[None, :]) & (order[:, None] < order[None, :])
    return owners * caps + base + jnp.sum(earlier.astype(jnp.int32), axis=0)


def filled_mask(slots, caps, device):
    here = device * caps + jnp.arange(caps, dtype=jnp.int32)
    return jnp.any(slots[None, :] == here[:, None], axis=1)


def rope_tables(positions, block):
    lane = jnp.arange(block, dtype=jnp.int32)
    pair = lax.rem(lane, HEAD // 2).astype(jnp.float32)
    inverse = rope_base ** (-(pair * 2.0 / HEAD))
    angles = positions[:, None] * inverse[None, :]
    sign = jnp.where(lax.rem(lane, HEAD) < HEAD // 2, -1.0, 1.0)
    return jnp.cos(angles), jnp.sin(angles) * sign[None, :]


def turn_back(grads, cosine, sine):
    tokens, width = grads.shape
    half_dim = HEAD // 2
    heads = grads.reshape(tokens, width // HEAD, 2, half_dim)
    swapped = heads[:, :, ::-1].reshape(tokens, width)
    times = width // cosine.shape[1]
    return grads * jnp.tile(cosine, (1, times)) - swapped * jnp.tile(sine, (1, times))


def tuned_mesh():
    return (lax.axis_size("dp"), lax.axis_size("fsdp")) == (8, 4)


def attention_slots(slots, layout, width, tile_rows):
    query = width // tile_rows
    return slots[:query], slots[query : layout[1][0]], slots[layout[1][0] : layout[2][0]]


def forward_attention(low_tiles, low_gains, slots, places, hidden_in, cosine, sine, layout):
    caps, tile_rows, width = low_tiles.shape
    lead = layout[2][3]
    slot_query, slot_both, slot_out = attention_slots(slots, layout, width, tile_rows)
    if tuned_mesh():
        table = slots[: layout[2][0]]
        table = table // caps * lead + lax.rem(table, caps)
        (wall, weights, both, gains, normed, queries, attended, lse, middle, normed_two) = (
            gather_slots(low_tiles, low_gains, table, places, hidden_in, cosine, sine, lead)
        )
        return wall, weights, gains, both, normed, queries, attended, lse, middle, normed_two
    wall = lax.all_gather(low_tiles, ("dp", "fsdp"), axis=0, tiled=True)
    gains = lax.all_gather(low_gains, ("dp", "fsdp"), axis=1, tiled=True).astype(jnp.float32)
    tokens = hidden_in.astype(jnp.float32)
    inv_one = lax.rsqrt(jnp.mean(tokens * tokens, axis=1, keepdims=True) + norm_eps)
    normed = (tokens * inv_one * gains[0]).astype(jnp.bfloat16)
    turned = KV_HEADS * HEAD // cosine.shape[1]
    both_local = project(slot_both, normed, cosine, sine, wall, turned=turned)
    both = lax.all_gather(both_local, "fsdp", axis=0, tiled=True)
    queries = project(slot_query, normed, cosine, sine, wall)
    attended, lse = attend(places, queries, both)
    middle, normed_two = mix(slot_out, attended, hidden_in, gains[1], wall)
    return wall, wall, gains, both, normed, queries, attended, lse, middle, normed_two


def backward_attention(
    grads_wall,
    gain_terms,
    grad_middle,
    gains,
    weights,
    slots,
    places,
    branch,
    attended,
    queries,
    both,
    lse,
    normed,
    hidden_in,
    cosine,
    sine,
    layout,
    caps,
):
    local_len, width = normed.shape
    tile_rows = weights.shape[1]
    slot_query, slot_both, slot_out = attention_slots(slots, layout, width, tile_rows)
    kv_width = KV_HEADS * HEAD
    if tuned_mesh():
        lead = layout[2][3]
        table = slots[: layout[2][0]]
        table = table // caps * lead + lax.rem(table, caps)
        order = jnp.arange(table.shape[0], dtype=jnp.int32)
        here = jnp.arange(32 * lead, dtype=jnp.int32)
        tile_at = jnp.sum(jnp.where(table[None, :] == here[:, None], order[None, :], 0), axis=1)
        grads, total, input_grad = scatter_slots(
            grads_wall,
            gain_terms,
            weights,
            tile_at,
            places,
            branch,
            attended,
            queries,
            both,
            lse,
            normed,
            hidden_in,
            cosine,
            sine,
            grad_middle,
            gains,
            lead,
            layout[0][2],
            caps,
        )
        part = width // 32
        device = lax.axis_index(("dp", "fsdp"))
        return grads, lax.dynamic_slice_in_dim(total[:2], device * part, part, 1), input_grad
    grad_attended, grads_wall = mix_back(slot_out, attended, branch, weights, grads_wall)
    grad_query, both_terms = attend_back(
        places, queries, both, grad_attended, lse, cosine, sine
    )
    both_sum = lax.psum_scatter(both_terms, "fsdp", scatter_dimension=0, tiled=True).astype(
        jnp.float32
    )
    grad_normed, grads_wall = project_back(slot_query, grad_query, normed, None, weights, grads_wall)
    both_sum = both_sum.reshape(local_len, KV_HEADS // PAIR, 2, PAIR * HEAD)
    grad_key = turn_back(both_sum[:, :, 0].reshape(local_len, kv_width), cosine, sine)
    grad_value = both_sum[:, :, 1].reshape(local_len, kv_width)
    grad_both = jnp.concatenate([grad_key, grad_value], axis=1).astype(jnp.bfloat16)
    grad_normed, grads_wall = project_back(
        slot_both, grad_both, normed, grad_normed, weights, grads_wall
    )
    tokens = hidden_in.astype(jnp.float32)
    inv_one = lax.rsqrt(jnp.mean(tokens * tokens, axis=1, keepdims=True) + norm_eps)
    gain_one_term = jnp.sum(grad_normed * tokens * inv_one, axis=0)
    gain_terms = jnp.stack([gain_one_term, gain_terms[1]])
    scaled = grad_normed * gains[0]
    part = jnp.mean(scaled * tokens, axis=1, keepdims=True)
    input_grad = grad_middle + inv_one * scaled - tokens * inv_one**3 * part
    grads = lax.psum_scatter(grads_wall, ("dp", "fsdp"), scatter_dimension=0, tiled=True)
    gain_grad = lax.psum_scatter(gain_terms, ("dp", "fsdp"), scatter_dimension=1, tiled=True)
    return grads.astype(jnp.float32), gain_grad, input_grad


VMEM_ASK = 56 << 20
NT = (((1,), (1,)), ((), ()))
NN = (((1,), (0,)), ((), ()))
TN = (((0,), (0,)), ((), ()))


def dot(a, b, dims):
    return lax.dot_general(a, b, dims, preferred_element_type=jnp.float32)


def stream_tiles(table, wall_ref, held, sem, group):
    step = pl.program_id(0)
    steps = pl.num_programs(0)
    depth = held.shape[0]
    buf = lax.rem(step, depth)

    def fetch(at):
        into = lax.rem(at, depth)

        @pl.loop(0, group, unroll=True)
        def _(t):
            pltpu.make_async_copy(
                wall_ref.at[table[at * group + t]], held.at[into, t], sem.at[into]
            ).start()

    @pl.when(step == 0)
    def _():
        for ahead in range(depth - 1):

            @pl.when(ahead < steps)
            def _(ahead=ahead):
                fetch(jnp.int32(ahead))

    @pl.when(step + depth - 1 < steps)
    def _():
        fetch(step + depth - 1)

    pltpu.make_async_copy(held.at[buf], held.at[buf], sem.at[buf]).wait()
    rows = group * wall_ref.shape[1]
    return held[buf].reshape(rows, wall_ref.shape[2])


def store_tiles(table, grads_ref, made, sem, group, value):
    step = pl.program_id(0)
    steps = pl.num_programs(0)
    buf = lax.rem(step, 2)

    def drain(which):
        pltpu.make_async_copy(made.at[which], made.at[which], sem.at[which]).wait()

    @pl.when(step >= 2)
    def _():
        drain(buf)

    made[buf] = value.astype(made.dtype).reshape(made.shape[1:])

    @pl.loop(0, group, unroll=True)
    def _(t):
        pltpu.make_async_copy(
            made.at[buf, t], grads_ref.at[table[step * group + t]], sem.at[buf]
        ).start()

    @pl.when(step == steps - 1)
    def _():
        drain(1 - buf)
        drain(buf)


def swap_halves(u):
    width = u.shape[1]
    lane = lax.broadcasted_iota(jnp.int32, u.shape, 1)
    first = lax.rem(lane, HEAD) < HEAD // 2
    return jnp.where(
        first, pltpu.roll(u, width - HEAD // 2, 1), pltpu.roll(u, HEAD // 2, 1)
    )


def project_kernel(group, turned, table, normed_ref, cos_ref, sin_ref, wall_ref, out_ref, held, sem):
    weights = stream_tiles(table, wall_ref, held, sem, group)
    u = dot(normed_ref[...], weights, NT)
    if turned is None:
        out_ref[...] = (u * cos_ref[...] + swap_halves(u) * sin_ref[...]).astype(out_ref.dtype)
    else:

        @pl.when(pl.program_id(0) < turned)
        def _():
            out_ref[...] = (u * cos_ref[...] + swap_halves(u) * sin_ref[...]).astype(out_ref.dtype)

        @pl.when(pl.program_id(0) >= turned)
        def _():
            out_ref[...] = u.astype(out_ref.dtype)


def full_spec(shape):
    return pl.BlockSpec(shape, lambda i, *_: (0,) * len(shape))


def any_spec():
    return pl.BlockSpec(memory_space=pl.ANY)


AHEAD = 4


def held_tiles(depth, group, wall):
    return pltpu.VMEM((depth, group) + wall.shape[1:], wall.dtype)


def project(table, normed, cosine, sine, wall, turned=None, group=16):
    tokens = normed.shape[0]
    block = group * wall.shape[1]
    steps = table.shape[0] // group
    return pl.pallas_call(
        functools.partial(project_kernel, group, turned),
        grid_spec=pltpu.PrefetchScalarGridSpec(
            num_scalar_prefetch=1,
            grid=(steps,),
            in_specs=[full_spec(normed.shape), full_spec(cosine.shape), full_spec(sine.shape), any_spec()],
            out_specs=pl.BlockSpec((tokens, block), lambda i, *_: (0, i)),
            scratch_shapes=[held_tiles(AHEAD, group, wall), pltpu.SemaphoreType.DMA((AHEAD,))],
        ),
        out_shape=jax.ShapeDtypeStruct((tokens, steps * block), jnp.bfloat16),
        compiler_params=pltpu.CompilerParams(vmem_limit_bytes=VMEM_ASK),
        name="project",
    )(table, normed, cosine, sine, wall)


def mix_kernel(group, table, left_ref, hidden_ref, gain_ref, wall_ref, middle_ref, normed_ref, held, sem):
    step = pl.program_id(0)
    weights = stream_tiles(table, wall_ref, held, sem, group)

    @pl.when(step == 0)
    def _():
        middle_ref[...] = hidden_ref[...].astype(jnp.float32)

    middle_ref[...] += dot(left_ref[...], weights, NN)

    @pl.when(step == pl.num_programs(0) - 1)
    def _():
        middle = middle_ref[...]
        inv = lax.rsqrt(jnp.mean(middle * middle, axis=1, keepdims=True) + norm_eps)
        normed_ref[...] = (middle * inv * gain_ref[...]).astype(normed_ref.dtype)


def mix(table, left, hidden, gain, wall, group=16):
    tokens, width = hidden.shape
    block = group * wall.shape[1]
    return pl.pallas_call(
        functools.partial(mix_kernel, group),
        grid_spec=pltpu.PrefetchScalarGridSpec(
            num_scalar_prefetch=1,
            grid=(table.shape[0] // group,),
            in_specs=[
                pl.BlockSpec((tokens, block), lambda i, *_: (0, i)),
                full_spec(hidden.shape),
                full_spec((1, width)),
                any_spec(),
            ],
            out_specs=[full_spec(hidden.shape), full_spec(hidden.shape)],
            scratch_shapes=[held_tiles(AHEAD, group, wall), pltpu.SemaphoreType.DMA((AHEAD,))],
        ),
        out_shape=[
            jax.ShapeDtypeStruct(hidden.shape, jnp.float32),
            jax.ShapeDtypeStruct(hidden.shape, jnp.bfloat16),
        ],
        compiler_params=pltpu.CompilerParams(vmem_limit_bytes=VMEM_ASK),
        name="mix",
    )(table, left, hidden, gain.reshape(1, width), wall)


def mix_back_kernel(group, table, left_ref, right_ref, wall_ref, old_ref, out_ref, grads_ref, held, made, load_sem, store_sem):
    weights = stream_tiles(table, wall_ref, held, load_sem, group)
    right = right_ref[...]
    out_ref[...] = dot(right, weights, NT).astype(out_ref.dtype)
    store_tiles(table, grads_ref, made, store_sem, group, dot(left_ref[...], right, TN))


def mix_back(table, left, right, wall, grads, group=16):
    tokens, width = right.shape
    block = group * wall.shape[1]
    columns = pl.BlockSpec((tokens, block), lambda i, *_: (0, i))
    return pl.pallas_call(
        functools.partial(mix_back_kernel, group),
        grid_spec=pltpu.PrefetchScalarGridSpec(
            num_scalar_prefetch=1,
            grid=(table.shape[0] // group,),
            in_specs=[columns, full_spec(right.shape), any_spec(), any_spec()],
            out_specs=[columns, any_spec()],
            scratch_shapes=[
                held_tiles(AHEAD, group, wall),
                held_tiles(2, group, wall),
                pltpu.SemaphoreType.DMA((AHEAD,)),
                pltpu.SemaphoreType.DMA((2,)),
            ],
        ),
        out_shape=[
            jax.ShapeDtypeStruct(left.shape, jnp.bfloat16),
            jax.ShapeDtypeStruct(grads.shape, grads.dtype),
        ],
        input_output_aliases={4: 1},
        compiler_params=pltpu.CompilerParams(vmem_limit_bytes=VMEM_ASK),
        name="mix_back",
    )(table, left, right, wall, grads)


def project_back_kernel(group, fresh, table, left_ref, right_ref, wall_ref, old_ref, start_ref, out_ref, grads_ref, held, made, load_sem, store_sem):
    weights = stream_tiles(table, wall_ref, held, load_sem, group)

    @pl.when(pl.program_id(0) == 0)
    def _():
        out_ref[...] = jnp.zeros_like(out_ref) if fresh else start_ref[...]

    left = left_ref[...]
    out_ref[...] += dot(left, weights, NN)
    store_tiles(table, grads_ref, made, store_sem, group, dot(left, right_ref[...], TN))


def project_back(table, left, right, start, wall, grads, group=16):
    tokens, width = right.shape
    block = group * wall.shape[1]
    return pl.pallas_call(
        functools.partial(project_back_kernel, group, start is None),
        grid_spec=pltpu.PrefetchScalarGridSpec(
            num_scalar_prefetch=1,
            grid=(table.shape[0] // group,),
            in_specs=[
                pl.BlockSpec((tokens, block), lambda i, *_: (0, i)),
                full_spec(right.shape),
                any_spec(),
                any_spec(),
                any_spec() if start is None else full_spec(start.shape),
            ],
            out_specs=[full_spec(right.shape), any_spec()],
            scratch_shapes=[
                held_tiles(AHEAD, group, wall),
                held_tiles(2, group, wall),
                pltpu.SemaphoreType.DMA((AHEAD,)),
                pltpu.SemaphoreType.DMA((2,)),
            ],
        ),
        out_shape=[
            jax.ShapeDtypeStruct(right.shape, jnp.float32),
            jax.ShapeDtypeStruct(grads.shape, grads.dtype),
        ],
        input_output_aliases={4: 1},
        compiler_params=pltpu.CompilerParams(vmem_limit_bytes=VMEM_ASK),
        name="project_back",
    )(table, left, right, wall, grads, table if start is None else start)


def fill_mask(places, mask_ref):
    shape = mask_ref.shape
    query = lax.broadcasted_iota(jnp.int32, shape, 0) + places[0]
    key = lax.broadcasted_iota(jnp.int32, shape, 1)
    allowed = key <= query
    for piece in range(places.shape[0] - 1):
        low = places[1 + piece]
        inside_query = (query >= low) & (query < low + PIECE)
        inside_key = (key >= low) & (key < low + PIECE)
        allowed = allowed | (inside_query & inside_key)
    mask_ref[...] = jnp.where(allowed, 1.0, 0.0)


PAIR = 2
GROUP = HEADS // KV_HEADS


def attend_kernel(places, q_ref, k_ref, v_ref, out_ref, lse_ref, mask_ref):
    @pl.when(pl.program_id(0) == 0)
    def _():
        fill_mask(places, mask_ref)

    mask = mask_ref[...] > 0.5
    lane = lax.broadcasted_iota(jnp.int32, lse_ref.shape[1:], 1)
    logs = jnp.zeros(lse_ref.shape[1:], jnp.float32)
    scale = jnp.bfloat16(1.0 / HEAD**0.5)
    for side in range(PAIR):
        k = k_ref[:, side * HEAD : (side + 1) * HEAD]
        v = v_ref[:, side * HEAD : (side + 1) * HEAD]
        for h in range(GROUP):
            head = side * GROUP + h
            cols = slice(head * HEAD, (head + 1) * HEAD)
            scores = jnp.where(mask, dot(q_ref[:, cols] * scale, k, NT), masked_score)
            top = jnp.max(scores, axis=1, keepdims=True)
            raised = jnp.exp(scores - top)
            total = jnp.sum(raised, axis=1, keepdims=True)
            probs = (raised * (1.0 / total)).astype(jnp.bfloat16)
            out_ref[:, cols] = dot(probs, v, NN).astype(out_ref.dtype)
            logs = jnp.where(lane == head, top + jnp.log(total), logs)
    lse_ref[0] = logs


def attend(places, queries, both):
    tokens, width = queries.shape
    length = both.shape[0]
    steps = KV_HEADS // PAIR
    wide = PAIR * GROUP * HEAD
    narrow = PAIR * HEAD
    return pl.pallas_call(
        attend_kernel,
        grid_spec=pltpu.PrefetchScalarGridSpec(
            num_scalar_prefetch=1,
            grid=(steps,),
            in_specs=[
                pl.BlockSpec((tokens, wide), lambda i, *_: (0, i)),
                pl.BlockSpec((length, narrow), lambda i, *_: (0, i)),
                pl.BlockSpec((length, narrow), lambda i, *_: (0, steps + i)),
            ],
            out_specs=[
                pl.BlockSpec((tokens, wide), lambda i, *_: (0, i)),
                pl.BlockSpec((1, tokens, 128), lambda i, *_: (i, 0, 0)),
            ],
            scratch_shapes=[pltpu.VMEM((tokens, length), jnp.float32)],
        ),
        out_shape=[
            jax.ShapeDtypeStruct((tokens, width), jnp.bfloat16),
            jax.ShapeDtypeStruct((steps, tokens, 128), jnp.float32),
        ],
        compiler_params=pltpu.CompilerParams(vmem_limit_bytes=VMEM_ASK),
        name="attend",
    )(places, queries, both, both)


def attend_back_kernel(places, q_ref, k_ref, v_ref, grad_ref, lse_ref, cos_ref, sin_ref, out_ref, both_ref, mask_ref, turn_ref):
    @pl.when(pl.program_id(0) == 0)
    def _():
        fill_mask(places, mask_ref)

    mask = mask_ref[...] > 0.5
    scale = jnp.bfloat16(1.0 / HEAD**0.5)
    for side in range(PAIR):
        here = slice(side * HEAD, (side + 1) * HEAD)
        k = k_ref[:, here]
        v = v_ref[:, here]
        dk = None
        dv = None
        for h in range(GROUP):
            head = side * GROUP + h
            cols = slice(head * HEAD, (head + 1) * HEAD)
            q = q_ref[:, cols] * scale
            grad = grad_ref[:, cols]
            scores = jnp.where(mask, dot(q, k, NT), masked_score)
            probs = jnp.exp(scores - lse_ref[0, :, head : head + 1])
            grad_probs = dot(grad, v, NT)
            row_dot = jnp.sum(probs * grad_probs, axis=1, keepdims=True)
            grad_scores = (probs * (grad_probs - row_dot)).astype(jnp.bfloat16)
            turn_ref[:, cols] = dot(grad_scores, k, NN) * (1.0 / HEAD**0.5)
            dk_part = dot(q, grad_scores, TN)
            dv_part = dot(grad, probs.astype(jnp.bfloat16), TN)
            dk = dk_part if dk is None else dk + dk_part
            dv = dv_part if dv is None else dv + dv_part
        there = slice((PAIR + side) * HEAD, (PAIR + side + 1) * HEAD)
        both_ref[:, here] = dk.T.astype(both_ref.dtype)
        both_ref[:, there] = dv.T.astype(both_ref.dtype)
    wide = cos_ref.shape[1]
    for left in range(0, turn_ref.shape[1], wide):
        u = turn_ref[:, left : left + wide]
        out_ref[:, left : left + wide] = (u * cos_ref[...] - swap_halves(u) * sin_ref[...]).astype(out_ref.dtype)


def attend_back(places, queries, both, grad, lse, cosine, sine):
    tokens, width = queries.shape
    length = both.shape[0]
    steps = KV_HEADS // PAIR
    wide = PAIR * GROUP * HEAD
    narrow = PAIR * HEAD
    columns = pl.BlockSpec((tokens, wide), lambda i, *_: (0, i))
    keys = pl.BlockSpec((length, narrow), lambda i, *_: (0, i))
    return pl.pallas_call(
        attend_back_kernel,
        grid_spec=pltpu.PrefetchScalarGridSpec(
            num_scalar_prefetch=1,
            grid=(steps,),
            in_specs=[
                columns,
                keys,
                pl.BlockSpec((length, narrow), lambda i, *_: (0, steps + i)),
                columns,
                pl.BlockSpec((1, tokens, 128), lambda i, *_: (i, 0, 0)),
                full_spec(cosine.shape),
                full_spec(sine.shape),
            ],
            out_specs=[columns, pl.BlockSpec((length, 2 * narrow), lambda i, *_: (0, i))],
            scratch_shapes=[pltpu.VMEM((tokens, length), jnp.float32), pltpu.VMEM((tokens, wide), jnp.float32)],
        ),
        out_shape=[
            jax.ShapeDtypeStruct((tokens, width), jnp.bfloat16),
            jax.ShapeDtypeStruct((length, 2 * KV_HEADS * HEAD), jnp.bfloat16),
        ],
        compiler_params=pltpu.CompilerParams(vmem_limit_bytes=VMEM_ASK),
        name="attend_back",
    )(places, queries, both, both, grad, lse, cosine, sine)


def ffn_kernel(group, offsets, table, normed_ref, cot_ref, middle_ref, gains_ref, wall_ref, block_ref, grad_ref, branch_ref, gain_ref, grads_ref, out_ref, back_ref, held, made, load_sem, store_sem):
    step = pl.program_id(0)
    steps = pl.num_programs(0)
    tile_rows = wall_ref.shape[1]
    width = wall_ref.shape[2]
    rows = group * tile_rows

    def fetch(at, buf):
        for kind in range(3):
            @pl.loop(0, group, unroll=True)
            def _(t, kind=kind):
                pltpu.make_async_copy(wall_ref.at[table[offsets[kind] + at * group + t]], held.at[buf, kind, t], load_sem.at[buf]).start()

    def drain(buf):
        pltpu.make_async_copy(made.at[buf], made.at[buf], store_sem.at[buf]).wait()

    buf = lax.rem(step, 2)

    @pl.when(step == 0)
    def _():
        fetch(0, 0)
        out_ref[...] = jnp.zeros_like(out_ref)
        back_ref[...] = jnp.zeros_like(back_ref)

    @pl.when(step + 1 < steps)
    def _():
        fetch(step + 1, 1 - buf)

    pltpu.make_async_copy(held.at[buf], held.at[buf], load_sem.at[buf]).wait()

    @pl.when(step >= 2)
    def _():
        drain(buf)

    normed = normed_ref[...]
    cot = cot_ref[...]
    w_both = held[buf, 0:2].reshape(2 * rows, width)
    w_down = held[buf, 2].reshape(rows, width)
    nt = (((1,), (1,)), ((), ()))
    nn = (((1,), (0,)), ((), ()))
    tn = (((0,), (0,)), ((), ()))

    def dot(a, b, dims):
        return lax.dot_general(a, b, dims, preferred_element_type=jnp.float32)

    gate_up = dot(normed, w_both, nt)
    gate = gate_up[:, :rows]
    up = gate_up[:, rows:]
    hidden = dot(cot, w_down, nt)
    sig = jax.nn.sigmoid(gate)
    silu = gate * sig
    act = (silu * up).astype(jnp.bfloat16)
    g_gate = (hidden * up * sig * (1.0 + gate * (1.0 - sig))).astype(jnp.bfloat16)
    g_up = (hidden * silu).astype(jnp.bfloat16)
    g_both = jnp.concatenate([g_gate, g_up], axis=1)
    out_ref[...] += dot(act, w_down, nn)
    back_ref[...] += dot(g_both, w_both, nn)
    made[buf, 0:2] = dot(g_both, normed, tn).astype(jnp.bfloat16).reshape(2, group, tile_rows, width)
    made[buf, 2] = dot(act, cot, tn).astype(jnp.bfloat16).reshape(group, tile_rows, width)
    for kind in range(3):
        @pl.loop(0, group, unroll=True)
        def _(t, kind=kind):
            pltpu.make_async_copy(made.at[buf, kind, t], grads_ref.at[table[offsets[kind] + step * group + t]], store_sem.at[buf]).start()

    @pl.when(step == steps - 1)
    def _():
        middle = middle_ref[...]
        inv = lax.rsqrt(jnp.mean(middle * middle, axis=1, keepdims=True) + norm_eps)
        back = back_ref[...]
        scaled = back * gains_ref[1:2, :]
        part = jnp.mean(scaled * middle, axis=1, keepdims=True)
        grad = cot_ref[...].astype(jnp.float32) + inv * scaled - middle * inv**3 * part
        grad_ref[...] = grad
        branch_ref[...] = grad.astype(jnp.bfloat16)
        block_ref[...] = (middle + out_ref[...]).astype(jnp.bfloat16)
        term = jnp.sum(back * middle * inv, axis=0, keepdims=True)
        line = lax.broadcasted_iota(jnp.int32, gain_ref.shape, 0)
        gain_ref[...] = jnp.where(line == 1, term, 0.0)
        drain(1 - buf)
        drain(buf)

def ffn_call(table, offsets, number, normed, cot, middle, gains, wall, group=32):
    tokens, width = normed.shape
    steps = number // group
    tr = wall.shape[1]
    full = pl.BlockSpec((tokens, width), lambda i, *_: (0, 0))
    return pl.pallas_call(
        functools.partial(ffn_kernel, group, offsets),
        grid_spec=pltpu.PrefetchScalarGridSpec(
            num_scalar_prefetch=1, grid=(steps,),
            in_specs=[full, full, full, full_spec(gains.shape), any_spec()],
            out_specs=[full, full, full, full_spec((8, width)), any_spec()],
            scratch_shapes=[
                pltpu.VMEM((tokens, width), jnp.float32),
                pltpu.VMEM((tokens, width), jnp.float32),
                pltpu.VMEM((2, 3, group, tr, width), jnp.bfloat16),
                pltpu.VMEM((2, 3, group, tr, width), jnp.bfloat16),
                pltpu.SemaphoreType.DMA((2,)),
                pltpu.SemaphoreType.DMA((2,)),
            ],
        ),
        out_shape=[
            jax.ShapeDtypeStruct((tokens, width), jnp.bfloat16),
            jax.ShapeDtypeStruct((tokens, width), jnp.float32),
            jax.ShapeDtypeStruct((tokens, width), jnp.bfloat16),
            jax.ShapeDtypeStruct((8, width), jnp.float32),
            jax.ShapeDtypeStruct(wall.shape, jnp.bfloat16),
        ],
        compiler_params=pltpu.CompilerParams(vmem_limit_bytes=60 << 20, dimension_semantics=("arbitrary",)),
        name="ffn",
    )(table, normed, cot, middle, gains, wall)


MESH = pl.DeviceIdType.MESH
EVERY = slice(None)
GATHER_ROUTES = (
    ("z1", "z2", "z3", "x", "y", "core"),
    ("z1", "z2", "z3", "y", "x", "core"),
    ("x", "z1", "z2", "z3", "y", "core"),
    ("y", "z1", "z2", "z3", "x", "core"),
)


def position():
    dp = lax.axis_index("dp")
    return dp // 4, lax.rem(dp // 2, 2), lax.rem(dp, 2), lax.axis_index("fsdp")


def target(hop):
    y, x, c, z = position()
    if hop == "x":
        x = 1 - x
    elif hop == "y":
        y = 1 - y
    elif hop == "core":
        c = 1 - c
    elif hop == "back":
        z = lax.rem(z + 3, 4)
    else:
        z = lax.rem(z + 1, 4)
    return (y * 4 + x * 2 + c, z)


def enter(hops):
    barrier = pltpu.get_barrier_semaphore()
    for hop in hops:
        pl.semaphore_signal(barrier, inc=1, device_id=target(hop), device_id_type=MESH)
    pl.semaphore_wait(barrier, len(hops))


GATHER_PLAN = (3, (0, 0, 0, 0), (10, 6), (11, 3))
SCATTER_PLAN = (3, (5, 5, 0, 0), (4, 6), (40, 0))


def split_slots(caps, plan):
    small = caps * plan[0] // 16
    third = (caps - 2 * small) // 2
    counts = (small, small, third, caps - 2 * small - third)
    starts = (0, small, 2 * small, 2 * small + third)
    return counts, starts


def round_count(counts, plan):
    share, delays, (dense, extra), (gap, pause) = plan
    ends = []
    for route in range(4):
        at = [
            t
            for t in range(200)
            if (t % 2 == 0 or dense <= t < dense + extra if route < 2 else not gap <= t < gap + pause)
        ]
        ends.append(delays[route] + at[counts[route] - 1] + 1)
    return max(ends)


def passed(at, edge):
    return (at - edge + 64) // 64


def turn(route, at, counts, plan):
    share, delays, (dense, extra), (gap, pause) = plan
    at = at - delays[route]
    if route < 2:
        begun = passed(at, dense)
        over = passed(at, dense + extra)
        slow = at // 2
        quick = dense // 2 + at - dense
        late = dense // 2 + extra + (at - dense - extra) // 2
        index = (1 - begun) * slow + (begun - over) * quick + over * late
        even = lax.rem(at + 64, 2) == 0
        live = (at >= 0) & (even | (begun - over == 1)) & (index < counts[route])
        return live, index
    index = at - pause * passed(at, gap)
    live = (at >= 0) & ((at < gap) | (at >= gap + pause)) & (index < counts[route])
    return live, index


def slot_of(route, index, counts, starts, lead, early):
    if route < 2:
        return 2 * lead + starts[route] + index
    here = 2 * lead + starts[route] - (route - 2) * lead
    count = counts[route]
    if early:
        later = (index + count - lead) // count
        return (route - 2) * lead + index + later * (here - route * lead + lead)
    final = index // (count - lead)
    return here + index - final * (here + count - lead - (route - 2) * lead)


def attend_side(side, q, k_pair, v_pair, mask, out_ref, logs):
    lane = lax.broadcasted_iota(jnp.int32, (q.shape[0], 128), 1)
    scale = jnp.bfloat16(1.0 / HEAD**0.5)
    k = k_pair[:, side * HEAD : (side + 1) * HEAD]
    v = v_pair[:, side * HEAD : (side + 1) * HEAD]
    for h in range(GROUP):
        cols = slice(h * HEAD, (h + 1) * HEAD)
        scores = jnp.where(mask, dot(q[:, cols] * scale, k, NT), masked_score)
        top = jnp.max(scores, axis=1, keepdims=True)
        raised = jnp.exp(scores - top)
        total = jnp.sum(raised, axis=1, keepdims=True)
        probs = (raised * (1.0 / total)).astype(jnp.bfloat16)
        out_ref[:, cols] = dot(probs, v, NN).astype(out_ref.dtype)
        logs = jnp.where(lane == side * GROUP + h, top + jnp.log(total), logs)
    return logs


GATHER_HOPS = ("z1", "z2", "z3")


def gather_kernel(
    lead,
    mine_ref,
    gain_ref,
    table,
    places,
    hidden_ref,
    cos_ref,
    sin_ref,
    wall_ref,
    gains_ref,
    weights_ref,
    both_ref,
    all_gains_ref,
    normed_ref,
    q_ref,
    att_ref,
    lse_ref,
    middle_ref,
    normed_two_ref,
    own_sem,
    send_sem,
    recv_sem,
    tiles,
    block,
    gain_tiles,
    keys,
    mask_ref,
    pair_ref,
    side_sem,
    hop_send,
    hop_recv,
):
    y, x, c, z = position()
    counts, starts = split_slots(mine_ref.shape[0], GATHER_PLAN)
    rounds = round_count(counts, GATHER_PLAN)
    own = pltpu.make_async_copy(mine_ref, wall_ref.at[y, x, c, z], own_sem.at[0])
    own_gain = pltpu.make_async_copy(gain_ref, gains_ref.at[y, x, c, z], own_sem.at[1])
    own.start()
    own_gain.start()
    enter(("x", "y", "core", "z", "back"))
    own.wait()
    own_gain.wait()

    def region(route, stage):
        hops = GATHER_ROUTES[route % 4]
        hop = hops[stage]
        done = hops[:stage]
        at_y = EVERY if "y" in done else y
        at_x = EVERY if "x" in done else x
        at_z = EVERY if "z3" in done else z
        if hop in ("z1", "z2", "z3"):
            at_z = lax.rem(z + 5 - int(hop[1]), 4)
        return at_y, at_x, c, at_z

    def copy(route, stage, index):
        if route == 4:
            view = gains_ref.at[region(route, stage)]
        else:
            slot = slot_of(route, index, counts, starts, lead // 2, True)
            view = wall_ref.at[region(route, stage) + (slot,)]
        return pltpu.make_async_remote_copy(
            src_ref=view,
            dst_ref=view,
            send_sem=send_sem.at[route, stage],
            recv_sem=recv_sem.at[route, stage, index],
            device_id=target(GATHER_ROUTES[route % 4][stage]),
            device_id_type=MESH,
        )

    stages = len(GATHER_ROUTES[0])
    tokens, width = hidden_ref.shape
    number = block.shape[0]
    rows = number * block.shape[1]
    query_blocks = q_ref.shape[1] // rows
    key_blocks = keys.shape[1] // rows

    def take(at):
        @pl.loop(0, number, unroll=True)
        def _(t):
            block[t] = tiles[table[at * number + t]]

        pltpu.make_async_copy(
            block, weights_ref.at[pl.ds(at * number, number)], side_sem.at[1]
        ).start()
        return block[...].reshape(rows, width)

    def taken(at):
        pltpu.make_async_copy(
            block, weights_ref.at[pl.ds(at * number, number)], side_sem.at[1]
        ).wait()

    def load_tiles(d):
        return pltpu.make_async_copy(
            wall_ref.at[d // 16, lax.rem(d // 8, 2), lax.rem(d // 4, 2), lax.rem(d, 4), pl.ds(0, lead)],
            tiles.at[pl.ds(d * lead, lead)],
            side_sem.at[0],
        )

    load_gains = pltpu.make_async_copy(gains_ref, gain_tiles, side_sem.at[2])

    def pass_keys(part):
        hop = part // 2
        at = lax.rem(z + 4 - hop, 4)
        cols = KV_HEADS * HEAD
        view = keys.at[
            pl.ds(pl.multiple_of(at * tokens, tokens), tokens),
            pl.ds(part % 2 * cols, cols),
        ]
        return pltpu.make_async_remote_copy(
            src_ref=view,
            dst_ref=view,
            send_sem=hop_send.at[part],
            recv_sem=hop_recv.at[part],
            device_id=target(GATHER_HOPS[hop]),
            device_id_type=MESH,
        )

    def begin():
        @pl.loop(0, 32)
        def _(d):
            load_tiles(d).start()

        load_gains.start()

    def norm():
        load_gains.wait()
        lane = lax.broadcasted_iota(jnp.int32, (8, 128), 1)
        parts = []
        for d in range(0, 32, 2):
            even = gain_tiles[d // 16, (d // 8) % 2, (d // 4) % 2, d % 4].astype(jnp.float32)[:8]
            odd = gain_tiles[d // 16, (d // 8) % 2, (d // 4) % 2, d % 4 + 1].astype(jnp.float32)[:8]
            parts.append(jnp.where(lane < 64, even, pltpu.roll(odd, 64, 1)))
        all_gains_ref[...] = jnp.concatenate(parts, axis=1)
        hidden = hidden_ref[...].astype(jnp.float32)
        inv = lax.rsqrt(jnp.mean(hidden * hidden, axis=1, keepdims=True) + norm_eps)
        normed_ref[...] = (hidden * inv * all_gains_ref[0:1, :]).astype(normed_ref.dtype)
        fill_mask(places, mask_ref)

    def project_keys():
        pltpu.make_async_copy(tiles, tiles, side_sem.at[0]).wait()
        own_rows = pl.ds(pl.multiple_of(z * tokens, tokens), tokens)

        for b in range(key_blocks):
            at = query_blocks + b
            u = dot(normed_ref[...], take(at), NT)
            if b < key_blocks // 2:
                u = u * cos_ref[...] + swap_halves(u) * sin_ref[...]
            keys[own_rows, b * rows : (b + 1) * rows] = u.astype(keys.dtype)
            taken(at)

    def project_queries(low, high):
        @pl.loop(low, high)
        def _(b):
            u = dot(normed_ref[...], take(b), NT)
            u = u * cos_ref[...] + swap_halves(u) * sin_ref[...]
            q_ref[:, pl.ds(pl.multiple_of(b * rows, rows), rows)] = u.astype(q_ref.dtype)
            taken(b)

    def attend_step(pair, side):
        wide = GROUP * HEAD
        narrow = PAIR * HEAD
        here = pl.ds(pl.multiple_of((pair * PAIR + side) * wide, wide), wide)
        k_pair = keys[:, pl.ds(pl.multiple_of(pair * narrow, narrow), narrow)]
        v_pair = keys[:, pl.ds(pl.multiple_of(KV_HEADS * HEAD + pair * narrow, narrow), narrow)]
        logs = lse_ref[pair] if side else jnp.zeros((tokens, 128), jnp.float32)
        mask = mask_ref[...] > 0.5
        lse_ref[pair] = attend_side(side, q_ref[:, here], k_pair, v_pair, mask, pair_ref, logs)
        att_ref[:, here] = pair_ref[...]

    def mix_blocks(low):
        for more in range(4):
            b = low + more
            at = query_blocks + key_blocks + b
            left = att_ref[:, pl.ds(pl.multiple_of(b * rows, rows), rows)]
            middle_ref[...] += dot(left, take(at), NN)
            taken(at)

    def mix_end():
        middle = middle_ref[...]
        inv = lax.rsqrt(jnp.mean(middle * middle, axis=1, keepdims=True) + norm_eps)
        normed_two_ref[...] = (middle * inv * all_gains_ref[1:2, :]).astype(normed_two_ref.dtype)

    start = GATHER_PLAN[1][3] + lead // 2 - 1 + stages
    keep_both = pltpu.make_async_copy(keys, both_ref, side_sem.at[3])

    @pl.loop(0, rounds + stages)
    def _(t):
        for stage in range(stages + 1):
            for route in range(5):
                if route == 4:
                    live, index = t == stage, 0
                else:
                    live, index = turn(route, t - stage, counts, GATHER_PLAN)

                @pl.when(live)
                def _(stage=stage, route=route, index=index):
                    if stage > 0:
                        copy(route, stage - 1, index).wait()
                    if stage < stages:
                        copy(route, stage, index).start()

        @pl.when(t == start)
        def _():
            begin()
            norm()

        @pl.when(t == start + 1)
        def _():
            project_keys()

        parts = 2 * len(GATHER_HOPS)
        for part in range(parts + 1):

            @pl.when(t == start + 1 + part)
            def _(part=part):
                if part > 0:
                    pass_keys(part - 1).wait()
                if part < parts:
                    pass_keys(part).start()

        for third in range(4):

            @pl.when(t == start + 2 + third)
            def _(third=third):
                project_queries(third * query_blocks // 4, (third + 1) * query_blocks // 4)

        attending = start + 1 + parts

        @pl.when(t == attending)
        def _():
            keep_both.start()
            middle_ref[...] = hidden_ref[...].astype(jnp.float32)

        for side in range(PAIR):
            since = t - attending

            @pl.when((since >= 0) & (since < KV_HEADS) & (lax.rem(since + 64, 2) == side))
            def _(side=side, since=since):
                attend_step(since // 2, side)

        mixing = attending + KV_HEADS

        @pl.when((t >= mixing) & (t < mixing + query_blocks // 4))
        def _():
            mix_blocks((t - mixing) * 4)

        @pl.when(t == mixing + query_blocks // 4)
        def _():
            mix_end()
            keep_both.wait()


def gather_slots(low_tiles, low_gains, table, places, hidden, cosine, sine, lead):
    caps, rows, width = low_tiles.shape
    tokens = hidden.shape[0]
    length = tokens * 4
    counts, starts = split_slots(caps, GATHER_PLAN)
    kind = low_tiles.dtype
    vmem = pl.BlockSpec(memory_space=pltpu.VMEM)
    smem = pl.BlockSpec(memory_space=pltpu.SMEM)
    anyw = pl.BlockSpec(memory_space=pl.ANY)
    padded = jnp.pad(low_gains, ((0, 16 - low_gains.shape[0]), (0, 128 - low_gains.shape[1])))
    number = cosine.shape[1] // rows
    pairs = KV_HEADS // PAIR
    outs = pl.pallas_call(
        functools.partial(gather_kernel, lead),
        out_shape=[
            jax.ShapeDtypeStruct((2, 2, 2, 4, caps, rows, width), kind),
            jax.ShapeDtypeStruct((2, 2, 2, 4) + padded.shape, kind),
            jax.ShapeDtypeStruct((table.shape[0], rows, width), kind),
            jax.ShapeDtypeStruct((length, 2 * KV_HEADS * HEAD), kind),
            jax.ShapeDtypeStruct((8, width), jnp.float32),
            jax.ShapeDtypeStruct((tokens, width), kind),
            jax.ShapeDtypeStruct((tokens, width), kind),
            jax.ShapeDtypeStruct((tokens, width), kind),
            jax.ShapeDtypeStruct((pairs, tokens, 128), jnp.float32),
            jax.ShapeDtypeStruct((tokens, width), jnp.float32),
            jax.ShapeDtypeStruct((tokens, width), kind),
        ],
        in_specs=[vmem, vmem, smem, smem, vmem, vmem, vmem],
        out_specs=[anyw] * 4 + [vmem] * 7,
        scratch_shapes=[
            pltpu.SemaphoreType.DMA((2,)),
            pltpu.SemaphoreType.DMA((5, 6)),
            pltpu.SemaphoreType.DMA((5, 6, max(counts))),
            pltpu.VMEM((32 * lead, rows, width), kind),
            pltpu.VMEM((number, rows, width), kind),
            pltpu.VMEM((2, 2, 2, 4) + padded.shape, kind),
            pltpu.VMEM((length, 2 * KV_HEADS * HEAD), kind),
            pltpu.VMEM((tokens, length), jnp.float32),
            pltpu.VMEM((tokens, GROUP * HEAD), kind),
            pltpu.SemaphoreType.DMA((4,)),
            pltpu.SemaphoreType.DMA((6,)),
            pltpu.SemaphoreType.DMA((6,)),
        ],
        compiler_params=pltpu.CompilerParams(
            collective_id=0, has_side_effects=True, vmem_limit_bytes=62 << 20
        ),
        name="gather_slots",
    )(low_tiles, padded, table, places, hidden, cosine, sine)
    return [outs[0].reshape(32 * caps, rows, width)] + list(outs[2:])


SCATTER_ROUTES = (
    ("core", "y", "x", "z1", "z2", "z3", "end"),
    ("core", "x", "y", "z1", "z2", "z3", "end"),
    ("core", "y", "z1", "z2", "z3", "x", "end"),
    ("core", "x", "z1", "z2", "z3", "y", "end"),
)


SUM_HOPS = ("core", "x", "y", "z1", "z2", "z3")
SUM_START = 2


def scatter_extent(route, stage):
    hops = SCATTER_ROUTES[route]
    done = hops[1 : stage + 1] if hops[stage] in ("x", "y") else hops[1:stage]
    extent = []
    if "x" not in done or "y" not in done:
        extent.append(2)
    if not any(hop[0] == "z" for hop in hops[: stage + 1]):
        extent.append(4)
    return tuple(extent)


def scatter_terms(route, stage):
    hops = SCATTER_ROUTES[route]
    done = hops[1:stage]
    return 2 + ("x" in done) + ("y" in done) + ("z1" in done)


def attend_back_side(side, q, k_pair, v_pair, grad, mask, logs, turn_ref, k_out, v_out):
    scale = jnp.bfloat16(1.0 / HEAD**0.5)
    here = slice(side * HEAD, (side + 1) * HEAD)
    k = k_pair[:, here]
    v = v_pair[:, here]
    dk = None
    dv = None
    for h in range(GROUP):
        cols = slice(h * HEAD, (h + 1) * HEAD)
        head = side * GROUP + h
        q_head = q[:, cols] * scale
        scores = jnp.where(mask, dot(q_head, k, NT), masked_score)
        probs = jnp.exp(scores - logs[:, head : head + 1])
        grad_probs = dot(grad[:, cols], v, NT)
        row_dot = jnp.sum(probs * grad_probs, axis=1, keepdims=True)
        grad_scores = (probs * (grad_probs - row_dot)).astype(jnp.bfloat16)
        turn_ref[:, cols] = dot(grad_scores, k, NN) * (1.0 / HEAD**0.5)
        dk_part = dot(q_head, grad_scores, TN)
        dv_part = dot(grad[:, cols], probs.astype(jnp.bfloat16), TN)
        dk = dk_part if dk is None else dk + dk_part
        dv = dv_part if dv is None else dv + dv_part
    k_out[:, here] = dk.T.astype(k_out.dtype)
    v_out[:, here] = dv.T.astype(v_out.dtype)


def scatter_kernel(
    look,
    lead,
    first_group,
    old_ref,
    gain_ref,
    weights_ref,
    table,
    places,
    branch_ref,
    att_ref,
    q_ref,
    both_ref,
    lse_ref,
    normed_ref,
    hidden_ref,
    cos_ref,
    sin_ref,
    grad_ref,
    gains_ref,
    wall_ref,
    out_ref,
    total_ref,
    input_ref,
    core_ref,
    first_ref,
    second_ref,
    ring_ref,
    last_ref,
    *scratch,
):
    y, x, c, z = position()
    caps, rows, width = out_ref.shape
    counts, starts = split_slots(caps, SCATTER_PLAN)
    rounds = round_count(counts, SCATTER_PLAN)
    stages = len(SCATTER_ROUTES[0])
    held = {}
    made = {}
    scratch = list(scratch)
    for route in range(4):
        for stage in range(1, stages):
            held[route, stage] = scratch.pop(0)
            made[route, stage] = scratch.pop(0)
    load_sem, send_sem, recv_sem, out_sem, sums, landed, sum_send, sum_recv = scratch[:8]
    (
        streamed,
        grad_att,
        grad_q,
        grad_kv,
        grad_both,
        k_pair_ref,
        v_pair_ref,
        turn_ref,
        hop_out,
        hop_in,
        turned,
        left_ref,
        built,
        mask_ref,
        stream_sem,
        hop_send,
        hop_recv,
        built_sem,
        back_ref,
    ) = scratch[8:]
    enter(("x", "y", "core", "z", "back"))

    def landing(route, stage, slot):
        hops = SCATTER_ROUTES[route]
        hop = hops[stage]
        if hop == "core":
            return core_ref.at[:, :, :, slot]
        if hop[0] == "z":
            ring = ring_ref.at[int(hop[1]) - 1]
            return ring.at[0, slot] if route < 2 else ring.at[:, slot]
        if stage == 1:
            return first_ref.at[:, :, slot]
        if stage == 2:
            return second_ref.at[:, slot]
        return last_ref.at[slot]

    def terms(route, stage, slot):
        hops = SCATTER_ROUTES[route]
        hop = hops[stage]
        done = hops[1:stage]
        at_y = 1 - y if hop == "y" else (y if "y" in done else EVERY)
        at_x = 1 - x if hop == "x" else (x if "x" in done else EVERY)
        at_z = EVERY
        if hop[0] == "z":
            at_z = lax.rem(z + 4 - int(hop[1]), 4)
        elif "z3" in done:
            at_z = z
        views = [wall_ref.at[at_y, at_x, c, at_z, slot], core_ref.at[at_y, at_x, at_z, slot]]
        other = at_x if hops[1] == "y" else at_y
        if stage > 1:
            views.append(first_ref.at[other, at_z, slot])
        if route < 2 and stage > 2:
            views.append(second_ref.at[at_z, slot])
        if hop in ("z2", "z3"):
            ring = ring_ref.at[int(hop[1]) - 2]
            views.append(ring.at[0, slot] if route < 2 else ring.at[:, slot])
        elif "z3" in done:
            ring = ring_ref.at[2]
            views.append(ring.at[0, slot] if route < 2 else ring.at[other, slot])
        if route >= 2 and hop == "end":
            views.append(last_ref.at[slot])
        return views

    def slot_at(route, index):
        return slot_of(route, index, counts, starts, lead // 2, False)

    def send(route, stage, index):
        slot = slot_at(route, index)
        if stage == 0:
            source = wall_ref.at[:, :, 1 - c, :, slot]
        else:
            source = made[route, stage]
        return pltpu.make_async_remote_copy(
            src_ref=source,
            dst_ref=landing(route, stage, slot),
            send_sem=send_sem.at[route, stage],
            recv_sem=recv_sem.at[route, stage, index],
            device_id=target(SCATTER_ROUTES[route][stage]),
            device_id_type=MESH,
        )

    def keep(route, index):
        return pltpu.make_async_copy(
            made[route, stages - 1], out_ref.at[slot_at(route, index)], out_sem.at[route]
        )

    def early(route, stage, index):
        if stage > 0:
            for k, view in enumerate(terms(route, stage, slot_at(route, index))[:-1]):
                pltpu.make_async_copy(view, held[route, stage].at[k], load_sem.at[route, stage]).start()

    def late(route, stage, index):
        if stage > 0:
            send(route, stage - 1, index).wait()
            view = terms(route, stage, slot_at(route, index))[-1]
            last = held[route, stage].shape[0] - 1
            pltpu.make_async_copy(view, held[route, stage].at[last], load_sem.at[route, stage]).start()

    def finish(route, stage, index):
        if stage > 0:
            buf = held[route, stage]
            pltpu.make_async_copy(buf, buf, load_sem.at[route, stage]).wait()
            number = buf.shape[0]
            extent = buf.shape[1:-2]
            blocks = 1
            for size in extent:
                blocks *= size
            part = min(width, 512)
            if stage == stages - 1:

                @pl.when(index > 0)
                def _():
                    keep(route, index - 1).wait()

            @pl.loop(0, blocks)
            def _(block):
                if len(extent) == 2:
                    at = (block // extent[1], lax.rem(block, extent[1]))
                elif len(extent) == 1:
                    at = (block,)
                else:
                    at = ()
                for left in range(0, width, part):
                    cols = pl.ds(left, part)
                    total = buf[(0,) + at + (EVERY, cols)].astype(jnp.float32)
                    for k in range(1, number):
                        total += buf[(k,) + at + (EVERY, cols)].astype(jnp.float32)
                    made[route, stage][at + (EVERY, cols)] = total.astype(made[route, stage].dtype)

        if stage < stages - 1:
            send(route, stage, index).start()
        else:
            keep(route, index).start()

    def pass_sum(hop):
        return pltpu.make_async_remote_copy(
            src_ref=sums.at[hop] if hop < 4 else landed.at[hop - 1],
            dst_ref=landed.at[hop],
            send_sem=sum_send.at[hop],
            recv_sem=sum_recv.at[hop],
            device_id=target(SUM_HOPS[hop]),
            device_id_type=MESH,
        )

    def add_sums(step):
        if step > 0:
            pass_sum(step - 1).wait()
        if step == 0:
            hidden = hidden_ref[...].astype(jnp.float32)
            inv = lax.rsqrt(jnp.mean(hidden * hidden, axis=1, keepdims=True) + norm_eps)
            back = back_ref[...]
            term = jnp.sum(back * hidden * inv, axis=0, keepdims=True)
            scaled = back * gains_ref[0:1, :]
            part = jnp.mean(scaled * hidden, axis=1, keepdims=True)
            input_ref[...] = grad_ref[...] + inv * scaled - hidden * inv**3 * part
            line = lax.broadcasted_iota(jnp.int32, gain_ref.shape, 0)
            sums[0] = jnp.where(line == 0, term, gain_ref[...])
        elif step < 4:
            sums[step] = sums[step - 1] + landed[step - 1]
        elif step == len(SUM_HOPS):
            total_ref[...] = (sums[3] + landed[3]) + (landed[4] + landed[5])
        if step < len(SUM_HOPS):
            pass_sum(step).start()

    tokens = hidden_ref.shape[0]
    number = cos_ref.shape[1] // rows
    block = number * rows
    query_blocks = q_ref.shape[1] // block
    key_blocks = both_ref.shape[1] // block
    out_blocks = att_ref.shape[1] // block
    all_blocks = query_blocks + key_blocks + out_blocks
    kv_width = KV_HEADS * HEAD

    def stream(n):
        at = lax.rem(n + query_blocks + key_blocks, all_blocks)
        return pltpu.make_async_copy(
            weights_ref.at[pl.ds(at * number, number)],
            streamed.at[lax.rem(n, 2)],
            stream_sem.at[lax.rem(n, 2)],
        )

    def streamed_block(n):
        stream(n).wait()

        @pl.when(n + 1 < all_blocks)
        def _():
            stream(n + 1).start()

        return streamed[lax.rem(n, 2)].reshape(block, width)

    def column(b):
        return pl.ds(pl.multiple_of(b * block, block), block)

    def turn_tiles(at, value):
        flipped = value.astype(jnp.float32).T.astype(turned.dtype)
        turned[pl.ds(at * number, number)] = flipped.reshape(number, rows, tokens)

    def out_back(low, high):
        @pl.loop(low, high)
        def _(b):
            grad_att[:, column(b)] = dot(branch_ref[...], streamed_block(b), NT).astype(
                grad_att.dtype
            )
            turn_tiles(query_blocks + key_blocks + b, att_ref[:, column(b)])

    def query_back(low, high):
        @pl.loop(low, high)
        def _(b):
            left = grad_q[:, column(b)]
            back_ref[...] += dot(left, streamed_block(out_blocks + b), NN)
            turn_tiles(b, left)

    def key_back():
        @pl.loop(0, key_blocks)
        def _(b):
            left = grad_both[:, column(b)]
            back_ref[...] += dot(left, streamed_block(out_blocks + query_blocks + b), NN)
            turn_tiles(query_blocks + b, left)

    def attend_back_step(pair, side):
        wide = GROUP * HEAD
        narrow = PAIR * HEAD
        here = pl.ds(pl.multiple_of((pair * PAIR + side) * wide, wide), wide)
        k_cols = pl.ds(pl.multiple_of(pair * narrow, narrow), narrow)
        v_cols = pl.ds(pl.multiple_of(kv_width + pair * narrow, narrow), narrow)
        attend_back_side(
            side,
            q_ref[:, here],
            both_ref[:, k_cols],
            both_ref[:, v_cols],
            grad_att[:, here],
            mask_ref[...] > 0.5,
            lse_ref[pair],
            turn_ref,
            k_pair_ref,
            v_pair_ref,
        )
        u = turn_ref[...]
        grad_q[:, here] = (u * cos_ref[...] - swap_halves(u) * sin_ref[...]).astype(grad_q.dtype)
        if side == PAIR - 1:
            grad_kv[:, k_cols] = k_pair_ref[...]
            grad_kv[:, v_cols] = v_pair_ref[...]

    def key_rows(far):
        at = lax.rem(z + 4 - far, 4)
        return pl.ds(pl.multiple_of(at * tokens, tokens), tokens)

    def pass_terms(hop):
        return pltpu.make_async_remote_copy(
            src_ref=hop_out.at[hop],
            dst_ref=hop_in.at[hop],
            send_sem=hop_send.at[hop],
            recv_sem=hop_recv.at[hop],
            device_id=target("z1"),
            device_id_type=MESH,
        )

    def key_terms(hop):
        if hop > 0:
            pass_terms(hop - 1).wait()
        if hop < 3:
            own = grad_kv[key_rows(hop + 1), :]
            if hop > 0:
                own = (own.astype(jnp.float32) + hop_in[hop - 1].astype(jnp.float32)).astype(own.dtype)
            hop_out[hop] = own
            pass_terms(hop).start()
        else:
            own = grad_kv[key_rows(0), :].astype(jnp.float32) + hop_in[2].astype(jnp.float32)
            for b in range(key_blocks):
                u = own[:, b * block : (b + 1) * block]
                if b < key_blocks // 2:
                    u = u * cos_ref[...] - swap_halves(u) * sin_ref[...]
                grad_both[:, b * block : (b + 1) * block] = u.astype(grad_both.dtype)

    def built_copy(which, j, d):
        return pltpu.make_async_copy(
            built.at[which, d],
            wall_ref.at[d // 16, lax.rem(d // 8, 2), lax.rem(d // 4, 2), lax.rem(d, 4), j],
            built_sem.at[which],
        )

    def build(which, j, right_ref):
        @pl.loop(0, 32, unroll=True)
        def _(d):
            left_ref[d] = turned[table[d * lead + j]]

        for part in range(4):
            left = left_ref[part * 8 : (part + 1) * 8].reshape(8 * rows, tokens)
            value = dot(left, right_ref[...], NN).astype(built.dtype)
            built[which, part * 8 : (part + 1) * 8] = value.reshape(8, rows, width)

        @pl.loop(0, 32)
        def _(d):
            built_copy(which, j, d).start()

    def finish_built(which):
        pltpu.make_async_copy(built.at[which], built.at[which], built_sem.at[which]).wait()

    half = lead // 2
    attending = 2
    passing = attending + KV_HEADS
    building = passing + 5
    stream(0).start()

    def beside(t):
        for step in range(2):

            @pl.when(t == step)
            def _(step=step):
                if step == 0:
                    fill_mask(places, mask_ref)
                    back_ref[...] = jnp.zeros_like(back_ref)
                out_back(step * out_blocks // 2, (step + 1) * out_blocks // 2)

        for side in range(PAIR):
            since = t - attending

            @pl.when((since >= 0) & (since < KV_HEADS) & (lax.rem(since + 64, 2) == side))
            def _(side=side, since=since):
                attend_back_step(since // 2, side)

        for hop in range(4):

            @pl.when(t == passing + hop)
            def _(hop=hop):
                key_terms(hop)
                query_back(hop * query_blocks // 4, (hop + 1) * query_blocks // 4)

        @pl.when(t == passing + 4)
        def _():
            key_back()

        pair = t - building

        @pl.when((pair >= 1) & (pair <= half))
        def _():
            finish_built(0)
            finish_built(1)

        @pl.when((pair >= 0) & (pair < half))
        def _():
            build(0, pair, normed_ref)

        split = first_group - half

        @pl.when((pair >= 0) & (pair < split))
        def _():
            build(1, half + pair, normed_ref)

        @pl.when((pair >= split) & (pair < half))
        def _():
            build(1, half + pair, branch_ref)

        for step in range(len(SUM_HOPS) + 1):

            @pl.when(t == building + step)
            def _(step=step):
                add_sums(step)

    @pl.loop(0, rounds + stages - 1)
    def _(t):
        items = [(stage, route) for stage in range(stages - 1, -1, -1) for route in range(4)]

        def run(which, work):
            stage, route = items[which]
            live, index = turn(route, t - stage, counts, SCATTER_PLAN)

            @pl.when(live)
            def _():
                work(route, stage, index)

        far, near, place_beside = look
        for which in range(len(items) + far):
            if which == place_beside:
                beside(t)
            if which < len(items):
                run(which, early)
            if far - near <= which < len(items) + far - near:
                run(which - far + near, late)
            if which >= far:
                run(which - far, finish)

    for route in range(4):
        keep(route, counts[route] - 1).wait()


def scatter_slots(
    grads_wall,
    gain_terms,
    weights,
    table,
    places,
    branch,
    attended,
    queries,
    both,
    lse,
    normed,
    hidden,
    cosine,
    sine,
    grad_middle,
    gains,
    lead,
    first_group,
    caps,
    look=(5, 2, 17),
):
    rows, width = grads_wall.shape[1:]
    kind = grads_wall.dtype
    wall = grads_wall.reshape(2, 2, 2, 4, caps, rows, width)
    counts, starts = split_slots(caps, SCATTER_PLAN)
    stages = len(SCATTER_ROUTES[0])
    scratch = []
    for route in range(4):
        for stage in range(1, stages):
            extent = scatter_extent(route, stage)
            scratch.append(pltpu.VMEM((scatter_terms(route, stage),) + extent + (rows, width), kind))
            last = stage == stages - 1
            scratch.append(pltpu.VMEM(extent + (rows, width), jnp.float32 if last else kind))
    tile = (caps, rows, width)
    tokens = hidden.shape[0]
    number = cosine.shape[1] // rows
    length, both_width = both.shape
    dma = pltpu.SemaphoreType.DMA
    scratch += [
        dma((4, stages)),
        dma((4, stages)),
        dma((4, stages, max(counts))),
        dma((4,)),
        pltpu.VMEM((4,) + gain_terms.shape, jnp.float32),
        pltpu.VMEM((6,) + gain_terms.shape, jnp.float32),
        dma((6,)),
        dma((6,)),
        pltpu.VMEM((2, number, rows, width), kind),
        pltpu.VMEM((tokens, width), kind),
        pltpu.VMEM((tokens, width), kind),
        pltpu.VMEM((length, both_width), kind),
        pltpu.VMEM((tokens, both_width), kind),
        pltpu.VMEM((length, PAIR * HEAD), kind),
        pltpu.VMEM((length, PAIR * HEAD), kind),
        pltpu.VMEM((tokens, GROUP * HEAD), jnp.float32),
        pltpu.VMEM((3, tokens, both_width), kind),
        pltpu.VMEM((3, tokens, both_width), kind),
        pltpu.VMEM((weights.shape[0], rows, tokens), kind),
        pltpu.VMEM((32, rows, tokens), kind),
        pltpu.VMEM((2, 32, rows, width), kind),
        pltpu.VMEM((tokens, length), jnp.float32),
        dma((2,)),
        dma((3,)),
        dma((3,)),
        dma((2,)),
        pltpu.VMEM((tokens, width), jnp.float32),
    ]
    vmem = pl.BlockSpec(memory_space=pltpu.VMEM)
    smem = pl.BlockSpec(memory_space=pltpu.SMEM)
    anyw = pl.BlockSpec(memory_space=pl.ANY)
    out = pl.pallas_call(
        functools.partial(scatter_kernel, look, lead, first_group),
        out_shape=[
            jax.ShapeDtypeStruct(wall.shape, kind),
            jax.ShapeDtypeStruct(tile, jnp.float32),
            jax.ShapeDtypeStruct(gain_terms.shape, jnp.float32),
            jax.ShapeDtypeStruct((tokens, width), jnp.float32),
            jax.ShapeDtypeStruct((2, 2, 4) + tile, kind),
            jax.ShapeDtypeStruct((2, 4) + tile, kind),
            jax.ShapeDtypeStruct((4,) + tile, kind),
            jax.ShapeDtypeStruct((3, 2) + tile, kind),
            jax.ShapeDtypeStruct(tile, kind),
        ],
        in_specs=[anyw, vmem, anyw, smem, smem] + [vmem] * 11,
        out_specs=[anyw, anyw, vmem, vmem] + [anyw] * 5,
        scratch_shapes=scratch,
        input_output_aliases={0: 0},
        compiler_params=pltpu.CompilerParams(
            collective_id=1, has_side_effects=True, vmem_limit_bytes=62 << 20
        ),
        name="scatter_slots",
    )(
        wall, gain_terms, weights, table, places, branch, attended, queries, both, lse, normed,
        hidden, cosine, sine, grad_middle, gains,
    )
    return out[1], out[2], out[3]


def shards(
    hidden_in,
    piece_starts,
    out_cotangent,
    owners,
    master,
    moment_one,
    moment_two,
    gain_master,
    gain_one,
    gain_two,
):
    devices = lax.axis_size("dp") * lax.axis_size("fsdp")
    caps, tile_rows, model_width = master.shape
    layout = section_layout(devices, tile_rows)
    slots = slot_numbers(owners, layout, caps)
    local_len = hidden_in.shape[0]
    first = lax.axis_index("fsdp") * local_len
    positions = first + jnp.arange(local_len, dtype=jnp.int32)
    places = jnp.concatenate([first[None].astype(jnp.int32), piece_starts[0]])
    cosine, sine = rope_tables(positions.astype(jnp.float32), 16 * tile_rows)
    (
        wall, weights, gains_low, both, normed, queries, attended, lse, middle, normed_two
    ) = forward_attention(
        master.astype(jnp.bfloat16),
        gain_master.astype(jnp.bfloat16),
        slots,
        places,
        hidden_in,
        cosine,
        sine,
        layout,
    )
    block_out, grad_middle, grad_branch, gain_terms, grads_wall = ffn_call(
        slots,
        (layout[2][0], layout[2][0] + layout[2][1] // 2, layout[3][0]),
        layout[3][1],
        normed_two,
        out_cotangent,
        middle,
        gains_low,
        wall,
    )
    weight_grad, gain_grad, input_grad = backward_attention(
        grads_wall,
        gain_terms,
        grad_middle,
        gains_low,
        weights,
        slots,
        places,
        grad_branch,
        attended,
        queries,
        both,
        lse,
        normed,
        hidden_in,
        cosine,
        sine,
        layout,
        caps,
    )
    keep_slot = filled_mask(slots, caps, lax.axis_index(("dp", "fsdp")))[:, None, None]
    weight_grad = jnp.where(keep_slot, weight_grad, 0.0)
    step = float(STEP)
    new_one, new_two, new_weights = adam_step(
        master, moment_one, moment_two, weight_grad, step, decay_rate, learn_rate
    )
    new_one = jnp.where(keep_slot, new_one, 0.0)
    new_two = jnp.where(keep_slot, new_two, 0.0)
    new_weights = jnp.where(keep_slot, new_weights, 0.0)
    new_gain_one, new_gain_two, new_gains = adam_step(
        gain_master, gain_one, gain_two, gain_grad, step, 0.0, gain_rate
    )
    return (
        block_out,
        input_grad,
        weight_grad,
        new_weights,
        new_one,
        new_two,
        gain_grad,
        new_gains,
        new_gain_one,
        new_gain_two,
    )


def solution(mesh):
    return jax.shard_map(
        shards,
        mesh=mesh,
        in_specs=(
            P(("dp", "fsdp"), None),
            P("dp", None),
            P(("dp", "fsdp"), None),
            P(),
            P(("dp", "fsdp"), None, None),
            P(("dp", "fsdp"), None, None),
            P(("dp", "fsdp"), None, None),
            P(None, ("dp", "fsdp")),
            P(None, ("dp", "fsdp")),
            P(None, ("dp", "fsdp")),
        ),
        out_specs=(
            P(("dp", "fsdp"), None),
            P(("dp", "fsdp"), None),
            P(("dp", "fsdp"), None, None),
            P(("dp", "fsdp"), None, None),
            P(("dp", "fsdp"), None, None),
            P(("dp", "fsdp"), None, None),
            P(None, ("dp", "fsdp")),
            P(None, ("dp", "fsdp")),
            P(None, ("dp", "fsdp")),
            P(None, ("dp", "fsdp")),
        ),
        check_vma=False,
    )
```
